32 devices in a mesh: dp: 2 (over x), fsdp: 16 (over z, y, core).
Axes of the slice: x: 2, y: 2, z: 4, core: 2. Of those that a mesh axis runs over, the one named last changes fastest.
Arguments:
- tokens: int32 [32, 1024], P(('dp', 'fsdp')), may hold values from 0 to 50256
- positions: int32 [32, 192], P(('dp', 'fsdp')), may hold values from 0 to 1023, as said below
- strata: int32 [32], P(('dp', 'fsdp')), may hold values from 0 to 15, as said below
- groups: int32 [32], P(('dp', 'fsdp')), may hold values from 0 to 1, as said below
- embedding: float32 [768, 50304], P('fsdp'), may hold values from -6 to 6
- out_table: float32 [50304, 768], P('fsdp')
- norm_gains: float32 [3, 768], replicated, may hold values from 0.5 to 1.5
- attention: float32 [4, 768, 768], P(None, 'fsdp')
- feedforward: float32 [2, 3072, 768], P(None, 'fsdp')
- embed_moment_one: float32 [768, 50304], P('fsdp'), may hold values from -1.5258789e-05 to 1.5258789e-05
- embed_moment_two: float32 [768, 50304], P('fsdp'), may hold values from 6.3e-10 to 2.5e-09
- out_moment_one: float32 [50304, 768], P('fsdp'), may hold values from -7.6293945e-05 to 7.6293945e-05
- out_moment_two: float32 [50304, 768], P('fsdp'), may hold values from 1.2e-08 to 4.8e-08
- gain_moment_one: float32 [3, 768], replicated, may hold values from -0.0007324219 to 0.0007324219
- gain_moment_two: float32 [3, 768], replicated, may hold values from 6.3e-08 to 2.5e-07
- attention_left: float32 [4, 768, 768], P(None, 'fsdp'), as said below
- attention_right: float32 [4, 768, 768], P(None, 'fsdp'), as said below
- attention_left_root: float32 [4, 768, 768], P(None, 'fsdp'), as said below
- attention_right_root: float32 [4, 768, 768], P(None, 'fsdp'), as said below
- ff_left: float32 [2, 3072, 3072], P(None, 'fsdp'), as said below
- ff_right: float32 [2, 768, 768], P(None, 'fsdp'), as said below
- ff_left_root: float32 [2, 3072, 3072], P(None, 'fsdp'), as said below
- ff_right_root: float32 [2, 768, 768], P(None, 'fsdp'), as said below
- ema_embed: float32 [768, 50304], P('fsdp'), may hold values from -6 to 6
- ema_out: float32 [50304, 768], P('fsdp'), may hold values from -0.21875 to 0.21875
- ema_gains: float32 [3, 768], replicated, may hold values from 0.5 to 1.5
- ema_attention: float32 [4, 768, 768], P(None, 'fsdp'), may hold values from -0.21875 to 0.21875
- ema_feedforward: float32 [2, 3072, 768], P(None, 'fsdp'), may hold values from -0.21875 to 0.21875
Outputs:
- loss_sum: float32 [], replicated
- clip_norm: float32 [], replicated
- embed_new: float32 [768, 50304], P('fsdp')
- embed_one_new: float32 [768, 50304], P('fsdp')
- embed_two_new: float32 [768, 50304], P('fsdp')
- out_new: float32 [50304, 768], P('fsdp')
- out_one_new: float32 [50304, 768], P('fsdp')
- out_two_new: float32 [50304, 768], P('fsdp')
- gains_new: float32 [3, 768], replicated
- gains_one_new: float32 [3, 768], replicated
- gains_two_new: float32 [3, 768], replicated
- attention_new: float32 [4, 768, 768], P(None, 'fsdp')
- attention_grad: float32 [4, 768, 768], P(None, 'fsdp')
- attention_left_new: float32 [4, 768, 768], P(None, 'fsdp')
- attention_right_new: float32 [4, 768, 768], P(None, 'fsdp')
- ff_new: float32 [2, 3072, 768], P(None, 'fsdp')
- ff_grad: float32 [2, 3072, 768], P(None, 'fsdp')
- ff_left_new: float32 [2, 3072, 3072], P(None, 'fsdp')
- ff_right_new: float32 [2, 768, 768], P(None, 'fsdp')
- ema_embed_new: float32 [768, 50304], P('fsdp')
- ema_out_new: float32 [50304, 768], P('fsdp')
- ema_gains_new: float32 [3, 768], replicated
- ema_attention_new: float32 [4, 768, 768], P(None, 'fsdp')
- ema_ff_new: float32 [2, 3072, 768], P(None, 'fsdp')
The draws below stay inside these ranges and needn't reach their ends.
Inputs may be any that keep to these rules, and one draw needn't show every extreme that they name: Each row holds 192 different positions of its sequence. `strata`: every stratum from 0 to 15 is taken by some sequence. `groups`: some sequence of stratum 16 - 1 is in group 1. `attention_left`: symmetric in its last two dimensions. `attention_right`: symmetric in its last two dimensions. `attention_left_root`: symmetric in its last two dimensions. `attention_right_root`: symmetric in its last two dimensions. `ff_left`: symmetric in its last two dimensions. `ff_right`: symmetric in its last two dimensions. `ff_left_root`: symmetric in its last two dimensions. `ff_right_root`: symmetric in its last two dimensions.
All inputs are finite; a program needn't handle non-finite values.
Results may differ from the reference program's by a relative error of at most 0.012.
Values may be sent and summed in bfloat16 or wider, within the bound.
A program may use at most 448 MiB of HBM per device.

```python
import math
import jax
import jax.numpy as jnp
import numpy as np
from jax import lax

D = 768
HEADS = 12
HEAD = 64
FF = 3072
VOCAB = 50304
MASK_ID = 50257
LEN = 1024
CAP = 192
STRATA = 16
STEP = 10
NSEQ = 32


clip_level = 1.0


def grad_size():
    return clip_level / (2 * VOCAB * D + 4 * D * D + 2 * FF * D + 3 * D) ** 0.5


def stat_size(stack_count, matrix_order):
    return 0.15 * clip_level ** 2 / (2.4 * (stack_count * matrix_order) ** 0.5)


def strata_draw(key):
    perm_key, group_key = jax.random.split(key)
    strata = (jax.random.permutation(perm_key, NSEQ) % STRATA).astype(jnp.int32)
    picked = jax.random.randint(group_key, (NSEQ,), 0, 10) < 3
    groups = jnp.where(picked | (strata == STRATA - 1), 1, 0).astype(jnp.int32)
    return (strata, groups)


def draw_strata(key, part):
    return strata_draw(key)[0]


def draw_groups(key, part):
    return strata_draw(key)[1]


def draw_positions(key, part):
    key = jax.random.fold_in(key, 11)
    row_keys = jax.random.split(key, NSEQ)
    return jax.vmap(lambda row_key: jax.random.permutation(row_key, LEN)[:CAP])(row_keys).astype(jnp.int32)


def draw_out_table(key, part):
    key = jax.random.fold_in(key, 12)
    top_gain = 2.0
    rising = 1.0 + top_gain * jnp.arange(VOCAB, dtype=jnp.float32)[:, None] / (VOCAB - 1)
    return jax.random.normal(key, (VOCAB, D), jnp.float32) * rising / D ** 0.5


def draw_attention(key, part):
    key = jax.random.fold_in(key, 13)
    scales = jnp.array([1.0, 1.0, 1.0, 8.0], jnp.float32)[:, None, None] / D ** 0.5
    return jax.random.normal(key, (4, D, D), jnp.float32) * scales


def draw_feedforward(key, part):
    key = jax.random.fold_in(key, 14)
    scales = jnp.array([D ** (-0.5), FF ** (-0.5)], jnp.float32)[:, None, None]
    return jax.random.normal(key, (2, FF, D), jnp.float32) * scales


def spd_draw(key, stack_count, matrix_order, magnitude):
    diag_key, spread_key = jax.random.split(key)
    diagonal = jnp.exp(jax.random.uniform(diag_key, (stack_count, matrix_order), jnp.float32, 0.0, jnp.log(4.0)))
    spread_part = jax.random.uniform(spread_key, (stack_count, matrix_order, matrix_order), jnp.float32, -1.0, 1.0) / matrix_order ** 0.5
    symmetric = 0.5 * (spread_part + jnp.swapaxes(spread_part, 1, 2))
    return (symmetric + diagonal[:, :, None] * jnp.eye(matrix_order, dtype=jnp.float32)[None]) * magnitude


def draw_attention_left(key, part):
    key = jax.random.fold_in(key, 15)
    return spd_draw(key, 4, D, stat_size(4, D))


def draw_attention_right(key, part):
    key = jax.random.fold_in(key, 16)
    return spd_draw(key, 4, D, stat_size(4, D))


def draw_attention_left_root(key, part):
    key = jax.random.fold_in(key, 17)
    return spd_draw(key, 4, D, (D * grad_size() ** 2) ** (-0.25))


def draw_attention_right_root(key, part):
    key = jax.random.fold_in(key, 18)
    return spd_draw(key, 4, D, (D * grad_size() ** 2) ** (-0.25))


def draw_ff_left(key, part):
    key = jax.random.fold_in(key, 19)
    return spd_draw(key, 2, FF, stat_size(2, FF))


def draw_ff_right(key, part):
    key = jax.random.fold_in(key, 20)
    return spd_draw(key, 2, D, stat_size(2, D))


def draw_ff_left_root(key, part):
    key = jax.random.fold_in(key, 21)
    return spd_draw(key, 2, FF, (D * grad_size() ** 2) ** (-0.25))


def draw_ff_right_root(key, part):
    key = jax.random.fold_in(key, 22)
    return spd_draw(key, 2, D, (FF * grad_size() ** 2) ** (-0.25))


def set_ends(drawn, stream_key, low, top_value):
    shape = drawn.shape
    index_at = [jax.random.randint(jax.random.fold_in(stream_key, axis), (), 0, shape[axis]) for axis in range(len(shape))]
    drawn = drawn.at[tuple(index_at)].set(low)
    longest = shape.index(max(shape))
    index_at[longest] = (index_at[longest] + 1) % shape[longest]
    return drawn.at[tuple(index_at)].set(top_value)


def steps_of(own_key, dims, shards, least, high):
    def one(axis_at, parts):
        heights = jax.random.uniform(jax.random.fold_in(jax.random.fold_in(own_key, 6), axis_at), (parts,), jnp.float32, least / len(shards), high / len(shards))
        return jnp.repeat(jnp.exp(heights), dims[axis_at] // parts).reshape((-1,) + (1,) * (len(dims) - axis_at - 1))

    factor_of = one(*shards[0])
    for cut in shards[1:]:
        factor_of = factor_of * one(*cut)
    return factor_of


def rank_bounds(count, lean):
    portions = [(1 << 20) // math.isqrt(rank ** lean) + 1 for rank in range(1, count + 1)]
    scale = 1 + sum(portions) // (1 << 30)
    return np.cumsum(np.array([max(1, weight // scale) for weight in portions]))


def ranked_ids(rng, shape, amount, lean):
    grid = rank_bounds(amount, lean)
    ticket = jax.random.randint(jax.random.fold_in(rng, 1), shape, 0, int(grid[amount - 1]))
    standing = jnp.searchsorted(jnp.asarray(grid, jnp.int32), ticket, side="right")
    return jax.random.permutation(jax.random.fold_in(rng, 2), amount)[standing].astype(jnp.int32)


def gaussian(key, shape, width, limit, pieces=(), kind=jnp.bfloat16):
    drawn = jax.random.normal(key, shape, jnp.float32) * width
    if len(pieces) > 0:
        drawn = steps_of(key, shape, pieces, -0.22, 0.18) * drawn
    return jnp.clip(drawn, min=-limit, max=limit).astype(kind)


def setup_inputs(seed: int = 0) -> dict:
    seeds = jax.random.split(jax.random.key(seed), 29)
    return {
        "tokens": set_ends(ranked_ids(seeds[0], (NSEQ, LEN), MASK_ID, 2), jax.random.fold_in(seeds[0], 3), 0, MASK_ID - 1).astype(jnp.int32),
        "positions": draw_positions(jax.random.fold_in(seeds[28], 71), 0),
        "strata": draw_strata(jax.random.fold_in(seeds[28], 71), 0),
        "groups": draw_groups(jax.random.fold_in(seeds[28], 71), 0),
        "embedding": gaussian(seeds[4], (D, VOCAB), 1.0, 6.0, ((0, 16),), jnp.float32),
        "out_table": draw_out_table(jax.random.fold_in(seeds[28], 71), 0),
        "norm_gains": jnp.clip(1.0 + 0.1 * jax.random.normal(seeds[6], (3, D), jnp.float32), 0.5, 1.5),
        "attention": draw_attention(jax.random.fold_in(seeds[28], 71), 0),
        "feedforward": draw_feedforward(jax.random.fold_in(seeds[28], 71), 0),
        "embed_moment_one": gaussian(seeds[9], (D, VOCAB), 0.0000025, 1.52587890625e-05, ((0, 16),), jnp.float32),
        "embed_moment_two": jnp.clip(jnp.exp(math.log(2.4999999848063226e-09) - 1.3783262 * jax.random.uniform(seeds[10], (D, VOCAB), jnp.float32) ** steps_of(seeds[10], (D, VOCAB), ((0, 16),), -0.2, 0.2)), 6.299999966152825e-10, 2.4999999848063226e-09),
        "out_moment_one": gaussian(seeds[11], (VOCAB, D), 0.000012, 7.62939453125e-05, ((0, 16),), jnp.float32),
        "out_moment_two": jnp.clip(jnp.exp(math.log(4.800000041882413e-08) - 1.3862944 * jax.random.uniform(seeds[12], (VOCAB, D), jnp.float32) ** steps_of(seeds[12], (VOCAB, D), ((0, 16),), -0.2, 0.2)), 1.2000000104706032e-08, 4.800000041882413e-08),
        "gain_moment_one": gaussian(seeds[13], (3, D), 0.00012, 0.0007324219, (), jnp.float32),
        "gain_moment_two": jnp.clip(jnp.exp(jax.random.uniform(seeds[14], (3, D), jnp.float32, math.log(6.30000016599297e-08), math.log(2.499999993688107e-07))), 6.30000016599297e-08, 2.499999993688107e-07),
        "attention_left": draw_attention_left(jax.random.fold_in(seeds[28], 71), 0),
        "attention_right": draw_attention_right(jax.random.fold_in(seeds[28], 71), 0),
        "attention_left_root": draw_attention_left_root(jax.random.fold_in(seeds[28], 71), 0),
        "attention_right_root": draw_attention_right_root(jax.random.fold_in(seeds[28], 71), 0),
        "ff_left": draw_ff_left(jax.random.fold_in(seeds[28], 71), 0),
        "ff_right": draw_ff_right(jax.random.fold_in(seeds[28], 71), 0),
        "ff_left_root": draw_ff_left_root(jax.random.fold_in(seeds[28], 71), 0),
        "ff_right_root": draw_ff_right_root(jax.random.fold_in(seeds[28], 71), 0),
        "ema_embed": gaussian(seeds[23], (D, VOCAB), 1.0, 6.0, ((0, 16),), jnp.float32),
        "ema_out": gaussian(seeds[24], (VOCAB, D), D ** -0.5, 0.21875, ((0, 16),), jnp.float32),
        "ema_gains": jnp.clip(1.0 + 0.1 * jax.random.normal(seeds[25], (3, D), jnp.float32), 0.5, 1.5),
        "ema_attention": gaussian(seeds[26], (4, D, D), D ** -0.5, 0.21875, ((1, 16),), jnp.float32),
        "ema_feedforward": gaussian(seeds[27], (2, FF, D), D ** -0.5, 0.21875, ((1, 16),), jnp.float32),
    }


highest = lax.Precision.HIGHEST
norm_eps = 1e-05
clip_level = 1.0
beta_one = 0.9
beta_two = 0.95
adam_eps = 1e-08
adam_decay = 0.01
rate_embed = 2.0
rate_out = 0.25
rate_gain = 0.5
rate_shampoo = 0.3
shampoo_decay = 0.01
stat_decay = 0.5
ema_decay = 0.7
score_scale = 0.125

@jax.custom_vjp
def low(v):
    return lax.optimization_barrier(v.astype(jnp.bfloat16)).astype(jnp.float32)

@jax.custom_vjp
def low_back(v):
    return v

def low_keep(v):
    return (low(v), None)

def low_pass(kept, grad):
    return (grad,)

def back_keep(v):
    return (v, None)

def back_low(kept, grad):
    return (low(grad),)
low.defvjp(low_keep, low_pass)
low_back.defvjp(back_keep, back_low)

def matmul(left_side, right_side):
    return jnp.dot(left_side, right_side, precision=highest)

def normed(inputs, gain_row):
    centred = inputs - lax.optimization_barrier(jnp.mean(inputs, axis=-1, keepdims=True))
    spread = lax.optimization_barrier(jnp.mean(centred * centred, axis=-1, keepdims=True))
    return centred * lax.rsqrt(spread + norm_eps) * gain_row

def rotary_tables(length, half_width):
    inverse = 10000.0 ** (-jnp.arange(half_width, dtype=jnp.float32) / half_width)
    angles = jnp.arange(length, dtype=jnp.float32)[:, None] * inverse[None, :]
    return (jnp.cos(angles), jnp.sin(angles))

def rotate(inputs, cosine_table, sine_table):
    half_width = inputs.shape[-1] // 2
    cosine_part = cosine_table[:, None, :]
    sine_part = sine_table[:, None, :]
    first_half = inputs[..., :half_width]
    second_half = inputs[..., half_width:]
    return jnp.concatenate([first_half * cosine_part - second_half * sine_part, second_half * cosine_part + first_half * sine_part], axis=-1)

def sequence_loss(params, ids_in, places, targets, row_weight, cosine_table, sine_table):
    embedding, out_table, norm_gains, attention, feedforward = params
    attn_low = low(attention)
    ff_low = low(feedforward)
    x_first = low_back(jnp.take(low(embedding), ids_in, axis=1).T)
    hidden_first = low(normed(x_first, norm_gains[0]))
    query_raw = low_back(matmul(hidden_first, attn_low[0])).reshape(LEN, HEADS, HEAD)
    key_raw = low_back(matmul(hidden_first, attn_low[1])).reshape(LEN, HEADS, HEAD)
    value_rows = low(low_back(matmul(hidden_first, attn_low[2]))).reshape(LEN, HEADS, HEAD)
    query_rows = low(rotate(query_raw, cosine_table, sine_table))
    key_rows = low(rotate(key_raw, cosine_table, sine_table))
    scores = low_back(jnp.einsum('qhd,khd->hqk', query_rows, key_rows, precision=highest) * score_scale)
    weights_low = low(jax.nn.softmax(scores, axis=-1))
    mixed_rows = jnp.einsum('hqk,khd->qhd', weights_low, value_rows, precision=highest).reshape(LEN, D)
    mixed_rows = low_back(low(mixed_rows))
    x_second = x_first + low_back(matmul(mixed_rows, attn_low[3]))
    hidden_second = low(normed(x_second, norm_gains[1]))
    preactivation = low_back(matmul(hidden_second, ff_low[0].T))
    activation_output = low(jax.nn.gelu(preactivation, approximate=True))
    x_third = x_second + low_back(matmul(activation_output, ff_low[1]))
    final_rows = normed(x_third, norm_gains[2])
    head_in = low(final_rows[places])
    logits = low_back(matmul(head_in, low(out_table).T))
    columns = jnp.arange(VOCAB, dtype=jnp.int32)
    logits = jnp.where(columns[None, :] < MASK_ID, logits, -jnp.inf)
    log_total = jax.nn.logsumexp(logits, axis=-1)
    chosen_logit = jnp.take_along_axis(logits, targets[:, None], axis=1)[:, 0]
    return jnp.sum(row_weight * (log_total - chosen_logit))

def adamw(weight, moment_one, moment_two, gradient, step_rate):
    one_new = beta_one * moment_one + (1 - beta_one) * gradient
    two_new = beta_two * moment_two + (1 - beta_two) * gradient * gradient
    one_hat = one_new / (1 - beta_one ** STEP)
    two_hat = two_new / (1 - beta_two ** STEP)
    weight_new = weight - step_rate * (one_hat / (jnp.sqrt(two_hat) + adam_eps) + adam_decay * weight)
    return (weight_new, one_new, two_new)

def shampoo(weight, gradient, left_stat, right_stat, left_root, right_root):
    left_new = stat_decay * left_stat + (1 - stat_decay) * jnp.einsum('nik,njk->nij', gradient, gradient, precision=highest)
    right_new = stat_decay * right_stat + (1 - stat_decay) * jnp.einsum('nki,nkj->nij', gradient, gradient, precision=highest)
    update = jnp.einsum('nij,njk->nik', left_root, gradient, precision=highest)
    update = jnp.einsum('nik,nkl->nil', update, right_root, precision=highest)
    return (weight - rate_shampoo * (update + shampoo_decay * weight), left_new, right_new)

def reference(tokens, positions, strata, groups, embedding, out_table, norm_gains, attention, feedforward, embed_moment_one, embed_moment_two, out_moment_one, out_moment_two, gain_moment_one, gain_moment_two, attention_left, attention_right, attention_left_root, attention_right_root, ff_left, ff_right, ff_left_root, ff_right_root, ema_embed, ema_out, ema_gains, ema_attention, ema_feedforward):
    counts = jnp.maximum(1, (strata + 1) * CAP * (1 + groups) // (2 * STRATA))
    slot_iota = jnp.arange(CAP, dtype=jnp.int32)
    in_use = slot_iota[None, :] < counts[:, None]
    rows_index = jnp.arange(NSEQ, dtype=jnp.int32)[:, None]
    marked = jnp.zeros((NSEQ, LEN), jnp.int32).at[rows_index, positions].max(in_use.astype(jnp.int32))
    ids_in = jnp.where(marked > 0, MASK_ID, tokens)
    targets = jnp.take_along_axis(tokens, positions, axis=1)
    row_weight = jnp.where(in_use, LEN / counts[:, None].astype(jnp.float32), 0.0).astype(jnp.float32)
    cosine_table, sine_table = rotary_tables(LEN, HEAD // 2)
    params = (embedding, out_table, norm_gains, attention, feedforward)

    def loss_of(params):

        def accumulate(running, inputs):
            return (running + jax.checkpoint(sequence_loss)(params, *inputs, cosine_table, sine_table), None)
        running, _ = lax.scan(accumulate, jnp.zeros((), jnp.float32), (ids_in, positions, targets, row_weight))
        return running
    loss_sum, pullback = jax.vjp(loss_of, params)
    gradients = pullback(jnp.ones((), jnp.float32) / NSEQ)[0]
    squares = sum((jnp.sum(member * member) for member in gradients))
    clip_norm = jnp.sqrt(squares)
    factor = jnp.minimum(1.0, clip_level / clip_norm)
    clipped = [member * factor for member in gradients]
    embed_new, embed_one_new, embed_two_new = adamw(embedding, embed_moment_one, embed_moment_two, clipped[0], rate_embed)
    out_new, out_one_new, out_two_new = adamw(out_table, out_moment_one, out_moment_two, clipped[1], rate_out)
    gains_new, gains_one_new, gains_two_new = adamw(norm_gains, gain_moment_one, gain_moment_two, clipped[2], rate_gain)
    attention_new, attention_left_new, attention_right_new = shampoo(attention, clipped[3], attention_left, attention_right, attention_left_root, attention_right_root)
    ff_new, ff_left_new, ff_right_new = shampoo(feedforward, clipped[4], ff_left, ff_right, ff_left_root, ff_right_root)
    return (loss_sum, clip_norm, embed_new, embed_one_new, embed_two_new, out_new, out_one_new, out_two_new, gains_new, gains_one_new, gains_two_new, attention_new, clipped[3], attention_left_new, attention_right_new, ff_new, clipped[4], ff_left_new, ff_right_new, ema_decay * ema_embed + (1 - ema_decay) * embed_new, ema_decay * ema_out + (1 - ema_decay) * out_new, ema_decay * ema_gains + (1 - ema_decay) * gains_new, ema_decay * ema_attention + (1 - ema_decay) * attention_new, ema_decay * ema_feedforward + (1 - ema_decay) * ff_new)
```

```python
import functools

import jax
import jax.numpy as jnp
from jax import lax
from jax.experimental import pallas as pl
from jax.experimental.pallas import tpu as pltpu
from jax.sharding import PartitionSpec as P

F32, BF16 = jnp.float32, jnp.bfloat16
HEAD = 64
EPS = 1e-5
VL = 60 * 1024 * 1024

def dot(a, b, ca, cb):
    return lax.dot_general(a, b, (((ca,), (cb,)), ((), ())), preferred_element_type=F32)

def params(limit=VL):
    return pltpu.CompilerParams(vmem_limit_bytes=limit)

def whole(shape):
    return pl.BlockSpec(shape, lambda *a: (0,) * len(shape))

def attn_fwd_kernel(x_ref, gain_ref, cos_ref, sin_ref, w_ref, h_ref, q_ref, k_ref, v_ref, m_ref, lse_ref, kn_ref):
    width, length = x_ref.shape
    block = q_ref.shape[0]
    heads = block // HEAD
    half = HEAD // 2
    step = min(256, length)

    @pl.when(pl.program_id(0) == 0)
    def _():
        def cols(c, carry):
            at = pl.ds(pl.multiple_of(c * 128, 128), 128)
            x = x_ref[:, at].astype(F32)
            centred = x - jnp.mean(x, axis=0, keepdims=True)
            spread = jnp.mean(centred * centred, axis=0, keepdims=True)
            h_ref[:, at] = (centred * lax.rsqrt(spread + EPS) * gain_ref[...]).astype(BF16)
            return carry
        lax.fori_loop(0, length // 128, cols, 0)

    cosine, sine = cos_ref[...], sin_ref[...]
    hidden = h_ref[...]
    for j, out in ((0, q_ref), (1, k_ref)):
        p = dot(w_ref[j], hidden, 0, 0)
        for h in range(heads):
            a = p[h * HEAD : h * HEAD + half]
            b = p[h * HEAD + half : (h + 1) * HEAD]
            ra = (a * cosine - b * sine).astype(BF16)
            rb = (b * cosine + a * sine).astype(BF16)
            if j == 0:
                ra, rb = ra * 0.125, rb * 0.125
            out[h * HEAD : h * HEAD + half, :] = ra
            out[h * HEAD + half : (h + 1) * HEAD, :] = rb
    v_ref[...] = dot(w_ref[2], hidden, 0, 0).astype(BF16)
    for h in range(heads):
        rows = slice(h * HEAD, (h + 1) * HEAD)
        kn_ref[h] = k_ref[rows, :].T
    for h in range(heads):
        rows = slice(h * HEAD, (h + 1) * HEAD)
        def one(c, carry, h=h, rows=rows):
            at = pl.ds(pl.multiple_of(c * step, step), step)
            s = dot(kn_ref[h], q_ref[rows, at], 1, 0)
            top = jnp.max(s, axis=0, keepdims=True)
            e = jnp.exp(s - top)
            total = jnp.sum(e, axis=0, keepdims=True)
            o = dot(v_ref[rows, :], e.astype(BF16), 1, 0)
            m_ref[rows, at] = (o / total).astype(BF16)
            lse_ref[0, h : h + 1, at] = top + jnp.log(total)
            return carry
        lax.fori_loop(0, length // step, one, 0, unroll=True)

def attn_fwd(xT, gain, cosT, sinT, w):
    width, length = xT.shape
    block = 256
    n = width // block
    col = pl.BlockSpec((block, length), lambda i: (i, 0))
    t = jax.ShapeDtypeStruct((width, length), BF16)
    return pl.pallas_call(
        attn_fwd_kernel, grid=(n,), name="attn_fwd",
        in_specs=[whole((width, length)), whole((width, 1)), whole(cosT.shape), whole(sinT.shape),
                  pl.BlockSpec((3, width, block), lambda i: (0, 0, i))],
        out_specs=[whole((width, length)), col, col, col, col, pl.BlockSpec((1, 8, length), lambda i: (i, 0, 0))],
        out_shape=[t, t, t, t, t, jax.ShapeDtypeStruct((n, 8, length), F32)],
        scratch_shapes=[pltpu.VMEM((block // HEAD, length, HEAD), BF16)],
        compiler_params=params(),
    )(xT, gain, cosT, sinT, w)

def attn_bwd_kernel(x_ref, gain_ref, cos_ref, sin_ref, sg_ref, h_ref, q_ref, k_ref, v_ref, m_ref, lse_ref, w_ref, wo_ref,
                    first_ref, gg_ref, dw_ref, dwo_ref, hg_ref, low_ref, do_ref, kn_ref, vn_ref, dk_ref, dv_ref, dq_ref):
    width, length = x_ref.shape
    block = q_ref.shape[0]
    heads = block // HEAD
    half = HEAD // 2
    step = min(256, length)
    i = pl.program_id(0)

    @pl.when(i == 0)
    def _():
        low_ref[...] = sg_ref[...].astype(BF16)
        hg_ref[...] = jnp.zeros_like(hg_ref)

    do_ref[...] = dot(wo_ref[0], low_ref[...], 1, 0).astype(BF16)
    dwo_ref[0] = dot(m_ref[...], low_ref[...], 1, 1).astype(dwo_ref.dtype)
    cosine, sine = cos_ref[...], sin_ref[...]
    for h in range(heads):
        rows = slice(h * HEAD, (h + 1) * HEAD)
        kn_ref[h] = k_ref[rows, :].T
        vn_ref[h] = v_ref[rows, :].T
    for h in range(heads):
        rows = slice(h * HEAD, (h + 1) * HEAD)
        for c in range(length // step):
            at = slice(c * step, (c + 1) * step)
            s = dot(kn_ref[h], q_ref[rows, at], 1, 0)
            p = jnp.exp(s - lse_ref[0, h : h + 1, at])
            dp = dot(vn_ref[h], do_ref[rows, at], 1, 0)
            centre = jnp.sum(p * dp, axis=0, keepdims=True)
            ds = (p * (dp - centre)).astype(BF16)
            pb = p.astype(BF16)
            dv = dot(do_ref[rows, at], pb, 1, 1)
            dk = dot(q_ref[rows, at], ds, 1, 1)
            if c == 0:
                dv_ref[rows, :] = dv
                dk_ref[rows, :] = dk
            else:
                dv_ref[rows, :] += dv
                dk_ref[rows, :] += dk
            dq_ref[rows, at] = dot(k_ref[rows, :], ds, 1, 0) * 0.125
    hidden = h_ref[...]
    for j, ref in ((0, dq_ref), (1, dk_ref), (2, dv_ref)):
        if j == 2:
            g = ref[...].astype(BF16)
        else:
            parts = []
            for h in range(heads):
                a = ref[h * HEAD : h * HEAD + half, :]
                b = ref[h * HEAD + half : (h + 1) * HEAD, :]
                parts += [(a * cosine + b * sine).astype(BF16), (b * cosine - a * sine).astype(BF16)]
            g = jnp.concatenate(parts, axis=0)
        dw_ref[j] = dot(hidden, g, 1, 1).astype(dw_ref.dtype)
        hg_ref[...] += dot(w_ref[j], g, 1, 0)

    @pl.when(i == pl.num_programs(0) - 1)
    def _():
        def cols(c, acc):
            at = pl.ds(pl.multiple_of(c * 128, 128), 128)
            dx, gg = ln_back(x_ref[:, at].astype(F32), hg_ref[:, at], gain_ref[...])
            first_ref[:, at] = (sg_ref[:, at] + dx).astype(BF16)
            return acc + gg
        acc = lax.fori_loop(0, length // 128, cols, jnp.zeros((width, 128), F32))
        gg_ref[...] = jnp.sum(acc, axis=1, keepdims=True)

def ln_back(x, g, gain):
    centred = x - jnp.mean(x, axis=0, keepdims=True)
    spread = jnp.mean(centred * centred, axis=0, keepdims=True)
    rs = lax.rsqrt(spread + EPS)
    xh = centred * rs
    gx = g * gain
    dx = rs * (gx - jnp.mean(gx, axis=0, keepdims=True) - xh * jnp.mean(gx * xh, axis=0, keepdims=True))
    return dx, g * xh

def attn_bwd(xT, gain, cosT, sinT, sg, hT, q, k, v, m, lse, w):
    width, length = xT.shape
    block = 256
    n = width // block
    col = pl.BlockSpec((block, length), lambda i: (i, 0))
    full = whole((width, length))
    return pl.pallas_call(
        attn_bwd_kernel, grid=(n,), name="attn_bwd",
        in_specs=[full, whole((width, 1)), whole(cosT.shape), whole(sinT.shape), full, full, col, col, col, col,
                  pl.BlockSpec((1, 8, length), lambda i: (i, 0, 0)),
                  pl.BlockSpec((3, width, block), lambda i: (0, 0, i)),
                  pl.BlockSpec((1, block, width), lambda i: (3, i, 0))],
        out_specs=[full, whole((width, 1)), pl.BlockSpec((3, width, block), lambda i: (0, 0, i)), pl.BlockSpec((1, block, width), lambda i: (0, i, 0))],
        out_shape=[jax.ShapeDtypeStruct((width, length), BF16), jax.ShapeDtypeStruct((width, 1), F32),
                   jax.ShapeDtypeStruct((3, width, width), BF16), jax.ShapeDtypeStruct((1, width, width), BF16)],
        scratch_shapes=[pltpu.VMEM((width, length), F32), pltpu.VMEM((width, length), BF16), pltpu.VMEM((block, length), BF16),
                        pltpu.VMEM((block // HEAD, length, HEAD), BF16), pltpu.VMEM((block // HEAD, length, HEAD), BF16),
                        pltpu.VMEM((block, length), F32), pltpu.VMEM((block, length), F32), pltpu.VMEM((block, length), F32)],
        compiler_params=params(),
    )(xT, gain, cosT, sinT, sg, hT, q, k, v, m, lse, w, w)
def ff_fwd_kernel(x_ref, m_ref, g2_ref, g3_ref, pos_ref, wo_ref, up_ref, down_ref,
                  x2_ref, h2_ref, pre_ref, act_ref, x3_ref, head_ref, fin_ref):
    width, length = x_ref.shape
    i = pl.program_id(0)

    @pl.when(i == 0)
    def _():
        x2_ref[...] = x_ref[...].astype(F32) + dot(wo_ref[0], m_ref[...], 0, 0)
        x3_ref[...] = x2_ref[...]
        def cols(c, carry):
            at = pl.ds(pl.multiple_of(c * 128, 128), 128)
            h2_ref[:, at] = ln(x2_ref[:, at], g2_ref[...]).astype(BF16)
            return carry
        lax.fori_loop(0, length // 128, cols, 0)

    pre = dot(up_ref[0], h2_ref[...], 1, 0)
    pre_ref[...] = pre
    act = jax.nn.gelu(pre, approximate=True).astype(BF16)
    act_ref[...] = act
    x3_ref[...] += dot(down_ref[0], act, 0, 0)

    @pl.when(i == pl.num_programs(0) - 1)
    def _():
        def cols(c, carry):
            at = pl.ds(pl.multiple_of(c * 128, 128), 128)
            fin_ref[:, at] = ln(x3_ref[:, at], g3_ref[...]).astype(BF16)
            return carry
        lax.fori_loop(0, length // 128, cols, 0)
        slots = pos_ref.shape[0]
        onehot = (pos_ref[...] == lax.broadcasted_iota(jnp.int32, (slots, length), 1)).astype(BF16)
        head_ref[...] = dot(onehot, fin_ref[...], 1, 1).astype(BF16)

def ln(x, gain):
    centred = x - jnp.mean(x, axis=0, keepdims=True)
    spread = jnp.mean(centred * centred, axis=0, keepdims=True)
    return centred * lax.rsqrt(spread + EPS) * gain

def ff_fwd(xT, m, g2, g3, pos, attn_w, ff_w):
    width, length = xT.shape
    hidden = ff_w.shape[1]
    block = 512
    n = hidden // block
    slots = pos.shape[0]
    full = whole((width, length))
    col = pl.BlockSpec((block, length), lambda i: (i, 0))
    f = jax.ShapeDtypeStruct((width, length), F32)
    return pl.pallas_call(
        ff_fwd_kernel, grid=(n,), name="ff_fwd",
        in_specs=[full, full, whole((width, 1)), whole((width, 1)), whole((slots, 1)),
                  pl.BlockSpec((1, width, width), lambda i: (3, 0, 0)),
                  pl.BlockSpec((1, block, width), lambda i: (0, i, 0)),
                  pl.BlockSpec((1, block, width), lambda i: (1, i, 0))],
        out_specs=[full, full, col, col, full, whole((slots, width))],
        out_shape=[f, jax.ShapeDtypeStruct((width, length), BF16), jax.ShapeDtypeStruct((hidden, length), F32),
                   jax.ShapeDtypeStruct((hidden, length), BF16), f, jax.ShapeDtypeStruct((slots, width), BF16)],
        scratch_shapes=[pltpu.VMEM((width, length), BF16)],
        compiler_params=params(),
    )(xT, m, g2, g3, pos, attn_w, ff_w, ff_w)

def ff_bwd_kernel(x3_ref, x2_ref, h2_ref, rg_ref, pos_ref, g2_ref, g3_ref, pre_ref, act_ref, up_ref, down_ref,
                  sg_ref, gg2_ref, gg3_ref, dup_ref, ddn_ref, low_ref, hg_ref):
    width, length = x3_ref.shape
    i = pl.program_id(0)
    slots = pos_ref.shape[0]

    @pl.when(i == 0)
    def _():
        rows = rg_ref[...]
        high = rows.astype(BF16)
        rest = (rows - high.astype(F32)).astype(BF16)
        hg_ref[...] = jnp.zeros_like(hg_ref)
        def cols(c, acc):
            at = pl.ds(pl.multiple_of(c * 128, 128), 128)
            onehot = (pos_ref[...] == c * 128 + lax.broadcasted_iota(jnp.int32, (slots, 128), 1)).astype(BF16)
            fg = dot(high, onehot, 0, 0) + dot(rest, onehot, 0, 0)
            dx, gg = ln_back(x3_ref[:, at], fg, g3_ref[...])
            sg_ref[:, at] = dx
            low_ref[:, at] = dx.astype(BF16)
            return acc + gg
        acc = lax.fori_loop(0, length // 128, cols, jnp.zeros((width, 128), F32))
        gg3_ref[...] = jnp.sum(acc, axis=1, keepdims=True)

    ag = dot(down_ref[0], low_ref[...], 1, 0)
    pre = pre_ref[...]
    c0, c1 = 0.7978845608028654, 0.044715
    t = jnp.tanh(c0 * (pre + c1 * pre * pre * pre))
    slope = 0.5 * (1.0 + t) + 0.5 * pre * (1.0 - t * t) * (c0 * (1.0 + 3.0 * c1 * pre * pre))
    pg = (slope * ag).astype(BF16)
    ddn_ref[...] = dot(act_ref[...], low_ref[...], 1, 1).astype(ddn_ref.dtype)
    dup_ref[...] = dot(pg, h2_ref[...], 1, 1).astype(dup_ref.dtype)
    hg_ref[...] += dot(up_ref[0], pg, 0, 0)

    @pl.when(i == pl.num_programs(0) - 1)
    def _():
        def cols(c, acc):
            at = pl.ds(pl.multiple_of(c * 128, 128), 128)
            dx, gg = ln_back(x2_ref[:, at], hg_ref[:, at], g2_ref[...])
            sg_ref[:, at] += dx
            return acc + gg
        acc = lax.fori_loop(0, length // 128, cols, jnp.zeros((width, 128), F32))
        gg2_ref[...] = jnp.sum(acc, axis=1, keepdims=True)

def ff_bwd(x3, x2, h2, rg, pos, g2, g3, pre, act, ff_w):
    width, length = x3.shape
    hidden = ff_w.shape[1]
    block = 512
    n = hidden // block
    slots = pos.shape[0]
    full = whole((width, length))
    col = pl.BlockSpec((block, length), lambda i: (i, 0))
    wb = pl.BlockSpec((block, width), lambda i: (i, 0))
    g = jax.ShapeDtypeStruct((width, 1), F32)
    return pl.pallas_call(
        ff_bwd_kernel, grid=(n,), name="ff_bwd",
        in_specs=[full, full, full, whole((slots, width)), whole((slots, 1)), whole((width, 1)), whole((width, 1)), col, col,
                  pl.BlockSpec((1, block, width), lambda i: (0, i, 0)),
                  pl.BlockSpec((1, block, width), lambda i: (1, i, 0))],
        out_specs=[full, whole((width, 1)), whole((width, 1)), wb, wb],
        out_shape=[jax.ShapeDtypeStruct((width, length), F32), g, g, jax.ShapeDtypeStruct((hidden, width), BF16), jax.ShapeDtypeStruct((hidden, width), BF16)],
        scratch_shapes=[pltpu.VMEM((width, length), BF16), pltpu.VMEM((width, length), F32)],
        compiler_params=params(),
    )(x3, x2, h2, rg, pos, g2, g3, pre, act, ff_w, ff_w)
RB = 256

def pick(n, top=8):
    return max(k for k in range(1, top + 1) if n % k == 0)

def compact(meta_ref, rows_ref, comp_ref):
    nseq, slots, width = rows_ref.shape
    def clear(b, carry):
        comp_ref[pl.ds(pl.multiple_of(b * RB, RB), RB), :] = jnp.zeros((RB, width), BF16)
        return carry
    lax.fori_loop(0, meta_ref[2, 0], clear, 0)
    def seq(s, carry):
        def part(c, c2):
            comp_ref[pl.ds(pl.multiple_of((meta_ref[1, s] + c) * 16, 16), 16), :] = rows_ref[s, pl.ds(pl.multiple_of(c * 16, 16), 16), :]
            return c2
        lax.fori_loop(0, meta_ref[0, s], part, 0)
        return carry
    lax.fori_loop(0, nseq, seq, 0)

def vocab_fwd_kernel(meta_ref, limit_ref, rows_ref, table_ref, target_ref, *outs, chunk, least, inside):
    lse_ref, chosen_ref = outs[:2]
    comp_ref = outs[2] if inside else rows_ref
    nblk = target_ref.shape[0]
    vocab = table_ref.shape[0]
    if inside:
        nseq, slots, width = rows_ref.shape
        compact(meta_ref, rows_ref, comp_ref)
    lse_ref[...] = jnp.zeros_like(lse_ref)
    chosen_ref[...] = jnp.zeros_like(chosen_ref)
    limit = limit_ref[0]
    def block(b, carry):
        rows = comp_ref[pl.ds(pl.multiple_of(b * RB, RB), RB), :]
        target = target_ref[b]
        top = total = chosen = None
        for v in range(vocab // chunk):
            l = dot(table_ref[v * chunk:(v + 1) * chunk, :], rows, 1, 1)
            ids = v * chunk + lax.broadcasted_iota(jnp.int32, (chunk, RB), 0)
            hit = jnp.sum(jnp.where(ids == target, l, 0.0), axis=0, keepdims=True)
            if (v + 1) * chunk > least:
                l = jnp.where(ids < limit, l, -jnp.inf)
            m = jnp.max(l, axis=0, keepdims=True)
            if v == 0:
                top = m
                total = jnp.sum(jnp.exp(l - top), axis=0, keepdims=True)
                chosen = hit
            else:
                new = jnp.maximum(top, m)
                total = total * jnp.exp(top - new) + jnp.sum(jnp.exp(l - new), axis=0, keepdims=True)
                chosen = chosen + hit
                top = new
        lse_ref[b] = top + jnp.log(total)
        chosen_ref[b] = chosen
        return carry
    lax.fori_loop(0, meta_ref[2, 0], block, 0)

def vocab_fwd(meta, limit, rows, table, target, least):
    inside = rows.ndim == 3
    width = rows.shape[-1]
    nblk = target.shape[0]
    vocab = table.shape[0]
    chunk = 128 * pick(vocab // 128)
    smem = pl.BlockSpec(memory_space=pltpu.SMEM)
    vm = pl.BlockSpec(memory_space=pltpu.VMEM)
    st = jax.ShapeDtypeStruct((nblk, 1, RB), F32)
    comp = [jax.ShapeDtypeStruct((nblk * RB, width), BF16)] if inside else []
    out = pl.pallas_call(
        functools.partial(vocab_fwd_kernel, chunk=chunk, least=least, inside=inside), name="vocab_fwd",
        in_specs=[smem, smem, vm, vm, vm], out_specs=[vm, vm] + [vm] * len(comp),
        out_shape=[st, st] + comp,
        compiler_params=params())(meta, limit, rows, table, target)
    return out[2] if inside else rows, out[0], out[1]

def vocab_bwd_kernel(meta_ref, limit_ref, comp_ref, table_ref, turned_ref, target_ref, lse_ref, scale_ref,
                     og_ref, *refs, chunk, least, inside):
    if inside:
        rg_ref, acc_ref, rc_ref = refs
        nseq, slots, _ = rg_ref.shape
    else:
        rc_ref, acc_ref = refs
    vocab, width = table_ref.shape
    limit = limit_ref[0]
    nch = vocab // chunk
    def clear(b, carry):
        acc_ref[pl.ds(pl.multiple_of(b * 128, 128), 128), :] = jnp.zeros((128, width), F32)
        return carry
    lax.fori_loop(0, vocab // 128, clear, 0)
    def block(b, carry):
        rows = comp_ref[pl.ds(pl.multiple_of(b * RB, RB), RB), :]
        target, lse, scale = target_ref[b], lse_ref[b], scale_ref[b]
        rg = None
        for v in range(nch):
            l = dot(table_ref[v * chunk:(v + 1) * chunk, :], rows, 1, 1)
            ids = v * chunk + lax.broadcasted_iota(jnp.int32, (chunk, RB), 0)
            p = jnp.exp(l - lse)
            if (v + 1) * chunk > least:
                p = jnp.where(ids < limit, p, 0.0)
            g = (scale * jnp.where(ids == target, p - 1.0, p)).astype(BF16)
            acc_ref[v * chunk:(v + 1) * chunk, :] += dot(g, rows, 1, 0)
            part = dot(turned_ref[:, v * chunk:(v + 1) * chunk], g, 1, 0)
            rg = part if rg is None else rg + part
        rc_ref[pl.ds(pl.multiple_of(b * RB, RB), RB), :] = rg.T.astype(BF16)
        return carry
    lax.fori_loop(0, meta_ref[2, 0], block, 0)
    if inside:
      def seq(s, carry):
        rg_ref[s] = jnp.zeros((slots, width), BF16)
        def part(c, c2):
            rg_ref[s, pl.ds(pl.multiple_of(c * 16, 16), 16), :] = rc_ref[pl.ds(pl.multiple_of((meta_ref[1, s] + c) * 16, 16), 16), :]
            return c2
        lax.fori_loop(0, meta_ref[0, s], part, 0)
        return carry
      lax.fori_loop(0, nseq, seq, 0)
    def emit(b, carry):
        at = pl.ds(pl.multiple_of(b * 128, 128), 128)
        og_ref[at, :] = acc_ref[at, :].astype(BF16)
        return carry
    lax.fori_loop(0, vocab // 128, emit, 0)

def vocab_bwd(meta, limit, comp, table, turned, target, lse, scale, least, nseq, slots, inside):
    rows, width = comp.shape
    vocab = table.shape[0]
    chunk = 128 * pick(vocab // 128)
    smem = pl.BlockSpec(memory_space=pltpu.SMEM)
    vm = pl.BlockSpec(memory_space=pltpu.VMEM)
    shape = (nseq, slots, width) if inside else (rows, width)
    extra = [pltpu.VMEM((rows, width), BF16)] if inside else []
    return pl.pallas_call(
        functools.partial(vocab_bwd_kernel, chunk=chunk, least=least, inside=inside), name="vocab_bwd",
        in_specs=[smem, smem] + [vm] * 6, out_specs=[vm, vm],
        out_shape=[jax.ShapeDtypeStruct((vocab, width), BF16), jax.ShapeDtypeStruct(shape, BF16)],
        scratch_shapes=[pltpu.VMEM((vocab, width), F32)] + extra,
        compiler_params=params())(meta, limit, comp, table, turned, target, lse, scale)

def plan(counts, slots, length):
    nseq = counts.shape[0]
    units = (counts + 15) // 16
    ends = jnp.cumsum(units)
    offs = ends - units
    total = ends[-1] * 16
    nblk = (total + RB - 1) // RB
    cap = (nseq * slots + RB - 1) // RB * RB
    at = jnp.arange(cap, dtype=jnp.int32)
    seq = jnp.minimum(jnp.sum((at[:, None] >= ends[None, :] * 16).astype(jnp.int32), axis=1), nseq - 1)
    mine = (seq[:, None] == jnp.arange(nseq, dtype=jnp.int32)[None, :])
    slot = at - jnp.sum(jnp.where(mine, offs[None, :] * 16, 0), axis=1)
    cnt = jnp.sum(jnp.where(mine, counts[None, :], 0), axis=1)
    live = slot < cnt
    weight = jnp.where(live, length / cnt.astype(F32), 0.0)
    meta = jnp.stack([units, offs, jnp.full((nseq,), nblk)]).astype(jnp.int32)
    return meta, seq, slot, weight

def spread(values, seq, slot):
    nseq, slots = values.shape
    parts = jnp.concatenate([values // 256, values % 256], axis=1).astype(BF16)
    mine = (seq[:, None] == jnp.arange(nseq, dtype=jnp.int32)[None, :]).astype(BF16)
    rows = jnp.dot(mine, parts, preferred_element_type=F32)
    hit = slot[:, None] == jnp.arange(slots, dtype=jnp.int32)[None, :]
    both = rows[:, :slots] * 256.0 + rows[:, slots:]
    return jnp.sum(jnp.where(hit, both, 0.0), axis=1).astype(jnp.int32)

def halves(vocab):
    nb = vocab // 128
    low = (nb + 1) // 2
    return nb, low

def sections(count, size):
    return [(s, min(size, count - s)) for s in range(0, count, size)]

def gather_kernel(ids_ref, flag_ref, emb_ref, out_ref, tab_ref, raw_ref, row_ref, sem):
    feat, vocab = emb_ref.shape
    nseq, _, length = out_ref.shape
    nb, low = halves(vocab)
    size = -(-low // 6)
    secs = sections(low, size)
    def copies(k):
        s, n = secs[k]
        out = [pltpu.make_async_copy(emb_ref.at[:, pl.ds(s * 128, n * 128)], raw_ref.at[:, pl.ds(s * 128, n * 128)], sem.at[2 * k])]
        m = min(n, nb - low - s)
        if m > 0:
            out.append(pltpu.make_async_copy(emb_ref.at[:, pl.ds((low + s) * 128, m * 128)], raw_ref.at[:, pl.ds((low + s) * 128, m * 128)], sem.at[2 * k + 1]))
        return out
    for k in range(len(secs)):
        for c in copies(k):
            c.start()
    pad = jnp.zeros((64 - feat, 128), F32)
    for k in range(len(secs)):
        for c in copies(k):
            c.wait()
        s, n = secs[k]
        m = max(0, min(n, nb - low - s))
        def turn(b, carry):
            a = raw_ref[:, pl.ds(pl.multiple_of(b * 128, 128), 128)]
            h = raw_ref[:, pl.ds(pl.multiple_of((low + b) * 128, 128), 128)]
            tab_ref[pl.ds(pl.multiple_of(b * 128, 128), 128), :] = jnp.concatenate([a, pad, h, pad], axis=0).T
            return carry
        lax.fori_loop(s, s + m, turn, 0, unroll=3)
        for b in range(s + m, s + n):
            a = raw_ref[:, b * 128:(b + 1) * 128]
            tab_ref[b * 128:(b + 1) * 128, :] = jnp.concatenate([a, pad, pad, jnp.zeros((feat, 128), F32)], axis=0).T
    U = 32
    def seq(s, carry):
        def grp(g, c2):
            base = pl.multiple_of(g * U, U)
            for j in range(U):
                i = ids_ref[s * length + base + j]
                row_ref[pl.ds(base + j, 1), :] = tab_ref[pl.ds(i, 1), :]
            return c2
        lax.fori_loop(0, length // U, grp, 0)
        for c in range(length // 128):
            t = row_ref[c * 128:(c + 1) * 128, :].T
            f = flag_ref[s, :, c * 128:(c + 1) * 128] > 0
            out_ref[s, :, c * 128:(c + 1) * 128] = jnp.where(f, t[64:64 + feat], t[:feat]).astype(BF16)
        return carry
    lax.fori_loop(0, nseq, seq, 0)

def split_ids(ids, vocab):
    nb, low = halves(vocab)
    high = ids >= low * 128
    return jnp.where(high, ids - low * 128, ids), high.astype(jnp.int32)

def gather(ids, emb):
    nseq, length = ids.shape
    feat, vocab = emb.shape
    nb, low = halves(vocab)
    rid, flag = split_ids(ids, vocab)
    return pl.pallas_call(gather_kernel, name="emb_gather",
        in_specs=[pl.BlockSpec(memory_space=pltpu.SMEM), pl.BlockSpec(memory_space=pltpu.VMEM), pl.BlockSpec(memory_space=pl.ANY)],
        out_specs=pl.BlockSpec(memory_space=pltpu.VMEM),
        out_shape=jax.ShapeDtypeStruct((nseq, feat, length), BF16),
        scratch_shapes=[pltpu.VMEM((low * 128, 128), F32), pltpu.VMEM((feat, vocab), F32), pltpu.VMEM((length, 128), F32), pltpu.SemaphoreType.DMA((12,))],
        compiler_params=params())(rid.reshape(-1), flag.reshape(nseq, 1, length), emb)

def scatter_kernel(ids_ref, flag_ref, *refs, ng, per):
    g_refs = refs[:ng]
    out_ref, raw_ref, row_ref, sem = refs[ng:ng + 4]
    tabs = refs[ng + 4:]
    feat, vocab = out_ref.shape
    nseq, _, length = g_refs[0].shape
    nb, low = halves(vocab)
    zero128 = jnp.zeros((128, 128), F32)
    def zero(b, carry):
        for t in tabs:
            t[pl.ds(pl.multiple_of(b * 128, 128), 128), :] = zero128
        return carry
    lax.fori_loop(0, low, zero, 0)
    pad = jnp.zeros((64 - feat, 128), F32)
    U = 8
    streams = [(g, p) for g in range(ng) for p in range(per)]
    each = nseq // per
    def seq(s, carry):
        for k, (g, p) in enumerate(streams):
            q = p * each + s
            for c in range(length // 128):
                at = slice(c * 128, (c + 1) * 128)
                v = g_refs[g][q, :, at].astype(F32)
                f = flag_ref[g * nseq + q, :, at] > 0
                row_ref[k, at, :] = jnp.concatenate([jnp.where(f, 0.0, v), pad, jnp.where(f, v, 0.0), pad], axis=0).T
        def grp(n, c2):
            base = pl.multiple_of(n * U, U)
            for j in range(U):
                idx = [ids_ref[(g * nseq + p * each + s) * length + base + j] for g, p in streams]
                old = [tabs[k][pl.ds(idx[k], 1), :] for k in range(len(streams))]
                new = [old[k] + row_ref[k, pl.ds(base + j, 1), :] for k in range(len(streams))]
                for k in range(len(streams)):
                    tabs[k][pl.ds(idx[k], 1), :] = new[k]
            return c2
        lax.fori_loop(0, length // U, grp, 0)
        return carry
    lax.fori_loop(0, each, seq, 0)
    def tile(b):
        at = pl.ds(pl.multiple_of(b * 128, 128), 128)
        parts = [sum((tabs[g * per + p][at, :] for p in range(1, per)), tabs[g * per][at, :]) for g in range(ng)]
        return sum(parts[1:], parts[0]).T
    size = -(-low // 6)
    secs = sections(low, size)
    def copies(k):
        s, n = secs[k]
        out = [pltpu.make_async_copy(raw_ref.at[k % 2, 0, :, pl.ds(0, n * 128)], out_ref.at[:, pl.ds(s * 128, n * 128)], sem.at[2 * k])]
        m = min(n, nb - low - s)
        if m > 0:
            out.append(pltpu.make_async_copy(raw_ref.at[k % 2, 1, :, pl.ds(0, m * 128)], out_ref.at[:, pl.ds((low + s) * 128, m * 128)], sem.at[2 * k + 1]))
        return out
    for k, (s, n) in enumerate(secs):
        if k >= 2:
            for c in copies(k - 2):
                c.wait()
        def turn(b, carry, s=s, k=k):
            t = tile(b)
            at = pl.ds(pl.multiple_of((b - s) * 128, 128), 128)
            raw_ref[k % 2, 0, :, at] = t[:feat]
            raw_ref[k % 2, 1, :, at] = t[64:64 + feat]
            return carry
        lax.fori_loop(s, s + n, turn, 0, unroll=3)
        for c in copies(k):
            c.start()
    for k in range(max(0, len(secs) - 2), len(secs)):
        for c in copies(k):
            c.wait()

def scatter(ids, gs, vocab, per):
    nseq, feat, length = gs[0].shape
    nb, low = halves(vocab)
    rid, flag = split_ids(ids, vocab)
    ng = len(gs)
    size = -(-low // 6)
    vm = pl.BlockSpec(memory_space=pltpu.VMEM)
    return pl.pallas_call(functools.partial(scatter_kernel, ng=ng, per=per), name="emb_scatter",
        in_specs=[pl.BlockSpec(memory_space=pltpu.SMEM), vm] + [vm] * ng,
        out_specs=pl.BlockSpec(memory_space=pl.ANY),
        out_shape=jax.ShapeDtypeStruct((feat, vocab), F32),
        scratch_shapes=[pltpu.VMEM((2, 2, feat, size * 128), F32), pltpu.VMEM((ng * per, length, 128), F32), pltpu.SemaphoreType.DMA((12,))]
            + [pltpu.VMEM((low * 128, 128), F32)] * (ng * per),
        compiler_params=params(62 * 1024 * 1024))(rid.reshape(-1), flag.reshape(-1, 1, length), *gs)
MASK_ID = 50257
STRATA = 16
STEP = 10

clip_level = 1.0
beta_one = 0.9
beta_two = 0.95
adam_eps = 1e-08
adam_decay = 0.01
rate_embed = 2.0
rate_out = 0.25
rate_gain = 0.5
rate_shampoo = 0.3
shampoo_decay = 0.01
stat_decay = 0.5
ema_decay = 0.7


def rotary_tables(length, half_width):
    inverse = 10000.0 ** (-jnp.arange(half_width, dtype=F32) / half_width)
    angles = inverse[:, None] * jnp.arange(length, dtype=F32)[None, :]
    return (jnp.cos(angles), jnp.sin(angles))


def adamw(weight, moment_one, moment_two, gradient, step_rate):
    one_new = beta_one * moment_one + (1 - beta_one) * gradient
    two_new = beta_two * moment_two + (1 - beta_two) * gradient * gradient
    one_hat = one_new / (1 - beta_one**STEP)
    two_hat = two_new / (1 - beta_two**STEP)
    weight_new = weight - step_rate * (
        one_hat / (jnp.sqrt(two_hat) + adam_eps) + adam_decay * weight
    )
    return (weight_new, one_new, two_new)


def dp_other(x):
    return lax.ppermute(x, "dp", [(0, 1), (1, 0)])


def dp_sum(x):
    count = lax.axis_size("dp")
    if count == 1:
        return x.astype(F32)
    if count == 2:
        return x.astype(F32) + dp_other(x).astype(F32)
    return lax.psum(x, "dp").astype(F32)


def per_device(
    tokens, positions, strata, groups, embedding, out_table, norm_gains, attention, feedforward,
    embed_moment_one, embed_moment_two, out_moment_one, out_moment_two, gain_moment_one, gain_moment_two,
    attention_left, attention_right, attention_left_root, attention_right_root,
    ff_left, ff_right, ff_left_root, ff_right_root,
    ema_embed, ema_out, ema_gains, ema_attention, ema_feedforward,
):
    fs = lax.axis_size("fsdp")
    dps = lax.axis_size("dp")
    me = lax.axis_index("fsdp")
    replica = lax.axis_index("dp")
    seq_count, length = tokens.shape
    slots = positions.shape[1]
    features, vocab = embedding.shape
    width = features * fs
    shard = out_table.shape[0]

    counts = jnp.maximum(1, (strata + 1) * slots * (1 + groups) // (2 * STRATA))
    in_use = jnp.arange(slots, dtype=jnp.int32)[None, :] < counts[:, None]
    places = jnp.arange(length, dtype=jnp.int32)
    same = positions[0][:, None] == places[None, :]
    marked = jnp.any(same & in_use[0][:, None], axis=0)
    ids_in = jnp.where(marked, MASK_ID, tokens[0])
    targets = jnp.sum(jnp.where(same, tokens[0][None, :], 0), axis=1)
    packed = jnp.concatenate([ids_in, targets, counts])
    packed = jnp.pad(packed, (0, -packed.shape[0] % 1024))
    everyone = lax.all_gather(packed, ("dp", "fsdp"), axis=0)
    group = lax.dynamic_slice_in_dim(everyone, replica * fs, fs, 0)
    all_ids = everyone[:, :length]
    group_ids = group[:, :length]
    group_targets = group[:, length:length + slots]
    group_counts = group[:, length + slots]

    attn_w = lax.all_gather(attention.astype(BF16), "fsdp", axis=1, tiled=True)
    ff_w = lax.all_gather(feedforward.astype(BF16), "fsdp", axis=1, tiled=True)

    picked = gather(group_ids, embedding)
    xT = lax.all_to_all(picked, "fsdp", split_axis=0, concat_axis=0, tiled=True).reshape(width, length)

    cosT, sinT = rotary_tables(length, HEAD // 2)
    gain = [norm_gains[i][:, None] for i in range(3)]
    place = positions[0][:, None]
    hT, qT, kT, vT, mixT, lse = attn_fwd(xT, gain[0], cosT, sinT, attn_w)
    x2, h2, pre, act, x3, head = ff_fwd(xT, mixT, gain[1], gain[2], place, attn_w, ff_w)

    rows = lax.all_gather(head, "fsdp", axis=0)
    shard_pad = -(-shard // 128) * 128
    low = jnp.pad(out_table.astype(BF16), ((0, shard_pad - shard), (0, 0)))
    turned = low.T
    first_id = me * shard
    limit = jnp.clip(MASK_ID - first_id, 0, shard).reshape(1)
    least = min(shard, MASK_ID - (fs - 1) * shard)
    meta, seq, slot, weight = plan(group_counts, slots, length)
    nblk = seq.shape[0] // RB
    target = (spread(group_targets, seq, slot) - first_id).reshape(nblk, 1, RB)
    inside = fs * slots <= 4096
    if not inside:
        rows = jnp.take(rows.reshape(fs * slots, width), jnp.clip(seq * slots + slot, 0, fs * slots - 1), axis=0)
    comp, lse_own, chosen = vocab_fwd(meta, limit, rows, low, target, least)
    lse_all = lax.all_gather(lse_own.reshape(-1), "fsdp", axis=0)
    top = jnp.max(lse_all, axis=0)
    lse_sum = top + jnp.log(jnp.sum(jnp.exp(lse_all - top), axis=0))
    own_loss = jnp.sum(weight * (jnp.where(seq == me, lse_sum, 0.0) - chosen.reshape(-1)))
    scale = weight / (seq_count * fs * dps)
    out_grad, row_grads = vocab_bwd(
        meta, limit, comp, low, turned, target, lse_sum.reshape(nblk, 1, RB), scale.reshape(nblk, 1, RB),
        least, fs, slots, inside,
    )
    if not inside:
        at = jnp.arange(slots, dtype=jnp.int32)[None, :]
        row_grads = jnp.take(row_grads, jnp.minimum(meta[1][:, None] * 16 + at, seq.shape[0] - 1), axis=0)
        row_grads = jnp.where((at < group_counts[:, None])[:, :, None], row_grads, 0)
    own_rows = lax.psum_scatter(
        row_grads.reshape(fs * slots, width).astype(F32), "fsdp", scatter_dimension=0, tiled=True
    )
    out_grad = dp_sum(out_grad)[:shard]

    second, gg2, gg3, dup, ddown = ff_bwd(x3, x2, h2, own_rows, place, gain[1], gain[2], pre, act, ff_w)
    first, gg1, dqkv, dwo = attn_bwd(xT, gain[0], cosT, sinT, second, hT, qT, kT, vT, mixT, lse, attn_w)

    def reduced(x):
        return lax.psum_scatter(x, "fsdp", scatter_dimension=0, tiled=True)

    ff_grad = dp_sum(jnp.stack([reduced(dup), reduced(ddown)]))
    dqkv = dqkv.reshape(3, fs, width // fs, width).transpose(1, 0, 2, 3).reshape(-1, width)
    attn_grad = dp_sum(jnp.concatenate([reduced(dqkv).reshape(3, width // fs, width), reduced(dwo[0])[None]]))

    parts = lax.all_to_all(first.reshape(fs, features, length), "fsdp", split_axis=0, concat_axis=0, tiled=True)
    if dps == 2:
        other = dp_other(parts)
        own_ids = group_ids
        other_ids = lax.dynamic_slice_in_dim(everyone, (1 - replica) * fs, fs, 0)[:, :length]
        embed_grad = scatter(jnp.concatenate([own_ids, other_ids]), (parts, other), vocab, 2)
    else:
        embed_grad = dp_sum(scatter(group_ids, (parts,), vocab, 2).astype(BF16))

    gain_grad = jnp.concatenate([gg1, gg2, gg3], axis=1).T
    gain_grad, loss_sum = lax.psum((gain_grad, own_loss), ("dp", "fsdp"))
    squares = (
        jnp.sum(attn_grad * attn_grad)
        + jnp.sum(ff_grad * ff_grad)
        + jnp.sum(embed_grad * embed_grad)
        + jnp.sum(out_grad * out_grad)
    )
    squares = lax.psum(squares, "fsdp")
    clip_norm = jnp.sqrt(squares + jnp.sum(gain_grad * gain_grad))
    factor = jnp.minimum(1.0, clip_level / clip_norm)
    embed_new, embed_one_new, embed_two_new = adamw(
        embedding, embed_moment_one, embed_moment_two, embed_grad * factor, rate_embed
    )
    out_new, out_one_new, out_two_new = adamw(
        out_table, out_moment_one, out_moment_two, out_grad * factor, rate_out
    )
    gains_new, gains_one_new, gains_two_new = adamw(
        norm_gains, gain_moment_one, gain_moment_two, gain_grad * factor, rate_gain
    )

    def shampoo(weights, grad, left, right, left_root, right_root):
        whole_root = lax.all_gather(right_root.astype(BF16), "fsdp", axis=1, tiled=True)
        own = grad.astype(BF16)
        full = lax.all_gather(own, "fsdp", axis=1, tiled=True)
        columns = right.shape[1]
        own_columns = lax.dynamic_slice_in_dim(full, me * columns, columns, 2)

        def product(text, a, b):
            return jnp.einsum(text, a, b, preferred_element_type=F32)

        mix = (1 - stat_decay) * factor * factor
        left_new = stat_decay * left + mix * product("nik,njk->nij", own, full)
        right_new = stat_decay * right + mix * product("nki,nkj->nij", own_columns, full)
        part = product("nij,njk->nik", left_root.astype(BF16), full)
        update = product("nij,njk->nik", part.astype(BF16), whole_root) * factor
        new = weights - rate_shampoo * (update + shampoo_decay * weights)
        return new, grad * factor, left_new, right_new

    attention_new, attn_clip, attention_left_new, attention_right_new = shampoo(
        attention, attn_grad, attention_left, attention_right, attention_left_root, attention_right_root
    )
    ff_new, ff_clip, ff_left_new, ff_right_new = shampoo(
        feedforward, ff_grad, ff_left, ff_right, ff_left_root, ff_right_root
    )

    def averaged(average, new):
        return ema_decay * average + (1 - ema_decay) * new

    return (
        loss_sum, clip_norm, embed_new, embed_one_new, embed_two_new, out_new, out_one_new, out_two_new,
        gains_new, gains_one_new, gains_two_new, attention_new, attn_clip, attention_left_new, attention_right_new,
        ff_new, ff_clip, ff_left_new, ff_right_new,
        averaged(ema_embed, embed_new), averaged(ema_out, out_new), averaged(ema_gains, gains_new),
        averaged(ema_attention, attention_new), averaged(ema_feedforward, ff_new),
    )


def solution(mesh):
    seqs, rows, stack, none = P(("dp", "fsdp")), P("fsdp", None), P(None, "fsdp", None), P()
    in_specs = (
        seqs, seqs, seqs, seqs, rows, rows, none, stack, stack, rows, rows, rows, rows, none, none,
        stack, stack, stack, stack, stack, stack, stack, stack, rows, rows, none, stack, stack,
    )
    out_specs = (
        none, none, rows, rows, rows, rows, rows, rows, none, none, none, stack, stack, stack, stack,
        stack, stack, stack, stack, rows, rows, none, stack, stack,
    )
    return jax.shard_map(
        per_device, mesh=mesh, in_specs=in_specs, out_specs=out_specs, check_vma=False
    )
```

```python
import functools

import jax
import jax.numpy as jnp
from jax import lax
from jax.experimental import pallas as pl
from jax.experimental.pallas import tpu as pltpu
from jax.sharding import PartitionSpec as P

F32, BF16 = jnp.float32, jnp.bfloat16
HEAD = 64
EPS = 1e-5
BSTEP = 1024
VL = 60 * 1024 * 1024

def dot(a, b, ca, cb):
    return lax.dot_general(a, b, (((ca,), (cb,)), ((), ())), preferred_element_type=F32)

def params(limit=VL):
    return pltpu.CompilerParams(vmem_limit_bytes=limit)

def cost(us):
    return pl.CostEstimate(flops=int(us * 1.15e9), bytes_accessed=0, transcendentals=0)

def whole(shape):
    return pl.BlockSpec(shape, lambda *a: (0,) * len(shape))

def attn_fwd_kernel(x_ref, gain_ref, cos_ref, sin_ref, w_ref, h_ref, q_ref, k_ref, v_ref, m_ref, lse_ref, kn_ref):
    width, length = x_ref.shape
    block = q_ref.shape[0]
    heads = block // HEAD
    half = HEAD // 2

    @pl.when(pl.program_id(0) == 0)
    def _():
        def cols(c, carry):
            at = pl.ds(pl.multiple_of(c * 128, 128), 128)
            x = x_ref[:, at].astype(F32)
            centred = x - jnp.mean(x, axis=0, keepdims=True)
            spread = jnp.mean(centred * centred, axis=0, keepdims=True)
            h_ref[:, at] = (centred * lax.rsqrt(spread + EPS) * gain_ref[...]).astype(BF16)
            return carry
        lax.fori_loop(0, length // 128, cols, 0)

    cosine, sine = cos_ref[...], sin_ref[...]
    hidden = h_ref[...]
    for j, out in ((0, q_ref), (1, k_ref)):
        p = dot(w_ref[j], hidden, 0, 0)
        for h in range(heads):
            a = p[h * HEAD : h * HEAD + half]
            b = p[h * HEAD + half : (h + 1) * HEAD]
            ra = (a * cosine - b * sine).astype(BF16)
            rb = (b * cosine + a * sine).astype(BF16)
            if j == 0:
                ra, rb = ra * 0.125, rb * 0.125
            out[h * HEAD : h * HEAD + half, :] = ra
            out[h * HEAD + half : (h + 1) * HEAD, :] = rb
    v_ref[...] = dot(w_ref[2], hidden, 0, 0).astype(BF16)
    for h in range(heads):
        rows = slice(h * HEAD, (h + 1) * HEAD)
        kn_ref[h] = k_ref[rows, :].T
    def one(h, carry):
        rows = pl.ds(pl.multiple_of(h * HEAD, HEAD), HEAD)
        s = dot(kn_ref[h], q_ref[rows, :], 1, 0)
        top = jnp.max(s, axis=0, keepdims=True)
        e = jnp.exp(s - top)
        total = jnp.sum(e, axis=0, keepdims=True)
        o = dot(v_ref[rows, :], e.astype(BF16), 1, 0)
        m_ref[rows, :] = (o / total).astype(BF16)
        lse_ref[0, pl.ds(h, 1), :] = top + jnp.log(total)
        return carry
    lax.fori_loop(0, heads, one, 0)

def attn_fwd(xT, gain, cosT, sinT, w):
    width, length = xT.shape
    block = 256
    n = width // block
    col = pl.BlockSpec((block, length), lambda i: (i, 0))
    t = jax.ShapeDtypeStruct((width, length), BF16)
    return pl.pallas_call(
        attn_fwd_kernel, grid=(n,), name="attn_fwd", cost_estimate=cost(34),
        in_specs=[whole((width, length)), whole((width, 1)), whole(cosT.shape), whole(sinT.shape),
                  pl.BlockSpec((3, width, block), lambda i: (0, 0, i))],
        out_specs=[whole((width, length)), col, col, col, col, pl.BlockSpec((1, 8, length), lambda i: (i, 0, 0))],
        out_shape=[t, t, t, t, t, jax.ShapeDtypeStruct((n, 8, length), F32)],
        scratch_shapes=[pltpu.VMEM((block // HEAD, length, HEAD), BF16)],
        compiler_params=params(),
    )(xT, gain, cosT, sinT, w)

def attn_bwd_kernel(x_ref, gain_ref, cos_ref, sin_ref, sg_ref, h_ref, q_ref, k_ref, v_ref, m_ref, lse_ref, w_ref, wo_ref,
                    first_ref, gg_ref, dw_ref, dwo_ref, hg_ref, low_ref, do_ref, kn_ref, vn_ref, dk_ref, dv_ref, dq_ref):
    width, length = x_ref.shape
    block = q_ref.shape[0]
    heads = block // HEAD
    half = HEAD // 2
    step = min(BSTEP, length)
    i = pl.program_id(0)

    @pl.when(i == 0)
    def _():
        low_ref[...] = sg_ref[...].astype(BF16)
        hg_ref[...] = jnp.zeros_like(hg_ref)

    do_ref[...] = dot(wo_ref[0], low_ref[...], 1, 0).astype(BF16)
    dwo_ref[0] = dot(m_ref[...], low_ref[...], 1, 1).astype(dwo_ref.dtype)
    cosine, sine = cos_ref[...], sin_ref[...]
    for h in range(heads):
        rows = slice(h * HEAD, (h + 1) * HEAD)
        kn_ref[h] = k_ref[rows, :].T
        vn_ref[h] = v_ref[rows, :].T
    def one(h, carry):
        rows = pl.ds(pl.multiple_of(h * HEAD, HEAD), HEAD)
        for c in range(length // step):
            at = slice(c * step, (c + 1) * step)
            s = dot(kn_ref[h], q_ref[rows, at], 1, 0)
            p = jnp.exp(s - lse_ref[0, pl.ds(h, 1), at])
            dp = dot(vn_ref[h], do_ref[rows, at], 1, 0)
            centre = jnp.sum(p * dp, axis=0, keepdims=True)
            ds = (p * (dp - centre)).astype(BF16)
            pb = p.astype(BF16)
            dv = dot(do_ref[rows, at], pb, 1, 1)
            dk = dot(q_ref[rows, at], ds, 1, 1)
            if c == 0:
                dv_ref[rows, :] = dv
                dk_ref[rows, :] = dk
            else:
                dv_ref[rows, :] += dv
                dk_ref[rows, :] += dk
            dq_ref[rows, at] = dot(k_ref[rows, :], ds, 1, 0) * 0.125
        return carry
    lax.fori_loop(0, heads, one, 0)
    hidden = h_ref[...]
    for j, ref in ((0, dq_ref), (1, dk_ref), (2, dv_ref)):
        if j == 2:
            g = ref[...].astype(BF16)
        else:
            parts = []
            for h in range(heads):
                a = ref[h * HEAD : h * HEAD + half, :]
                b = ref[h * HEAD + half : (h + 1) * HEAD, :]
                parts += [(a * cosine + b * sine).astype(BF16), (b * cosine - a * sine).astype(BF16)]
            g = jnp.concatenate(parts, axis=0)
        dw_ref[j] = dot(hidden, g, 1, 1).astype(dw_ref.dtype)
        hg_ref[...] += dot(w_ref[j], g, 1, 0)

    @pl.when(i == pl.num_programs(0) - 1)
    def _():
        def cols(c, acc):
            at = pl.ds(pl.multiple_of(c * 128, 128), 128)
            dx, gg = ln_back(x_ref[:, at].astype(F32), hg_ref[:, at], gain_ref[...])
            first_ref[:, at] = (sg_ref[:, at] + dx).astype(BF16)
            return acc + gg
        acc = lax.fori_loop(0, length // 128, cols, jnp.zeros((width, 128), F32))
        gg_ref[...] = jnp.sum(acc, axis=1, keepdims=True)

def ln_back(x, g, gain):
    centred = x - jnp.mean(x, axis=0, keepdims=True)
    spread = jnp.mean(centred * centred, axis=0, keepdims=True)
    rs = lax.rsqrt(spread + EPS)
    xh = centred * rs
    gx = g * gain
    dx = rs * (gx - jnp.mean(gx, axis=0, keepdims=True) - xh * jnp.mean(gx * xh, axis=0, keepdims=True))
    return dx, g * xh

def attn_bwd(xT, gain, cosT, sinT, sg, hT, q, k, v, m, lse, w):
    width, length = xT.shape
    block = 256
    n = width // block
    col = pl.BlockSpec((block, length), lambda i: (i, 0))
    full = whole((width, length))
    return pl.pallas_call(
        attn_bwd_kernel, grid=(n,), name="attn_bwd", cost_estimate=cost(62),
        in_specs=[full, whole((width, 1)), whole(cosT.shape), whole(sinT.shape), full, full, col, col, col, col,
                  pl.BlockSpec((1, 8, length), lambda i: (i, 0, 0)),
                  pl.BlockSpec((3, width, block), lambda i: (0, 0, i)),
                  pl.BlockSpec((1, block, width), lambda i: (3, i, 0))],
        out_specs=[full, whole((width, 1)), pl.BlockSpec((3, width, block), lambda i: (0, 0, i)), pl.BlockSpec((1, block, width), lambda i: (0, i, 0))],
        out_shape=[jax.ShapeDtypeStruct((width, length), BF16), jax.ShapeDtypeStruct((width, 1), F32),
                   jax.ShapeDtypeStruct((3, width, width), BF16), jax.ShapeDtypeStruct((1, width, width), BF16)],
        scratch_shapes=[pltpu.VMEM((width, length), F32), pltpu.VMEM((width, length), BF16), pltpu.VMEM((block, length), BF16),
                        pltpu.VMEM((block // HEAD, length, HEAD), BF16), pltpu.VMEM((block // HEAD, length, HEAD), BF16),
                        pltpu.VMEM((block, length), F32), pltpu.VMEM((block, length), F32), pltpu.VMEM((block, length), F32)],
        compiler_params=params(),
    )(xT, gain, cosT, sinT, sg, hT, q, k, v, m, lse, w, w)
def ff_fwd_kernel(x_ref, m_ref, g2_ref, g3_ref, pos_ref, wo_ref, up_ref, down_ref,
                  x2_ref, h2_ref, x3_ref, head_ref, fin_ref):
    width, length = x_ref.shape
    i = pl.program_id(0)

    @pl.when(i == 0)
    def _():
        x2_ref[...] = x_ref[...].astype(F32) + dot(wo_ref[0], m_ref[...], 0, 0)
        x3_ref[...] = x2_ref[...]
        def cols(c, carry):
            at = pl.ds(pl.multiple_of(c * 128, 128), 128)
            h2_ref[:, at] = ln(x2_ref[:, at], g2_ref[...]).astype(BF16)
            return carry
        lax.fori_loop(0, length // 128, cols, 0)

    pre = dot(up_ref[0], h2_ref[...], 1, 0)
    act = jax.nn.gelu(pre, approximate=True).astype(BF16)
    x3_ref[...] += dot(down_ref[0], act, 0, 0)

    @pl.when(i == pl.num_programs(0) - 1)
    def _():
        def cols(c, carry):
            at = pl.ds(pl.multiple_of(c * 128, 128), 128)
            fin_ref[:, at] = ln(x3_ref[:, at], g3_ref[...]).astype(BF16)
            return carry
        lax.fori_loop(0, length // 128, cols, 0)
        slots = pos_ref.shape[0]
        onehot = (pos_ref[...] == lax.broadcasted_iota(jnp.int32, (slots, length), 1)).astype(BF16)
        head_ref[...] = dot(onehot, fin_ref[...], 1, 1).astype(BF16)

def ln(x, gain):
    centred = x - jnp.mean(x, axis=0, keepdims=True)
    spread = jnp.mean(centred * centred, axis=0, keepdims=True)
    return centred * lax.rsqrt(spread + EPS) * gain

def ff_fwd(xT, m, g2, g3, pos, attn_w, ff_w):
    width, length = xT.shape
    hidden = ff_w.shape[1]
    block = 512
    n = hidden // block
    slots = pos.shape[0]
    full = whole((width, length))
    f = jax.ShapeDtypeStruct((width, length), F32)
    return pl.pallas_call(
        ff_fwd_kernel, grid=(n,), name="ff_fwd", cost_estimate=cost(34),
        in_specs=[full, full, whole((width, 1)), whole((width, 1)), whole((slots, 1)),
                  pl.BlockSpec((1, width, width), lambda i: (3, 0, 0)),
                  pl.BlockSpec((1, block, width), lambda i: (0, i, 0)),
                  pl.BlockSpec((1, block, width), lambda i: (1, i, 0))],
        out_specs=[full, full, full, whole((slots, width))],
        out_shape=[f, jax.ShapeDtypeStruct((width, length), BF16), f, jax.ShapeDtypeStruct((slots, width), BF16)],
        scratch_shapes=[pltpu.VMEM((width, length), BF16)],
        compiler_params=params(),
    )(xT, m, g2, g3, pos, attn_w, ff_w, ff_w)

def ff_bwd_kernel(x3_ref, x2_ref, h2_ref, rg_ref, pos_ref, g2_ref, g3_ref, up_ref, down_ref,
                  sg_ref, gg2_ref, gg3_ref, dup_ref, ddn_ref, low_ref, hg_ref):
    width, length = x3_ref.shape
    i = pl.program_id(0)
    slots = pos_ref.shape[0]

    @pl.when(i == 0)
    def _():
        rows = rg_ref[...]
        high = rows.astype(BF16)
        rest = (rows - high.astype(F32)).astype(BF16)
        hg_ref[...] = jnp.zeros_like(hg_ref)
        def cols(c, acc):
            at = pl.ds(pl.multiple_of(c * 128, 128), 128)
            onehot = (pos_ref[...] == c * 128 + lax.broadcasted_iota(jnp.int32, (slots, 128), 1)).astype(BF16)
            fg = dot(high, onehot, 0, 0) + dot(rest, onehot, 0, 0)
            dx, gg = ln_back(x3_ref[:, at], fg, g3_ref[...])
            sg_ref[:, at] = dx
            low_ref[:, at] = dx.astype(BF16)
            return acc + gg
        acc = lax.fori_loop(0, length // 128, cols, jnp.zeros((width, 128), F32))
        gg3_ref[...] = jnp.sum(acc, axis=1, keepdims=True)

    ag = dot(down_ref[0], low_ref[...], 1, 0)
    pre = dot(up_ref[0], h2_ref[...], 1, 0)
    c0, c1 = 0.7978845608028654, 0.044715
    t = jnp.tanh(c0 * (pre + c1 * pre * pre * pre))
    half = 0.5 * (1.0 + t)
    act = (pre * half).astype(BF16)
    slope = half + 0.5 * pre * (1.0 - t * t) * (c0 * (1.0 + 3.0 * c1 * pre * pre))
    pg = (slope * ag).astype(BF16)
    ddn_ref[...] = dot(act, low_ref[...], 1, 1).astype(ddn_ref.dtype)
    dup_ref[...] = dot(pg, h2_ref[...], 1, 1).astype(dup_ref.dtype)
    hg_ref[...] += dot(up_ref[0], pg, 0, 0)

    @pl.when(i == pl.num_programs(0) - 1)
    def _():
        def cols(c, acc):
            at = pl.ds(pl.multiple_of(c * 128, 128), 128)
            dx, gg = ln_back(x2_ref[:, at], hg_ref[:, at], g2_ref[...])
            sg_ref[:, at] += dx
            return acc + gg
        acc = lax.fori_loop(0, length // 128, cols, jnp.zeros((width, 128), F32))
        gg2_ref[...] = jnp.sum(acc, axis=1, keepdims=True)

def ff_bwd(x3, x2, h2, rg, pos, g2, g3, ff_w):
    width, length = x3.shape
    hidden = ff_w.shape[1]
    block = 512
    n = hidden // block
    slots = pos.shape[0]
    full = whole((width, length))
    wb = pl.BlockSpec((block, width), lambda i: (i, 0))
    g = jax.ShapeDtypeStruct((width, 1), F32)
    return pl.pallas_call(
        ff_bwd_kernel, grid=(n,), name="ff_bwd", cost_estimate=cost(45),
        in_specs=[full, full, full, whole((slots, width)), whole((slots, 1)), whole((width, 1)), whole((width, 1)),
                  pl.BlockSpec((1, block, width), lambda i: (0, i, 0)),
                  pl.BlockSpec((1, block, width), lambda i: (1, i, 0))],
        out_specs=[full, whole((width, 1)), whole((width, 1)), wb, wb],
        out_shape=[jax.ShapeDtypeStruct((width, length), F32), g, g, jax.ShapeDtypeStruct((hidden, width), BF16), jax.ShapeDtypeStruct((hidden, width), BF16)],
        scratch_shapes=[pltpu.VMEM((width, length), BF16), pltpu.VMEM((width, length), F32)],
        compiler_params=params(),
    )(x3, x2, h2, rg, pos, g2, g3, ff_w, ff_w)
RB = 256
FCH, BCH = 8, 8

def pick(n, top=8):
    return max(k for k in range(1, top + 1) if n % k == 0)

def compact(meta_ref, rows_ref, comp_ref):
    nseq, slots, width = rows_ref.shape
    def clear(b, carry):
        comp_ref[pl.ds(pl.multiple_of(b * RB, RB), RB), :] = jnp.zeros((RB, width), BF16)
        return carry
    lax.fori_loop(0, meta_ref[2, 0], clear, 0)
    def seq(s, carry):
        def part(c, c2):
            comp_ref[pl.ds(pl.multiple_of((meta_ref[1, s] + c) * 16, 16), 16), :] = rows_ref[s, pl.ds(pl.multiple_of(c * 16, 16), 16), :]
            return c2
        lax.fori_loop(0, meta_ref[0, s], part, 0)
        return carry
    lax.fori_loop(0, nseq, seq, 0)

def vocab_fwd_kernel(meta_ref, limit_ref, rows_ref, source_ref, target_ref, lse_ref, chosen_ref, table_ref, *outs, chunk, least, inside):
    comp_ref = outs[0] if inside else rows_ref
    shard, width = source_ref.shape
    def cast(b, carry):
        at = pl.ds(pl.multiple_of(b * 128, 128), 128)
        table_ref[at, :] = source_ref[at, :].astype(BF16)
        return carry
    lax.fori_loop(0, shard // 128, cast, 0)
    full = shard // 128 * 128
    if full < shard:
        tail = jnp.concatenate([source_ref[full:, :], jnp.zeros((full + 128 - shard, width), F32)], axis=0)
        table_ref[full:, :] = tail.astype(BF16)
    vocab = table_ref.shape[0]
    if inside:
        nseq, slots, width = rows_ref.shape
        compact(meta_ref, rows_ref, comp_ref)
    lse_ref[...] = jnp.zeros_like(lse_ref)
    chosen_ref[...] = jnp.zeros_like(chosen_ref)
    limit = limit_ref[0]
    def block(b, carry):
        rows = comp_ref[pl.ds(pl.multiple_of(b * RB, RB), RB), :]
        target = target_ref[b]
        top = total = chosen = None
        for v in range(vocab // chunk):
            l = dot(table_ref[v * chunk:(v + 1) * chunk, :], rows, 1, 1)
            ids = v * chunk + lax.broadcasted_iota(jnp.int32, (chunk, RB), 0)
            hit = jnp.sum(jnp.where(ids == target, l, 0.0), axis=0, keepdims=True)
            if (v + 1) * chunk > least:
                l = jnp.where(ids < limit, l, -jnp.inf)
            m = jnp.max(l, axis=0, keepdims=True)
            if v == 0:
                top = m
                total = jnp.sum(jnp.exp(l - top), axis=0, keepdims=True)
                chosen = hit
            else:
                new = jnp.maximum(top, m)
                total = total * jnp.exp(top - new) + jnp.sum(jnp.exp(l - new), axis=0, keepdims=True)
                chosen = chosen + hit
                top = new
        lse_ref[b] = top + jnp.log(total)
        chosen_ref[b] = chosen
        return carry
    lax.fori_loop(0, meta_ref[2, 0], block, 0)

def vocab_fwd(meta, limit, rows, source, target, least):
    inside = rows.ndim == 3
    width = rows.shape[-1]
    nblk = target.shape[0]
    vocab = -(-source.shape[0] // 128) * 128
    chunk = 128 * pick(vocab // 128, FCH)
    smem = pl.BlockSpec(memory_space=pltpu.SMEM)
    vm = pl.BlockSpec(memory_space=pltpu.VMEM)
    st = jax.ShapeDtypeStruct((nblk, 1, RB), F32)
    comp = [jax.ShapeDtypeStruct((nblk * RB, width), BF16)] if inside else []
    out = pl.pallas_call(
        functools.partial(vocab_fwd_kernel, chunk=chunk, least=least, inside=inside), name="vocab_fwd", cost_estimate=cost(20),
        in_specs=[smem, smem, vm, vm, vm], out_specs=[vm] * (3 + len(comp)),
        out_shape=[st, st, jax.ShapeDtypeStruct((vocab, width), BF16)] + comp,
        compiler_params=params())(meta, limit, rows, source, target)
    return out[3] if inside else rows, out[2], out[0], out[1]

def vocab_bwd_kernel(meta_ref, limit_ref, comp_ref, table_ref, target_ref, lse_ref, scale_ref,
                     og_ref, rg_ref, acc_ref, rc_ref, low_ref, back_ref, sem, *, chunk, least, inside):
    vocab, width = table_ref.shape
    limit = limit_ref[0]
    nch = vocab // chunk
    def clear(b, carry):
        acc_ref[pl.ds(pl.multiple_of(b * 128, 128), 128), :] = jnp.zeros((128, width), F32)
        return carry
    lax.fori_loop(0, vocab // 128, clear, 0)
    def block(b, carry):
        rows = comp_ref[pl.ds(pl.multiple_of(b * RB, RB), RB), :]
        target, lse, scale = target_ref[b], lse_ref[b], scale_ref[b]
        rg = None
        for v in range(nch):
            l = dot(table_ref[v * chunk:(v + 1) * chunk, :], rows, 1, 1)
            ids = v * chunk + lax.broadcasted_iota(jnp.int32, (chunk, RB), 0)
            p = jnp.exp(l - lse)
            if (v + 1) * chunk > least:
                p = jnp.where(ids < limit, p, 0.0)
            g = (scale * jnp.where(ids == target, p - 1.0, p)).astype(BF16)
            acc_ref[v * chunk:(v + 1) * chunk, :] += dot(g, rows, 1, 0)
            part = dot(g, table_ref[v * chunk:(v + 1) * chunk, :], 0, 0)
            rg = part if rg is None else rg + part
        rc_ref[pl.ds(pl.multiple_of(b * RB, RB), RB), :] = rg.astype(BF16)
        return carry
    lax.fori_loop(0, meta_ref[2, 0], block, 0)
    if inside:
        nseq, slots, _ = back_ref.shape
        def seq(s, carry):
            back_ref[s] = jnp.zeros((slots, width), BF16)
            def part(c, c2):
                back_ref[s, pl.ds(pl.multiple_of(c * 16, 16), 16), :] = rc_ref[pl.ds(pl.multiple_of((meta_ref[1, s] + c) * 16, 16), 16), :]
                return c2
            lax.fori_loop(0, meta_ref[0, s], part, 0)
            return carry
        lax.fori_loop(0, nseq, seq, 0)
        out = pltpu.make_async_copy(back_ref, rg_ref, sem.at[0])
    else:
        out = pltpu.make_async_copy(rc_ref, rg_ref, sem.at[0])
    out.start()
    outs = [out]
    for v in range(nch):
        at = pl.ds(v * chunk, chunk)
        low_ref[at, :] = acc_ref[at, :].astype(BF16)
        outs.append(pltpu.make_async_copy(low_ref.at[at], og_ref.at[at], sem.at[1 + v]))
        outs[-1].start()
    for o in outs:
        o.wait()

def vocab_bwd(meta, limit, comp, table, target, lse, scale, least, nseq, slots, inside):
    rows, width = comp.shape
    vocab = table.shape[0]
    chunk = 128 * pick(vocab // 128, BCH)
    smem = pl.BlockSpec(memory_space=pltpu.SMEM)
    vm = pl.BlockSpec(memory_space=pltpu.VMEM)
    hbm = pl.BlockSpec(memory_space=pl.ANY)
    shape = (nseq, slots, width) if inside else (rows, width)
    return pl.pallas_call(
        functools.partial(vocab_bwd_kernel, chunk=chunk, least=least, inside=inside), name="vocab_bwd", cost_estimate=cost(40),
        in_specs=[smem, smem] + [vm] * 5, out_specs=[hbm, hbm],
        out_shape=[jax.ShapeDtypeStruct((vocab, width), BF16), jax.ShapeDtypeStruct(shape, BF16)],
        scratch_shapes=[pltpu.VMEM((vocab, width), F32), pltpu.VMEM((rows, width), BF16),
                        pltpu.VMEM((vocab, width), BF16), pltpu.VMEM(shape if inside else (1, 16, width), BF16),
                        pltpu.SemaphoreType.DMA((1 + vocab // chunk,))],
        compiler_params=params())(meta, limit, comp, table, target, lse, scale)

def plan(counts, slots, length):
    nseq = counts.shape[0]
    units = (counts + 15) // 16
    ends = jnp.cumsum(units)
    offs = ends - units
    total = ends[-1] * 16
    nblk = (total + RB - 1) // RB
    cap = (nseq * slots + RB - 1) // RB * RB
    at = jnp.arange(cap, dtype=jnp.int32)
    seq = jnp.minimum(jnp.sum((at[:, None] >= ends[None, :] * 16).astype(jnp.int32), axis=1), nseq - 1)
    mine = (seq[:, None] == jnp.arange(nseq, dtype=jnp.int32)[None, :])
    slot = at - jnp.sum(jnp.where(mine, offs[None, :] * 16, 0), axis=1)
    cnt = jnp.sum(jnp.where(mine, counts[None, :], 0), axis=1)
    live = slot < cnt
    weight = jnp.where(live, length / cnt.astype(F32), 0.0)
    meta = jnp.stack([units, offs, jnp.full((nseq,), nblk)]).astype(jnp.int32)
    return meta, seq, slot, weight

def spread(values, seq, slot):
    nseq, slots = values.shape
    parts = jnp.concatenate([values // 256, values % 256], axis=1).astype(BF16)
    mine = (seq[:, None] == jnp.arange(nseq, dtype=jnp.int32)[None, :]).astype(BF16)
    rows = jnp.dot(mine, parts, preferred_element_type=F32)
    hit = slot[:, None] == jnp.arange(slots, dtype=jnp.int32)[None, :]
    both = rows[:, :slots] * 256.0 + rows[:, slots:]
    return jnp.sum(jnp.where(hit, both, 0.0), axis=1).astype(jnp.int32)

def halves(vocab):
    nb = vocab // 128
    low = (nb + 1) // 2
    return nb, low

def sections(count, size):
    return [(s, min(size, count - s)) for s in range(0, count, size)]

def gather_kernel(ids_ref, flag_ref, emb_ref, out_ref, tab_ref, raw_ref, row_ref, sem):
    feat, vocab = emb_ref.shape
    nseq, _, length = out_ref.shape
    nb, low = halves(vocab)
    size = -(-low // 6)
    secs = sections(low, size)
    def copies(k):
        s, n = secs[k]
        out = [pltpu.make_async_copy(emb_ref.at[:, pl.ds(s * 128, n * 128)], raw_ref.at[:, pl.ds(s * 128, n * 128)], sem.at[2 * k])]
        m = min(n, nb - low - s)
        if m > 0:
            out.append(pltpu.make_async_copy(emb_ref.at[:, pl.ds((low + s) * 128, m * 128)], raw_ref.at[:, pl.ds((low + s) * 128, m * 128)], sem.at[2 * k + 1]))
        return out
    for k in range(len(secs)):
        for c in copies(k):
            c.start()
    pad = jnp.zeros((64 - feat, 128), F32)
    for k in range(len(secs)):
        for c in copies(k):
            c.wait()
        s, n = secs[k]
        m = max(0, min(n, nb - low - s))
        def turn(b, carry):
            a = raw_ref[:, pl.ds(pl.multiple_of(b * 128, 128), 128)]
            h = raw_ref[:, pl.ds(pl.multiple_of((low + b) * 128, 128), 128)]
            tab_ref[pl.ds(pl.multiple_of(b * 128, 128), 128), :] = jnp.concatenate([a, pad, h, pad], axis=0).T
            return carry
        lax.fori_loop(s, s + m, turn, 0, unroll=3)
        for b in range(s + m, s + n):
            a = raw_ref[:, b * 128:(b + 1) * 128]
            tab_ref[b * 128:(b + 1) * 128, :] = jnp.concatenate([a, pad, pad, jnp.zeros((feat, 128), F32)], axis=0).T
    U = 32
    def seq(s, carry):
        def grp(g, c2):
            base = pl.multiple_of(g * U, U)
            for j in range(U):
                i = ids_ref[s * length + base + j]
                row_ref[pl.ds(base + j, 1), :] = tab_ref[pl.ds(i, 1), :]
            return c2
        lax.fori_loop(0, length // U, grp, 0)
        for c in range(length // 128):
            t = row_ref[c * 128:(c + 1) * 128, :].T
            f = flag_ref[s, :, c * 128:(c + 1) * 128] > 0
            out_ref[s, :, c * 128:(c + 1) * 128] = jnp.where(f, t[64:64 + feat], t[:feat]).astype(BF16)
        return carry
    lax.fori_loop(0, nseq, seq, 0)

def split_ids(ids, vocab):
    nb, low = halves(vocab)
    high = ids >= low * 128
    return jnp.where(high, ids - low * 128, ids), high.astype(jnp.int32)

def gather(ids, emb):
    nseq, length = ids.shape
    feat, vocab = emb.shape
    nb, low = halves(vocab)
    rid, flag = split_ids(ids, vocab)
    return pl.pallas_call(gather_kernel, name="emb_gather", cost_estimate=cost(32),
        in_specs=[pl.BlockSpec(memory_space=pltpu.SMEM), pl.BlockSpec(memory_space=pltpu.VMEM), pl.BlockSpec(memory_space=pl.ANY)],
        out_specs=pl.BlockSpec(memory_space=pltpu.VMEM),
        out_shape=jax.ShapeDtypeStruct((nseq, feat, length), BF16),
        scratch_shapes=[pltpu.VMEM((low * 128, 128), F32), pltpu.VMEM((feat, vocab), F32), pltpu.VMEM((length, 128), F32), pltpu.SemaphoreType.DMA((12,))],
        compiler_params=params())(rid.reshape(-1), flag.reshape(nseq, 1, length), emb)

def scatter_kernel(ids_ref, flag_ref, *refs, ng, per):
    g_refs = refs[:ng]
    out_ref, raw_ref, row_ref, sem = refs[ng:ng + 4]
    tabs = refs[ng + 4:]
    feat, vocab = out_ref.shape
    nseq, _, length = g_refs[0].shape
    nb, low = halves(vocab)
    zero128 = jnp.zeros((128, 128), F32)
    def zero(b, carry):
        for t in tabs:
            t[pl.ds(pl.multiple_of(b * 128, 128), 128), :] = zero128
        return carry
    lax.fori_loop(0, low, zero, 0)
    pad = jnp.zeros((64 - feat, 128), F32)
    U = 8
    streams = [(g, p) for g in range(ng) for p in range(per)]
    each = nseq // per
    def seq(s, carry):
        for k, (g, p) in enumerate(streams):
            q = p * each + s
            for c in range(length // 128):
                at = slice(c * 128, (c + 1) * 128)
                v = g_refs[g][q, :, at].astype(F32)
                f = flag_ref[g * nseq + q, :, at] > 0
                row_ref[k, at, :] = jnp.concatenate([jnp.where(f, 0.0, v), pad, jnp.where(f, v, 0.0), pad], axis=0).T
        def grp(n, c2):
            base = pl.multiple_of(n * U, U)
            for j in range(U):
                idx = [ids_ref[(g * nseq + p * each + s) * length + base + j] for g, p in streams]
                old = [tabs[k][pl.ds(idx[k], 1), :] for k in range(len(streams))]
                new = [old[k] + row_ref[k, pl.ds(base + j, 1), :] for k in range(len(streams))]
                for k in range(len(streams)):
                    tabs[k][pl.ds(idx[k], 1), :] = new[k]
            return c2
        lax.fori_loop(0, length // U, grp, 0)
        return carry
    lax.fori_loop(0, each, seq, 0)
    def tile(b):
        at = pl.ds(pl.multiple_of(b * 128, 128), 128)
        parts = [sum((tabs[g * per + p][at, :] for p in range(1, per)), tabs[g * per][at, :]) for g in range(ng)]
        return sum(parts[1:], parts[0]).T
    size = -(-low // 6)
    secs = sections(low, size)
    def copies(k):
        s, n = secs[k]
        out = [pltpu.make_async_copy(raw_ref.at[k % 2, 0, :, pl.ds(0, n * 128)], out_ref.at[:, pl.ds(s * 128, n * 128)], sem.at[2 * k])]
        m = min(n, nb - low - s)
        if m > 0:
            out.append(pltpu.make_async_copy(raw_ref.at[k % 2, 1, :, pl.ds(0, m * 128)], out_ref.at[:, pl.ds((low + s) * 128, m * 128)], sem.at[2 * k + 1]))
        return out
    for k, (s, n) in enumerate(secs):
        if k >= 2:
            for c in copies(k - 2):
                c.wait()
        def turn(b, carry, s=s, k=k):
            t = tile(b)
            at = pl.ds(pl.multiple_of((b - s) * 128, 128), 128)
            raw_ref[k % 2, 0, :, at] = t[:feat]
            raw_ref[k % 2, 1, :, at] = t[64:64 + feat]
            return carry
        lax.fori_loop(s, s + n, turn, 0, unroll=3)
        for c in copies(k):
            c.start()
    for k in range(max(0, len(secs) - 2), len(secs)):
        for c in copies(k):
            c.wait()

def scatter(ids, gs, vocab, per):
    nseq, feat, length = gs[0].shape
    nb, low = halves(vocab)
    rid, flag = split_ids(ids, vocab)
    ng = len(gs)
    size = -(-low // 6)
    vm = pl.BlockSpec(memory_space=pltpu.VMEM)
    return pl.pallas_call(functools.partial(scatter_kernel, ng=ng, per=per), name="emb_scatter", cost_estimate=cost(66),
        in_specs=[pl.BlockSpec(memory_space=pltpu.SMEM), vm] + [vm] * ng,
        out_specs=pl.BlockSpec(memory_space=pl.ANY),
        out_shape=jax.ShapeDtypeStruct((feat, vocab), F32),
        scratch_shapes=[pltpu.VMEM((2, 2, feat, size * 128), F32), pltpu.VMEM((ng * per, length, 128), F32), pltpu.SemaphoreType.DMA((12,))]
            + [pltpu.VMEM((low * 128, 128), F32)] * (ng * per),
        compiler_params=params(62 * 1024 * 1024))(rid.reshape(-1), flag.reshape(-1, 1, length), *gs)
MESH_ID = pl.DeviceIdType.MESH

def comm_params(ident):
    return pltpu.CompilerParams(collective_id=ident, has_side_effects=True, vmem_limit_bytes=VL)

def meet(peers):
    barrier = pltpu.get_barrier_semaphore()
    for p in peers:
        pl.semaphore_signal(barrier, inc=1, device_id=p, device_id_type=MESH_ID)
    pl.semaphore_wait(barrier, len(peers))

def remote(src, dst, send, recv, peer):
    return pltpu.make_async_remote_copy(src_ref=src, dst_ref=dst, send_sem=send, recv_sem=recv, device_id=peer, device_id_type=MESH_ID)

def small_kernel(x_ref, *refs, fs, dps, wide, finish):
    out_ref = refs[0]
    got_ref = refs[1] if finish else out_ref
    send, recv = refs[-2:]
    d, f = lax.axis_index("dp"), lax.axis_index("fsdp")
    n = fs * dps if wide else fs
    me = d * fs + f if wide else f
    def peer(k):
        j = lax.rem(me + k, n)
        return (lax.div(j, fs), lax.rem(j, fs)) if wide else (d, j)
    barrier = pltpu.get_barrier_semaphore()
    def greet(k, carry):
        pl.semaphore_signal(barrier, inc=1, device_id=peer(k), device_id_type=MESH_ID)
        return carry
    lax.fori_loop(1, n, greet, 0)
    pl.semaphore_wait(barrier, n - 1)
    def copy(k):
        return remote(x_ref, got_ref.at[me], send.at[k], recv.at[k], peer(k))
    def begin(k, carry):
        copy(k).start()
        return carry
    lax.fori_loop(1, n, begin, 0)
    got_ref[me] = x_ref[...]
    def end(k, carry):
        copy(k).wait()
        return carry
    lax.fori_loop(1, n, end, 0)
    if finish:
        finish(got_ref, out_ref, n)

def lse_finish(got_ref, out_ref, n):
    top = got_ref[0]
    for i in range(1, n):
        top = jnp.maximum(top, got_ref[i])
    total = jnp.exp(got_ref[0] - top)
    for i in range(1, n):
        total = total + jnp.exp(got_ref[i] - top)
    out_ref[...] = top + jnp.log(total)

def sum_finish(got_ref, out_ref, n):
    total = got_ref[0]
    for i in range(1, n):
        total = total + got_ref[i]
    out_ref[...] = total

def small_gather(x, ident, wide=False, finish=None, name="small_gather"):
    fs, dps = lax.axis_size("fsdp"), lax.axis_size("dp")
    n = fs * dps if wide else fs
    vm = pl.BlockSpec(memory_space=pltpu.VMEM)
    got = (n,) + x.shape
    return pl.pallas_call(
        functools.partial(small_kernel, fs=fs, dps=dps, wide=wide, finish=finish), name=name,
        in_specs=[vm], out_specs=vm,
        out_shape=jax.ShapeDtypeStruct(x.shape if finish else got, x.dtype),
        scratch_shapes=([pltpu.VMEM(got, x.dtype)] if finish else []) + [pltpu.SemaphoreType.DMA((n,)), pltpu.SemaphoreType.DMA((n,))],
        cost_estimate=cost(12), compiler_params=comm_params(ident))(x)

def exchange_kernel(*refs, fs, both, aux):
    refs = list(refs)
    x_ref = refs.pop(0)
    aux_ref = refs.pop(0) if aux else None
    out_ref = refs.pop(0)
    other_ref = refs.pop(0) if both else None
    if aux:
        sum_ref, near_ref, over_ref = refs.pop(0), refs.pop(-2), refs.pop(-1)
    send, recv, send2, recv2, own = refs[:5]
    d, f = lax.axis_index("dp"), lax.axis_index("fsdp")
    across = (1 - d, f)
    barrier = pltpu.get_barrier_semaphore()
    def greet(k, carry):
        pl.semaphore_signal(barrier, inc=1, device_id=(d, lax.rem(f + k, fs)), device_id_type=MESH_ID)
        return carry
    lax.fori_loop(1, fs, greet, 0)
    if both:
        pl.semaphore_signal(barrier, inc=1, device_id=across, device_id_type=MESH_ID)
    pl.semaphore_wait(barrier, fs if both else fs - 1)
    def copies(k):
        j = lax.rem(f + k, fs)
        out = [remote(x_ref.at[j], out_ref.at[f], send.at[0, k], recv.at[0, k], (d, j))]
        if aux:
            out.append(remote(aux_ref, near_ref.at[f], send.at[1, k], recv.at[1, k], (d, j)))
        return out
    def passed(k):
        s = lax.rem(f + fs - k, fs)
        out = [remote(out_ref.at[s], other_ref.at[s], send2.at[0, k], recv2.at[0, k], across)]
        if aux:
            out.append(remote(near_ref.at[s], over_ref.at[s], send2.at[1, k], recv2.at[1, k], across))
        return out
    def first():
        out = [remote(x_ref.at[f], other_ref.at[f], send2.at[0, 0], recv2.at[0, 0], across)]
        if aux:
            out.append(remote(aux_ref, over_ref.at[f], send2.at[1, 0], recv2.at[1, 0], across))
        return out
    if both:
        for c in first():
            c.start()
    def begin(k, carry):
        for c in copies(k):
            c.start()
        return carry
    lax.fori_loop(1, fs, begin, 0)
    mine = pltpu.make_async_copy(x_ref.at[f], out_ref.at[f], own)
    mine.start()
    if aux:
        near_ref[f] = aux_ref[...]
    mine.wait()
    def arrive(k, carry):
        for c in copies(k):
            c.wait_recv()
        if both:
            for c in passed(k):
                c.start()
        return carry
    lax.fori_loop(1, fs, arrive, 0)
    def end(k, carry):
        for c in copies(k):
            c.wait_send()
        if both:
            for c in passed(k):
                c.wait()
        return carry
    lax.fori_loop(1, fs, end, 0)
    if both:
        for c in first():
            c.wait()
    if aux:
        total = near_ref[0]
        for i in range(1, fs):
            total = total + near_ref[i]
        if both:
            rest = over_ref[0]
            for i in range(1, fs):
                rest = rest + over_ref[i]
            total = total + rest
        sum_ref[...] = total

def exchange(x, ident, both, name, aux=None):
    fs = lax.axis_size("fsdp")
    vm = pl.BlockSpec(memory_space=pltpu.VMEM)
    shape = jax.ShapeDtypeStruct(x.shape, x.dtype)
    sem = pltpu.SemaphoreType.DMA((2, fs))
    more = [] if aux is None else [pltpu.VMEM((fs,) + aux.shape, F32)] * 2
    outs = [shape] * (2 if both else 1) + ([] if aux is None else [jax.ShapeDtypeStruct(aux.shape, F32)])
    return pl.pallas_call(
        functools.partial(exchange_kernel, fs=fs, both=both, aux=aux is not None), name=name,
        in_specs=[vm] * (1 if aux is None else 2), out_specs=[vm] * len(outs), out_shape=outs,
        scratch_shapes=[sem, sem, sem, sem, pltpu.SemaphoreType.DMA] + more,
        cost_estimate=cost(55),
        compiler_params=comm_params(ident))(*([x] if aux is None else [x, aux]))

def rows_gather_kernel(x_ref, out_ref, send, recv, *, high):
    d, f = lax.axis_index("dp"), lax.axis_index("fsdp")
    h, m, c = lax.div(f, 4), lax.rem(lax.div(f, 2), 2), lax.rem(f, 2)
    side, twin = (d, h * 4 + (1 - m) * 2 + c), (d, h * 4 + m * 2 + 1 - c)
    def far(k):
        return (d, lax.rem(h + k, high) * 4 + m * 2 + c)
    meet([far(k) for k in range(1, high)] + [side, twin])
    sent = []
    def go(src, block, peer):
        r = remote(src, out_ref.at[block], send.at[len(sent)], recv.at[block], peer)
        r.start()
        sent.append(r)
    def arrived(block):
        remote(x_ref, out_ref.at[block], send.at[0], recv.at[block], twin).wait_recv()
    for k in range(1, high):
        go(x_ref, f, far(k))
    go(x_ref, f, side)
    go(x_ref, f, twin)
    out_ref[f] = x_ref[...]
    for k in range(1, high):
        b = lax.rem(h + high - k, high) * 4 + m * 2 + c
        arrived(b)
        go(out_ref.at[b], b, side)
        go(out_ref.at[b], b, twin)
    for k in range(high):
        b = lax.rem(h + high - k, high) * 4 + (1 - m) * 2 + c
        arrived(b)
        go(out_ref.at[b], b, twin)
    for mm in range(2):
        for k in range(high):
            arrived(lax.rem(h + high - k, high) * 4 + lax.rem(m + mm, 2) * 2 + 1 - c)
    for r in sent:
        r.wait_send()

def rows_gather(x, ident, name="rows_gather"):
    fs = lax.axis_size("fsdp")
    vm = pl.BlockSpec(memory_space=pltpu.VMEM)
    high = fs // 4
    return pl.pallas_call(
        functools.partial(rows_gather_kernel, high=high), name=name,
        in_specs=[vm], out_specs=vm, out_shape=jax.ShapeDtypeStruct((fs,) + x.shape, x.dtype),
        scratch_shapes=[pltpu.SemaphoreType.DMA((4 * high,)), pltpu.SemaphoreType.DMA((fs,))],
        cost_estimate=cost(44), compiler_params=comm_params(ident))(x)

def rows_reduce_kernel(x_ref, out_ref, twin_ref, side_ref, far_ref, a_ref, b_ref, s1, r1, s2, r2, s3, r3, *, high):
    d, f = lax.axis_index("dp"), lax.axis_index("fsdp")
    h, m, c = lax.div(f, 4), lax.rem(lax.div(f, 2), 2), lax.rem(f, 2)
    side, twin = (d, h * 4 + (1 - m) * 2 + c), (d, h * 4 + m * 2 + 1 - c)
    def far(k):
        return (d, lax.rem(h + k, high) * 4 + m * 2 + c)
    meet([far(k) for k in range(1, high)] + [side, twin])
    order = list(range(1, high)) + [0]
    def at(k):
        return lax.rem(h + k, high)
    def one(k, mm):
        slot = at(k) * 2 + mm
        return remote(x_ref.at[at(k) * 4 + mm * 2 + 1 - c], twin_ref.at[slot], s1.at[slot], r1.at[slot], twin)
    def two(k):
        return remote(a_ref.at[at(k)], side_ref.at[at(k)], s2.at[at(k)], r2.at[at(k)], side)
    def three(k):
        return remote(b_ref.at[k], far_ref.at[k], s3.at[k], r3.at[k], far(k))
    for k in order:
        one(k, 1 - m).start()
    for k in order:
        one(k, m).start()
    for k in order:
        one(k, 1 - m).wait_recv()
        a_ref[at(k)] = (x_ref[at(k) * 4 + (1 - m) * 2 + c].astype(F32) + twin_ref[at(k) * 2 + 1 - m].astype(F32)).astype(a_ref.dtype)
        two(k).start()
    for k in order:
        one(k, m).wait_recv()
        two(k).wait_recv()
        total = x_ref[at(k) * 4 + m * 2 + c].astype(F32) + twin_ref[at(k) * 2 + m].astype(F32) + side_ref[at(k)].astype(F32)
        if k == 0:
            out_ref[...] = total
        else:
            b_ref[k] = total.astype(b_ref.dtype)
            three(k).start()
    for k in range(1, high):
        three(k).wait_recv()
        out_ref[...] += far_ref[k].astype(F32)
    for k in order:
        one(k, m).wait_send()
        one(k, 1 - m).wait_send()
        two(k).wait_send()
        if k:
            three(k).wait_send()

def rows_reduce(x, ident, name="rows_reduce"):
    fs = lax.axis_size("fsdp")
    vm = pl.BlockSpec(memory_space=pltpu.VMEM)
    high = fs // 4
    block = x.shape[1:]
    def sem(n):
        return pltpu.SemaphoreType.DMA((n,))
    def buf(n):
        return pltpu.VMEM((n,) + block, x.dtype)
    return pl.pallas_call(
        functools.partial(rows_reduce_kernel, high=high), name=name,
        in_specs=[vm], out_specs=vm, out_shape=jax.ShapeDtypeStruct(block, F32),
        scratch_shapes=[buf(2 * high), buf(high), buf(high), buf(high), buf(high),
                        sem(2 * high), sem(2 * high), sem(high), sem(high), sem(high), sem(high)],
        cost_estimate=cost(45), compiler_params=comm_params(ident))(x)
MASK_ID = 50257
STRATA = 16
STEP = 10

clip_level = 1.0
beta_one = 0.9
beta_two = 0.95
adam_eps = 1e-08
adam_decay = 0.01
rate_embed = 2.0
rate_out = 0.25
rate_gain = 0.5
rate_shampoo = 0.3
shampoo_decay = 0.01
stat_decay = 0.5
ema_decay = 0.7


def rotary_tables(length, half_width):
    inverse = 10000.0 ** (-jnp.arange(half_width, dtype=F32) / half_width)
    angles = inverse[:, None] * jnp.arange(length, dtype=F32)[None, :]
    return (jnp.cos(angles), jnp.sin(angles))


def adamw(weight, moment_one, moment_two, gradient, step_rate):
    one_new = beta_one * moment_one + (1 - beta_one) * gradient
    two_new = beta_two * moment_two + (1 - beta_two) * gradient * gradient
    one_hat = one_new / (1 - beta_one**STEP)
    two_hat = two_new / (1 - beta_two**STEP)
    weight_new = weight - step_rate * (
        one_hat / (jnp.sqrt(two_hat) + adam_eps) + adam_decay * weight
    )
    return (weight_new, one_new, two_new)


def dp_other(x):
    return lax.ppermute(x, "dp", [(0, 1), (1, 0)])


def dp_sum(x):
    count = lax.axis_size("dp")
    if count == 1:
        return x.astype(F32)
    if count == 2:
        return x.astype(F32) + dp_other(x).astype(F32)
    return lax.psum(x, "dp").astype(F32)


def per_device(
    tokens, positions, strata, groups, embedding, out_table, norm_gains, attention, feedforward,
    embed_moment_one, embed_moment_two, out_moment_one, out_moment_two, gain_moment_one, gain_moment_two,
    attention_left, attention_right, attention_left_root, attention_right_root,
    ff_left, ff_right, ff_left_root, ff_right_root,
    ema_embed, ema_out, ema_gains, ema_attention, ema_feedforward,
):
    fs = lax.axis_size("fsdp")
    dps = lax.axis_size("dp")
    me = lax.axis_index("fsdp")
    replica = lax.axis_index("dp")
    seq_count, length = tokens.shape
    slots = positions.shape[1]
    features, vocab = embedding.shape
    width = features * fs
    shard = out_table.shape[0]

    counts = jnp.maximum(1, (strata + 1) * slots * (1 + groups) // (2 * STRATA))
    in_use = jnp.arange(slots, dtype=jnp.int32)[None, :] < counts[:, None]
    places = jnp.arange(length, dtype=jnp.int32)
    same = positions[0][:, None] == places[None, :]
    marked = jnp.any(same & in_use[0][:, None], axis=0)
    ids_in = jnp.where(marked, MASK_ID, tokens[0])
    targets = jnp.sum(jnp.where(same, tokens[0][None, :], 0), axis=1)
    packed = jnp.concatenate([ids_in, targets, counts])
    packed = jnp.pad(packed, (0, -packed.shape[0] % 1024))
    everyone = small_gather(packed.reshape(-1, 128), 1, wide=True, name="ids_gather").reshape(fs * dps, -1)
    group = lax.dynamic_slice_in_dim(everyone, replica * fs, fs, 0)
    all_ids = everyone[:, :length]
    group_ids = group[:, :length]
    group_targets = group[:, length:length + slots]
    group_counts = group[:, length + slots]

    attn_w = lax.all_gather(attention.astype(BF16), "fsdp", axis=1, tiled=True)
    ff_w = lax.all_gather(feedforward.astype(BF16), "fsdp", axis=1, tiled=True)

    picked = gather(group_ids, embedding)
    xT = exchange(picked, 2, False, "features")[0].reshape(width, length)

    cosT, sinT = rotary_tables(length, HEAD // 2)
    gain = [norm_gains[i][:, None] for i in range(3)]
    place = positions[0][:, None]
    hT, qT, kT, vT, mixT, lse = attn_fwd(xT, gain[0], cosT, sinT, attn_w)
    x2, h2, x3, head = ff_fwd(xT, mixT, gain[1], gain[2], place, attn_w, ff_w)

    rows = rows_gather(head, 3)
    first_id = me * shard
    limit = jnp.clip(MASK_ID - first_id, 0, shard).reshape(1)
    least = min(shard, MASK_ID - (fs - 1) * shard)
    meta, seq, slot, weight = plan(group_counts, slots, length)
    nblk = seq.shape[0] // RB
    target = (spread(group_targets, seq, slot) - first_id).reshape(nblk, 1, RB)
    inside = fs * slots <= 4096
    if not inside:
        rows = jnp.take(rows.reshape(fs * slots, width), jnp.clip(seq * slots + slot, 0, fs * slots - 1), axis=0)
    comp, low, lse_own, chosen = vocab_fwd(meta, limit, rows, out_table, target, least)
    lse_sum = small_gather(lse_own, 4, finish=lse_finish, name="lse_gather")
    own_loss = jnp.sum(weight * (jnp.where(seq == me, lse_sum.reshape(-1), 0.0) - chosen.reshape(-1)))
    scale = weight / (seq_count * fs * dps)
    out_grad, row_grads = vocab_bwd(
        meta, limit, comp, low, target, lse_sum, scale.reshape(nblk, 1, RB),
        least, fs, slots, inside,
    )
    if not inside:
        at = jnp.arange(slots, dtype=jnp.int32)[None, :]
        row_grads = jnp.take(row_grads, jnp.minimum(meta[1][:, None] * 16 + at, seq.shape[0] - 1), axis=0)
        row_grads = jnp.where((at < group_counts[:, None])[:, :, None], row_grads, 0)
    own_rows = rows_reduce(row_grads, 5)
    out_grad = dp_sum(out_grad)[:shard]

    second, gg2, gg3, dup, ddown = ff_bwd(x3, x2, h2, own_rows, place, gain[1], gain[2], ff_w)
    first, gg1, dqkv, dwo = attn_bwd(xT, gain[0], cosT, sinT, second, hT, qT, kT, vT, mixT, lse, attn_w)

    def reduced(x):
        return lax.psum_scatter(x, "fsdp", scatter_dimension=0, tiled=True)

    dff = jnp.stack([dup.reshape(fs, -1, width), ddown.reshape(fs, -1, width)], axis=1).reshape(-1, width)
    ff_grad = dp_sum(reduced(dff).reshape(2, -1, width))
    dqkv = dqkv.reshape(3, fs, width // fs, width).transpose(1, 0, 2, 3)
    dattn = jnp.concatenate([dqkv, dwo.reshape(fs, 1, width // fs, width)], axis=1).reshape(-1, width)
    attn_grad = dp_sum(reduced(dattn).reshape(4, width // fs, width))

    aux = jnp.concatenate([jnp.concatenate([gg1, gg2, gg3], axis=1).T.reshape(-1), own_loss[None]])
    aux = jnp.pad(aux, (0, -aux.shape[0] % 1024)).reshape(-1, 128)
    out = exchange(first.reshape(fs, features, length), 6, dps == 2, "gradients", aux)
    if dps == 2:
        parts, other, aux = out
        other_ids = lax.dynamic_slice_in_dim(everyone, (1 - replica) * fs, fs, 0)[:, :length]
        embed_grad = scatter(jnp.concatenate([group_ids, other_ids]), (parts, other), vocab, 2)
    else:
        parts, aux = out
        embed_grad = dp_sum(scatter(group_ids, (parts,), vocab, 2).astype(BF16))
        if dps > 1:
            aux = lax.psum(aux, "dp")
    aux = aux.reshape(-1)
    gain_grad, loss_sum = aux[: 3 * width].reshape(3, width), aux[3 * width]
    squares = (
        jnp.sum(attn_grad * attn_grad)
        + jnp.sum(ff_grad * ff_grad)
        + jnp.sum(embed_grad * embed_grad)
        + jnp.sum(out_grad * out_grad)
    )
    squares = small_gather(jnp.full((8, 128), squares), 7, finish=sum_finish, name="squares")[0, 0]
    clip_norm = jnp.sqrt(squares + jnp.sum(gain_grad * gain_grad))
    factor = jnp.minimum(1.0, clip_level / clip_norm)
    embed_new, embed_one_new, embed_two_new = adamw(
        embedding, embed_moment_one, embed_moment_two, embed_grad * factor, rate_embed
    )
    out_new, out_one_new, out_two_new = adamw(
        out_table, out_moment_one, out_moment_two, out_grad * factor, rate_out
    )
    gains_new, gains_one_new, gains_two_new = adamw(
        norm_gains, gain_moment_one, gain_moment_two, gain_grad * factor, rate_gain
    )

    def shampoo(weights, grad, left, right, left_root, right_root):
        whole_root = lax.all_gather(right_root.astype(BF16), "fsdp", axis=1, tiled=True)
        own = grad.astype(BF16)
        full = lax.all_gather(own, "fsdp", axis=1, tiled=True)
        columns = right.shape[1]
        own_columns = lax.dynamic_slice_in_dim(full, me * columns, columns, 2)

        def product(text, a, b):
            return jnp.einsum(text, a, b, preferred_element_type=F32)

        mix = (1 - stat_decay) * factor * factor
        left_new = stat_decay * left + mix * product("nik,njk->nij", own, full)
        right_new = stat_decay * right + mix * product("nki,nkj->nij", own_columns, full)
        part = product("nij,njk->nik", left_root.astype(BF16), full)
        update = product("nij,njk->nik", part.astype(BF16), whole_root) * factor
        new = weights - rate_shampoo * (update + shampoo_decay * weights)
        return new, grad * factor, left_new, right_new

    attention_new, attn_clip, attention_left_new, attention_right_new = shampoo(
        attention, attn_grad, attention_left, attention_right, attention_left_root, attention_right_root
    )
    ff_new, ff_clip, ff_left_new, ff_right_new = shampoo(
        feedforward, ff_grad, ff_left, ff_right, ff_left_root, ff_right_root
    )

    def averaged(average, new):
        return ema_decay * average + (1 - ema_decay) * new

    return (
        loss_sum, clip_norm, embed_new, embed_one_new, embed_two_new, out_new, out_one_new, out_two_new,
        gains_new, gains_one_new, gains_two_new, attention_new, attn_clip, attention_left_new, attention_right_new,
        ff_new, ff_clip, ff_left_new, ff_right_new,
        averaged(ema_embed, embed_new), averaged(ema_out, out_new), averaged(ema_gains, gains_new),
        averaged(ema_attention, attention_new), averaged(ema_feedforward, ff_new),
    )


def solution(mesh):
    seqs, rows, stack, none = P(("dp", "fsdp")), P("fsdp", None), P(None, "fsdp", None), P()
    in_specs = (
        seqs, seqs, seqs, seqs, rows, rows, none, stack, stack, rows, rows, rows, rows, none, none,
        stack, stack, stack, stack, stack, stack, stack, stack, rows, rows, none, stack, stack,
    )
    out_specs = (
        none, none, rows, rows, rows, rows, rows, rows, none, none, none, stack, stack, stack, stack,
        stack, stack, stack, stack, rows, rows, none, stack, stack,
    )
    return jax.shard_map(
        per_device, mesh=mesh, in_specs=in_specs, out_specs=out_specs, check_vma=False
    )
```

```python
import functools

import jax
import jax.numpy as jnp
from jax import lax
from jax.experimental import pallas as pl
from jax.experimental.pallas import tpu as pltpu
from jax.sharding import PartitionSpec as P

F32, BF16 = jnp.float32, jnp.bfloat16
HEAD = 64
EPS = 1e-5
BSTEP = 1024
VL = 60 * 1024 * 1024

def dot(a, b, ca, cb):
    return lax.dot_general(a, b, (((ca,), (cb,)), ((), ())), preferred_element_type=F32)

def params(limit=VL):
    return pltpu.CompilerParams(vmem_limit_bytes=limit)

def cost(us):
    return pl.CostEstimate(flops=int(us * 1.15e9), bytes_accessed=0, transcendentals=0)

def whole(shape):
    return pl.BlockSpec(shape, lambda *a: (0,) * len(shape))

def attn_fwd_kernel(x_ref, gain_ref, cos_ref, sin_ref, w_ref, h_ref, q_ref, k_ref, v_ref, m_ref, lse_ref, kn_ref):
    width, length = x_ref.shape
    block = q_ref.shape[0]
    heads = block // HEAD
    half = HEAD // 2

    @pl.when(pl.program_id(0) == 0)
    def _():
        def cols(c, carry):
            at = pl.ds(pl.multiple_of(c * 128, 128), 128)
            x = x_ref[:, at].astype(F32)
            centred = x - jnp.mean(x, axis=0, keepdims=True)
            spread = jnp.mean(centred * centred, axis=0, keepdims=True)
            h_ref[:, at] = (centred * lax.rsqrt(spread + EPS) * gain_ref[...]).astype(BF16)
            return carry
        lax.fori_loop(0, length // 128, cols, 0)

    cosine, sine = cos_ref[...], sin_ref[...]
    hidden = h_ref[...]
    for j, out in ((0, q_ref), (1, k_ref)):
        p = dot(w_ref[j], hidden, 0, 0)
        for h in range(heads):
            a = p[h * HEAD : h * HEAD + half]
            b = p[h * HEAD + half : (h + 1) * HEAD]
            ra = (a * cosine - b * sine).astype(BF16)
            rb = (b * cosine + a * sine).astype(BF16)
            if j == 0:
                ra, rb = ra * 0.125, rb * 0.125
            out[h * HEAD : h * HEAD + half, :] = ra
            out[h * HEAD + half : (h + 1) * HEAD, :] = rb
    v_ref[...] = dot(w_ref[2], hidden, 0, 0).astype(BF16)
    for h in range(heads):
        rows = slice(h * HEAD, (h + 1) * HEAD)
        kn_ref[h] = k_ref[rows, :].T
    def one(h, carry):
        rows = pl.ds(pl.multiple_of(h * HEAD, HEAD), HEAD)
        s = dot(kn_ref[h], q_ref[rows, :], 1, 0)
        top = jnp.max(s, axis=0, keepdims=True)
        e = jnp.exp(s - top)
        total = jnp.sum(e, axis=0, keepdims=True)
        o = dot(v_ref[rows, :], e.astype(BF16), 1, 0)
        m_ref[rows, :] = (o / total).astype(BF16)
        lse_ref[0, pl.ds(h, 1), :] = top + jnp.log(total)
        return carry
    lax.fori_loop(0, heads, one, 0)

def attn_fwd(xT, gain, cosT, sinT, w):
    width, length = xT.shape
    block = 256
    n = width // block
    col = pl.BlockSpec((block, length), lambda i: (i, 0))
    t = jax.ShapeDtypeStruct((width, length), BF16)
    return pl.pallas_call(
        attn_fwd_kernel, grid=(n,), name="attn_fwd", cost_estimate=cost(34),
        in_specs=[whole((width, length)), whole((width, 1)), whole(cosT.shape), whole(sinT.shape),
                  pl.BlockSpec((3, width, block), lambda i: (0, 0, i))],
        out_specs=[whole((width, length)), col, col, col, col, pl.BlockSpec((1, 8, length), lambda i: (i, 0, 0))],
        out_shape=[t, t, t, t, t, jax.ShapeDtypeStruct((n, 8, length), F32)],
        scratch_shapes=[pltpu.VMEM((block // HEAD, length, HEAD), BF16)],
        compiler_params=params(),
    )(xT, gain, cosT, sinT, w)

def attn_bwd_kernel(x_ref, gain_ref, cos_ref, sin_ref, sg_ref, h_ref, q_ref, k_ref, v_ref, m_ref, lse_ref, w_ref, wo_ref,
                    first_ref, gg_ref, dw_ref, hg_ref, low_ref, do_ref, kn_ref, vn_ref, dk_ref, dv_ref, dq_ref, dwo_ref):
    width, length = x_ref.shape
    block = q_ref.shape[0]
    heads = block // HEAD
    half = HEAD // 2
    step = min(BSTEP, length)
    i = pl.program_id(0)

    @pl.when(i == 0)
    def _():
        low_ref[...] = sg_ref[...].astype(BF16)
        hg_ref[...] = jnp.zeros_like(hg_ref)

    do_ref[...] = dot(wo_ref[0], low_ref[...], 1, 0).astype(BF16)
    fs, _, each, _ = dw_ref.shape
    dwo_ref[pl.ds(pl.multiple_of(i * block, block), block), :] = dot(m_ref[...], low_ref[...], 1, 1).astype(BF16)
    cosine, sine = cos_ref[...], sin_ref[...]
    for h in range(heads):
        rows = slice(h * HEAD, (h + 1) * HEAD)
        kn_ref[h] = k_ref[rows, :].T
        vn_ref[h] = v_ref[rows, :].T
    def one(h, carry):
        rows = pl.ds(pl.multiple_of(h * HEAD, HEAD), HEAD)
        for c in range(length // step):
            at = slice(c * step, (c + 1) * step)
            s = dot(kn_ref[h], q_ref[rows, at], 1, 0)
            p = jnp.exp(s - lse_ref[0, pl.ds(h, 1), at])
            dp = dot(vn_ref[h], do_ref[rows, at], 1, 0)
            centre = jnp.sum(p * dp, axis=0, keepdims=True)
            ds = (p * (dp - centre)).astype(BF16)
            pb = p.astype(BF16)
            dv = dot(do_ref[rows, at], pb, 1, 1)
            dk = dot(q_ref[rows, at], ds, 1, 1)
            if c == 0:
                dv_ref[rows, :] = dv
                dk_ref[rows, :] = dk
            else:
                dv_ref[rows, :] += dv
                dk_ref[rows, :] += dk
            dq_ref[rows, at] = dot(k_ref[rows, :], ds, 1, 0) * 0.125
        return carry
    lax.fori_loop(0, heads, one, 0)
    hidden = h_ref[...]
    for j, ref in ((0, dq_ref), (1, dk_ref), (2, dv_ref)):
        if j == 2:
            g = ref[...].astype(BF16)
        else:
            parts = []
            for h in range(heads):
                a = ref[h * HEAD : h * HEAD + half, :]
                b = ref[h * HEAD + half : (h + 1) * HEAD, :]
                parts += [(a * cosine + b * sine).astype(BF16), (b * cosine - a * sine).astype(BF16)]
            g = jnp.concatenate(parts, axis=0)
        dw_ref[:, j, :, pl.ds(pl.multiple_of(i * block, block), block)] = dot(hidden, g, 1, 1).astype(BF16).reshape(fs, each, block)
        hg_ref[...] += dot(w_ref[j], g, 1, 0)

    @pl.when(i == pl.num_programs(0) - 1)
    def _():
        dw_ref[:, 3] = dwo_ref[...].reshape(fs, each, width)
        def cols(c, acc):
            at = pl.ds(pl.multiple_of(c * 128, 128), 128)
            dx, gg = ln_back(x_ref[:, at].astype(F32), hg_ref[:, at], gain_ref[...])
            first_ref[:, at] = (sg_ref[:, at] + dx).astype(BF16)
            return acc + gg
        acc = lax.fori_loop(0, length // 128, cols, jnp.zeros((width, 128), F32))
        gg_ref[...] = jnp.sum(acc, axis=1, keepdims=True)

def ln_back(x, g, gain):
    centred = x - jnp.mean(x, axis=0, keepdims=True)
    spread = jnp.mean(centred * centred, axis=0, keepdims=True)
    rs = lax.rsqrt(spread + EPS)
    xh = centred * rs
    gx = g * gain
    dx = rs * (gx - jnp.mean(gx, axis=0, keepdims=True) - xh * jnp.mean(gx * xh, axis=0, keepdims=True))
    return dx, g * xh

def attn_bwd(xT, gain, cosT, sinT, sg, hT, q, k, v, m, lse, w, fs):
    width, length = xT.shape
    block = 256
    n = width // block
    col = pl.BlockSpec((block, length), lambda i: (i, 0))
    full = whole((width, length))
    return pl.pallas_call(
        attn_bwd_kernel, grid=(n,), name="attn_bwd", cost_estimate=cost(62),
        in_specs=[full, whole((width, 1)), whole(cosT.shape), whole(sinT.shape), full, full, col, col, col, col,
                  pl.BlockSpec((1, 8, length), lambda i: (i, 0, 0)),
                  pl.BlockSpec((3, width, block), lambda i: (0, 0, i)),
                  pl.BlockSpec((1, block, width), lambda i: (3, i, 0))],
        out_specs=[full, whole((width, 1)), whole((fs, 4, width // fs, width))],
        out_shape=[jax.ShapeDtypeStruct((width, length), BF16), jax.ShapeDtypeStruct((width, 1), F32),
                   jax.ShapeDtypeStruct((fs, 4, width // fs, width), BF16)],
        scratch_shapes=[pltpu.VMEM((width, length), F32), pltpu.VMEM((width, length), BF16), pltpu.VMEM((block, length), BF16),
                        pltpu.VMEM((block // HEAD, length, HEAD), BF16), pltpu.VMEM((block // HEAD, length, HEAD), BF16),
                        pltpu.VMEM((block, length), F32), pltpu.VMEM((block, length), F32), pltpu.VMEM((block, length), F32),
                        pltpu.VMEM((width, width), BF16)],
        compiler_params=params(),
    )(xT, gain, cosT, sinT, sg, hT, q, k, v, m, lse, w, w)
def ff_fwd_kernel(x_ref, m_ref, g2_ref, g3_ref, pos_ref, wo_ref, up_ref, down_ref,
                  x2_ref, h2_ref, x3_ref, head_ref, fin_ref):
    width, length = x_ref.shape
    i = pl.program_id(0)

    @pl.when(i == 0)
    def _():
        x2_ref[...] = x_ref[...].astype(F32) + dot(wo_ref[0], m_ref[...], 0, 0)
        x3_ref[...] = x2_ref[...]
        def cols(c, carry):
            at = pl.ds(pl.multiple_of(c * 128, 128), 128)
            h2_ref[:, at] = ln(x2_ref[:, at], g2_ref[...]).astype(BF16)
            return carry
        lax.fori_loop(0, length // 128, cols, 0)

    pre = dot(up_ref[0], h2_ref[...], 1, 0)
    act = jax.nn.gelu(pre, approximate=True).astype(BF16)
    x3_ref[...] += dot(down_ref[0], act, 0, 0)

    @pl.when(i == pl.num_programs(0) - 1)
    def _():
        def cols(c, carry):
            at = pl.ds(pl.multiple_of(c * 128, 128), 128)
            fin_ref[:, at] = ln(x3_ref[:, at], g3_ref[...]).astype(BF16)
            return carry
        lax.fori_loop(0, length // 128, cols, 0)
        slots = pos_ref.shape[0]
        onehot = (pos_ref[...] == lax.broadcasted_iota(jnp.int32, (slots, length), 1)).astype(BF16)
        head_ref[...] = dot(onehot, fin_ref[...], 1, 1).astype(BF16)

def ln(x, gain):
    centred = x - jnp.mean(x, axis=0, keepdims=True)
    spread = jnp.mean(centred * centred, axis=0, keepdims=True)
    return centred * lax.rsqrt(spread + EPS) * gain

def ff_fwd(xT, m, g2, g3, pos, attn_w, ff_w):
    width, length = xT.shape
    hidden = ff_w.shape[1]
    block = 512
    n = hidden // block
    slots = pos.shape[0]
    full = whole((width, length))
    f = jax.ShapeDtypeStruct((width, length), F32)
    return pl.pallas_call(
        ff_fwd_kernel, grid=(n,), name="ff_fwd", cost_estimate=cost(34),
        in_specs=[full, full, whole((width, 1)), whole((width, 1)), whole((slots, 1)),
                  pl.BlockSpec((1, width, width), lambda i: (3, 0, 0)),
                  pl.BlockSpec((1, block, width), lambda i: (0, i, 0)),
                  pl.BlockSpec((1, block, width), lambda i: (1, i, 0))],
        out_specs=[full, full, full, whole((slots, width))],
        out_shape=[f, jax.ShapeDtypeStruct((width, length), BF16), f, jax.ShapeDtypeStruct((slots, width), BF16)],
        scratch_shapes=[pltpu.VMEM((width, length), BF16)],
        compiler_params=params(),
    )(xT, m, g2, g3, pos, attn_w, ff_w, ff_w)

def ff_bwd_kernel(x3_ref, x2_ref, h2_ref, rg_ref, pos_ref, g2_ref, g3_ref, up_ref, down_ref,
                  sg_ref, gg2_ref, gg3_ref, dw_ref, low_ref, hg_ref):
    width, length = x3_ref.shape
    i = pl.program_id(0)
    slots = pos_ref.shape[0]

    @pl.when(i == 0)
    def _():
        rows = rg_ref[...]
        high = rows.astype(BF16)
        rest = (rows - high.astype(F32)).astype(BF16)
        hg_ref[...] = jnp.zeros_like(hg_ref)
        def cols(c, acc):
            at = pl.ds(pl.multiple_of(c * 128, 128), 128)
            onehot = (pos_ref[...] == c * 128 + lax.broadcasted_iota(jnp.int32, (slots, 128), 1)).astype(BF16)
            fg = dot(high, onehot, 0, 0) + dot(rest, onehot, 0, 0)
            dx, gg = ln_back(x3_ref[:, at], fg, g3_ref[...])
            sg_ref[:, at] = dx
            low_ref[:, at] = dx.astype(BF16)
            return acc + gg
        acc = lax.fori_loop(0, length // 128, cols, jnp.zeros((width, 128), F32))
        gg3_ref[...] = jnp.sum(acc, axis=1, keepdims=True)

    ag = dot(down_ref[0], low_ref[...], 1, 0)
    pre = dot(up_ref[0], h2_ref[...], 1, 0)
    c0, c1 = 0.7978845608028654, 0.044715
    t = jnp.tanh(c0 * (pre + c1 * pre * pre * pre))
    half = 0.5 * (1.0 + t)
    act = (pre * half).astype(BF16)
    slope = half + 0.5 * pre * (1.0 - t * t) * (c0 * (1.0 + 3.0 * c1 * pre * pre))
    pg = (slope * ag).astype(BF16)
    shape = (dw_ref.shape[0],) + dw_ref.shape[2:]
    dw_ref[:, 1] = dot(act, low_ref[...], 1, 1).astype(BF16).reshape(shape)
    dw_ref[:, 0] = dot(pg, h2_ref[...], 1, 1).astype(BF16).reshape(shape)
    hg_ref[...] += dot(up_ref[0], pg, 0, 0)

    @pl.when(i == pl.num_programs(0) - 1)
    def _():
        def cols(c, acc):
            at = pl.ds(pl.multiple_of(c * 128, 128), 128)
            dx, gg = ln_back(x2_ref[:, at], hg_ref[:, at], g2_ref[...])
            sg_ref[:, at] += dx
            return acc + gg
        acc = lax.fori_loop(0, length // 128, cols, jnp.zeros((width, 128), F32))
        gg2_ref[...] = jnp.sum(acc, axis=1, keepdims=True)

def ff_bwd(x3, x2, h2, rg, pos, g2, g3, ff_w, fs):
    width, length = x3.shape
    hidden = ff_w.shape[1]
    each = hidden // fs
    block = each * max(1, 768 // each)
    n = hidden // block
    slots = pos.shape[0]
    full = whole((width, length))
    wb = pl.BlockSpec((block // each, 2, each, width), lambda i: (i, 0, 0, 0))
    g = jax.ShapeDtypeStruct((width, 1), F32)
    return pl.pallas_call(
        ff_bwd_kernel, grid=(n,), name="ff_bwd", cost_estimate=cost(45),
        in_specs=[full, full, full, whole((slots, width)), whole((slots, 1)), whole((width, 1)), whole((width, 1)),
                  pl.BlockSpec((1, block, width), lambda i: (0, i, 0)),
                  pl.BlockSpec((1, block, width), lambda i: (1, i, 0))],
        out_specs=[full, whole((width, 1)), whole((width, 1)), wb],
        out_shape=[jax.ShapeDtypeStruct((width, length), F32), g, g, jax.ShapeDtypeStruct((fs, 2, each, width), BF16)],
        scratch_shapes=[pltpu.VMEM((width, length), BF16), pltpu.VMEM((width, length), F32)],
        compiler_params=params(),
    )(x3, x2, h2, rg, pos, g2, g3, ff_w, ff_w)
RB = 256
FCH, BCH = 8, 8

def pick(n, top=8):
    return max(k for k in range(1, top + 1) if n % k == 0)

def compact(meta_ref, rows_ref, comp_ref):
    nseq, slots, width = rows_ref.shape
    def clear(b, carry):
        comp_ref[pl.ds(pl.multiple_of(b * RB, RB), RB), :] = jnp.zeros((RB, width), BF16)
        return carry
    lax.fori_loop(0, meta_ref[2, 0], clear, 0)
    def seq(s, carry):
        def part(c, c2):
            comp_ref[pl.ds(pl.multiple_of((meta_ref[1, s] + c) * 16, 16), 16), :] = rows_ref[s, pl.ds(pl.multiple_of(c * 16, 16), 16), :]
            return c2
        lax.fori_loop(0, meta_ref[0, s], part, 0)
        return carry
    lax.fori_loop(0, nseq, seq, 0)

def vocab_fwd_kernel(meta_ref, limit_ref, rows_ref, source_ref, target_ref, lse_ref, chosen_ref, table_ref, *outs, chunk, least, inside):
    comp_ref = outs[0] if inside else rows_ref
    shard, width = source_ref.shape
    def cast(b, carry):
        at = pl.ds(pl.multiple_of(b * 128, 128), 128)
        table_ref[at, :] = source_ref[at, :].astype(BF16)
        return carry
    lax.fori_loop(0, shard // 128, cast, 0)
    full = shard // 128 * 128
    if full < shard:
        tail = jnp.concatenate([source_ref[full:, :], jnp.zeros((full + 128 - shard, width), F32)], axis=0)
        table_ref[full:, :] = tail.astype(BF16)
    vocab = table_ref.shape[0]
    if inside:
        nseq, slots, width = rows_ref.shape
        compact(meta_ref, rows_ref, comp_ref)
    lse_ref[...] = jnp.zeros_like(lse_ref)
    chosen_ref[...] = jnp.zeros_like(chosen_ref)
    limit = limit_ref[0]
    def block(b, carry):
        rows = comp_ref[pl.ds(pl.multiple_of(b * RB, RB), RB), :]
        target = target_ref[b]
        top = total = chosen = None
        for v in range(vocab // chunk):
            l = dot(table_ref[v * chunk:(v + 1) * chunk, :], rows, 1, 1)
            ids = v * chunk + lax.broadcasted_iota(jnp.int32, (chunk, RB), 0)
            hit = jnp.sum(jnp.where(ids == target, l, 0.0), axis=0, keepdims=True)
            if (v + 1) * chunk > least:
                l = jnp.where(ids < limit, l, -jnp.inf)
            m = jnp.max(l, axis=0, keepdims=True)
            if v == 0:
                top = m
                total = jnp.sum(jnp.exp(l - top), axis=0, keepdims=True)
                chosen = hit
            else:
                new = jnp.maximum(top, m)
                total = total * jnp.exp(top - new) + jnp.sum(jnp.exp(l - new), axis=0, keepdims=True)
                chosen = chosen + hit
                top = new
        lse_ref[b] = top + jnp.log(total)
        chosen_ref[b] = chosen
        return carry
    lax.fori_loop(0, meta_ref[2, 0], block, 0)

def vocab_fwd(meta, limit, rows, source, target, least):
    inside = rows.ndim == 3
    width = rows.shape[-1]
    nblk = target.shape[0]
    vocab = -(-source.shape[0] // 128) * 128
    chunk = 128 * pick(vocab // 128, FCH)
    smem = pl.BlockSpec(memory_space=pltpu.SMEM)
    vm = pl.BlockSpec(memory_space=pltpu.VMEM)
    st = jax.ShapeDtypeStruct((nblk, 1, RB), F32)
    comp = [jax.ShapeDtypeStruct((nblk * RB, width), BF16)] if inside else []
    out = pl.pallas_call(
        functools.partial(vocab_fwd_kernel, chunk=chunk, least=least, inside=inside), name="vocab_fwd", cost_estimate=cost(20),
        in_specs=[smem, smem, vm, vm, vm], out_specs=[vm] * (3 + len(comp)),
        out_shape=[st, st, jax.ShapeDtypeStruct((vocab, width), BF16)] + comp,
        compiler_params=params())(meta, limit, rows, source, target)
    return out[3] if inside else rows, out[2], out[0], out[1]

def vocab_bwd_kernel(meta_ref, limit_ref, comp_ref, table_ref, target_ref, lse_ref, scale_ref,
                     og_ref, og2_ref, rg_ref, acc_ref, rc_ref, low_ref, back_ref, sem, *, chunk, least, inside):
    vocab, width = table_ref.shape
    limit = limit_ref[0]
    nch = vocab // chunk
    def clear(b, carry):
        acc_ref[pl.ds(pl.multiple_of(b * 128, 128), 128), :] = jnp.zeros((128, width), F32)
        return carry
    lax.fori_loop(0, vocab // 128, clear, 0)
    def block(b, carry):
        rows = comp_ref[pl.ds(pl.multiple_of(b * RB, RB), RB), :]
        target, lse, scale = target_ref[b], lse_ref[b], scale_ref[b]
        rg = None
        for v in range(nch):
            l = dot(table_ref[v * chunk:(v + 1) * chunk, :], rows, 1, 1)
            ids = v * chunk + lax.broadcasted_iota(jnp.int32, (chunk, RB), 0)
            p = jnp.exp(l - lse)
            if (v + 1) * chunk > least:
                p = jnp.where(ids < limit, p, 0.0)
            g = (scale * jnp.where(ids == target, p - 1.0, p)).astype(BF16)
            acc_ref[v * chunk:(v + 1) * chunk, :] += dot(g, rows, 1, 0)
            part = dot(g, table_ref[v * chunk:(v + 1) * chunk, :], 0, 0)
            rg = part if rg is None else rg + part
        rc_ref[pl.ds(pl.multiple_of(b * RB, RB), RB), :] = rg.astype(BF16)
        return carry
    lax.fori_loop(0, meta_ref[2, 0], block, 0)
    if inside:
        nseq, slots, _ = back_ref.shape
        def seq(s, carry):
            back_ref[s] = jnp.zeros((slots, width), BF16)
            def part(c, c2):
                back_ref[s, pl.ds(pl.multiple_of(c * 16, 16), 16), :] = rc_ref[pl.ds(pl.multiple_of((meta_ref[1, s] + c) * 16, 16), 16), :]
                return c2
            lax.fori_loop(0, meta_ref[0, s], part, 0)
            return carry
        lax.fori_loop(0, nseq, seq, 0)
        out = pltpu.make_async_copy(back_ref, rg_ref, sem.at[0])
    else:
        out = pltpu.make_async_copy(rc_ref, rg_ref, sem.at[0])
    out.start()
    outs = [out]
    part = og_ref.shape[0]
    for v, (ref, start) in enumerate(((og_ref, 0), (og2_ref, part))):
        at = pl.ds(start, ref.shape[0])
        low_ref[at, :] = acc_ref[at, :].astype(BF16)
        outs.append(pltpu.make_async_copy(low_ref.at[at], ref, sem.at[1 + v]))
        outs[-1].start()
    for o in outs:
        o.wait()

def vocab_bwd(meta, limit, comp, table, target, lse, scale, least, nseq, slots, inside):
    rows, width = comp.shape
    vocab = table.shape[0]
    chunk = 128 * pick(vocab // 128, BCH)
    smem = pl.BlockSpec(memory_space=pltpu.SMEM)
    vm = pl.BlockSpec(memory_space=pltpu.VMEM)
    hbm = pl.BlockSpec(memory_space=pl.ANY)
    shape = (nseq, slots, width) if inside else (rows, width)
    part = vocab // 256 * 128
    return pl.pallas_call(
        functools.partial(vocab_bwd_kernel, chunk=chunk, least=least, inside=inside), name="vocab_bwd", cost_estimate=cost(40),
        in_specs=[smem, smem] + [vm] * 5, out_specs=[hbm, hbm, hbm],
        out_shape=[jax.ShapeDtypeStruct((part, width), BF16), jax.ShapeDtypeStruct((vocab - part, width), BF16), jax.ShapeDtypeStruct(shape, BF16)],
        scratch_shapes=[pltpu.VMEM((vocab, width), F32), pltpu.VMEM((rows, width), BF16),
                        pltpu.VMEM((vocab, width), BF16), pltpu.VMEM(shape if inside else (1, 16, width), BF16),
                        pltpu.SemaphoreType.DMA((3,))],
        compiler_params=params())(meta, limit, comp, table, target, lse, scale)

def plan(counts, slots, length):
    nseq = counts.shape[0]
    units = (counts + 15) // 16
    ends = jnp.cumsum(units)
    offs = ends - units
    total = ends[-1] * 16
    nblk = (total + RB - 1) // RB
    cap = (nseq * slots + RB - 1) // RB * RB
    at = jnp.arange(cap, dtype=jnp.int32)
    seq = jnp.minimum(jnp.sum((at[:, None] >= ends[None, :] * 16).astype(jnp.int32), axis=1), nseq - 1)
    mine = (seq[:, None] == jnp.arange(nseq, dtype=jnp.int32)[None, :])
    slot = at - jnp.sum(jnp.where(mine, offs[None, :] * 16, 0), axis=1)
    cnt = jnp.sum(jnp.where(mine, counts[None, :], 0), axis=1)
    live = slot < cnt
    weight = jnp.where(live, length / cnt.astype(F32), 0.0)
    meta = jnp.stack([units, offs, jnp.full((nseq,), nblk)]).astype(jnp.int32)
    return meta, seq, slot, weight

def spread(values, seq, slot):
    nseq, slots = values.shape
    parts = jnp.concatenate([values // 256, values % 256], axis=1).astype(BF16)
    mine = (seq[:, None] == jnp.arange(nseq, dtype=jnp.int32)[None, :]).astype(BF16)
    rows = jnp.dot(mine, parts, preferred_element_type=F32)
    hit = slot[:, None] == jnp.arange(slots, dtype=jnp.int32)[None, :]
    both = rows[:, :slots] * 256.0 + rows[:, slots:]
    return jnp.sum(jnp.where(hit, both, 0.0), axis=1).astype(jnp.int32)

def halves(vocab):
    nb = vocab // 128
    low = (nb + 1) // 2
    return nb, low

def sections(count, size):
    return [(s, min(size, count - s)) for s in range(0, count, size)]

def gather_kernel(ids_ref, flag_ref, emb_ref, out_ref, tab_ref, raw_ref, row_ref, sem):
    feat, vocab = emb_ref.shape
    nseq, _, length = out_ref.shape
    nb, low = halves(vocab)
    size = -(-low // 6)
    secs = sections(low, size)
    def copies(k):
        s, n = secs[k]
        out = [pltpu.make_async_copy(emb_ref.at[:, pl.ds(s * 128, n * 128)], raw_ref.at[:, pl.ds(s * 128, n * 128)], sem.at[2 * k])]
        m = min(n, nb - low - s)
        if m > 0:
            out.append(pltpu.make_async_copy(emb_ref.at[:, pl.ds((low + s) * 128, m * 128)], raw_ref.at[:, pl.ds((low + s) * 128, m * 128)], sem.at[2 * k + 1]))
        return out
    for k in range(len(secs)):
        for c in copies(k):
            c.start()
    pad = jnp.zeros((64 - feat, 128), F32)
    for k in range(len(secs)):
        for c in copies(k):
            c.wait()
        s, n = secs[k]
        m = max(0, min(n, nb - low - s))
        def turn(b, carry):
            a = raw_ref[:, pl.ds(pl.multiple_of(b * 128, 128), 128)]
            h = raw_ref[:, pl.ds(pl.multiple_of((low + b) * 128, 128), 128)]
            tab_ref[pl.ds(pl.multiple_of(b * 128, 128), 128), :] = jnp.concatenate([a, pad, h, pad], axis=0).T
            return carry
        lax.fori_loop(s, s + m, turn, 0, unroll=3)
        for b in range(s + m, s + n):
            a = raw_ref[:, b * 128:(b + 1) * 128]
            tab_ref[b * 128:(b + 1) * 128, :] = jnp.concatenate([a, pad, pad, jnp.zeros((feat, 128), F32)], axis=0).T
    U = 32
    def seq(s, carry):
        def grp(g, c2):
            base = pl.multiple_of(g * U, U)
            for j in range(U):
                i = ids_ref[s * length + base + j]
                row_ref[pl.ds(base + j, 1), :] = tab_ref[pl.ds(i, 1), :]
            return c2
        lax.fori_loop(0, length // U, grp, 0)
        for c in range(length // 128):
            t = row_ref[c * 128:(c + 1) * 128, :].T
            f = flag_ref[s, :, c * 128:(c + 1) * 128] > 0
            out_ref[s, :, c * 128:(c + 1) * 128] = jnp.where(f, t[64:64 + feat], t[:feat]).astype(BF16)
        return carry
    lax.fori_loop(0, nseq, seq, 0)

def split_ids(ids, vocab):
    nb, low = halves(vocab)
    high = ids >= low * 128
    return jnp.where(high, ids - low * 128, ids), high.astype(jnp.int32)

def gather(ids, emb):
    nseq, length = ids.shape
    feat, vocab = emb.shape
    nb, low = halves(vocab)
    rid, flag = split_ids(ids, vocab)
    return pl.pallas_call(gather_kernel, name="emb_gather", cost_estimate=cost(32),
        in_specs=[pl.BlockSpec(memory_space=pltpu.SMEM), pl.BlockSpec(memory_space=pltpu.VMEM), pl.BlockSpec(memory_space=pl.ANY)],
        out_specs=pl.BlockSpec(memory_space=pltpu.VMEM),
        out_shape=jax.ShapeDtypeStruct((nseq, feat, length), BF16),
        scratch_shapes=[pltpu.VMEM((low * 128, 128), F32), pltpu.VMEM((feat, vocab), F32), pltpu.VMEM((length, 128), F32), pltpu.SemaphoreType.DMA((12,))],
        compiler_params=params())(rid.reshape(-1), flag.reshape(nseq, 1, length), emb)

def scatter_kernel(ids_ref, flag_ref, *refs, ng, per):
    g_refs = refs[:ng]
    out_ref, sq_ref, raw_ref, row_ref, sem = refs[ng:ng + 5]
    tabs = refs[ng + 5:]
    feat, vocab = out_ref.shape
    nseq, _, length = g_refs[0].shape
    nb, low = halves(vocab)
    zero128 = jnp.zeros((128, 128), F32)
    def zero(b, carry):
        for t in tabs:
            t[pl.ds(pl.multiple_of(b * 128, 128), 128), :] = zero128
        return carry
    lax.fori_loop(0, low, zero, 0)
    pad = jnp.zeros((64 - feat, 128), F32)
    U = 8
    streams = [(g, p) for g in range(ng) for p in range(per)]
    each = nseq // per
    def seq(s, carry):
        for k, (g, p) in enumerate(streams):
            q = p * each + s
            for c in range(length // 128):
                at = slice(c * 128, (c + 1) * 128)
                v = g_refs[g][q, :, at].astype(F32)
                f = flag_ref[g * nseq + q, :, at] > 0
                row_ref[k, at, :] = jnp.concatenate([jnp.where(f, 0.0, v), pad, jnp.where(f, v, 0.0), pad], axis=0).T
        def grp(n, c2):
            base = pl.multiple_of(n * U, U)
            for j in range(U):
                idx = [ids_ref[(g * nseq + p * each + s) * length + base + j] for g, p in streams]
                old = [tabs[k][pl.ds(idx[k], 1), :] for k in range(len(streams))]
                new = [old[k] + row_ref[k, pl.ds(base + j, 1), :] for k in range(len(streams))]
                for k in range(len(streams)):
                    tabs[k][pl.ds(idx[k], 1), :] = new[k]
            return c2
        lax.fori_loop(0, length // U, grp, 0)
        return carry
    lax.fori_loop(0, each, seq, 0)
    def tile(b):
        at = pl.ds(pl.multiple_of(b * 128, 128), 128)
        parts = [sum((tabs[g * per + p][at, :] for p in range(1, per)), tabs[g * per][at, :]) for g in range(ng)]
        return sum(parts[1:], parts[0]).T
    size = -(-low // 6)
    secs = sections(low, size)
    def copies(k):
        s, n = secs[k]
        out = [pltpu.make_async_copy(raw_ref.at[k % 2, 0, :, pl.ds(0, n * 128)], out_ref.at[:, pl.ds(s * 128, n * 128)], sem.at[2 * k])]
        m = min(n, nb - low - s)
        if m > 0:
            out.append(pltpu.make_async_copy(raw_ref.at[k % 2, 1, :, pl.ds(0, m * 128)], out_ref.at[:, pl.ds((low + s) * 128, m * 128)], sem.at[2 * k + 1]))
        return out
    squares = jnp.zeros((128, 128), F32)
    for k, (s, n) in enumerate(secs):
        if k >= 2:
            for c in copies(k - 2):
                c.wait()
        def turn(b, carry, s=s, k=k):
            t = tile(b)
            at = pl.ds(pl.multiple_of((b - s) * 128, 128), 128)
            raw_ref[k % 2, 0, :, at] = t[:feat]
            raw_ref[k % 2, 1, :, at] = t[64:64 + feat]
            return carry + t * t
        squares = lax.fori_loop(s, s + n, turn, squares, unroll=3)
        for c in copies(k):
            c.start()
    sq_ref[...] = squares
    for k in range(max(0, len(secs) - 2), len(secs)):
        for c in copies(k):
            c.wait()

def scatter(ids, gs, vocab, per):
    nseq, feat, length = gs[0].shape
    nb, low = halves(vocab)
    rid, flag = split_ids(ids, vocab)
    ng = len(gs)
    size = -(-low // 6)
    vm = pl.BlockSpec(memory_space=pltpu.VMEM)
    return pl.pallas_call(functools.partial(scatter_kernel, ng=ng, per=per), name="emb_scatter", cost_estimate=cost(66),
        in_specs=[pl.BlockSpec(memory_space=pltpu.SMEM), vm] + [vm] * ng,
        out_specs=[pl.BlockSpec(memory_space=pl.ANY), vm],
        out_shape=[jax.ShapeDtypeStruct((feat, vocab), F32), jax.ShapeDtypeStruct((128, 128), F32)],
        scratch_shapes=[pltpu.VMEM((2, 2, feat, size * 128), F32), pltpu.VMEM((ng * per, length, 128), F32), pltpu.SemaphoreType.DMA((12,))]
            + [pltpu.VMEM((low * 128, 128), F32)] * (ng * per),
        compiler_params=params(62 * 1024 * 1024))(rid.reshape(-1), flag.reshape(-1, 1, length), *gs)
MESH_ID = pl.DeviceIdType.MESH

def comm_params(ident):
    return pltpu.CompilerParams(collective_id=ident, has_side_effects=True, vmem_limit_bytes=VL)

def meet(peers):
    barrier = pltpu.get_barrier_semaphore()
    for p in peers:
        pl.semaphore_signal(barrier, inc=1, device_id=p, device_id_type=MESH_ID)
    pl.semaphore_wait(barrier, len(peers))

def remote(src, dst, send, recv, peer):
    return pltpu.make_async_remote_copy(src_ref=src, dst_ref=dst, send_sem=send, recv_sem=recv, device_id=peer, device_id_type=MESH_ID)

def small_kernel(x_ref, *refs, fs, dps, wide, finish):
    out_ref = refs[0]
    got_ref = refs[1] if finish else out_ref
    send, recv = refs[-2:]
    d, f = lax.axis_index("dp"), lax.axis_index("fsdp")
    n = fs * dps if wide else fs
    me = d * fs + f if wide else f
    def peer(k):
        j = lax.rem(me + k, n)
        return (lax.div(j, fs), lax.rem(j, fs)) if wide else (d, j)
    barrier = pltpu.get_barrier_semaphore()
    def greet(k, carry):
        pl.semaphore_signal(barrier, inc=1, device_id=peer(k), device_id_type=MESH_ID)
        return carry
    lax.fori_loop(1, n, greet, 0)
    pl.semaphore_wait(barrier, n - 1)
    def copy(k):
        return remote(x_ref, got_ref.at[me], send.at[k], recv.at[k], peer(k))
    def begin(k, carry):
        copy(k).start()
        return carry
    lax.fori_loop(1, n, begin, 0)
    got_ref[me] = x_ref[...]
    def end(k, carry):
        copy(k).wait()
        return carry
    lax.fori_loop(1, n, end, 0)
    if finish:
        finish(got_ref, out_ref, n)

def lse_finish(got_ref, out_ref, n):
    top = got_ref[0]
    for i in range(1, n):
        top = jnp.maximum(top, got_ref[i])
    total = jnp.exp(got_ref[0] - top)
    for i in range(1, n):
        total = total + jnp.exp(got_ref[i] - top)
    out_ref[...] = top + jnp.log(total)

def sum_finish(got_ref, out_ref, n):
    total = got_ref[0]
    for i in range(1, n):
        total = total + got_ref[i]
    out_ref[...] = total

def small_gather(x, ident, wide=False, finish=None, name="small_gather"):
    fs, dps = lax.axis_size("fsdp"), lax.axis_size("dp")
    n = fs * dps if wide else fs
    vm = pl.BlockSpec(memory_space=pltpu.VMEM)
    got = (n,) + x.shape
    return pl.pallas_call(
        functools.partial(small_kernel, fs=fs, dps=dps, wide=wide, finish=finish), name=name,
        in_specs=[vm], out_specs=vm,
        out_shape=jax.ShapeDtypeStruct(x.shape if finish else got, x.dtype),
        scratch_shapes=([pltpu.VMEM(got, x.dtype)] if finish else []) + [pltpu.SemaphoreType.DMA((n,)), pltpu.SemaphoreType.DMA((n,))],
        cost_estimate=cost(12), compiler_params=comm_params(ident))(x)

def exchange_kernel(*refs, fs, both, aux):
    refs = list(refs)
    x_ref = refs.pop(0)
    aux_ref = refs.pop(0) if aux else None
    out_ref = refs.pop(0)
    other_ref = refs.pop(0) if both else None
    if aux:
        sum_ref, near_ref, over_ref = refs.pop(0), refs.pop(-2), refs.pop(-1)
    send, recv, send2, recv2, own = refs[:5]
    d, f = lax.axis_index("dp"), lax.axis_index("fsdp")
    across = (1 - d, f)
    barrier = pltpu.get_barrier_semaphore()
    def greet(k, carry):
        pl.semaphore_signal(barrier, inc=1, device_id=(d, lax.rem(f + k, fs)), device_id_type=MESH_ID)
        return carry
    lax.fori_loop(1, fs, greet, 0)
    if both:
        pl.semaphore_signal(barrier, inc=1, device_id=across, device_id_type=MESH_ID)
    pl.semaphore_wait(barrier, fs if both else fs - 1)
    def copies(k):
        j = lax.rem(f + k, fs)
        out = [remote(x_ref.at[j], out_ref.at[f], send.at[0, k], recv.at[0, k], (d, j))]
        if aux:
            out.append(remote(aux_ref, near_ref.at[f], send.at[1, k], recv.at[1, k], (d, j)))
        return out
    def passed(k):
        s = lax.rem(f + fs - k, fs)
        out = [remote(out_ref.at[s], other_ref.at[s], send2.at[0, k], recv2.at[0, k], across)]
        if aux:
            out.append(remote(near_ref.at[s], over_ref.at[s], send2.at[1, k], recv2.at[1, k], across))
        return out
    def first():
        out = [remote(x_ref.at[f], other_ref.at[f], send2.at[0, 0], recv2.at[0, 0], across)]
        if aux:
            out.append(remote(aux_ref, over_ref.at[f], send2.at[1, 0], recv2.at[1, 0], across))
        return out
    if both:
        for c in first():
            c.start()
    def begin(k, carry):
        for c in copies(k):
            c.start()
        return carry
    lax.fori_loop(1, fs, begin, 0)
    mine = pltpu.make_async_copy(x_ref.at[f], out_ref.at[f], own)
    mine.start()
    if aux:
        near_ref[f] = aux_ref[...]
    mine.wait()
    def arrive(k, carry):
        for c in copies(k):
            c.wait_recv()
        if both:
            for c in passed(k):
                c.start()
        return carry
    lax.fori_loop(1, fs, arrive, 0)
    def end(k, carry):
        for c in copies(k):
            c.wait_send()
        if both:
            for c in passed(k):
                c.wait()
        return carry
    lax.fori_loop(1, fs, end, 0)
    if both:
        for c in first():
            c.wait()
    if aux:
        total = near_ref[0]
        for i in range(1, fs):
            total = total + near_ref[i]
        if both:
            rest = over_ref[0]
            for i in range(1, fs):
                rest = rest + over_ref[i]
            total = total + rest
        sum_ref[...] = total

def exchange(x, ident, both, name, aux=None):
    fs = lax.axis_size("fsdp")
    vm = pl.BlockSpec(memory_space=pltpu.VMEM)
    shape = jax.ShapeDtypeStruct(x.shape, x.dtype)
    sem = pltpu.SemaphoreType.DMA((2, fs))
    more = [] if aux is None else [pltpu.VMEM((fs,) + aux.shape, F32)] * 2
    outs = [shape] * (2 if both else 1) + ([] if aux is None else [jax.ShapeDtypeStruct(aux.shape, F32)])
    return pl.pallas_call(
        functools.partial(exchange_kernel, fs=fs, both=both, aux=aux is not None), name=name,
        in_specs=[vm] * (1 if aux is None else 2), out_specs=[vm] * len(outs), out_shape=outs,
        scratch_shapes=[sem, sem, sem, sem, pltpu.SemaphoreType.DMA] + more,
        cost_estimate=cost(55),
        compiler_params=comm_params(ident))(*([x] if aux is None else [x, aux]))

def rows_gather_kernel(x_ref, out_ref, send, recv, *, high):
    d, f = lax.axis_index("dp"), lax.axis_index("fsdp")
    h, m, c = lax.div(f, 4), lax.rem(lax.div(f, 2), 2), lax.rem(f, 2)
    side, twin = (d, h * 4 + (1 - m) * 2 + c), (d, h * 4 + m * 2 + 1 - c)
    def far(k):
        return (d, lax.rem(h + k, high) * 4 + m * 2 + c)
    meet([far(k) for k in range(1, high)] + [side, twin])
    sent = []
    def go(src, block, peer):
        r = remote(src, out_ref.at[block], send.at[len(sent)], recv.at[block], peer)
        r.start()
        sent.append(r)
    def arrived(block):
        remote(x_ref, out_ref.at[block], send.at[0], recv.at[block], twin).wait_recv()
    for k in range(1, high):
        go(x_ref, f, far(k))
    go(x_ref, f, side)
    go(x_ref, f, twin)
    out_ref[f] = x_ref[...]
    for k in range(1, high):
        b = lax.rem(h + high - k, high) * 4 + m * 2 + c
        arrived(b)
        go(out_ref.at[b], b, side)
        go(out_ref.at[b], b, twin)
    for k in range(high):
        b = lax.rem(h + high - k, high) * 4 + (1 - m) * 2 + c
        arrived(b)
        go(out_ref.at[b], b, twin)
    for mm in range(2):
        for k in range(high):
            arrived(lax.rem(h + high - k, high) * 4 + lax.rem(m + mm, 2) * 2 + 1 - c)
    for r in sent:
        r.wait_send()

def rows_gather(x, ident, name="rows_gather"):
    fs = lax.axis_size("fsdp")
    vm = pl.BlockSpec(memory_space=pltpu.VMEM)
    high = fs // 4
    return pl.pallas_call(
        functools.partial(rows_gather_kernel, high=high), name=name,
        in_specs=[vm], out_specs=vm, out_shape=jax.ShapeDtypeStruct((fs,) + x.shape, x.dtype),
        scratch_shapes=[pltpu.SemaphoreType.DMA((4 * high,)), pltpu.SemaphoreType.DMA((fs,))],
        cost_estimate=cost(44), compiler_params=comm_params(ident))(x)

def rows_reduce_kernel(x_ref, out_ref, twin_ref, side_ref, far_ref, a_ref, b_ref, s1, r1, s2, r2, s3, r3, *, high, both):
    d, f = lax.axis_index("dp"), lax.axis_index("fsdp")
    h, m, c = lax.div(f, 4), lax.rem(lax.div(f, 2), 2), lax.rem(f, 2)
    side, twin = (d, h * 4 + (1 - m) * 2 + c), (d, h * 4 + m * 2 + 1 - c)
    def far(k):
        return (d, lax.rem(h + k, high) * 4 + m * 2 + c)
    across = (1 - d, f)
    meet([far(k) for k in range(1, high)] + [side, twin] + ([across] if both else []))
    order = list(range(1, high)) + [0]
    def at(k):
        return lax.rem(h + k, high)
    def one(k, mm):
        slot = at(k) * 2 + mm
        return remote(x_ref.at[at(k) * 4 + mm * 2 + 1 - c], twin_ref.at[slot], s1.at[slot], r1.at[slot], twin)
    def two(k):
        return remote(a_ref.at[at(k)], side_ref.at[at(k)], s2.at[at(k)], r2.at[at(k)], side)
    def three(k):
        return remote(b_ref.at[k], far_ref.at[k], s3.at[k], r3.at[k], far(k))
    for k in order:
        one(k, 1 - m).start()
    for k in order:
        one(k, m).start()
    for k in order:
        one(k, 1 - m).wait_recv()
        a_ref[at(k)] = (x_ref[at(k) * 4 + (1 - m) * 2 + c].astype(F32) + twin_ref[at(k) * 2 + 1 - m].astype(F32)).astype(a_ref.dtype)
        two(k).start()
    for k in order:
        one(k, m).wait_recv()
        two(k).wait_recv()
        total = x_ref[at(k) * 4 + m * 2 + c].astype(F32) + twin_ref[at(k) * 2 + m].astype(F32) + side_ref[at(k)].astype(F32)
        if k == 0:
            out_ref[...] = total
        else:
            b_ref[k] = total.astype(b_ref.dtype)
            three(k).start()
    for k in range(1, high):
        three(k).wait_recv()
        out_ref[...] += far_ref[k].astype(F32)
    if both:
        b_ref[0] = out_ref[...].astype(b_ref.dtype)
        last = remote(b_ref.at[0], far_ref.at[0], s3.at[0], r3.at[0], across)
        last.start()
        last.wait()
        out_ref[...] = b_ref[0].astype(F32) + far_ref[0].astype(F32)
    for k in order:
        one(k, m).wait_send()
        one(k, 1 - m).wait_send()
        two(k).wait_send()
        if k:
            three(k).wait_send()

def rows_reduce(x, ident, name="rows_reduce", both=False):
    fs = lax.axis_size("fsdp")
    vm = pl.BlockSpec(memory_space=pltpu.VMEM)
    high = fs // 4
    block = x.shape[1:]
    def sem(n):
        return pltpu.SemaphoreType.DMA((n,))
    def buf(n):
        return pltpu.VMEM((n,) + block, x.dtype)
    return pl.pallas_call(
        functools.partial(rows_reduce_kernel, high=high, both=both), name=name,
        in_specs=[vm], out_specs=vm, out_shape=jax.ShapeDtypeStruct(block, F32),
        scratch_shapes=[buf(2 * high), buf(high), buf(high), buf(high), buf(high),
                        sem(2 * high), sem(2 * high), sem(high), sem(high), sem(high), sem(high)],
        cost_estimate=cost(45), compiler_params=comm_params(ident))(x)
MASK_ID = 50257
STRATA = 16
STEP = 10

clip_level = 1.0
beta_one = 0.9
beta_two = 0.95
adam_eps = 1e-08
adam_decay = 0.01
rate_embed = 2.0
rate_out = 0.25
rate_gain = 0.5
rate_shampoo = 0.3
shampoo_decay = 0.01
stat_decay = 0.5
ema_decay = 0.7


def rotary_tables(length, half_width):
    inverse = 10000.0 ** (-jnp.arange(half_width, dtype=F32) / half_width)
    angles = inverse[:, None] * jnp.arange(length, dtype=F32)[None, :]
    return (jnp.cos(angles), jnp.sin(angles))


def adamw(weight, moment_one, moment_two, gradient, step_rate):
    one_new = beta_one * moment_one + (1 - beta_one) * gradient
    two_new = beta_two * moment_two + (1 - beta_two) * gradient * gradient
    one_hat = one_new / (1 - beta_one**STEP)
    two_hat = two_new / (1 - beta_two**STEP)
    weight_new = weight - step_rate * (
        one_hat / (jnp.sqrt(two_hat) + adam_eps) + adam_decay * weight
    )
    return (weight_new, one_new, two_new)


def dp_other(x):
    return lax.ppermute(x, "dp", [(0, 1), (1, 0)])


def dp_sum(x):
    count = lax.axis_size("dp")
    if count == 1:
        return x.astype(F32)
    if count == 2:
        return x.astype(F32) + dp_other(x).astype(F32)
    return lax.psum(x, "dp").astype(F32)


def spread_out(x):
    return lax.all_gather(x.astype(BF16), "fsdp", axis=1, tiled=True)


def per_device(
    tokens, positions, strata, groups, embedding, out_table, norm_gains, attention, feedforward,
    embed_moment_one, embed_moment_two, out_moment_one, out_moment_two, gain_moment_one, gain_moment_two,
    attention_left, attention_right, attention_left_root, attention_right_root,
    ff_left, ff_right, ff_left_root, ff_right_root,
    ema_embed, ema_out, ema_gains, ema_attention, ema_feedforward,
):
    fs = lax.axis_size("fsdp")
    dps = lax.axis_size("dp")
    me = lax.axis_index("fsdp")
    replica = lax.axis_index("dp")
    seq_count, length = tokens.shape
    slots = positions.shape[1]
    features, vocab = embedding.shape
    width = features * fs
    shard = out_table.shape[0]

    counts = jnp.maximum(1, (strata + 1) * slots * (1 + groups) // (2 * STRATA))
    in_use = jnp.arange(slots, dtype=jnp.int32)[None, :] < counts[:, None]
    places = jnp.arange(length, dtype=jnp.int32)
    same = positions[0][:, None] == places[None, :]
    marked = jnp.any(same & in_use[0][:, None], axis=0)
    ids_in = jnp.where(marked, MASK_ID, tokens[0])
    targets = jnp.sum(jnp.where(same, tokens[0][None, :], 0), axis=1)
    packed = jnp.concatenate([ids_in, targets, counts])
    packed = jnp.pad(packed, (0, -packed.shape[0] % 1024))
    everyone = small_gather(packed.reshape(-1, 128), 1, wide=True, name="ids_gather").reshape(fs * dps, -1)
    group = lax.dynamic_slice_in_dim(everyone, replica * fs, fs, 0)
    all_ids = everyone[:, :length]
    group_ids = group[:, :length]
    group_targets = group[:, length:length + slots]
    group_counts = group[:, length + slots]

    attn_w = spread_out(attention)
    ff_w = spread_out(feedforward)
    attn_root = spread_out(attention_right_root)
    ff_root = spread_out(ff_right_root)

    picked = gather(group_ids, embedding)
    xT = exchange(picked, 2, False, "features")[0].reshape(width, length)

    cosT, sinT = rotary_tables(length, HEAD // 2)
    gain = [norm_gains[i][:, None] for i in range(3)]
    place = positions[0][:, None]
    hT, qT, kT, vT, mixT, lse = attn_fwd(xT, gain[0], cosT, sinT, attn_w)
    x2, h2, x3, head = ff_fwd(xT, mixT, gain[1], gain[2], place, attn_w, ff_w)

    rows = rows_gather(head, 3)
    first_id = me * shard
    limit = jnp.clip(MASK_ID - first_id, 0, shard).reshape(1)
    least = min(shard, MASK_ID - (fs - 1) * shard)
    meta, seq, slot, weight = plan(group_counts, slots, length)
    nblk = seq.shape[0] // RB
    target = (spread(group_targets, seq, slot) - first_id).reshape(nblk, 1, RB)
    inside = fs * slots <= 4096
    if not inside:
        rows = jnp.take(rows.reshape(fs * slots, width), jnp.clip(seq * slots + slot, 0, fs * slots - 1), axis=0)
    comp, low, lse_own, chosen = vocab_fwd(meta, limit, rows, out_table, target, least)
    lse_sum = small_gather(lse_own, 4, finish=lse_finish, name="lse_gather")
    own_loss = jnp.sum(weight * (jnp.where(seq == me, lse_sum.reshape(-1), 0.0) - chosen.reshape(-1)))
    scale = weight / (seq_count * fs * dps)
    lse_sum, attn_root, ff_root = lax.optimization_barrier((lse_sum, attn_root, ff_root))
    out_one, out_two, row_grads = vocab_bwd(
        meta, limit, comp, low, target, lse_sum, scale.reshape(nblk, 1, RB),
        least, fs, slots, inside,
    )
    if not inside:
        at = jnp.arange(slots, dtype=jnp.int32)[None, :]
        row_grads = jnp.take(row_grads, jnp.minimum(meta[1][:, None] * 16 + at, seq.shape[0] - 1), axis=0)
        row_grads = jnp.where((at < group_counts[:, None])[:, :, None], row_grads, 0)
    own_rows = rows_reduce(row_grads, 5)
    halves_low = (out_one, out_two)
    if dps == 2:
        others = [dp_other(x) for x in halves_low]

    second, gg2, gg3, dff = ff_bwd(x3, x2, h2, own_rows, place, gain[1], gain[2], ff_w, fs)
    if dps == 2:
        second, others[0] = lax.optimization_barrier((second, others[0]))
    first, gg1, dattn = attn_bwd(xT, gain[0], cosT, sinT, second, hT, qT, kT, vT, mixT, lse, attn_w, fs)

    ff_part = lax.psum_scatter(dff.reshape(-1, width), "fsdp", scatter_dimension=0, tiled=True)

    aux = jnp.concatenate([jnp.concatenate([gg1, gg2, gg3], axis=1).T.reshape(-1), own_loss[None]])
    aux = jnp.pad(aux, (0, -aux.shape[0] % 1024)).reshape(-1, 128)
    if dps == 2:
        first, others[1] = lax.optimization_barrier((first, others[1]))
        out_grad = [a.astype(F32) + b.astype(F32) for a, b in zip(halves_low, others)]
    else:
        out_grad = [dp_sum(a) for a in halves_low]
    out_grad = jnp.concatenate(out_grad)[:shard]
    out = exchange(first.reshape(fs, features, length), 6, dps == 2, "gradients", aux)
    if dps == 2:
        parts, other, aux = out
        parts, ff_part = lax.optimization_barrier((parts, ff_part))
        ff_grad = dp_sum(ff_part.reshape(2, -1, width))
        parts, ff_grad = lax.optimization_barrier((parts, ff_grad))
        other_ids = lax.dynamic_slice_in_dim(everyone, (1 - replica) * fs, fs, 0)[:, :length]
        embed_grad, embed_sq = scatter(jnp.concatenate([group_ids, other_ids]), (parts, other), vocab, 2)
        embed_sq = jnp.sum(embed_sq)
    else:
        parts, aux = out
        ff_grad = dp_sum(ff_part.reshape(2, -1, width))
        embed_grad = dp_sum(scatter(group_ids, (parts,), vocab, 2)[0].astype(BF16))
        embed_sq = jnp.sum(embed_grad * embed_grad)
        if dps > 1:
            aux = lax.psum(aux, "dp")
    dattn, embed_sq = lax.optimization_barrier((dattn, embed_sq))
    attn_grad = rows_reduce(dattn.reshape(fs, -1, width), 8, "attn_reduce", dps == 2).reshape(4, -1, width)
    if dps != 2:
        attn_grad = dp_sum(attn_grad.astype(BF16))
    aux = aux.reshape(-1)
    gain_grad, loss_sum = aux[: 3 * width].reshape(3, width), aux[3 * width]
    squares = (
        jnp.sum(attn_grad * attn_grad)
        + jnp.sum(ff_grad * ff_grad)
        + embed_sq
        + jnp.sum(out_grad * out_grad)
    )
    attn_full, ff_full = spread_out(attn_grad), spread_out(ff_grad)
    squares, ff_full = lax.optimization_barrier((squares, ff_full))
    squares = small_gather(jnp.full((8, 128), squares), 7, finish=sum_finish, name="squares")[0, 0]
    clip_norm = jnp.sqrt(squares + jnp.sum(gain_grad * gain_grad))
    factor = jnp.minimum(1.0, clip_level / clip_norm)
    embed_new, embed_one_new, embed_two_new = adamw(
        embedding, embed_moment_one, embed_moment_two, embed_grad * factor, rate_embed
    )
    out_new, out_one_new, out_two_new = adamw(
        out_table, out_moment_one, out_moment_two, out_grad * factor, rate_out
    )
    gains_new, gains_one_new, gains_two_new = adamw(
        norm_gains, gain_moment_one, gain_moment_two, gain_grad * factor, rate_gain
    )

    def shampoo(weights, grad, left, right, left_root, whole_root, full):
        own = grad.astype(BF16)
        columns = right.shape[1]
        own_columns = lax.dynamic_slice_in_dim(full, me * columns, columns, 2)

        def product(text, a, b):
            return jnp.einsum(text, a, b, preferred_element_type=F32)

        mix = (1 - stat_decay) * factor * factor
        left_new = stat_decay * left + mix * product("nik,njk->nij", own, full)
        right_new = stat_decay * right + mix * product("nki,nkj->nij", own_columns, full)
        part = product("nij,njk->nik", left_root.astype(BF16), full)
        update = product("nij,njk->nik", part.astype(BF16), whole_root) * factor
        new = weights - rate_shampoo * (update + shampoo_decay * weights)
        return new, grad * factor, left_new, right_new

    attention_new, attn_clip, attention_left_new, attention_right_new = shampoo(
        attention, attn_grad, attention_left, attention_right, attention_left_root, attn_root, attn_full
    )
    ff_new, ff_clip, ff_left_new, ff_right_new = shampoo(
        feedforward, ff_grad, ff_left, ff_right, ff_left_root, ff_root, ff_full
    )

    def averaged(average, new):
        return ema_decay * average + (1 - ema_decay) * new

    return (
        loss_sum, clip_norm, embed_new, embed_one_new, embed_two_new, out_new, out_one_new, out_two_new,
        gains_new, gains_one_new, gains_two_new, attention_new, attn_clip, attention_left_new, attention_right_new,
        ff_new, ff_clip, ff_left_new, ff_right_new,
        averaged(ema_embed, embed_new), averaged(ema_out, out_new), averaged(ema_gains, gains_new),
        averaged(ema_attention, attention_new), averaged(ema_feedforward, ff_new),
    )


def solution(mesh):
    seqs, rows, stack, none = P(("dp", "fsdp")), P("fsdp", None), P(None, "fsdp", None), P()
    in_specs = (
        seqs, seqs, seqs, seqs, rows, rows, none, stack, stack, rows, rows, rows, rows, none, none,
        stack, stack, stack, stack, stack, stack, stack, stack, rows, rows, none, stack, stack,
    )
    out_specs = (
        none, none, rows, rows, rows, rows, rows, rows, none, none, none, stack, stack, stack, stack,
        stack, stack, stack, stack, rows, rows, none, stack, stack,
    )
    return jax.shard_map(
        per_device, mesh=mesh, in_specs=in_specs, out_specs=out_specs, check_vma=False
    )
```

```python
import functools

import jax
import jax.numpy as jnp
from jax import lax
from jax.experimental import pallas as pl
from jax.experimental.pallas import tpu as pltpu
from jax.sharding import PartitionSpec as P

F32, BF16 = jnp.float32, jnp.bfloat16
HEAD = 64
EPS = 1e-5
BSTEP = 1024
VL = 60 * 1024 * 1024

def dot(a, b, ca, cb):
    return lax.dot_general(a, b, (((ca,), (cb,)), ((), ())), preferred_element_type=F32)

def params(limit=VL):
    return pltpu.CompilerParams(vmem_limit_bytes=limit)

def cost(us):
    return pl.CostEstimate(flops=int(us * 1.15e9), bytes_accessed=0, transcendentals=0)

def whole(shape):
    return pl.BlockSpec(shape, lambda *a: (0,) * len(shape))

def attn_fwd_kernel(x_ref, gain_ref, cos_ref, sin_ref, w_ref, h_ref, q_ref, k_ref, v_ref, m_ref, lse_ref, kn_ref):
    width, length = x_ref.shape
    block = q_ref.shape[0]
    heads = block // HEAD
    half = HEAD // 2

    @pl.when(pl.program_id(0) == 0)
    def _():
        def cols(c, carry):
            at = pl.ds(pl.multiple_of(c * 128, 128), 128)
            x = x_ref[:, at].astype(F32)
            centred = x - jnp.mean(x, axis=0, keepdims=True)
            spread = jnp.mean(centred * centred, axis=0, keepdims=True)
            h_ref[:, at] = (centred * lax.rsqrt(spread + EPS) * gain_ref[...]).astype(BF16)
            return carry
        lax.fori_loop(0, length // 128, cols, 0)

    cosine, sine = cos_ref[...], sin_ref[...]
    hidden = h_ref[...]
    for j, out in ((0, q_ref), (1, k_ref)):
        p = dot(w_ref[j], hidden, 0, 0)
        for h in range(heads):
            a = p[h * HEAD : h * HEAD + half]
            b = p[h * HEAD + half : (h + 1) * HEAD]
            ra = (a * cosine - b * sine).astype(BF16)
            rb = (b * cosine + a * sine).astype(BF16)
            if j == 0:
                ra, rb = ra * 0.125, rb * 0.125
            out[h * HEAD : h * HEAD + half, :] = ra
            out[h * HEAD + half : (h + 1) * HEAD, :] = rb
    v_ref[...] = dot(w_ref[2], hidden, 0, 0).astype(BF16)
    for h in range(heads):
        rows = slice(h * HEAD, (h + 1) * HEAD)
        kn_ref[h] = k_ref[rows, :].T
    def one(h, carry):
        rows = pl.ds(pl.multiple_of(h * HEAD, HEAD), HEAD)
        s = dot(kn_ref[h], q_ref[rows, :], 1, 0)
        top = jnp.max(s, axis=0, keepdims=True)
        e = jnp.exp(s - top)
        total = jnp.sum(e, axis=0, keepdims=True)
        o = dot(v_ref[rows, :], e.astype(BF16), 1, 0)
        m_ref[rows, :] = (o / total).astype(BF16)
        lse_ref[0, pl.ds(h, 1), :] = top + jnp.log(total)
        return carry
    lax.fori_loop(0, heads, one, 0)

def attn_fwd(xT, gain, cosT, sinT, w):
    width, length = xT.shape
    block = 256
    n = width // block
    col = pl.BlockSpec((block, length), lambda i: (i, 0))
    t = jax.ShapeDtypeStruct((width, length), BF16)
    return pl.pallas_call(
        attn_fwd_kernel, grid=(n,), name="attn_fwd", cost_estimate=cost(34),
        in_specs=[whole((width, length)), whole((width, 1)), whole(cosT.shape), whole(sinT.shape),
                  pl.BlockSpec((3, width, block), lambda i: (0, 0, i))],
        out_specs=[whole((width, length)), col, col, col, col, pl.BlockSpec((1, 8, length), lambda i: (i, 0, 0))],
        out_shape=[t, t, t, t, t, jax.ShapeDtypeStruct((n, 8, length), F32)],
        scratch_shapes=[pltpu.VMEM((block // HEAD, length, HEAD), BF16)],
        compiler_params=params(),
    )(xT, gain, cosT, sinT, w)

def attn_bwd_kernel(x_ref, gain_ref, cos_ref, sin_ref, sg_ref, h_ref, q_ref, k_ref, v_ref, m_ref, lse_ref, w_ref, wo_ref,
                    first_ref, gg_ref, dw_ref, hg_ref, low_ref, do_ref, kn_ref, vn_ref, dk_ref, dv_ref, dq_ref, dwo_ref):
    width, length = x_ref.shape
    block = q_ref.shape[0]
    heads = block // HEAD
    half = HEAD // 2
    step = min(BSTEP, length)
    i = pl.program_id(0)

    @pl.when(i == 0)
    def _():
        low_ref[...] = sg_ref[...].astype(BF16)
        hg_ref[...] = jnp.zeros_like(hg_ref)

    do_ref[...] = dot(wo_ref[0], low_ref[...], 1, 0).astype(BF16)
    fs, _, each, _ = dw_ref.shape
    dwo_ref[pl.ds(pl.multiple_of(i * block, block), block), :] = dot(m_ref[...], low_ref[...], 1, 1).astype(BF16)
    cosine, sine = cos_ref[...], sin_ref[...]
    for h in range(heads):
        rows = slice(h * HEAD, (h + 1) * HEAD)
        kn_ref[h] = k_ref[rows, :].T
        vn_ref[h] = v_ref[rows, :].T
    def one(h, carry):
        rows = pl.ds(pl.multiple_of(h * HEAD, HEAD), HEAD)
        for c in range(length // step):
            at = slice(c * step, (c + 1) * step)
            s = dot(kn_ref[h], q_ref[rows, at], 1, 0)
            p = jnp.exp(s - lse_ref[0, pl.ds(h, 1), at])
            dp = dot(vn_ref[h], do_ref[rows, at], 1, 0)
            centre = jnp.sum(p * dp, axis=0, keepdims=True)
            ds = (p * (dp - centre)).astype(BF16)
            pb = p.astype(BF16)
            dv = dot(do_ref[rows, at], pb, 1, 1)
            dk = dot(q_ref[rows, at], ds, 1, 1)
            if c == 0:
                dv_ref[rows, :] = dv
                dk_ref[rows, :] = dk
            else:
                dv_ref[rows, :] += dv
                dk_ref[rows, :] += dk
            dq_ref[rows, at] = dot(k_ref[rows, :], ds, 1, 0) * 0.125
        return carry
    lax.fori_loop(0, heads, one, 0)
    hidden = h_ref[...]
    for j, ref in ((0, dq_ref), (1, dk_ref), (2, dv_ref)):
        if j == 2:
            g = ref[...].astype(BF16)
        else:
            parts = []
            for h in range(heads):
                a = ref[h * HEAD : h * HEAD + half, :]
                b = ref[h * HEAD + half : (h + 1) * HEAD, :]
                parts += [(a * cosine + b * sine).astype(BF16), (b * cosine - a * sine).astype(BF16)]
            g = jnp.concatenate(parts, axis=0)
        dw_ref[:, j, :, pl.ds(pl.multiple_of(i * block, block), block)] = dot(hidden, g, 1, 1).astype(BF16).reshape(fs, each, block)
        hg_ref[...] += dot(w_ref[j], g, 1, 0)

    @pl.when(i == pl.num_programs(0) - 1)
    def _():
        dw_ref[:, 3] = dwo_ref[...].reshape(fs, each, width)
        def cols(c, acc):
            at = pl.ds(pl.multiple_of(c * 128, 128), 128)
            dx, gg = ln_back(x_ref[:, at].astype(F32), hg_ref[:, at], gain_ref[...])
            first_ref[:, at] = (sg_ref[:, at] + dx).astype(BF16)
            return acc + gg
        acc = lax.fori_loop(0, length // 128, cols, jnp.zeros((width, 128), F32))
        gg_ref[...] = jnp.sum(acc, axis=1, keepdims=True)

def ln_back(x, g, gain):
    centred = x - jnp.mean(x, axis=0, keepdims=True)
    spread = jnp.mean(centred * centred, axis=0, keepdims=True)
    rs = lax.rsqrt(spread + EPS)
    xh = centred * rs
    gx = g * gain
    dx = rs * (gx - jnp.mean(gx, axis=0, keepdims=True) - xh * jnp.mean(gx * xh, axis=0, keepdims=True))
    return dx, g * xh

def attn_bwd(xT, gain, cosT, sinT, sg, hT, q, k, v, m, lse, w, fs):
    width, length = xT.shape
    block = 256
    n = width // block
    col = pl.BlockSpec((block, length), lambda i: (i, 0))
    full = whole((width, length))
    return pl.pallas_call(
        attn_bwd_kernel, grid=(n,), name="attn_bwd", cost_estimate=cost(62),
        in_specs=[full, whole((width, 1)), whole(cosT.shape), whole(sinT.shape), full, full, col, col, col, col,
                  pl.BlockSpec((1, 8, length), lambda i: (i, 0, 0)),
                  pl.BlockSpec((3, width, block), lambda i: (0, 0, i)),
                  pl.BlockSpec((1, block, width), lambda i: (3, i, 0))],
        out_specs=[full, whole((width, 1)), whole((fs, 4, width // fs, width))],
        out_shape=[jax.ShapeDtypeStruct((width, length), BF16), jax.ShapeDtypeStruct((width, 1), F32),
                   jax.ShapeDtypeStruct((fs, 4, width // fs, width), BF16)],
        scratch_shapes=[pltpu.VMEM((width, length), F32), pltpu.VMEM((width, length), BF16), pltpu.VMEM((block, length), BF16),
                        pltpu.VMEM((block // HEAD, length, HEAD), BF16), pltpu.VMEM((block // HEAD, length, HEAD), BF16),
                        pltpu.VMEM((block, length), F32), pltpu.VMEM((block, length), F32), pltpu.VMEM((block, length), F32),
                        pltpu.VMEM((width, width), BF16)],
        compiler_params=params(),
    )(xT, gain, cosT, sinT, sg, hT, q, k, v, m, lse, w, w)
def ff_fwd_kernel(x_ref, m_ref, g2_ref, g3_ref, pos_ref, wo_ref, up_ref, down_ref,
                  x2_ref, h2_ref, x3_ref, head_ref, fin_ref):
    width, length = x_ref.shape
    i = pl.program_id(0)

    @pl.when(i == 0)
    def _():
        x2_ref[...] = x_ref[...].astype(F32) + dot(wo_ref[0], m_ref[...], 0, 0)
        x3_ref[...] = x2_ref[...]
        def cols(c, carry):
            at = pl.ds(pl.multiple_of(c * 128, 128), 128)
            h2_ref[:, at] = ln(x2_ref[:, at], g2_ref[...]).astype(BF16)
            return carry
        lax.fori_loop(0, length // 128, cols, 0)

    pre = dot(up_ref[0], h2_ref[...], 1, 0)
    act = jax.nn.gelu(pre, approximate=True).astype(BF16)
    x3_ref[...] += dot(down_ref[0], act, 0, 0)

    @pl.when(i == pl.num_programs(0) - 1)
    def _():
        def cols(c, carry):
            at = pl.ds(pl.multiple_of(c * 128, 128), 128)
            fin_ref[:, at] = ln(x3_ref[:, at], g3_ref[...]).astype(BF16)
            return carry
        lax.fori_loop(0, length // 128, cols, 0)
        slots = pos_ref.shape[0]
        onehot = (pos_ref[...] == lax.broadcasted_iota(jnp.int32, (slots, length), 1)).astype(BF16)
        head_ref[...] = dot(onehot, fin_ref[...], 1, 1).astype(BF16)

def ln(x, gain):
    centred = x - jnp.mean(x, axis=0, keepdims=True)
    spread = jnp.mean(centred * centred, axis=0, keepdims=True)
    return centred * lax.rsqrt(spread + EPS) * gain

def ff_fwd(xT, m, g2, g3, pos, attn_w, ff_w):
    width, length = xT.shape
    hidden = ff_w.shape[1]
    block = 512
    n = hidden // block
    slots = pos.shape[0]
    full = whole((width, length))
    f = jax.ShapeDtypeStruct((width, length), F32)
    return pl.pallas_call(
        ff_fwd_kernel, grid=(n,), name="ff_fwd", cost_estimate=cost(34),
        in_specs=[full, full, whole((width, 1)), whole((width, 1)), whole((slots, 1)),
                  pl.BlockSpec((1, width, width), lambda i: (3, 0, 0)),
                  pl.BlockSpec((1, block, width), lambda i: (0, i, 0)),
                  pl.BlockSpec((1, block, width), lambda i: (1, i, 0))],
        out_specs=[full, full, full, whole((slots, width))],
        out_shape=[f, jax.ShapeDtypeStruct((width, length), BF16), f, jax.ShapeDtypeStruct((slots, width), BF16)],
        scratch_shapes=[pltpu.VMEM((width, length), BF16)],
        compiler_params=params(),
    )(xT, m, g2, g3, pos, attn_w, ff_w, ff_w)

def ff_bwd_kernel(x3_ref, x2_ref, h2_ref, rg_ref, pos_ref, g2_ref, g3_ref, up_ref, down_ref,
                  sg_ref, gg2_ref, gg3_ref, dw_ref, low_ref, hg_ref):
    width, length = x3_ref.shape
    i = pl.program_id(0)
    slots = pos_ref.shape[0]

    @pl.when(i == 0)
    def _():
        rows = rg_ref[...]
        high = rows.astype(BF16)
        rest = (rows - high.astype(F32)).astype(BF16)
        hg_ref[...] = jnp.zeros_like(hg_ref)
        def cols(c, acc):
            at = pl.ds(pl.multiple_of(c * 128, 128), 128)
            onehot = (pos_ref[...] == c * 128 + lax.broadcasted_iota(jnp.int32, (slots, 128), 1)).astype(BF16)
            fg = dot(high, onehot, 0, 0) + dot(rest, onehot, 0, 0)
            dx, gg = ln_back(x3_ref[:, at], fg, g3_ref[...])
            sg_ref[:, at] = dx
            low_ref[:, at] = dx.astype(BF16)
            return acc + gg
        acc = lax.fori_loop(0, length // 128, cols, jnp.zeros((width, 128), F32))
        gg3_ref[...] = jnp.sum(acc, axis=1, keepdims=True)

    ag = dot(down_ref[0], low_ref[...], 1, 0)
    pre = dot(up_ref[0], h2_ref[...], 1, 0)
    c0, c1 = 0.7978845608028654, 0.044715
    t = jnp.tanh(c0 * (pre + c1 * pre * pre * pre))
    half = 0.5 * (1.0 + t)
    act = (pre * half).astype(BF16)
    slope = half + 0.5 * pre * (1.0 - t * t) * (c0 * (1.0 + 3.0 * c1 * pre * pre))
    pg = (slope * ag).astype(BF16)
    shape = (dw_ref.shape[0],) + dw_ref.shape[2:]
    dw_ref[:, 1] = dot(act, low_ref[...], 1, 1).astype(BF16).reshape(shape)
    dw_ref[:, 0] = dot(pg, h2_ref[...], 1, 1).astype(BF16).reshape(shape)
    hg_ref[...] += dot(up_ref[0], pg, 0, 0)

    @pl.when(i == pl.num_programs(0) - 1)
    def _():
        def cols(c, acc):
            at = pl.ds(pl.multiple_of(c * 128, 128), 128)
            dx, gg = ln_back(x2_ref[:, at], hg_ref[:, at], g2_ref[...])
            sg_ref[:, at] += dx
            return acc + gg
        acc = lax.fori_loop(0, length // 128, cols, jnp.zeros((width, 128), F32))
        gg2_ref[...] = jnp.sum(acc, axis=1, keepdims=True)

def ff_bwd(x3, x2, h2, rg, pos, g2, g3, ff_w, fs):
    width, length = x3.shape
    hidden = ff_w.shape[1]
    each = hidden // fs
    block = each * max(1, 768 // each)
    n = hidden // block
    slots = pos.shape[0]
    full = whole((width, length))
    wb = pl.BlockSpec((block // each, 2, each, width), lambda i: (i, 0, 0, 0))
    g = jax.ShapeDtypeStruct((width, 1), F32)
    return pl.pallas_call(
        ff_bwd_kernel, grid=(n,), name="ff_bwd", cost_estimate=cost(45),
        in_specs=[full, full, full, whole((slots, width)), whole((slots, 1)), whole((width, 1)), whole((width, 1)),
                  pl.BlockSpec((1, block, width), lambda i: (0, i, 0)),
                  pl.BlockSpec((1, block, width), lambda i: (1, i, 0))],
        out_specs=[full, whole((width, 1)), whole((width, 1)), wb],
        out_shape=[jax.ShapeDtypeStruct((width, length), F32), g, g, jax.ShapeDtypeStruct((fs, 2, each, width), BF16)],
        scratch_shapes=[pltpu.VMEM((width, length), BF16), pltpu.VMEM((width, length), F32)],
        compiler_params=params(),
    )(x3, x2, h2, rg, pos, g2, g3, ff_w, ff_w)
RB = 256
FCH, BCH = 8, 8

def pick(n, top=8):
    return max(k for k in range(1, top + 1) if n % k == 0)

def table_kernel(source_ref, low_ref, turned_ref, *, shard):
    block = source_ref.shape[0]
    ids = pl.program_id(0) * block + lax.broadcasted_iota(jnp.int32, source_ref.shape, 0)
    low = jnp.where(ids < shard, source_ref[...], 0.0).astype(BF16)
    low_ref[...] = low
    turned_ref[...] = low.T

def table_both(table):
    shard, width = table.shape
    vocab = -(-shard // 128) * 128
    block = 640 if vocab % 640 == 0 else 128
    return pl.pallas_call(
        functools.partial(table_kernel, shard=shard), name="table_both", grid=(vocab // block,), cost_estimate=cost(12),
        in_specs=[pl.BlockSpec((block, width), lambda i: (i, 0))],
        out_specs=[pl.BlockSpec((block, width), lambda i: (i, 0)), pl.BlockSpec((width, block), lambda i: (0, i))],
        out_shape=[jax.ShapeDtypeStruct((vocab, width), BF16), jax.ShapeDtypeStruct((width, vocab), BF16)],
        compiler_params=params())(table)

def compact(meta_ref, rows_ref, comp_ref):
    nseq, slots, width = rows_ref.shape
    def clear(b, carry):
        comp_ref[pl.ds(pl.multiple_of(b * RB, RB), RB), :] = jnp.zeros((RB, width), BF16)
        return carry
    lax.fori_loop(0, meta_ref[2, 0], clear, 0)
    def seq(s, carry):
        def part(c, c2):
            comp_ref[pl.ds(pl.multiple_of((meta_ref[1, s] + c) * 16, 16), 16), :] = rows_ref[s, pl.ds(pl.multiple_of(c * 16, 16), 16), :]
            return c2
        lax.fori_loop(0, meta_ref[0, s], part, 0)
        return carry
    lax.fori_loop(0, nseq, seq, 0)

def vocab_fwd_kernel(meta_ref, limit_ref, rows_ref, table_ref, target_ref, lse_ref, chosen_ref, *outs, chunk, least, inside):
    comp_ref = outs[0] if inside else rows_ref
    vocab = table_ref.shape[0]
    if inside:
        nseq, slots, width = rows_ref.shape
        compact(meta_ref, rows_ref, comp_ref)
    lse_ref[...] = jnp.zeros_like(lse_ref)
    chosen_ref[...] = jnp.zeros_like(chosen_ref)
    limit = limit_ref[0]
    def block(b, carry):
        rows = comp_ref[pl.ds(pl.multiple_of(b * RB, RB), RB), :]
        target = target_ref[b]
        top = total = chosen = None
        for v in range(vocab // chunk):
            l = dot(table_ref[v * chunk:(v + 1) * chunk, :], rows, 1, 1)
            ids = v * chunk + lax.broadcasted_iota(jnp.int32, (chunk, RB), 0)
            hit = jnp.sum(jnp.where(ids == target, l, 0.0), axis=0, keepdims=True)
            if (v + 1) * chunk > least:
                l = jnp.where(ids < limit, l, -jnp.inf)
            m = jnp.max(l, axis=0, keepdims=True)
            if v == 0:
                top = m
                total = jnp.sum(jnp.exp(l - top), axis=0, keepdims=True)
                chosen = hit
            else:
                new = jnp.maximum(top, m)
                total = total * jnp.exp(top - new) + jnp.sum(jnp.exp(l - new), axis=0, keepdims=True)
                chosen = chosen + hit
                top = new
        lse_ref[b] = top + jnp.log(total)
        chosen_ref[b] = chosen
        return carry
    lax.fori_loop(0, meta_ref[2, 0], block, 0)

def vocab_fwd(meta, limit, rows, table, target, least):
    inside = rows.ndim == 3
    width = rows.shape[-1]
    nblk = target.shape[0]
    vocab = table.shape[0]
    chunk = 128 * pick(vocab // 128, FCH)
    smem = pl.BlockSpec(memory_space=pltpu.SMEM)
    vm = pl.BlockSpec(memory_space=pltpu.VMEM)
    st = jax.ShapeDtypeStruct((nblk, 1, RB), F32)
    comp = [jax.ShapeDtypeStruct((nblk * RB, width), BF16)] if inside else []
    out = pl.pallas_call(
        functools.partial(vocab_fwd_kernel, chunk=chunk, least=least, inside=inside), name="vocab_fwd", cost_estimate=cost(20),
        in_specs=[smem, smem, vm, vm, vm], out_specs=[vm] * (2 + len(comp)),
        out_shape=[st, st] + comp,
        compiler_params=params())(meta, limit, rows, table, target)
    return out[2] if inside else rows, out[0], out[1]

def vocab_bwd_kernel(meta_ref, limit_ref, comp_ref, table_ref, turned_ref, target_ref, lse_ref, scale_ref,
                     og_ref, og2_ref, rg_ref, acc_ref, rc_ref, low_ref, back_ref, sem, *, chunk, least, inside):
    vocab, width = table_ref.shape
    limit = limit_ref[0]
    nch = vocab // chunk
    def clear(b, carry):
        acc_ref[pl.ds(pl.multiple_of(b * 128, 128), 128), :] = jnp.zeros((128, width), F32)
        return carry
    lax.fori_loop(0, vocab // 128, clear, 0)
    def block(b, carry):
        rows = comp_ref[pl.ds(pl.multiple_of(b * RB, RB), RB), :]
        target, lse, scale = target_ref[b], lse_ref[b], scale_ref[b]
        rg = None
        for v in range(nch):
            l = dot(table_ref[v * chunk:(v + 1) * chunk, :], rows, 1, 1)
            ids = v * chunk + lax.broadcasted_iota(jnp.int32, (chunk, RB), 0)
            p = jnp.exp(l - lse)
            p = jnp.where(ids == target, p - 1.0, p)
            if (v + 1) * chunk > least:
                p = jnp.where(ids < limit, p, 0.0)
            g = (scale * p).astype(BF16)
            acc_ref[v * chunk:(v + 1) * chunk, :] += dot(g, rows, 1, 0)
            part = dot(turned_ref[:, v * chunk:(v + 1) * chunk], g, 1, 0)
            rg = part if rg is None else rg + part
        rc_ref[pl.ds(pl.multiple_of(b * RB, RB), RB), :] = rg.T.astype(BF16)
        return carry
    lax.fori_loop(0, meta_ref[2, 0], block, 0)
    if inside:
        nseq, slots, _ = back_ref.shape
        def seq(s, carry):
            back_ref[s] = jnp.zeros((slots, width), BF16)
            def part(c, c2):
                back_ref[s, pl.ds(pl.multiple_of(c * 16, 16), 16), :] = rc_ref[pl.ds(pl.multiple_of((meta_ref[1, s] + c) * 16, 16), 16), :]
                return c2
            lax.fori_loop(0, meta_ref[0, s], part, 0)
            return carry
        lax.fori_loop(0, nseq, seq, 0)
        out = pltpu.make_async_copy(back_ref, rg_ref, sem.at[0])
    else:
        out = pltpu.make_async_copy(rc_ref, rg_ref, sem.at[0])
    out.start()
    outs = [out]
    part = og_ref.shape[0]
    for v, (ref, start) in enumerate(((og_ref, 0), (og2_ref, part))):
        at = pl.ds(start, ref.shape[0])
        low_ref[at, :] = acc_ref[at, :].astype(BF16)
        outs.append(pltpu.make_async_copy(low_ref.at[at], ref, sem.at[1 + v]))
        outs[-1].start()
    for o in outs:
        o.wait()

def vocab_bwd(meta, limit, comp, table, turned, target, lse, scale, least, nseq, slots, inside):
    rows, width = comp.shape
    vocab = table.shape[0]
    chunk = 128 * pick(vocab // 128, BCH)
    smem = pl.BlockSpec(memory_space=pltpu.SMEM)
    vm = pl.BlockSpec(memory_space=pltpu.VMEM)
    hbm = pl.BlockSpec(memory_space=pl.ANY)
    shape = (nseq, slots, width) if inside else (rows, width)
    part = vocab // 256 * 128
    return pl.pallas_call(
        functools.partial(vocab_bwd_kernel, chunk=chunk, least=least, inside=inside), name="vocab_bwd", cost_estimate=cost(40),
        in_specs=[smem, smem] + [vm] * 6, out_specs=[hbm, hbm, hbm],
        out_shape=[jax.ShapeDtypeStruct((part, width), BF16), jax.ShapeDtypeStruct((vocab - part, width), BF16), jax.ShapeDtypeStruct(shape, BF16)],
        scratch_shapes=[pltpu.VMEM((vocab, width), F32), pltpu.VMEM((rows, width), BF16),
                        pltpu.VMEM((vocab, width), BF16), pltpu.VMEM(shape if inside else (1, 16, width), BF16),
                        pltpu.SemaphoreType.DMA((3,))],
        compiler_params=params())(meta, limit, comp, table, turned, target, lse, scale)

def plan(counts, slots, length):
    nseq = counts.shape[0]
    units = (counts + 15) // 16
    ends = jnp.cumsum(units)
    offs = ends - units
    total = ends[-1] * 16
    nblk = (total + RB - 1) // RB
    cap = (nseq * slots + RB - 1) // RB * RB
    at = jnp.arange(cap, dtype=jnp.int32)
    seq = jnp.minimum(jnp.sum((at[:, None] >= ends[None, :] * 16).astype(jnp.int32), axis=1), nseq - 1)
    mine = (seq[:, None] == jnp.arange(nseq, dtype=jnp.int32)[None, :])
    slot = at - jnp.sum(jnp.where(mine, offs[None, :] * 16, 0), axis=1)
    cnt = jnp.sum(jnp.where(mine, counts[None, :], 0), axis=1)
    live = slot < cnt
    weight = jnp.where(live, length / cnt.astype(F32), 0.0)
    meta = jnp.stack([units, offs, jnp.full((nseq,), nblk)]).astype(jnp.int32)
    return meta, seq, slot, weight

def spread(values, seq, slot):
    nseq, slots = values.shape
    parts = jnp.concatenate([values // 256, values % 256], axis=1).astype(BF16)
    mine = (seq[:, None] == jnp.arange(nseq, dtype=jnp.int32)[None, :]).astype(BF16)
    rows = jnp.dot(mine, parts, preferred_element_type=F32)
    hit = slot[:, None] == jnp.arange(slots, dtype=jnp.int32)[None, :]
    both = rows[:, :slots] * 256.0 + rows[:, slots:]
    return jnp.sum(jnp.where(hit, both, 0.0), axis=1).astype(jnp.int32)

def halves(vocab):
    nb = vocab // 128
    low = (nb + 1) // 2
    return nb, low

def sections(count, size):
    return [(s, min(size, count - s)) for s in range(0, count, size)]

def gather_kernel(ids_ref, flag_ref, emb_ref, out_ref, tab_ref, raw_ref, row_ref, sem):
    feat, vocab = emb_ref.shape
    nseq, _, length = out_ref.shape
    nb, low = halves(vocab)
    size = -(-low // 6)
    secs = sections(low, size)
    def copies(k):
        s, n = secs[k]
        out = [pltpu.make_async_copy(emb_ref.at[:, pl.ds(s * 128, n * 128)], raw_ref.at[:, pl.ds(s * 128, n * 128)], sem.at[2 * k])]
        m = min(n, nb - low - s)
        if m > 0:
            out.append(pltpu.make_async_copy(emb_ref.at[:, pl.ds((low + s) * 128, m * 128)], raw_ref.at[:, pl.ds((low + s) * 128, m * 128)], sem.at[2 * k + 1]))
        return out
    for k in range(len(secs)):
        for c in copies(k):
            c.start()
    pad = jnp.zeros((64 - feat, 128), F32)
    for k in range(len(secs)):
        for c in copies(k):
            c.wait()
        s, n = secs[k]
        m = max(0, min(n, nb - low - s))
        def turn(b, carry):
            a = raw_ref[:, pl.ds(pl.multiple_of(b * 128, 128), 128)]
            h = raw_ref[:, pl.ds(pl.multiple_of((low + b) * 128, 128), 128)]
            tab_ref[pl.ds(pl.multiple_of(b * 128, 128), 128), :] = jnp.concatenate([a, pad, h, pad], axis=0).T
            return carry
        lax.fori_loop(s, s + m, turn, 0, unroll=3)
        for b in range(s + m, s + n):
            a = raw_ref[:, b * 128:(b + 1) * 128]
            tab_ref[b * 128:(b + 1) * 128, :] = jnp.concatenate([a, pad, pad, jnp.zeros((feat, 128), F32)], axis=0).T
    U = 32
    def seq(s, carry):
        def grp(g, c2):
            base = pl.multiple_of(g * U, U)
            for j in range(U):
                i = ids_ref[s * length + base + j]
                row_ref[pl.ds(base + j, 1), :] = tab_ref[pl.ds(i, 1), :]
            return c2
        lax.fori_loop(0, length // U, grp, 0)
        for c in range(length // 128):
            t = row_ref[c * 128:(c + 1) * 128, :].T
            f = flag_ref[s, :, c * 128:(c + 1) * 128] > 0
            out_ref[s, :, c * 128:(c + 1) * 128] = jnp.where(f, t[64:64 + feat], t[:feat]).astype(BF16)
        return carry
    lax.fori_loop(0, nseq, seq, 0)

def split_ids(ids, vocab):
    nb, low = halves(vocab)
    high = ids >= low * 128
    return jnp.where(high, ids - low * 128, ids), high.astype(jnp.int32)

def gather(ids, emb):
    nseq, length = ids.shape
    feat, vocab = emb.shape
    nb, low = halves(vocab)
    rid, flag = split_ids(ids, vocab)
    return pl.pallas_call(gather_kernel, name="emb_gather", cost_estimate=cost(32),
        in_specs=[pl.BlockSpec(memory_space=pltpu.SMEM), pl.BlockSpec(memory_space=pltpu.VMEM), pl.BlockSpec(memory_space=pl.ANY)],
        out_specs=pl.BlockSpec(memory_space=pltpu.VMEM),
        out_shape=jax.ShapeDtypeStruct((nseq, feat, length), BF16),
        scratch_shapes=[pltpu.VMEM((low * 128, 128), F32), pltpu.VMEM((feat, vocab), F32), pltpu.VMEM((length, 128), F32), pltpu.SemaphoreType.DMA((12,))],
        compiler_params=params())(rid.reshape(-1), flag.reshape(nseq, 1, length), emb)

def scatter_kernel(ids_ref, flag_ref, *refs, ng, per):
    g_refs = refs[:ng]
    out_ref, sq_ref, raw_ref, row_ref, sem = refs[ng:ng + 5]
    tabs = refs[ng + 5:]
    feat, vocab = out_ref.shape
    nseq, _, length = g_refs[0].shape
    nb, low = halves(vocab)
    zero128 = jnp.zeros((128, 128), F32)
    def zero(b, carry):
        for t in tabs:
            t[pl.ds(pl.multiple_of(b * 128, 128), 128), :] = zero128
        return carry
    lax.fori_loop(0, low, zero, 0)
    pad = jnp.zeros((64 - feat, 128), F32)
    U = 8
    streams = [(g, p) for g in range(ng) for p in range(per)]
    each = nseq // per
    def seq(s, carry):
        for k, (g, p) in enumerate(streams):
            q = p * each + s
            for c in range(length // 128):
                at = slice(c * 128, (c + 1) * 128)
                v = g_refs[g][q, :, at].astype(F32)
                f = flag_ref[g * nseq + q, :, at] > 0
                row_ref[k, at, :] = jnp.concatenate([jnp.where(f, 0.0, v), pad, jnp.where(f, v, 0.0), pad], axis=0).T
        def grp(n, c2):
            base = pl.multiple_of(n * U, U)
            for j in range(U):
                idx = [ids_ref[(g * nseq + p * each + s) * length + base + j] for g, p in streams]
                old = [tabs[k][pl.ds(idx[k], 1), :] for k in range(len(streams))]
                new = [old[k] + row_ref[k, pl.ds(base + j, 1), :] for k in range(len(streams))]
                for k in range(len(streams)):
                    tabs[k][pl.ds(idx[k], 1), :] = new[k]
            return c2
        lax.fori_loop(0, length // U, grp, 0)
        return carry
    lax.fori_loop(0, each, seq, 0)
    def tile(b):
        at = pl.ds(pl.multiple_of(b * 128, 128), 128)
        parts = [sum((tabs[g * per + p][at, :] for p in range(1, per)), tabs[g * per][at, :]) for g in range(ng)]
        return sum(parts[1:], parts[0]).T
    size = -(-low // 6)
    secs = sections(low, size)
    def copies(k):
        s, n = secs[k]
        out = [pltpu.make_async_copy(raw_ref.at[k % 2, 0, :, pl.ds(0, n * 128)], out_ref.at[:, pl.ds(s * 128, n * 128)], sem.at[2 * k])]
        m = min(n, nb - low - s)
        if m > 0:
            out.append(pltpu.make_async_copy(raw_ref.at[k % 2, 1, :, pl.ds(0, m * 128)], out_ref.at[:, pl.ds((low + s) * 128, m * 128)], sem.at[2 * k + 1]))
        return out
    squares = jnp.zeros((128, 128), F32)
    for k, (s, n) in enumerate(secs):
        if k >= 2:
            for c in copies(k - 2):
                c.wait()
        def turn(b, carry, s=s, k=k):
            t = tile(b)
            at = pl.ds(pl.multiple_of((b - s) * 128, 128), 128)
            raw_ref[k % 2, 0, :, at] = t[:feat]
            raw_ref[k % 2, 1, :, at] = t[64:64 + feat]
            return carry + t * t
        squares = lax.fori_loop(s, s + n, turn, squares, unroll=3)
        for c in copies(k):
            c.start()
    sq_ref[...] = squares
    for k in range(max(0, len(secs) - 2), len(secs)):
        for c in copies(k):
            c.wait()

def scatter(ids, gs, vocab, per):
    nseq, feat, length = gs[0].shape
    nb, low = halves(vocab)
    rid, flag = split_ids(ids, vocab)
    ng = len(gs)
    size = -(-low // 6)
    vm = pl.BlockSpec(memory_space=pltpu.VMEM)
    return pl.pallas_call(functools.partial(scatter_kernel, ng=ng, per=per), name="emb_scatter", cost_estimate=cost(1),
        in_specs=[pl.BlockSpec(memory_space=pltpu.SMEM), vm] + [vm] * ng,
        out_specs=[pl.BlockSpec(memory_space=pl.ANY), vm],
        out_shape=[jax.ShapeDtypeStruct((feat, vocab), F32), jax.ShapeDtypeStruct((128, 128), F32)],
        scratch_shapes=[pltpu.VMEM((2, 2, feat, size * 128), F32), pltpu.VMEM((ng * per, length, 128), F32), pltpu.SemaphoreType.DMA((12,))]
            + [pltpu.VMEM((low * 128, 128), F32)] * (ng * per),
        compiler_params=params(62 * 1024 * 1024))(rid.reshape(-1), flag.reshape(-1, 1, length), *gs)
AHEAD = 2
MESH_ID = pl.DeviceIdType.MESH

def comm_params(ident):
    return pltpu.CompilerParams(collective_id=ident, has_side_effects=True, vmem_limit_bytes=VL)

def meet(peers):
    barrier = pltpu.get_barrier_semaphore()
    for p in peers:
        pl.semaphore_signal(barrier, inc=1, device_id=p, device_id_type=MESH_ID)
    pl.semaphore_wait(barrier, len(peers))

def remote(src, dst, send, recv, peer):
    return pltpu.make_async_remote_copy(src_ref=src, dst_ref=dst, send_sem=send, recv_sem=recv, device_id=peer, device_id_type=MESH_ID)

def small_kernel(x_ref, *refs, fs, dps, wide, finish):
    out_ref = refs[0]
    got_ref = refs[1] if finish else out_ref
    send, recv = refs[-2:]
    d, f = lax.axis_index("dp"), lax.axis_index("fsdp")
    n = fs * dps if wide else fs
    me = d * fs + f if wide else f
    def peer(k):
        j = lax.rem(me + k, n)
        return (lax.div(j, fs), lax.rem(j, fs)) if wide else (d, j)
    barrier = pltpu.get_barrier_semaphore()
    def greet(k, carry):
        pl.semaphore_signal(barrier, inc=1, device_id=peer(k), device_id_type=MESH_ID)
        return carry
    lax.fori_loop(1, n, greet, 0)
    pl.semaphore_wait(barrier, n - 1)
    def copy(k):
        return remote(x_ref, got_ref.at[me], send.at[k], recv.at[k], peer(k))
    def begin(k, carry):
        copy(k).start()
        return carry
    lax.fori_loop(1, n, begin, 0)
    got_ref[me] = x_ref[...]
    def end(k, carry):
        copy(k).wait()
        return carry
    lax.fori_loop(1, n, end, 0)
    if finish:
        finish(got_ref, out_ref, n)

def lse_finish(got_ref, out_ref, n):
    top = got_ref[0]
    for i in range(1, n):
        top = jnp.maximum(top, got_ref[i])
    total = jnp.exp(got_ref[0] - top)
    for i in range(1, n):
        total = total + jnp.exp(got_ref[i] - top)
    out_ref[...] = top + jnp.log(total)

def sum_finish(got_ref, out_ref, n):
    total = got_ref[0]
    for i in range(1, n):
        total = total + got_ref[i]
    out_ref[...] = total

def small_gather(x, ident, wide=False, finish=None, name="small_gather"):
    fs, dps = lax.axis_size("fsdp"), lax.axis_size("dp")
    n = fs * dps if wide else fs
    vm = pl.BlockSpec(memory_space=pltpu.VMEM)
    got = (n,) + x.shape
    return pl.pallas_call(
        functools.partial(small_kernel, fs=fs, dps=dps, wide=wide, finish=finish), name=name,
        in_specs=[vm], out_specs=vm,
        out_shape=jax.ShapeDtypeStruct(x.shape if finish else got, x.dtype),
        scratch_shapes=([pltpu.VMEM(got, x.dtype)] if finish else []) + [pltpu.SemaphoreType.DMA((n,)), pltpu.SemaphoreType.DMA((n,))],
        cost_estimate=cost(12), compiler_params=comm_params(ident))(x)

def exchange_kernel(*refs, fs, both, aux):
    refs = list(refs)
    x_ref = refs.pop(0)
    aux_ref = refs.pop(0) if aux else None
    out_ref = refs.pop(0)
    other_ref = refs.pop(0) if both else None
    if aux:
        sum_ref, near_ref, over_ref = refs.pop(0), refs.pop(-2), refs.pop(-1)
    send, recv, send2, recv2, own = refs[:5]
    d, f = lax.axis_index("dp"), lax.axis_index("fsdp")
    across = (1 - d, f)
    barrier = pltpu.get_barrier_semaphore()
    def greet(k, carry):
        pl.semaphore_signal(barrier, inc=1, device_id=(d, lax.rem(f + k, fs)), device_id_type=MESH_ID)
        return carry
    lax.fori_loop(1, fs, greet, 0)
    if both:
        pl.semaphore_signal(barrier, inc=1, device_id=across, device_id_type=MESH_ID)
    pl.semaphore_wait(barrier, fs if both else fs - 1)
    def copies(k):
        j = lax.rem(f + k, fs)
        out = [remote(x_ref.at[j], out_ref.at[f], send.at[0, k], recv.at[0, k], (d, j))]
        if aux:
            out.append(remote(aux_ref, near_ref.at[f], send.at[1, k], recv.at[1, k], (d, j)))
        return out
    def passed(k):
        s = lax.rem(f + fs - k, fs)
        out = [remote(out_ref.at[s], other_ref.at[s], send2.at[0, k], recv2.at[0, k], across)]
        if aux:
            out.append(remote(near_ref.at[s], over_ref.at[s], send2.at[1, k], recv2.at[1, k], across))
        return out
    def first():
        out = [remote(x_ref.at[f], other_ref.at[f], send2.at[0, 0], recv2.at[0, 0], across)]
        if aux:
            out.append(remote(aux_ref, over_ref.at[f], send2.at[1, 0], recv2.at[1, 0], across))
        return out
    if both:
        for c in first():
            c.start()
    def begin(k, carry):
        for c in copies(k):
            c.start()
        return carry
    lax.fori_loop(1, fs, begin, 0)
    mine = pltpu.make_async_copy(x_ref.at[f], out_ref.at[f], own)
    mine.start()
    if aux:
        near_ref[f] = aux_ref[...]
    mine.wait()
    def arrive(k, carry):
        for c in copies(k):
            c.wait_recv()
        if both:
            for c in passed(k):
                c.start()
        return carry
    lax.fori_loop(1, fs, arrive, 0)
    def end(k, carry):
        for c in copies(k):
            c.wait_send()
        if both:
            for c in passed(k):
                c.wait()
        return carry
    lax.fori_loop(1, fs, end, 0)
    if both:
        for c in first():
            c.wait()
    if aux:
        total = near_ref[0]
        for i in range(1, fs):
            total = total + near_ref[i]
        if both:
            rest = over_ref[0]
            for i in range(1, fs):
                rest = rest + over_ref[i]
            total = total + rest
        sum_ref[...] = total

def exchange(x, ident, both, name, aux=None):
    fs = lax.axis_size("fsdp")
    vm = pl.BlockSpec(memory_space=pltpu.VMEM)
    shape = jax.ShapeDtypeStruct(x.shape, x.dtype)
    sem = pltpu.SemaphoreType.DMA((2, fs))
    more = [] if aux is None else [pltpu.VMEM((fs,) + aux.shape, F32)] * 2
    outs = [shape] * (2 if both else 1) + ([] if aux is None else [jax.ShapeDtypeStruct(aux.shape, F32)])
    return pl.pallas_call(
        functools.partial(exchange_kernel, fs=fs, both=both, aux=aux is not None), name=name,
        in_specs=[vm] * (1 if aux is None else 2), out_specs=[vm] * len(outs), out_shape=outs,
        scratch_shapes=[sem, sem, sem, sem, pltpu.SemaphoreType.DMA] + more,
        cost_estimate=cost(55),
        compiler_params=comm_params(ident))(*([x] if aux is None else [x, aux]))

def cuts(rows):
    n = 4 if rows % 64 == 0 else 1
    return n, rows // n

def rows_gather_kernel(x_ref, out_ref, send, recv, *, high):
    d, f = lax.axis_index("dp"), lax.axis_index("fsdp")
    h, m, c = lax.div(f, 4), lax.rem(lax.div(f, 2), 2), lax.rem(f, 2)
    side, twin = (d, h * 4 + (1 - m) * 2 + c), (d, h * 4 + m * 2 + 1 - c)
    parts, size = cuts(x_ref.shape[0])
    def far(k):
        return (d, lax.rem(h + k, high) * 4 + m * 2 + c)
    meet([far(k) for k in range(1, high)] + [side, twin])
    sent = []
    def go(src, block, p, peer):
        at = pl.ds(p * size, size)
        r = remote(src.at[at], out_ref.at[block, at], send.at[len(sent)], recv.at[block, p], peer)
        r.start()
        sent.append(r)
    def arrived(block, p):
        at = pl.ds(p * size, size)
        remote(x_ref.at[at], out_ref.at[block, at], send.at[0], recv.at[block, p], twin).wait_recv()
    def back(k, row):
        return lax.rem(h + high - k, high) * 4 + row * 2 + c
    def launch(p):
        for k in range(1, high):
            go(x_ref, f, p, far(k))
        go(x_ref, f, p, side)
        go(x_ref, f, p, twin)
    ahead = min(AHEAD, parts)
    for p in range(ahead):
        launch(p)
    out_ref[f] = x_ref[...]
    for p in range(parts + 1):
        if p < parts:
            for k in range(1, high):
                b = back(k, m)
                arrived(b, p)
                go(out_ref.at[b], b, p, side)
                go(out_ref.at[b], b, p, twin)
            if p + ahead < parts:
                launch(p + ahead)
        if p > 0:
            for k in range(high):
                b = back(k, 1 - m)
                arrived(b, p - 1)
                go(out_ref.at[b], b, p - 1, twin)
    for row in range(2):
        for k in range(high):
            for p in range(parts):
                arrived(lax.rem(h + high - k, high) * 4 + lax.rem(m + row, 2) * 2 + 1 - c, p)
    for r in sent:
        r.wait_send()

def rows_gather(x, ident, name="rows_gather"):
    fs = lax.axis_size("fsdp")
    vm = pl.BlockSpec(memory_space=pltpu.VMEM)
    high = fs // 4
    parts = cuts(x.shape[0])[0]
    return pl.pallas_call(
        functools.partial(rows_gather_kernel, high=high), name=name,
        in_specs=[vm], out_specs=vm, out_shape=jax.ShapeDtypeStruct((fs,) + x.shape, x.dtype),
        scratch_shapes=[pltpu.SemaphoreType.DMA((4 * high * parts,)), pltpu.SemaphoreType.DMA((fs, parts))],
        cost_estimate=cost(40), compiler_params=comm_params(ident))(x)

def rows_reduce_kernel(x_ref, out_ref, twin_ref, side_ref, far_ref, a_ref, b_ref, s1, r1, s2, r2, s3, r3, *, high, both):
    d, f = lax.axis_index("dp"), lax.axis_index("fsdp")
    h, m, c = lax.div(f, 4), lax.rem(lax.div(f, 2), 2), lax.rem(f, 2)
    side, twin = (d, h * 4 + (1 - m) * 2 + c), (d, h * 4 + m * 2 + 1 - c)
    def far(k):
        return (d, lax.rem(h + k, high) * 4 + m * 2 + c)
    across = (1 - d, f)
    meet([far(k) for k in range(1, high)] + [side, twin] + ([across] if both else []))
    order = list(range(1, high)) + [0]
    parts, size = cuts(x_ref.shape[1])
    def rows(p):
        return pl.ds(p * size, size)
    def at(k):
        return lax.rem(h + k, high)
    def one(k, row, p):
        slot = at(k) * 2 + row
        return remote(x_ref.at[at(k) * 4 + row * 2 + 1 - c, rows(p)], twin_ref.at[slot, rows(p)], s1.at[slot, p], r1.at[slot, p], twin)
    def two(k, p):
        return remote(a_ref.at[at(k), rows(p)], side_ref.at[at(k), rows(p)], s2.at[at(k), p], r2.at[at(k), p], side)
    def three(k, p):
        return remote(b_ref.at[k, rows(p)], far_ref.at[k, rows(p)], s3.at[k, p], r3.at[k, p], far(k))
    for p in range(parts):
        for k in order:
            one(k, 1 - m, p).start()
        for k in order:
            one(k, m, p).start()
    for p in range(parts + 1):
        if p < parts:
            if p >= 2:
                for k in order:
                    two(k, p - 2).wait_send()
            for k in order:
                one(k, 1 - m, p).wait_recv()
                a_ref[at(k), rows(p)] = (x_ref[at(k) * 4 + (1 - m) * 2 + c, rows(p)].astype(F32) + twin_ref[at(k) * 2 + 1 - m, rows(p)].astype(F32)).astype(a_ref.dtype)
                two(k, p).start()
        if p > 0:
            q = p - 1
            for k in order:
                one(k, m, q).wait_recv()
                two(k, q).wait_recv()
                total = x_ref[at(k) * 4 + m * 2 + c, rows(q)].astype(F32) + twin_ref[at(k) * 2 + m, rows(q)].astype(F32) + side_ref[at(k), rows(q)].astype(F32)
                if k == 0:
                    out_ref[rows(q)] = total
                else:
                    b_ref[k, rows(q)] = total.astype(b_ref.dtype)
                    three(k, q).start()
    for p in range(parts):
        for k in range(1, high):
            three(k, p).wait_recv()
            out_ref[rows(p)] += far_ref[k, rows(p)].astype(F32)
        if both:
            b_ref[0, rows(p)] = out_ref[rows(p)].astype(b_ref.dtype)
            remote(b_ref.at[0, rows(p)], far_ref.at[0, rows(p)], s3.at[0, p], r3.at[0, p], across).start()
    for p in range(parts):
        if both:
            remote(b_ref.at[0, rows(p)], far_ref.at[0, rows(p)], s3.at[0, p], r3.at[0, p], across).wait()
            out_ref[rows(p)] = b_ref[0, rows(p)].astype(F32) + far_ref[0, rows(p)].astype(F32)
        for k in order:
            one(k, m, p).wait_send()
            one(k, 1 - m, p).wait_send()
            if p + 2 >= parts:
                two(k, p).wait_send()
            if k:
                three(k, p).wait_send()

def rows_reduce(x, ident, name="rows_reduce", both=False):
    fs = lax.axis_size("fsdp")
    vm = pl.BlockSpec(memory_space=pltpu.VMEM)
    high = fs // 4
    block = x.shape[1:]
    parts = cuts(block[0])[0]
    def sem(n):
        return pltpu.SemaphoreType.DMA((n, parts))
    def buf(n):
        return pltpu.VMEM((n,) + block, x.dtype)
    return pl.pallas_call(
        functools.partial(rows_reduce_kernel, high=high, both=both), name=name,
        in_specs=[vm], out_specs=vm, out_shape=jax.ShapeDtypeStruct(block, F32),
        scratch_shapes=[buf(2 * high), buf(high), buf(high), buf(high), buf(high),
                        sem(2 * high), sem(2 * high), sem(high), sem(high), sem(high), sem(high)],
        cost_estimate=cost(45), compiler_params=comm_params(ident))(x)
def adam_kernel(factor_ref, w_ref, one_ref, two_ref, avg_ref, *refs, rate, first):
    outs = refs[-4:]
    grads = [r[...].astype(F32) for r in refs[:-4]]
    if first is None:
        g = grads[0]
    else:
        g = jnp.where(pl.program_id(0) < first, grads[0] + grads[1], grads[2] + grads[3])
    new, one, two = adamw(w_ref[...], one_ref[...], two_ref[...], g * factor_ref[0], rate)
    outs[0][...] = new
    outs[1][...] = one
    outs[2][...] = two
    outs[3][...] = ema_decay * avg_ref[...] + (1 - ema_decay) * new

def adam_table(factor, w, one, two, avg, grads, rate, by_rows):
    rows, cols = w.shape
    if by_rows:
        block, first = (256, cols), grads[0].shape[0] // 256
        steps = -(-rows // 256)
        spec = pl.BlockSpec(block, lambda i: (i, 0))
        early = pl.BlockSpec(block, lambda i: (jnp.minimum(i, first - 1), 0))
        late = pl.BlockSpec(block, lambda i: (jnp.maximum(i - first, 0), 0))
        gspecs = [early, early, late, late]
    else:
        block, first = (rows, 3072), None
        steps = -(-cols // 3072)
        spec = pl.BlockSpec(block, lambda i: (0, i))
        gspecs = [spec]
    shape = jax.ShapeDtypeStruct(w.shape, F32)
    return pl.pallas_call(
        functools.partial(adam_kernel, rate=rate, first=first), name="adam_rows" if by_rows else "adam_columns",
        grid=(steps,), cost_estimate=cost(1),
        in_specs=[pl.BlockSpec(memory_space=pltpu.SMEM)] + [spec] * 4 + gspecs, out_specs=[spec] * 4, out_shape=[shape] * 4,
        compiler_params=params())(factor.reshape(1), w, one, two, avg, *grads)
MASK_ID = 50257
STRATA = 16
STEP = 10

clip_level = 1.0
beta_one = 0.9
beta_two = 0.95
adam_eps = 1e-08
adam_decay = 0.01
rate_embed = 2.0
rate_out = 0.25
rate_gain = 0.5
rate_shampoo = 0.3
shampoo_decay = 0.01
stat_decay = 0.5
ema_decay = 0.7


def rotary_tables(length, half_width):
    inverse = 10000.0 ** (-jnp.arange(half_width, dtype=F32) / half_width)
    angles = inverse[:, None] * jnp.arange(length, dtype=F32)[None, :]
    return (jnp.cos(angles), jnp.sin(angles))


def adamw(weight, moment_one, moment_two, gradient, step_rate):
    one_new = beta_one * moment_one + (1 - beta_one) * gradient
    two_new = beta_two * moment_two + (1 - beta_two) * gradient * gradient
    one_hat = one_new / (1 - beta_one**STEP)
    two_hat = two_new / (1 - beta_two**STEP)
    weight_new = weight - step_rate * (
        one_hat / (jnp.sqrt(two_hat) + adam_eps) + adam_decay * weight
    )
    return (weight_new, one_new, two_new)


def dp_other(x):
    return lax.ppermute(x, "dp", [(0, 1), (1, 0)])


def dp_sum(x):
    count = lax.axis_size("dp")
    if count == 1:
        return x.astype(F32)
    if count == 2:
        return x.astype(F32) + dp_other(x).astype(F32)
    return lax.psum(x, "dp").astype(F32)


def spread_out(x):
    return lax.all_gather(x.astype(BF16), "fsdp", axis=1, tiled=True)


def per_device(
    tokens, positions, strata, groups, embedding, out_table, norm_gains, attention, feedforward,
    embed_moment_one, embed_moment_two, out_moment_one, out_moment_two, gain_moment_one, gain_moment_two,
    attention_left, attention_right, attention_left_root, attention_right_root,
    ff_left, ff_right, ff_left_root, ff_right_root,
    ema_embed, ema_out, ema_gains, ema_attention, ema_feedforward,
):
    fs = lax.axis_size("fsdp")
    dps = lax.axis_size("dp")
    me = lax.axis_index("fsdp")
    replica = lax.axis_index("dp")
    seq_count, length = tokens.shape
    slots = positions.shape[1]
    features, vocab = embedding.shape
    width = features * fs
    shard = out_table.shape[0]

    counts = jnp.maximum(1, (strata + 1) * slots * (1 + groups) // (2 * STRATA))
    in_use = jnp.arange(slots, dtype=jnp.int32)[None, :] < counts[:, None]
    places = jnp.arange(length, dtype=jnp.int32)
    same = positions[0][:, None] == places[None, :]
    marked = jnp.any(same & in_use[0][:, None], axis=0)
    ids_in = jnp.where(marked, MASK_ID, tokens[0])
    targets = jnp.sum(jnp.where(same, tokens[0][None, :], 0), axis=1)
    packed = jnp.concatenate([ids_in, targets, counts])
    packed = jnp.pad(packed, (0, -packed.shape[0] % 1024))
    everyone = small_gather(packed.reshape(-1, 128), 1, wide=True, name="ids_gather").reshape(fs * dps, -1)
    group = lax.dynamic_slice_in_dim(everyone, replica * fs, fs, 0)
    all_ids = everyone[:, :length]
    group_ids = group[:, :length]
    group_targets = group[:, length:length + slots]
    group_counts = group[:, length + slots]

    attn_w = spread_out(attention)
    ff_w = spread_out(feedforward)
    attn_root = spread_out(attention_right_root)
    ff_root = spread_out(ff_right_root)

    picked = gather(group_ids, embedding)
    xT = exchange(picked, 2, False, "features")[0].reshape(width, length)

    cosT, sinT = rotary_tables(length, HEAD // 2)
    gain = [norm_gains[i][:, None] for i in range(3)]
    place = positions[0][:, None]
    hT, qT, kT, vT, mixT, lse = attn_fwd(xT, gain[0], cosT, sinT, attn_w)
    hT, source = lax.optimization_barrier((hT, out_table))
    low, turned = table_both(source)
    mixT, low, turned = lax.optimization_barrier((mixT, low, turned))
    x2, h2, x3, head = ff_fwd(xT, mixT, gain[1], gain[2], place, attn_w, ff_w)

    rows = rows_gather(head, 3)
    first_id = me * shard
    limit = jnp.clip(MASK_ID - first_id, 0, shard).reshape(1)
    least = min(shard, MASK_ID - (fs - 1) * shard)
    meta, seq, slot, weight = plan(group_counts, slots, length)
    nblk = seq.shape[0] // RB
    target = (spread(group_targets, seq, slot) - first_id).reshape(nblk, 1, RB)
    inside = fs * slots <= 4096
    if not inside:
        rows = jnp.take(rows.reshape(fs * slots, width), jnp.clip(seq * slots + slot, 0, fs * slots - 1), axis=0)
    comp, lse_own, chosen = vocab_fwd(meta, limit, rows, low, target, least)
    lse_sum = small_gather(lse_own, 4, finish=lse_finish, name="lse_gather")
    own_loss = jnp.sum(weight * (jnp.where(seq == me, lse_sum.reshape(-1), 0.0) - chosen.reshape(-1)))
    scale = weight / (seq_count * fs * dps)
    lse_sum, attn_root, ff_root = lax.optimization_barrier((lse_sum, attn_root, ff_root))
    out_one, out_two, row_grads = vocab_bwd(
        meta, limit, comp, low, turned, target, lse_sum, scale.reshape(nblk, 1, RB),
        least, fs, slots, inside,
    )
    if not inside:
        at = jnp.arange(slots, dtype=jnp.int32)[None, :]
        row_grads = jnp.take(row_grads, jnp.minimum(meta[1][:, None] * 16 + at, seq.shape[0] - 1), axis=0)
        row_grads = jnp.where((at < group_counts[:, None])[:, :, None], row_grads, 0)
    own_rows = rows_reduce(row_grads, 5)
    halves_low = (out_one, out_two)
    if dps == 2:
        others = [dp_other(x) for x in halves_low]

    second, gg2, gg3, dff = ff_bwd(x3, x2, h2, own_rows, place, gain[1], gain[2], ff_w, fs)
    if dps == 2:
        second, others[0] = lax.optimization_barrier((second, others[0]))
    first, gg1, dattn = attn_bwd(xT, gain[0], cosT, sinT, second, hT, qT, kT, vT, mixT, lse, attn_w, fs)

    ff_part = lax.psum_scatter(dff.reshape(-1, width), "fsdp", scatter_dimension=0, tiled=True)

    aux = jnp.concatenate([jnp.concatenate([gg1, gg2, gg3], axis=1).T.reshape(-1), own_loss[None]])
    aux = jnp.pad(aux, (0, -aux.shape[0] % 1024)).reshape(-1, 128)
    if dps == 2:
        first, others[1] = lax.optimization_barrier((first, others[1]))
        out_sq = sum(jnp.sum(jnp.square(a.astype(F32) + b.astype(F32))) for a, b in zip(halves_low, others))
    else:
        out_grad = jnp.concatenate([dp_sum(a) for a in halves_low])[:shard]
        out_sq = jnp.sum(out_grad * out_grad)
    out = exchange(first.reshape(fs, features, length), 6, dps == 2, "gradients", aux)
    dattn, ff_part, aux = lax.optimization_barrier((dattn, ff_part, out[-1]))
    ff_grad = dp_sum(ff_part.reshape(2, -1, width))
    attn_grad = rows_reduce(dattn.reshape(fs, -1, width), 8, "attn_reduce", dps == 2).reshape(4, -1, width)
    if dps != 2:
        attn_grad = dp_sum(attn_grad.astype(BF16))
    if dps == 2:
        parts, other = out[:2]
        parts, ff_grad, attn_grad = lax.optimization_barrier((parts, ff_grad, attn_grad))
        other_ids = lax.dynamic_slice_in_dim(everyone, (1 - replica) * fs, fs, 0)[:, :length]
        embed_grad, embed_sq = scatter(jnp.concatenate([group_ids, other_ids]), (parts, other), vocab, 2)
        embed_sq = jnp.sum(embed_sq)
    else:
        parts = out[0]
        embed_grad = dp_sum(scatter(group_ids, (parts,), vocab, 2)[0].astype(BF16))
        embed_sq = jnp.sum(embed_grad * embed_grad)
        if dps > 1:
            aux = lax.psum(aux, "dp")
    aux = aux.reshape(-1)
    gain_grad, loss_sum = aux[: 3 * width].reshape(3, width), aux[3 * width]
    squares = (
        jnp.sum(attn_grad * attn_grad)
        + jnp.sum(ff_grad * ff_grad)
        + embed_sq
        + out_sq
    )
    attn_full, ff_full = spread_out(attn_grad), spread_out(ff_grad)
    squares, attn_full = lax.optimization_barrier((squares, attn_full))
    squares = small_gather(jnp.full((8, 128), squares), 7, finish=sum_finish, name="squares")[0, 0]
    clip_norm = jnp.sqrt(squares + jnp.sum(gain_grad * gain_grad))
    factor = jnp.minimum(1.0, clip_level / clip_norm)
    embed_new, embed_one_new, embed_two_new, ema_embed_new = adam_table(
        factor, embedding, embed_moment_one, embed_moment_two, ema_embed, [embed_grad], rate_embed, False
    )
    if dps == 2:
        out_new, out_one_new, out_two_new, ema_out_new = adam_table(
            factor, out_table, out_moment_one, out_moment_two, ema_out,
            [halves_low[0], others[0], halves_low[1], others[1]], rate_out, True
        )
    else:
        out_new, out_one_new, out_two_new = adamw(
            out_table, out_moment_one, out_moment_two, out_grad * factor, rate_out
        )
        ema_out_new = ema_decay * ema_out + (1 - ema_decay) * out_new
    gains_new, gains_one_new, gains_two_new = adamw(
        norm_gains, gain_moment_one, gain_moment_two, gain_grad * factor, rate_gain
    )

    def shampoo(weights, grad, left, right, left_root, whole_root, full):
        own = grad.astype(BF16)
        columns = right.shape[1]
        own_columns = lax.dynamic_slice_in_dim(full, me * columns, columns, 2)

        def product(text, a, b):
            return jnp.einsum(text, a, b, preferred_element_type=F32)

        mix = (1 - stat_decay) * factor * factor
        left_new = stat_decay * left + mix * product("nik,njk->nij", own, full)
        right_new = stat_decay * right + mix * product("nki,nkj->nij", own_columns, full)
        part = product("nij,njk->nik", left_root.astype(BF16), full)
        update = product("nij,njk->nik", part.astype(BF16), whole_root) * factor
        new = weights - rate_shampoo * (update + shampoo_decay * weights)
        return new, grad * factor, left_new, right_new

    attention_new, attn_clip, attention_left_new, attention_right_new = shampoo(
        attention, attn_grad, attention_left, attention_right, attention_left_root, attn_root, attn_full
    )
    ff_new, ff_clip, ff_left_new, ff_right_new = shampoo(
        feedforward, ff_grad, ff_left, ff_right, ff_left_root, ff_root, ff_full
    )

    def averaged(average, new):
        return ema_decay * average + (1 - ema_decay) * new

    return (
        loss_sum, clip_norm, embed_new, embed_one_new, embed_two_new, out_new, out_one_new, out_two_new,
        gains_new, gains_one_new, gains_two_new, attention_new, attn_clip, attention_left_new, attention_right_new,
        ff_new, ff_clip, ff_left_new, ff_right_new,
        ema_embed_new, ema_out_new, averaged(ema_gains, gains_new),
        averaged(ema_attention, attention_new), averaged(ema_feedforward, ff_new),
    )


def solution(mesh):
    seqs, rows, stack, none = P(("dp", "fsdp")), P("fsdp", None), P(None, "fsdp", None), P()
    in_specs = (
        seqs, seqs, seqs, seqs, rows, rows, none, stack, stack, rows, rows, rows, rows, none, none,
        stack, stack, stack, stack, stack, stack, stack, stack, rows, rows, none, stack, stack,
    )
    out_specs = (
        none, none, rows, rows, rows, rows, rows, rows, none, none, none, stack, stack, stack, stack,
        stack, stack, stack, stack, rows, rows, none, stack, stack,
    )
    return jax.shard_map(
        per_device, mesh=mesh, in_specs=in_specs, out_specs=out_specs, check_vma=False
    )
```

```python
import functools

import jax
import jax.numpy as jnp
import numpy as np
from jax import lax
from jax.experimental import pallas as pl
from jax.experimental.pallas import tpu as pltpu
from jax.sharding import PartitionSpec as P

F32, BF16 = jnp.float32, jnp.bfloat16
HEAD = 64
EPS = 1e-5
BSTEP = 1024
VL = 60 * 1024 * 1024

def dot(a, b, ca, cb):
    return lax.dot_general(a, b, (((ca,), (cb,)), ((), ())), preferred_element_type=F32)

def params(limit=VL):
    return pltpu.CompilerParams(vmem_limit_bytes=limit)

def cost(us):
    return pl.CostEstimate(flops=int(us * 1.15e9), bytes_accessed=0, transcendentals=0)

def whole(shape):
    return pl.BlockSpec(shape, lambda *a: (0,) * len(shape))

def attn_fwd_kernel(x_ref, gain_ref, cos_ref, sin_ref, w_ref, h_ref, q_ref, k_ref, v_ref, m_ref, lse_ref, kn_ref):
    width, length = x_ref.shape
    block = q_ref.shape[0]
    heads = block // HEAD
    half = HEAD // 2

    @pl.when(pl.program_id(0) == 0)
    def _():
        def cols(c, carry):
            at = pl.ds(pl.multiple_of(c * 128, 128), 128)
            x = x_ref[:, at].astype(F32)
            centred = x - jnp.mean(x, axis=0, keepdims=True)
            spread = jnp.mean(centred * centred, axis=0, keepdims=True)
            h_ref[:, at] = (centred * lax.rsqrt(spread + EPS) * gain_ref[:, 0:1]).astype(BF16)
            return carry
        lax.fori_loop(0, length // 128, cols, 0)

    cosine, sine = cos_ref[...], sin_ref[...]
    hidden = h_ref[...]
    for j, out in ((0, q_ref), (1, k_ref)):
        p = dot(w_ref[j], hidden, 0, 0)
        for h in range(heads):
            a = p[h * HEAD : h * HEAD + half]
            b = p[h * HEAD + half : (h + 1) * HEAD]
            ra = (a * cosine - b * sine).astype(BF16)
            rb = (b * cosine + a * sine).astype(BF16)
            if j == 0:
                ra, rb = ra * 0.125, rb * 0.125
            out[h * HEAD : h * HEAD + half, :] = ra
            out[h * HEAD + half : (h + 1) * HEAD, :] = rb
    v_ref[...] = dot(w_ref[2], hidden, 0, 0).astype(BF16)
    for h in range(heads):
        rows = slice(h * HEAD, (h + 1) * HEAD)
        kn_ref[h] = k_ref[rows, :].T
    def one(h, carry):
        rows = pl.ds(pl.multiple_of(h * HEAD, HEAD), HEAD)
        s = dot(kn_ref[h], q_ref[rows, :], 1, 0)
        top = jnp.max(s, axis=0, keepdims=True)
        e = jnp.exp(s - top)
        total = jnp.sum(e, axis=0, keepdims=True)
        o = dot(v_ref[rows, :], e.astype(BF16), 1, 0)
        m_ref[rows, :] = (o / total).astype(BF16)
        lse_ref[0, pl.ds(h, 1), :] = top + jnp.log(total)
        return carry
    lax.fori_loop(0, heads, one, 0)

def attn_fwd(xT, gain, cosT, sinT, w):
    width, length = xT.shape
    block = 256
    n = width // block
    col = pl.BlockSpec((block, length), lambda i: (i, 0))
    t = jax.ShapeDtypeStruct((width, length), BF16)
    return pl.pallas_call(
        attn_fwd_kernel, grid=(n,), name="attn_fwd", cost_estimate=cost(34),
        in_specs=[whole((width, length)), whole(gain.shape), whole(cosT.shape), whole(sinT.shape),
                  pl.BlockSpec((3, width, block), lambda i: (0, 0, i))],
        out_specs=[whole((width, length)), col, col, col, col, pl.BlockSpec((1, 8, length), lambda i: (i, 0, 0))],
        out_shape=[t, t, t, t, t, jax.ShapeDtypeStruct((n, 8, length), F32)],
        scratch_shapes=[pltpu.VMEM((block // HEAD, length, HEAD), BF16)],
        compiler_params=params(),
    )(xT, gain, cosT, sinT, w)

def attn_bwd_kernel(x_ref, gain_ref, cos_ref, sin_ref, sg_ref, h_ref, q_ref, k_ref, v_ref, m_ref, lse_ref, w_ref, wo_ref,
                    first_ref, gg_ref, dw_ref, hg_ref, low_ref, do_ref, kn_ref, vn_ref, dk_ref, dv_ref, dq_ref, dwo_ref):
    width, length = x_ref.shape
    block = q_ref.shape[0]
    heads = block // HEAD
    half = HEAD // 2
    step = min(BSTEP, length)
    i = pl.program_id(0)

    @pl.when(i == 0)
    def _():
        low_ref[...] = sg_ref[...].astype(BF16)
        hg_ref[...] = jnp.zeros_like(hg_ref)

    do_ref[...] = dot(wo_ref[0], low_ref[...], 1, 0).astype(BF16)
    fs, _, each, _ = dw_ref.shape
    dwo_ref[pl.ds(pl.multiple_of(i * block, block), block), :] = dot(m_ref[...], low_ref[...], 1, 1).astype(BF16)
    cosine, sine = cos_ref[...], sin_ref[...]
    for h in range(heads):
        rows = slice(h * HEAD, (h + 1) * HEAD)
        kn_ref[h] = k_ref[rows, :].T
        vn_ref[h] = v_ref[rows, :].T
    def one(h, carry):
        rows = pl.ds(pl.multiple_of(h * HEAD, HEAD), HEAD)
        for c in range(length // step):
            at = slice(c * step, (c + 1) * step)
            s = dot(kn_ref[h], q_ref[rows, at], 1, 0)
            p = jnp.exp(s - lse_ref[0, pl.ds(h, 1), at])
            dp = dot(vn_ref[h], do_ref[rows, at], 1, 0)
            centre = jnp.sum(p * dp, axis=0, keepdims=True)
            ds = (p * (dp - centre)).astype(BF16)
            pb = p.astype(BF16)
            dv = dot(do_ref[rows, at], pb, 1, 1)
            dk = dot(q_ref[rows, at], ds, 1, 1)
            if c == 0:
                dv_ref[rows, :] = dv
                dk_ref[rows, :] = dk
            else:
                dv_ref[rows, :] += dv
                dk_ref[rows, :] += dk
            dq_ref[rows, at] = dot(k_ref[rows, :], ds, 1, 0) * 0.125
        return carry
    lax.fori_loop(0, heads, one, 0)
    hidden = h_ref[...]
    for j, ref in ((0, dq_ref), (1, dk_ref), (2, dv_ref)):
        if j == 2:
            g = ref[...].astype(BF16)
        else:
            parts = []
            for h in range(heads):
                a = ref[h * HEAD : h * HEAD + half, :]
                b = ref[h * HEAD + half : (h + 1) * HEAD, :]
                parts += [(a * cosine + b * sine).astype(BF16), (b * cosine - a * sine).astype(BF16)]
            g = jnp.concatenate(parts, axis=0)
        dw_ref[:, j, :, pl.ds(pl.multiple_of(i * block, block), block)] = dot(hidden, g, 1, 1).astype(BF16).reshape(fs, each, block)
        hg_ref[...] += dot(w_ref[j], g, 1, 0)

    @pl.when(i == pl.num_programs(0) - 1)
    def _():
        dw_ref[:, 3] = dwo_ref[...].reshape(fs, each, width)
        def cols(c, acc):
            at = pl.ds(pl.multiple_of(c * 128, 128), 128)
            dx, gg = ln_back(x_ref[:, at].astype(F32), hg_ref[:, at], gain_ref[:, 0:1])
            first_ref[:, at] = (sg_ref[:, at] + dx).astype(BF16)
            return acc + gg
        acc = lax.fori_loop(0, length // 128, cols, jnp.zeros((width, 128), F32))
        gg_ref[...] = jnp.sum(acc, axis=1, keepdims=True)

def ln_back(x, g, gain):
    centred = x - jnp.mean(x, axis=0, keepdims=True)
    spread = jnp.mean(centred * centred, axis=0, keepdims=True)
    rs = lax.rsqrt(spread + EPS)
    xh = centred * rs
    gx = g * gain
    dx = rs * (gx - jnp.mean(gx, axis=0, keepdims=True) - xh * jnp.mean(gx * xh, axis=0, keepdims=True))
    return dx, g * xh

def attn_bwd(xT, gain, cosT, sinT, sg, hT, q, k, v, m, lse, w, fs):
    width, length = xT.shape
    block = 256
    n = width // block
    col = pl.BlockSpec((block, length), lambda i: (i, 0))
    full = whole((width, length))
    return pl.pallas_call(
        attn_bwd_kernel, grid=(n,), name="attn_bwd", cost_estimate=cost(62),
        in_specs=[full, whole(gain.shape), whole(cosT.shape), whole(sinT.shape), full, full, col, col, col, col,
                  pl.BlockSpec((1, 8, length), lambda i: (i, 0, 0)),
                  pl.BlockSpec((3, width, block), lambda i: (0, 0, i)),
                  pl.BlockSpec((1, block, width), lambda i: (3, i, 0))],
        out_specs=[full, whole((width, 1)), whole((fs, 4, width // fs, width))],
        out_shape=[jax.ShapeDtypeStruct((width, length), BF16), jax.ShapeDtypeStruct((width, 1), F32),
                   jax.ShapeDtypeStruct((fs, 4, width // fs, width), BF16)],
        scratch_shapes=[pltpu.VMEM((width, length), F32), pltpu.VMEM((width, length), BF16), pltpu.VMEM((block, length), BF16),
                        pltpu.VMEM((block // HEAD, length, HEAD), BF16), pltpu.VMEM((block // HEAD, length, HEAD), BF16),
                        pltpu.VMEM((block, length), F32), pltpu.VMEM((block, length), F32), pltpu.VMEM((block, length), F32),
                        pltpu.VMEM((width, width), BF16)],
        compiler_params=params(),
    )(xT, gain, cosT, sinT, sg, hT, q, k, v, m, lse, w, w)
def ff_fwd_kernel(x_ref, m_ref, g2_ref, g3_ref, pos_ref, wo_ref, up_ref, down_ref,
                  x2_ref, h2_ref, x3_ref, head_ref, fin_ref):
    width, length = x_ref.shape
    i = pl.program_id(0)

    @pl.when(i == 0)
    def _():
        x2_ref[...] = x_ref[...].astype(F32) + dot(wo_ref[0], m_ref[...], 0, 0)
        x3_ref[...] = x2_ref[...]
        def cols(c, carry):
            at = pl.ds(pl.multiple_of(c * 128, 128), 128)
            h2_ref[:, at] = ln(x2_ref[:, at], g2_ref[:, 1:2]).astype(BF16)
            return carry
        lax.fori_loop(0, length // 128, cols, 0)

    pre = dot(up_ref[0], h2_ref[...], 1, 0)
    act = jax.nn.gelu(pre, approximate=True).astype(BF16)
    x3_ref[...] += dot(down_ref[0], act, 0, 0)

    @pl.when(i == pl.num_programs(0) - 1)
    def _():
        def cols(c, carry):
            at = pl.ds(pl.multiple_of(c * 128, 128), 128)
            fin_ref[:, at] = ln(x3_ref[:, at], g3_ref[:, 2:3]).astype(BF16)
            return carry
        lax.fori_loop(0, length // 128, cols, 0)
        slots = pos_ref.shape[0]
        onehot = (pos_ref[...] == lax.broadcasted_iota(jnp.int32, (slots, length), 1)).astype(BF16)
        head_ref[...] = dot(onehot, fin_ref[...], 1, 1).astype(BF16)

def ln(x, gain):
    centred = x - jnp.mean(x, axis=0, keepdims=True)
    spread = jnp.mean(centred * centred, axis=0, keepdims=True)
    return centred * lax.rsqrt(spread + EPS) * gain

def ff_fwd(xT, m, g2, g3, pos, attn_w, ff_w):
    width, length = xT.shape
    hidden = ff_w.shape[1]
    block = 512
    n = hidden // block
    slots = pos.shape[0]
    full = whole((width, length))
    f = jax.ShapeDtypeStruct((width, length), F32)
    return pl.pallas_call(
        ff_fwd_kernel, grid=(n,), name="ff_fwd", cost_estimate=cost(34),
        in_specs=[full, full, whole(g2.shape), whole(g3.shape), whole((slots, 1)),
                  pl.BlockSpec((1, width, width), lambda i: (3, 0, 0)),
                  pl.BlockSpec((1, block, width), lambda i: (0, i, 0)),
                  pl.BlockSpec((1, block, width), lambda i: (1, i, 0))],
        out_specs=[full, full, full, whole((slots, width))],
        out_shape=[f, jax.ShapeDtypeStruct((width, length), BF16), f, jax.ShapeDtypeStruct((slots, width), BF16)],
        scratch_shapes=[pltpu.VMEM((width, length), BF16)],
        compiler_params=params(),
    )(xT, m, g2, g3, pos, attn_w, ff_w, ff_w)

def ff_bwd_kernel(x3_ref, x2_ref, h2_ref, rg_ref, pos_ref, g2_ref, g3_ref, up_ref, down_ref,
                  sg_ref, gg2_ref, gg3_ref, dw_ref, low_ref, hg_ref):
    width, length = x3_ref.shape
    i = pl.program_id(0)
    slots = pos_ref.shape[0]

    @pl.when(i == 0)
    def _():
        rows = rg_ref[...]
        high = rows.astype(BF16)
        rest = (rows - high.astype(F32)).astype(BF16)
        hg_ref[...] = jnp.zeros_like(hg_ref)
        def cols(c, acc):
            at = pl.ds(pl.multiple_of(c * 128, 128), 128)
            onehot = (pos_ref[...] == c * 128 + lax.broadcasted_iota(jnp.int32, (slots, 128), 1)).astype(BF16)
            fg = dot(high, onehot, 0, 0) + dot(rest, onehot, 0, 0)
            dx, gg = ln_back(x3_ref[:, at], fg, g3_ref[:, 2:3])
            sg_ref[:, at] = dx
            low_ref[:, at] = dx.astype(BF16)
            return acc + gg
        acc = lax.fori_loop(0, length // 128, cols, jnp.zeros((width, 128), F32))
        gg3_ref[...] = jnp.sum(acc, axis=1, keepdims=True)

    ag = dot(down_ref[0], low_ref[...], 1, 0)
    pre = dot(up_ref[0], h2_ref[...], 1, 0)
    c0, c1 = 0.7978845608028654, 0.044715
    t = jnp.tanh(c0 * (pre + c1 * pre * pre * pre))
    half = 0.5 * (1.0 + t)
    act = (pre * half).astype(BF16)
    slope = half + 0.5 * pre * (1.0 - t * t) * (c0 * (1.0 + 3.0 * c1 * pre * pre))
    pg = (slope * ag).astype(BF16)
    shape = (dw_ref.shape[0],) + dw_ref.shape[2:]
    dw_ref[:, 1] = dot(act, low_ref[...], 1, 1).astype(BF16).reshape(shape)
    dw_ref[:, 0] = dot(pg, h2_ref[...], 1, 1).astype(BF16).reshape(shape)
    hg_ref[...] += dot(up_ref[0], pg, 0, 0)

    @pl.when(i == pl.num_programs(0) - 1)
    def _():
        def cols(c, acc):
            at = pl.ds(pl.multiple_of(c * 128, 128), 128)
            dx, gg = ln_back(x2_ref[:, at], hg_ref[:, at], g2_ref[:, 1:2])
            sg_ref[:, at] += dx
            return acc + gg
        acc = lax.fori_loop(0, length // 128, cols, jnp.zeros((width, 128), F32))
        gg2_ref[...] = jnp.sum(acc, axis=1, keepdims=True)

def ff_bwd(x3, x2, h2, rg, pos, g2, g3, ff_w, fs):
    width, length = x3.shape
    hidden = ff_w.shape[1]
    each = hidden // fs
    block = each * max(1, 768 // each)
    n = hidden // block
    slots = pos.shape[0]
    full = whole((width, length))
    wb = pl.BlockSpec((block // each, 2, each, width), lambda i: (i, 0, 0, 0))
    g = jax.ShapeDtypeStruct((width, 1), F32)
    return pl.pallas_call(
        ff_bwd_kernel, grid=(n,), name="ff_bwd", cost_estimate=cost(45),
        in_specs=[full, full, full, whole((slots, width)), whole((slots, 1)), whole(g2.shape), whole(g3.shape),
                  pl.BlockSpec((1, block, width), lambda i: (0, i, 0)),
                  pl.BlockSpec((1, block, width), lambda i: (1, i, 0))],
        out_specs=[full, whole((width, 1)), whole((width, 1)), wb],
        out_shape=[jax.ShapeDtypeStruct((width, length), F32), g, g, jax.ShapeDtypeStruct((fs, 2, each, width), BF16)],
        scratch_shapes=[pltpu.VMEM((width, length), BF16), pltpu.VMEM((width, length), F32)],
        compiler_params=params(),
    )(x3, x2, h2, rg, pos, g2, g3, ff_w, ff_w)
RB = 256
FCH, BCH = 8, 8

def pick(n, top=8):
    return max(k for k in range(1, top + 1) if n % k == 0)

def table_kernel(source_ref, low_ref, turned_ref, *, shard):
    block = source_ref.shape[0]
    ids = pl.program_id(0) * block + lax.broadcasted_iota(jnp.int32, source_ref.shape, 0)
    low = jnp.where(ids < shard, source_ref[...], 0.0).astype(BF16)
    low_ref[...] = low
    turned_ref[...] = low.T

def table_both(table):
    shard, width = table.shape
    vocab = -(-shard // 128) * 128
    block = 640 if vocab % 640 == 0 else 128
    return pl.pallas_call(
        functools.partial(table_kernel, shard=shard), name="table_both", grid=(vocab // block,), cost_estimate=cost(12),
        in_specs=[pl.BlockSpec((block, width), lambda i: (i, 0))],
        out_specs=[pl.BlockSpec((block, width), lambda i: (i, 0)), pl.BlockSpec((width, block), lambda i: (0, i))],
        out_shape=[jax.ShapeDtypeStruct((vocab, width), BF16), jax.ShapeDtypeStruct((width, vocab), BF16)],
        compiler_params=params())(table)

def compact(meta_ref, rows_ref, comp_ref):
    nseq, slots, width = rows_ref.shape
    def clear(b, carry):
        comp_ref[pl.ds(pl.multiple_of(b * RB, RB), RB), :] = jnp.zeros((RB, width), BF16)
        return carry
    lax.fori_loop(0, meta_ref[2, 0], clear, 0)
    def seq(s, carry):
        def part(c, c2):
            comp_ref[pl.ds(pl.multiple_of((meta_ref[1, s] + c) * 16, 16), 16), :] = rows_ref[s, pl.ds(pl.multiple_of(c * 16, 16), 16), :]
            return c2
        lax.fori_loop(0, meta_ref[0, s], part, 0)
        return carry
    lax.fori_loop(0, nseq, seq, 0)

def vocab_fwd_kernel(meta_ref, limit_ref, rows_ref, table_ref, target_ref, lse_ref, chosen_ref, *outs, chunk, least, inside):
    comp_ref = outs[0] if inside else rows_ref
    vocab = table_ref.shape[0]
    if inside:
        nseq, slots, width = rows_ref.shape
        compact(meta_ref, rows_ref, comp_ref)
    lse_ref[...] = jnp.zeros_like(lse_ref)
    chosen_ref[...] = jnp.zeros_like(chosen_ref)
    limit = limit_ref[0]
    def block(b, carry):
        rows = comp_ref[pl.ds(pl.multiple_of(b * RB, RB), RB), :]
        target = target_ref[b]
        top = total = chosen = None
        for v in range(vocab // chunk):
            l = dot(table_ref[v * chunk:(v + 1) * chunk, :], rows, 1, 1)
            ids = v * chunk + lax.broadcasted_iota(jnp.int32, (chunk, RB), 0)
            hit = jnp.sum(jnp.where(ids == target, l, 0.0), axis=0, keepdims=True)
            if (v + 1) * chunk > least:
                l = jnp.where(ids < limit, l, -jnp.inf)
            m = jnp.max(l, axis=0, keepdims=True)
            if v == 0:
                top = m
                total = jnp.sum(jnp.exp(l - top), axis=0, keepdims=True)
                chosen = hit
            else:
                new = jnp.maximum(top, m)
                total = total * jnp.exp(top - new) + jnp.sum(jnp.exp(l - new), axis=0, keepdims=True)
                chosen = chosen + hit
                top = new
        lse_ref[b] = top + jnp.log(total)
        chosen_ref[b] = chosen
        return carry
    lax.fori_loop(0, meta_ref[2, 0], block, 0)

def vocab_fwd(meta, limit, rows, table, target, least):
    inside = rows.ndim == 3
    width = rows.shape[-1]
    nblk = target.shape[0]
    vocab = table.shape[0]
    chunk = 128 * pick(vocab // 128, FCH)
    smem = pl.BlockSpec(memory_space=pltpu.SMEM)
    vm = pl.BlockSpec(memory_space=pltpu.VMEM)
    st = jax.ShapeDtypeStruct((nblk, 1, RB), F32)
    comp = [jax.ShapeDtypeStruct((nblk * RB, width), BF16)] if inside else []
    out = pl.pallas_call(
        functools.partial(vocab_fwd_kernel, chunk=chunk, least=least, inside=inside), name="vocab_fwd", cost_estimate=cost(20),
        in_specs=[smem, smem, vm, vm, vm], out_specs=[vm] * (2 + len(comp)),
        out_shape=[st, st] + comp,
        compiler_params=params())(meta, limit, rows, table, target)
    return out[2] if inside else rows, out[0], out[1]

def vocab_bwd_kernel(meta_ref, limit_ref, comp_ref, table_ref, turned_ref, target_ref, lse_ref, scale_ref,
                     og_ref, og2_ref, rg_ref, acc_ref, rc_ref, low_ref, back_ref, sem, *, chunk, least, inside):
    vocab, width = table_ref.shape
    limit = limit_ref[0]
    nch = vocab // chunk
    def clear(b, carry):
        acc_ref[pl.ds(pl.multiple_of(b * 128, 128), 128), :] = jnp.zeros((128, width), F32)
        return carry
    lax.fori_loop(0, vocab // 128, clear, 0)
    def block(b, carry):
        rows = comp_ref[pl.ds(pl.multiple_of(b * RB, RB), RB), :]
        target, lse, scale = target_ref[b], lse_ref[b], scale_ref[b]
        rg = None
        for v in range(nch):
            l = dot(table_ref[v * chunk:(v + 1) * chunk, :], rows, 1, 1)
            ids = v * chunk + lax.broadcasted_iota(jnp.int32, (chunk, RB), 0)
            p = jnp.exp(l - lse)
            p = jnp.where(ids == target, p - 1.0, p)
            if (v + 1) * chunk > least:
                p = jnp.where(ids < limit, p, 0.0)
            g = (scale * p).astype(BF16)
            acc_ref[v * chunk:(v + 1) * chunk, :] += dot(g, rows, 1, 0)
            part = dot(turned_ref[:, v * chunk:(v + 1) * chunk], g, 1, 0)
            rg = part if rg is None else rg + part
        rc_ref[pl.ds(pl.multiple_of(b * RB, RB), RB), :] = rg.T.astype(BF16)
        return carry
    lax.fori_loop(0, meta_ref[2, 0], block, 0)
    if inside:
        nseq, slots, _ = back_ref.shape
        def seq(s, carry):
            back_ref[s] = jnp.zeros((slots, width), BF16)
            def part(c, c2):
                back_ref[s, pl.ds(pl.multiple_of(c * 16, 16), 16), :] = rc_ref[pl.ds(pl.multiple_of((meta_ref[1, s] + c) * 16, 16), 16), :]
                return c2
            lax.fori_loop(0, meta_ref[0, s], part, 0)
            return carry
        lax.fori_loop(0, nseq, seq, 0)
        out = pltpu.make_async_copy(back_ref, rg_ref, sem.at[0])
    else:
        out = pltpu.make_async_copy(rc_ref, rg_ref, sem.at[0])
    out.start()
    outs = [out]
    part = og_ref.shape[0]
    for v, (ref, start) in enumerate(((og_ref, 0), (og2_ref, part))):
        at = pl.ds(start, ref.shape[0])
        low_ref[at, :] = acc_ref[at, :].astype(BF16)
        outs.append(pltpu.make_async_copy(low_ref.at[at], ref, sem.at[1 + v]))
        outs[-1].start()
    for o in outs:
        o.wait()

def vocab_bwd(meta, limit, comp, table, turned, target, lse, scale, least, nseq, slots, inside):
    rows, width = comp.shape
    vocab = table.shape[0]
    chunk = 128 * pick(vocab // 128, BCH)
    smem = pl.BlockSpec(memory_space=pltpu.SMEM)
    vm = pl.BlockSpec(memory_space=pltpu.VMEM)
    hbm = pl.BlockSpec(memory_space=pl.ANY)
    shape = (nseq, slots, width) if inside else (rows, width)
    part = vocab // 256 * 128
    return pl.pallas_call(
        functools.partial(vocab_bwd_kernel, chunk=chunk, least=least, inside=inside), name="vocab_bwd", cost_estimate=cost(40),
        in_specs=[smem, smem] + [vm] * 6, out_specs=[hbm, hbm, hbm],
        out_shape=[jax.ShapeDtypeStruct((part, width), BF16), jax.ShapeDtypeStruct((vocab - part, width), BF16), jax.ShapeDtypeStruct(shape, BF16)],
        scratch_shapes=[pltpu.VMEM((vocab, width), F32), pltpu.VMEM((rows, width), BF16),
                        pltpu.VMEM((vocab, width), BF16), pltpu.VMEM(shape if inside else (1, 16, width), BF16),
                        pltpu.SemaphoreType.DMA((3,))],
        compiler_params=params())(meta, limit, comp, table, turned, target, lse, scale)

def plan(counts, slots, length):
    nseq = counts.shape[0]
    units = (counts + 15) // 16
    ends = jnp.cumsum(units)
    offs = ends - units
    total = ends[-1] * 16
    nblk = (total + RB - 1) // RB
    cap = (nseq * slots + RB - 1) // RB * RB
    at = jnp.arange(cap, dtype=jnp.int32)
    seq = jnp.minimum(jnp.sum((at[:, None] >= ends[None, :] * 16).astype(jnp.int32), axis=1), nseq - 1)
    mine = (seq[:, None] == jnp.arange(nseq, dtype=jnp.int32)[None, :])
    slot = at - jnp.sum(jnp.where(mine, offs[None, :] * 16, 0), axis=1)
    cnt = jnp.sum(jnp.where(mine, counts[None, :], 0), axis=1)
    live = slot < cnt
    weight = jnp.where(live, length / cnt.astype(F32), 0.0)
    meta = jnp.stack([units, offs, jnp.full((nseq,), nblk)]).astype(jnp.int32)
    return meta, seq, slot, weight

def spread(values, seq, slot):
    nseq, slots = values.shape
    parts = jnp.concatenate([values // 256, values % 256], axis=1).astype(BF16)
    mine = (seq[:, None] == jnp.arange(nseq, dtype=jnp.int32)[None, :]).astype(BF16)
    rows = jnp.dot(mine, parts, preferred_element_type=F32)
    hit = slot[:, None] == jnp.arange(slots, dtype=jnp.int32)[None, :]
    both = rows[:, :slots] * 256.0 + rows[:, slots:]
    return jnp.sum(jnp.where(hit, both, 0.0), axis=1).astype(jnp.int32)

def halves(vocab):
    nb = vocab // 128
    low = (nb + 1) // 2
    return nb, low

def sections(count, size):
    return [(s, min(size, count - s)) for s in range(0, count, size)]

def gather_kernel(ids_ref, flag_ref, emb_ref, out_ref, tab_ref, raw_ref, row_ref, sem):
    feat, vocab = emb_ref.shape
    nseq, _, length = out_ref.shape
    nb, low = halves(vocab)
    size = -(-low // 6)
    secs = sections(low, size)
    def copies(k):
        s, n = secs[k]
        out = [pltpu.make_async_copy(emb_ref.at[:, pl.ds(s * 128, n * 128)], raw_ref.at[:, pl.ds(s * 128, n * 128)], sem.at[2 * k])]
        m = min(n, nb - low - s)
        if m > 0:
            out.append(pltpu.make_async_copy(emb_ref.at[:, pl.ds((low + s) * 128, m * 128)], raw_ref.at[:, pl.ds((low + s) * 128, m * 128)], sem.at[2 * k + 1]))
        return out
    for k in range(len(secs)):
        for c in copies(k):
            c.start()
    pad = jnp.zeros((64 - feat, 128), F32)
    for k in range(len(secs)):
        for c in copies(k):
            c.wait()
        s, n = secs[k]
        m = max(0, min(n, nb - low - s))
        def turn(b, carry):
            a = raw_ref[:, pl.ds(pl.multiple_of(b * 128, 128), 128)]
            h = raw_ref[:, pl.ds(pl.multiple_of((low + b) * 128, 128), 128)]
            tab_ref[pl.ds(pl.multiple_of(b * 128, 128), 128), :] = jnp.concatenate([a, pad, h, pad], axis=0).T
            return carry
        lax.fori_loop(s, s + m, turn, 0, unroll=3)
        for b in range(s + m, s + n):
            a = raw_ref[:, b * 128:(b + 1) * 128]
            tab_ref[b * 128:(b + 1) * 128, :] = jnp.concatenate([a, pad, pad, jnp.zeros((feat, 128), F32)], axis=0).T
    U = 32
    def seq(s, carry):
        def grp(g, c2):
            base = pl.multiple_of(g * U, U)
            for j in range(U):
                i = ids_ref[s * length + base + j]
                row_ref[pl.ds(base + j, 1), :] = tab_ref[pl.ds(i, 1), :]
            return c2
        lax.fori_loop(0, length // U, grp, 0)
        for c in range(length // 128):
            t = row_ref[c * 128:(c + 1) * 128, :].T
            f = flag_ref[s, :, c * 128:(c + 1) * 128] > 0
            out_ref[s, :, c * 128:(c + 1) * 128] = jnp.where(f, t[64:64 + feat], t[:feat]).astype(BF16)
        return carry
    lax.fori_loop(0, nseq, seq, 0)

def split_ids(ids, vocab):
    nb, low = halves(vocab)
    high = ids >= low * 128
    return jnp.where(high, ids - low * 128, ids), high.astype(jnp.int32)

def gather(ids, emb):
    nseq, length = ids.shape
    feat, vocab = emb.shape
    nb, low = halves(vocab)
    rid, flag = split_ids(ids, vocab)
    return pl.pallas_call(gather_kernel, name="emb_gather", cost_estimate=cost(32),
        in_specs=[pl.BlockSpec(memory_space=pltpu.SMEM), pl.BlockSpec(memory_space=pltpu.VMEM), pl.BlockSpec(memory_space=pl.ANY)],
        out_specs=pl.BlockSpec(memory_space=pltpu.VMEM),
        out_shape=jax.ShapeDtypeStruct((nseq, feat, length), BF16),
        scratch_shapes=[pltpu.VMEM((low * 128, 128), F32), pltpu.VMEM((feat, vocab), F32), pltpu.VMEM((length, 128), F32), pltpu.SemaphoreType.DMA((12,))],
        compiler_params=params())(rid.reshape(-1), flag.reshape(nseq, 1, length), emb)

def scatter_kernel(ids_ref, flag_ref, *refs, ng, per):
    g_refs = refs[:ng]
    out_ref, sq_ref, raw_ref, row_ref, sem = refs[ng:ng + 5]
    tabs = refs[ng + 5:]
    feat, vocab = out_ref.shape
    nseq, _, length = g_refs[0].shape
    nb, low = halves(vocab)
    zero128 = jnp.zeros((128, 128), F32)
    def zero(b, carry):
        for t in tabs:
            t[pl.ds(pl.multiple_of(b * 128, 128), 128), :] = zero128
        return carry
    lax.fori_loop(0, low, zero, 0)
    pad = jnp.zeros((64 - feat, 128), F32)
    U = 8
    streams = [(g, p) for g in range(ng) for p in range(per)]
    each = nseq // per
    def seq(s, carry):
        for k, (g, p) in enumerate(streams):
            q = p * each + s
            for c in range(length // 128):
                at = slice(c * 128, (c + 1) * 128)
                v = g_refs[g][q, :, at].astype(F32)
                f = flag_ref[g * nseq + q, :, at] > 0
                row_ref[k, at, :] = jnp.concatenate([jnp.where(f, 0.0, v), pad, jnp.where(f, v, 0.0), pad], axis=0).T
        def grp(n, c2):
            base = pl.multiple_of(n * U, U)
            for j in range(U):
                idx = [ids_ref[(g * nseq + p * each + s) * length + base + j] for g, p in streams]
                old = [tabs[k][pl.ds(idx[k], 1), :] for k in range(len(streams))]
                new = [old[k] + row_ref[k, pl.ds(base + j, 1), :] for k in range(len(streams))]
                for k in range(len(streams)):
                    tabs[k][pl.ds(idx[k], 1), :] = new[k]
            return c2
        lax.fori_loop(0, length // U, grp, 0)
        return carry
    lax.fori_loop(0, each, seq, 0)
    def tile(b):
        at = pl.ds(pl.multiple_of(b * 128, 128), 128)
        parts = [sum((tabs[g * per + p][at, :] for p in range(1, per)), tabs[g * per][at, :]) for g in range(ng)]
        return sum(parts[1:], parts[0]).T
    size = -(-low // 6)
    secs = sections(low, size)
    def copies(k):
        s, n = secs[k]
        out = [pltpu.make_async_copy(raw_ref.at[k % 2, 0, :, pl.ds(0, n * 128)], out_ref.at[:, pl.ds(s * 128, n * 128)], sem.at[2 * k])]
        m = min(n, nb - low - s)
        if m > 0:
            out.append(pltpu.make_async_copy(raw_ref.at[k % 2, 1, :, pl.ds(0, m * 128)], out_ref.at[:, pl.ds((low + s) * 128, m * 128)], sem.at[2 * k + 1]))
        return out
    squares = jnp.zeros((128, 128), F32)
    for k, (s, n) in enumerate(secs):
        if k >= 2:
            for c in copies(k - 2):
                c.wait()
        def turn(b, carry, s=s, k=k):
            t = tile(b)
            at = pl.ds(pl.multiple_of((b - s) * 128, 128), 128)
            raw_ref[k % 2, 0, :, at] = t[:feat]
            raw_ref[k % 2, 1, :, at] = t[64:64 + feat]
            return carry + t * t
        squares = lax.fori_loop(s, s + n, turn, squares, unroll=3)
        for c in copies(k):
            c.start()
    sq_ref[...] = squares
    for k in range(max(0, len(secs) - 2), len(secs)):
        for c in copies(k):
            c.wait()

def scatter(ids, gs, vocab, per):
    nseq, feat, length = gs[0].shape
    nb, low = halves(vocab)
    rid, flag = split_ids(ids, vocab)
    ng = len(gs)
    size = -(-low // 6)
    vm = pl.BlockSpec(memory_space=pltpu.VMEM)
    return pl.pallas_call(functools.partial(scatter_kernel, ng=ng, per=per), name="emb_scatter", cost_estimate=cost(1),
        in_specs=[pl.BlockSpec(memory_space=pltpu.SMEM), vm] + [vm] * ng,
        out_specs=[pl.BlockSpec(memory_space=pl.ANY), vm],
        out_shape=[jax.ShapeDtypeStruct((feat, vocab), F32), jax.ShapeDtypeStruct((128, 128), F32)],
        scratch_shapes=[pltpu.VMEM((2, 2, feat, size * 128), F32), pltpu.VMEM((ng * per, length, 128), F32), pltpu.SemaphoreType.DMA((12,))]
            + [pltpu.VMEM((low * 128, 128), F32)] * (ng * per),
        compiler_params=params(62 * 1024 * 1024))(rid.reshape(-1), flag.reshape(-1, 1, length), *gs)
AHEAD = 2
MESH_ID = pl.DeviceIdType.MESH

def comm_params(ident):
    return pltpu.CompilerParams(collective_id=ident, has_side_effects=True, vmem_limit_bytes=VL)

def meet(peers):
    barrier = pltpu.get_barrier_semaphore()
    for p in peers:
        pl.semaphore_signal(barrier, inc=1, device_id=p, device_id_type=MESH_ID)
    pl.semaphore_wait(barrier, len(peers))

def remote(src, dst, send, recv, peer):
    return pltpu.make_async_remote_copy(src_ref=src, dst_ref=dst, send_sem=send, recv_sem=recv, device_id=peer, device_id_type=MESH_ID)

def small_kernel(x_ref, *refs, fs, dps, wide, finish):
    out_ref = refs[0]
    got_ref = refs[1] if finish else out_ref
    send, recv = refs[-2:]
    d, f = lax.axis_index("dp"), lax.axis_index("fsdp")
    n = fs * dps if wide else fs
    me = d * fs + f if wide else f
    def peer(k):
        j = lax.rem(me + k, n)
        return (lax.div(j, fs), lax.rem(j, fs)) if wide else (d, j)
    barrier = pltpu.get_barrier_semaphore()
    def greet(k, carry):
        pl.semaphore_signal(barrier, inc=1, device_id=peer(k), device_id_type=MESH_ID)
        return carry
    lax.fori_loop(1, n, greet, 0)
    pl.semaphore_wait(barrier, n - 1)
    def copy(k):
        return remote(x_ref, got_ref.at[me], send.at[k], recv.at[k], peer(k))
    def begin(k, carry):
        copy(k).start()
        return carry
    lax.fori_loop(1, n, begin, 0)
    got_ref[me] = x_ref[...]
    def end(k, carry):
        copy(k).wait()
        return carry
    lax.fori_loop(1, n, end, 0)
    if finish:
        finish(got_ref, out_ref, n)

def lse_finish(got_ref, out_ref, n):
    top = got_ref[0]
    for i in range(1, n):
        top = jnp.maximum(top, got_ref[i])
    total = jnp.exp(got_ref[0] - top)
    for i in range(1, n):
        total = total + jnp.exp(got_ref[i] - top)
    out_ref[...] = top + jnp.log(total)

def sum_finish(got_ref, out_ref, n):
    total = got_ref[0]
    for i in range(1, n):
        total = total + got_ref[i]
    out_ref[...] = total

def small_gather(x, ident, wide=False, finish=None, name="small_gather"):
    fs, dps = lax.axis_size("fsdp"), lax.axis_size("dp")
    n = fs * dps if wide else fs
    vm = pl.BlockSpec(memory_space=pltpu.VMEM)
    got = (n,) + x.shape
    return pl.pallas_call(
        functools.partial(small_kernel, fs=fs, dps=dps, wide=wide, finish=finish), name=name,
        in_specs=[vm], out_specs=vm,
        out_shape=jax.ShapeDtypeStruct(x.shape if finish else got, x.dtype),
        scratch_shapes=([pltpu.VMEM(got, x.dtype)] if finish else []) + [pltpu.SemaphoreType.DMA((n,)), pltpu.SemaphoreType.DMA((n,))],
        cost_estimate=cost(12), compiler_params=comm_params(ident))(x)

def exchange_kernel(*refs, fs, both, aux, reduce):
    refs = list(refs)
    x_ref = refs.pop(0)
    aux_ref = refs.pop(0) if aux else None
    w_ref = refs.pop(0) if reduce else None
    out_ref = refs.pop(0)
    other_ref = refs.pop(0) if both else None
    sum_ref = refs.pop(0) if aux else None
    red_ref = refs.pop(0) if reduce else None
    send, recv, send2, recv2, own = refs[:5]
    refs = refs[5:]
    if aux:
        near_ref, over_ref = refs.pop(0), refs.pop(0)
    if reduce:
        _, parts, red_begin, red_middle, red_end = reduce_phases(w_ref, red_ref, *refs, high=fs // 4, both=both)
    d, f = lax.axis_index("dp"), lax.axis_index("fsdp")
    across = (1 - d, f)
    barrier = pltpu.get_barrier_semaphore()
    def greet(k, carry):
        pl.semaphore_signal(barrier, inc=1, device_id=(d, lax.rem(f + k, fs)), device_id_type=MESH_ID)
        return carry
    lax.fori_loop(1, fs, greet, 0)
    if both:
        pl.semaphore_signal(barrier, inc=1, device_id=across, device_id_type=MESH_ID)
    pl.semaphore_wait(barrier, fs if both else fs - 1)
    def copies(k):
        j = lax.rem(f + k, fs)
        out = [remote(x_ref.at[j], out_ref.at[f], send.at[0, k], recv.at[0, k], (d, j))]
        if aux:
            out.append(remote(aux_ref, near_ref.at[f], send.at[1, k], recv.at[1, k], (d, j)))
        return out
    def passed(k):
        s = lax.rem(f + fs - k, fs)
        out = [remote(out_ref.at[s], other_ref.at[s], send2.at[0, k], recv2.at[0, k], across)]
        if aux:
            out.append(remote(near_ref.at[s], over_ref.at[s], send2.at[1, k], recv2.at[1, k], across))
        return out
    def first():
        out = [remote(x_ref.at[f], other_ref.at[f], send2.at[0, 0], recv2.at[0, 0], across)]
        if aux:
            out.append(remote(aux_ref, over_ref.at[f], send2.at[1, 0], recv2.at[1, 0], across))
        return out
    if reduce:
        red_begin()
    if both:
        for c in first():
            c.start()
    def begin(k, carry):
        for c in copies(k):
            c.start()
        return carry
    lax.fori_loop(1, fs, begin, 0)
    mine = pltpu.make_async_copy(x_ref.at[f], out_ref.at[f], own)
    mine.start()
    if aux:
        near_ref[f] = aux_ref[...]
    mine.wait()
    def arrive(k, carry):
        for c in copies(k):
            c.wait_recv()
        if both:
            for c in passed(k):
                c.start()
        return carry
    steps = parts + 1 if reduce else 1
    marks = [1 + (fs - 1) * i // steps for i in range(steps + 1)]
    for i in range(steps):
        if reduce:
            red_middle(i)
        lax.fori_loop(marks[i], marks[i + 1], arrive, 0)
    if reduce:
        red_end()
    def end(k, carry):
        for c in copies(k):
            c.wait_send()
        if both:
            for c in passed(k):
                c.wait()
        return carry
    lax.fori_loop(1, fs, end, 0)
    if both:
        for c in first():
            c.wait()
    if aux:
        total = near_ref[0]
        for i in range(1, fs):
            total = total + near_ref[i]
        if both:
            rest = over_ref[0]
            for i in range(1, fs):
                rest = rest + over_ref[i]
            total = total + rest
        sum_ref[...] = total

def exchange(x, ident, both, name, aux=None, reduce=None):
    fs = lax.axis_size("fsdp")
    vm = pl.BlockSpec(memory_space=pltpu.VMEM)
    shape = jax.ShapeDtypeStruct(x.shape, x.dtype)
    sem = pltpu.SemaphoreType.DMA((2, fs))
    more = [] if aux is None else [pltpu.VMEM((fs,) + aux.shape, F32)] * 2
    outs = [shape] * (2 if both else 1) + ([] if aux is None else [jax.ShapeDtypeStruct(aux.shape, F32)])
    args = [x] + [a for a in (aux, reduce) if a is not None]
    if reduce is not None:
        block = reduce.shape[1:]
        outs.append(jax.ShapeDtypeStruct(block, F32))
        more = more + reduce_scratch(block, reduce.dtype, fs // 4)
    return pl.pallas_call(
        functools.partial(exchange_kernel, fs=fs, both=both, aux=aux is not None, reduce=reduce is not None), name=name,
        in_specs=[vm] * len(args), out_specs=[vm] * len(outs), out_shape=outs,
        scratch_shapes=[sem, sem, sem, sem, pltpu.SemaphoreType.DMA] + more,
        cost_estimate=cost(55),
        compiler_params=comm_params(ident))(*args)

def cuts(rows):
    n = 4 if rows % 64 == 0 else 1
    return n, rows // n

def rows_gather_kernel(x_ref, out_ref, send, recv, *, high):
    d, f = lax.axis_index("dp"), lax.axis_index("fsdp")
    h, m, c = lax.div(f, 4), lax.rem(lax.div(f, 2), 2), lax.rem(f, 2)
    side, twin = (d, h * 4 + (1 - m) * 2 + c), (d, h * 4 + m * 2 + 1 - c)
    parts, size = cuts(x_ref.shape[0])
    def far(k):
        return (d, lax.rem(h + k, high) * 4 + m * 2 + c)
    meet([far(k) for k in range(1, high)] + [side, twin])
    sent = []
    def go(src, block, p, peer):
        at = pl.ds(p * size, size)
        r = remote(src.at[at], out_ref.at[block, at], send.at[len(sent)], recv.at[block, p], peer)
        r.start()
        sent.append(r)
    def arrived(block, p):
        at = pl.ds(p * size, size)
        remote(x_ref.at[at], out_ref.at[block, at], send.at[0], recv.at[block, p], twin).wait_recv()
    def back(k, row):
        return lax.rem(h + high - k, high) * 4 + row * 2 + c
    def launch(p):
        for k in range(1, high):
            go(x_ref, f, p, far(k))
        go(x_ref, f, p, side)
        go(x_ref, f, p, twin)
    ahead = min(AHEAD, parts)
    for p in range(ahead):
        launch(p)
    out_ref[f] = x_ref[...]
    for p in range(parts + 1):
        if p < parts:
            for k in range(1, high):
                b = back(k, m)
                arrived(b, p)
                go(out_ref.at[b], b, p, side)
                go(out_ref.at[b], b, p, twin)
            if p + ahead < parts:
                launch(p + ahead)
        if p > 0:
            for k in range(high):
                b = back(k, 1 - m)
                arrived(b, p - 1)
                go(out_ref.at[b], b, p - 1, twin)
    for row in range(2):
        for k in range(high):
            for p in range(parts):
                arrived(lax.rem(h + high - k, high) * 4 + lax.rem(m + row, 2) * 2 + 1 - c, p)
    for r in sent:
        r.wait_send()

def rows_gather(x, ident, name="rows_gather"):
    fs = lax.axis_size("fsdp")
    vm = pl.BlockSpec(memory_space=pltpu.VMEM)
    high = fs // 4
    parts = cuts(x.shape[0])[0]
    return pl.pallas_call(
        functools.partial(rows_gather_kernel, high=high), name=name,
        in_specs=[vm], out_specs=vm, out_shape=jax.ShapeDtypeStruct((fs,) + x.shape, x.dtype),
        scratch_shapes=[pltpu.SemaphoreType.DMA((4 * high * parts,)), pltpu.SemaphoreType.DMA((fs, parts))],
        cost_estimate=cost(40), compiler_params=comm_params(ident))(x)

def reduce_phases(x_ref, out_ref, twin_ref, side_ref, far_ref, a_ref, b_ref, s1, r1, s2, r2, s3, r3, *, high, both):
    d, f = lax.axis_index("dp"), lax.axis_index("fsdp")
    h, m, c = lax.div(f, 4), lax.rem(lax.div(f, 2), 2), lax.rem(f, 2)
    side, twin = (d, h * 4 + (1 - m) * 2 + c), (d, h * 4 + m * 2 + 1 - c)
    def far(k):
        return (d, lax.rem(h + k, high) * 4 + m * 2 + c)
    across = (1 - d, f)
    peers = [far(k) for k in range(1, high)] + [side, twin] + ([across] if both else [])
    order = list(range(1, high)) + [0]
    parts, size = cuts(x_ref.shape[1])
    def rows(p):
        return pl.ds(p * size, size)
    def at(k):
        return lax.rem(h + k, high)
    def one(k, row, p):
        slot = at(k) * 2 + row
        return remote(x_ref.at[at(k) * 4 + row * 2 + 1 - c, rows(p)], twin_ref.at[slot, rows(p)], s1.at[slot, p], r1.at[slot, p], twin)
    def two(k, p):
        return remote(a_ref.at[at(k), rows(p)], side_ref.at[at(k), rows(p)], s2.at[at(k), p], r2.at[at(k), p], side)
    def three(k, p):
        return remote(b_ref.at[k, rows(p)], far_ref.at[k, rows(p)], s3.at[k, p], r3.at[k, p], far(k))
    def last(p):
        return remote(b_ref.at[0, rows(p)], far_ref.at[0, rows(p)], s3.at[0, p], r3.at[0, p], across)
    def begin():
        for p in range(parts):
            for k in order:
                one(k, 1 - m, p).start()
            for k in order:
                one(k, m, p).start()
    def middle(p):
        if p < parts:
            if p >= 2:
                for k in order:
                    two(k, p - 2).wait_send()
            for k in order:
                one(k, 1 - m, p).wait_recv()
                a_ref[at(k), rows(p)] = (x_ref[at(k) * 4 + (1 - m) * 2 + c, rows(p)].astype(F32) + twin_ref[at(k) * 2 + 1 - m, rows(p)].astype(F32)).astype(a_ref.dtype)
                two(k, p).start()
        if p > 0:
            q = p - 1
            for k in order:
                one(k, m, q).wait_recv()
                two(k, q).wait_recv()
                total = x_ref[at(k) * 4 + m * 2 + c, rows(q)].astype(F32) + twin_ref[at(k) * 2 + m, rows(q)].astype(F32) + side_ref[at(k), rows(q)].astype(F32)
                if k == 0:
                    out_ref[rows(q)] = total
                else:
                    b_ref[k, rows(q)] = total.astype(b_ref.dtype)
                    three(k, q).start()
    def end():
        for p in range(parts):
            for k in range(1, high):
                three(k, p).wait_recv()
                out_ref[rows(p)] += far_ref[k, rows(p)].astype(F32)
            if both:
                b_ref[0, rows(p)] = out_ref[rows(p)].astype(b_ref.dtype)
                last(p).start()
        for p in range(parts):
            if both:
                last(p).wait()
                out_ref[rows(p)] = b_ref[0, rows(p)].astype(F32) + far_ref[0, rows(p)].astype(F32)
            for k in order:
                one(k, m, p).wait_send()
                one(k, 1 - m, p).wait_send()
                if p + 2 >= parts:
                    two(k, p).wait_send()
                if k:
                    three(k, p).wait_send()
    return peers, parts, begin, middle, end

def rows_reduce_kernel(*refs, high, both):
    peers, parts, begin, middle, end = reduce_phases(*refs, high=high, both=both)
    meet(peers)
    begin()
    for p in range(parts + 1):
        middle(p)
    end()

def reduce_scratch(block, dtype, high):
    parts = cuts(block[0])[0]
    def sem(n):
        return pltpu.SemaphoreType.DMA((n, parts))
    def buf(n):
        return pltpu.VMEM((n,) + block, dtype)
    return [buf(2 * high), buf(high), buf(high), buf(high), buf(high),
            sem(2 * high), sem(2 * high), sem(high), sem(high), sem(high), sem(high)]

def rows_reduce(x, ident, name="rows_reduce", both=False):
    vm = pl.BlockSpec(memory_space=pltpu.VMEM)
    high = lax.axis_size("fsdp") // 4
    block = x.shape[1:]
    return pl.pallas_call(
        functools.partial(rows_reduce_kernel, high=high, both=both), name=name,
        in_specs=[vm], out_specs=vm, out_shape=jax.ShapeDtypeStruct(block, F32),
        scratch_shapes=reduce_scratch(block, x.dtype, high),
        cost_estimate=cost(45), compiler_params=comm_params(ident))(x)
def adam_kernel(factor_ref, w_ref, one_ref, two_ref, avg_ref, *refs, rate, first):
    outs = refs[-4:]
    grads = [r[...].astype(F32) for r in refs[:-4]]
    if first is None:
        g = grads[0]
    else:
        g = jnp.where(pl.program_id(0) < first, grads[0] + grads[1], grads[2] + grads[3])
    new, one, two = adamw(w_ref[...], one_ref[...], two_ref[...], g * factor_ref[0], rate)
    outs[0][...] = new
    outs[1][...] = one
    outs[2][...] = two
    outs[3][...] = ema_decay * avg_ref[...] + (1 - ema_decay) * new

def adam_table(factor, w, one, two, avg, grads, rate, by_rows):
    rows, cols = w.shape
    if by_rows:
        block, first = (256, cols), grads[0].shape[0] // 256
        steps = -(-rows // 256)
        spec = pl.BlockSpec(block, lambda i: (i, 0))
        early = pl.BlockSpec(block, lambda i: (jnp.minimum(i, first - 1), 0))
        late = pl.BlockSpec(block, lambda i: (jnp.maximum(i - first, 0), 0))
        gspecs = [early, early, late, late]
    else:
        block, first = (rows, 3072), None
        steps = -(-cols // 3072)
        spec = pl.BlockSpec(block, lambda i: (0, i))
        gspecs = [spec]
    shape = jax.ShapeDtypeStruct(w.shape, F32)
    return pl.pallas_call(
        functools.partial(adam_kernel, rate=rate, first=first), name="adam_rows" if by_rows else "adam_columns",
        grid=(steps,), cost_estimate=cost(1),
        in_specs=[pl.BlockSpec(memory_space=pltpu.SMEM)] + [spec] * 4 + gspecs, out_specs=[spec] * 4, out_shape=[shape] * 4,
        compiler_params=params())(factor.reshape(1), w, one, two, avg, *grads)
MASK_ID = 50257
STRATA = 16
STEP = 10

clip_level = 1.0
beta_one = 0.9
beta_two = 0.95
adam_eps = 1e-08
adam_decay = 0.01
rate_embed = 2.0
rate_out = 0.25
rate_gain = 0.5
rate_shampoo = 0.3
shampoo_decay = 0.01
stat_decay = 0.5
ema_decay = 0.7


def rotary_tables(length, half_width):
    inverse = 10000.0 ** (-np.arange(half_width, dtype=np.float64) / half_width)
    angles = inverse[:, None] * np.arange(length, dtype=np.float64)[None, :]
    return (jnp.asarray(np.cos(angles), F32), jnp.asarray(np.sin(angles), F32))


def adamw(weight, moment_one, moment_two, gradient, step_rate):
    one_new = beta_one * moment_one + (1 - beta_one) * gradient
    two_new = beta_two * moment_two + (1 - beta_two) * gradient * gradient
    one_hat = one_new * (1 / (1 - beta_one**STEP))
    two_hat = two_new * (1 / (1 - beta_two**STEP))
    weight_new = weight - step_rate * (
        one_hat / (jnp.sqrt(two_hat) + adam_eps) + adam_decay * weight
    )
    return (weight_new, one_new, two_new)


def dp_other(x):
    return lax.ppermute(x, "dp", [(0, 1), (1, 0)])


def dp_sum(x):
    count = lax.axis_size("dp")
    if count == 1:
        return x.astype(F32)
    if count == 2:
        return x.astype(F32) + dp_other(x).astype(F32)
    return lax.psum(x, "dp").astype(F32)


def spread_out(x):
    return lax.all_gather(x.astype(BF16), "fsdp", axis=1, tiled=True)


def per_device(
    tokens, positions, strata, groups, embedding, out_table, norm_gains, attention, feedforward,
    embed_moment_one, embed_moment_two, out_moment_one, out_moment_two, gain_moment_one, gain_moment_two,
    attention_left, attention_right, attention_left_root, attention_right_root,
    ff_left, ff_right, ff_left_root, ff_right_root,
    ema_embed, ema_out, ema_gains, ema_attention, ema_feedforward,
):
    fs = lax.axis_size("fsdp")
    dps = lax.axis_size("dp")
    me = lax.axis_index("fsdp")
    replica = lax.axis_index("dp")
    seq_count, length = tokens.shape
    slots = positions.shape[1]
    features, vocab = embedding.shape
    width = features * fs
    shard = out_table.shape[0]

    counts = jnp.maximum(1, (strata + 1) * slots * (1 + groups) // (2 * STRATA))
    in_use = jnp.arange(slots, dtype=jnp.int32)[None, :] < counts[:, None]
    places = jnp.arange(length, dtype=jnp.int32)
    same = positions[0][:, None] == places[None, :]
    marked = jnp.any(same & in_use[0][:, None], axis=0)
    ids_in = jnp.where(marked, MASK_ID, tokens[0])
    targets = jnp.sum(jnp.where(same, tokens[0][None, :], 0), axis=1)
    packed = jnp.concatenate([ids_in, targets, counts])
    packed = jnp.pad(packed, (0, -packed.shape[0] % 1024))
    everyone = small_gather(packed.reshape(-1, 128), 1, wide=True, name="ids_gather").reshape(fs * dps, -1)
    group = lax.dynamic_slice_in_dim(everyone, replica * fs, fs, 0)
    all_ids = everyone[:, :length]
    group_ids = group[:, :length]
    group_targets = group[:, length:length + slots]
    group_counts = group[:, length + slots]

    attn_w = spread_out(attention)
    ff_w = spread_out(feedforward)
    attn_root = spread_out(attention_right_root)
    ff_root = spread_out(ff_right_root)

    picked = gather(group_ids, embedding)
    xT = exchange(picked, 2, False, "features")[0].reshape(width, length)

    cosT, sinT = rotary_tables(length, HEAD // 2)
    gain = [norm_gains.T] * 3
    place = positions[0][:, None]
    hT, qT, kT, vT, mixT, lse = attn_fwd(xT, gain[0], cosT, sinT, attn_w)
    hT, source = lax.optimization_barrier((hT, out_table))
    low, turned = table_both(source)
    mixT, low, turned = lax.optimization_barrier((mixT, low, turned))
    x2, h2, x3, head = ff_fwd(xT, mixT, gain[1], gain[2], place, attn_w, ff_w)

    rows = rows_gather(head, 3)
    first_id = me * shard
    limit = jnp.clip(MASK_ID - first_id, 0, shard).reshape(1)
    least = min(shard, MASK_ID - (fs - 1) * shard)
    meta, seq, slot, weight = plan(group_counts, slots, length)
    nblk = seq.shape[0] // RB
    target = (spread(group_targets, seq, slot) - first_id).reshape(nblk, 1, RB)
    inside = fs * slots <= 4096
    if not inside:
        rows = jnp.take(rows.reshape(fs * slots, width), jnp.clip(seq * slots + slot, 0, fs * slots - 1), axis=0)
    comp, lse_own, chosen = vocab_fwd(meta, limit, rows, low, target, least)
    lse_sum = small_gather(lse_own, 4, finish=lse_finish, name="lse_gather")
    own_loss = jnp.sum(weight * (jnp.where(seq == me, lse_sum.reshape(-1), 0.0) - chosen.reshape(-1)))
    scale = weight / (seq_count * fs * dps)
    out_one, out_two, row_grads = vocab_bwd(
        meta, limit, comp, low, turned, target, lse_sum, scale.reshape(nblk, 1, RB),
        least, fs, slots, inside,
    )
    if not inside:
        at = jnp.arange(slots, dtype=jnp.int32)[None, :]
        row_grads = jnp.take(row_grads, jnp.minimum(meta[1][:, None] * 16 + at, seq.shape[0] - 1), axis=0)
        row_grads = jnp.where((at < group_counts[:, None])[:, :, None], row_grads, 0)
    own_rows = rows_reduce(row_grads, 5)
    halves_low = (out_one, out_two)
    if dps == 2:
        others = [dp_other(x) for x in halves_low]

    own_rows, attn_root, ff_root = lax.optimization_barrier((own_rows, attn_root, ff_root))
    second, gg2, gg3, dff = ff_bwd(x3, x2, h2, own_rows, place, gain[1], gain[2], ff_w, fs)
    if dps == 2:
        second, others[0] = lax.optimization_barrier((second, others[0]))
    first, gg1, dattn = attn_bwd(xT, gain[0], cosT, sinT, second, hT, qT, kT, vT, mixT, lse, attn_w, fs)

    ff_part = lax.psum_scatter(dff.reshape(-1, width), "fsdp", scatter_dimension=0, tiled=True)

    aux = jnp.concatenate([jnp.concatenate([gg1, gg2, gg3], axis=1).T.reshape(-1), own_loss[None]])
    aux = jnp.pad(aux, (0, -aux.shape[0] % 1024)).reshape(-1, 128)
    if dps == 2:
        first, others[1] = lax.optimization_barrier((first, others[1]))
        out_sq = sum(jnp.sum(jnp.square(a.astype(F32) + b.astype(F32))) for a, b in zip(halves_low, others))
    else:
        out_grad = jnp.concatenate([dp_sum(a) for a in halves_low])[:shard]
        out_sq = jnp.sum(out_grad * out_grad)
    out = exchange(first.reshape(fs, features, length), 6, dps == 2, "gradients", aux, dattn.reshape(fs, -1, width))
    attn_grad = out[-1].reshape(4, -1, width)
    aux, ff_part = lax.optimization_barrier((out[-2], ff_part))
    ff_grad = dp_sum(ff_part.reshape(2, -1, width))
    if dps != 2:
        attn_grad = dp_sum(attn_grad.astype(BF16))
    if dps == 2:
        parts, other = out[:2]
        other_ids = lax.dynamic_slice_in_dim(everyone, (1 - replica) * fs, fs, 0)[:, :length]
        embed_grad, embed_sq = scatter(jnp.concatenate([group_ids, other_ids]), (parts, other), vocab, 2)
        embed_sq = jnp.sum(embed_sq)
    else:
        parts = out[0]
        embed_grad = dp_sum(scatter(group_ids, (parts,), vocab, 2)[0].astype(BF16))
        embed_sq = jnp.sum(embed_grad * embed_grad)
        if dps > 1:
            aux = lax.psum(aux, "dp")
    aux = aux.reshape(-1)
    gain_grad, loss_sum = aux[: 3 * width].reshape(3, width), aux[3 * width]
    squares = (
        jnp.sum(attn_grad * attn_grad)
        + jnp.sum(ff_grad * ff_grad)
        + embed_sq
        + out_sq
    )
    attn_full, ff_full = spread_out(attn_grad), spread_out(ff_grad)
    squares, attn_full = lax.optimization_barrier((squares, attn_full))
    squares = small_gather(jnp.full((8, 128), squares), 7, finish=sum_finish, name="squares")[0, 0]
    clip_norm = jnp.sqrt(squares + jnp.sum(gain_grad * gain_grad))
    factor = jnp.minimum(1.0, clip_level / clip_norm)
    embed_new, embed_one_new, embed_two_new, ema_embed_new = adam_table(
        factor, embedding, embed_moment_one, embed_moment_two, ema_embed, [embed_grad], rate_embed, False
    )
    if dps == 2:
        out_new, out_one_new, out_two_new, ema_out_new = adam_table(
            factor, out_table, out_moment_one, out_moment_two, ema_out,
            [halves_low[0], others[0], halves_low[1], others[1]], rate_out, True
        )
    else:
        out_new, out_one_new, out_two_new = adamw(
            out_table, out_moment_one, out_moment_two, out_grad * factor, rate_out
        )
        ema_out_new = ema_decay * ema_out + (1 - ema_decay) * out_new
    gains_new, gains_one_new, gains_two_new = adamw(
        norm_gains, gain_moment_one, gain_moment_two, gain_grad * factor, rate_gain
    )

    def shampoo(weights, grad, left, right, left_root, whole_root, full):
        own = grad.astype(BF16)
        columns = right.shape[1]
        own_columns = lax.dynamic_slice_in_dim(full, me * columns, columns, 2)

        def product(text, a, b):
            return jnp.einsum(text, a, b, preferred_element_type=F32)

        mix = (1 - stat_decay) * factor * factor
        left_new = stat_decay * left + mix * product("nik,njk->nij", own, full)
        right_new = stat_decay * right + mix * product("nki,nkj->nij", own_columns, full)
        part = product("nij,njk->nik", left_root.astype(BF16), full)
        update = product("nij,njk->nik", part.astype(BF16), whole_root) * factor
        new = weights - rate_shampoo * (update + shampoo_decay * weights)
        return new, grad * factor, left_new, right_new

    attention_new, attn_clip, attention_left_new, attention_right_new = shampoo(
        attention, attn_grad, attention_left, attention_right, attention_left_root, attn_root, attn_full
    )
    ff_new, ff_clip, ff_left_new, ff_right_new = shampoo(
        feedforward, ff_grad, ff_left, ff_right, ff_left_root, ff_root, ff_full
    )

    def averaged(average, new):
        return ema_decay * average + (1 - ema_decay) * new

    return (
        loss_sum, clip_norm, embed_new, embed_one_new, embed_two_new, out_new, out_one_new, out_two_new,
        gains_new, gains_one_new, gains_two_new, attention_new, attn_clip, attention_left_new, attention_right_new,
        ff_new, ff_clip, ff_left_new, ff_right_new,
        ema_embed_new, ema_out_new, averaged(ema_gains, gains_new),
        averaged(ema_attention, attention_new), averaged(ema_feedforward, ff_new),
    )


def solution(mesh):
    seqs, rows, stack, none = P(("dp", "fsdp")), P("fsdp", None), P(None, "fsdp", None), P()
    in_specs = (
        seqs, seqs, seqs, seqs, rows, rows, none, stack, stack, rows, rows, rows, rows, none, none,
        stack, stack, stack, stack, stack, stack, stack, stack, rows, rows, none, stack, stack,
    )
    out_specs = (
        none, none, rows, rows, rows, rows, rows, rows, none, none, none, stack, stack, stack, stack,
        stack, stack, stack, stack, rows, rows, none, stack, stack,
    )
    return jax.shard_map(
        per_device, mesh=mesh, in_specs=in_specs, out_specs=out_specs, check_vma=False
    )
```

```python
import functools

import jax
import jax.numpy as jnp
import numpy as np
from jax import lax
from jax.experimental import pallas as pl
from jax.experimental.pallas import tpu as pltpu
from jax.sharding import PartitionSpec as P

F32, BF16 = jnp.float32, jnp.bfloat16
HEAD = 64
EPS = 1e-5
BSTEP = 1024
VL = 60 * 1024 * 1024

def dot(a, b, ca, cb):
    return lax.dot_general(a, b, (((ca,), (cb,)), ((), ())), preferred_element_type=F32)

def params(limit=VL):
    return pltpu.CompilerParams(vmem_limit_bytes=limit)

def cost(us):
    return pl.CostEstimate(flops=int(us * 1.15e9), bytes_accessed=0, transcendentals=0)

def whole(shape):
    return pl.BlockSpec(shape, lambda *a: (0,) * len(shape))

def attn_fwd_kernel(x_ref, gain_ref, cos_ref, sin_ref, w_ref, h_ref, q_ref, k_ref, v_ref, m_ref, lse_ref, kn_ref):
    width, length = x_ref.shape
    block = q_ref.shape[0]
    heads = block // HEAD
    half = HEAD // 2

    @pl.when(pl.program_id(0) == 0)
    def _():
        def cols(c, carry):
            at = pl.ds(pl.multiple_of(c * 128, 128), 128)
            x = x_ref[:, at].astype(F32)
            centred = x - jnp.mean(x, axis=0, keepdims=True)
            spread = jnp.mean(centred * centred, axis=0, keepdims=True)
            h_ref[:, at] = (centred * lax.rsqrt(spread + EPS) * gain_ref[:, 0:1]).astype(BF16)
            return carry
        lax.fori_loop(0, length // 128, cols, 0)

    cosine, sine = cos_ref[...], sin_ref[...]
    hidden = h_ref[...]
    for j, out in ((0, q_ref), (1, k_ref)):
        p = dot(w_ref[j], hidden, 0, 0)
        for h in range(heads):
            a = p[h * HEAD : h * HEAD + half]
            b = p[h * HEAD + half : (h + 1) * HEAD]
            ra = (a * cosine - b * sine).astype(BF16)
            rb = (b * cosine + a * sine).astype(BF16)
            if j == 0:
                ra, rb = ra * 0.125, rb * 0.125
            out[h * HEAD : h * HEAD + half, :] = ra
            out[h * HEAD + half : (h + 1) * HEAD, :] = rb
    v_ref[...] = dot(w_ref[2], hidden, 0, 0).astype(BF16)
    for h in range(heads):
        rows = slice(h * HEAD, (h + 1) * HEAD)
        kn_ref[h] = k_ref[rows, :].T
    def one(h, carry):
        rows = pl.ds(pl.multiple_of(h * HEAD, HEAD), HEAD)
        s = dot(kn_ref[h], q_ref[rows, :], 1, 0)
        top = jnp.max(s, axis=0, keepdims=True)
        e = jnp.exp(s - top)
        total = jnp.sum(e, axis=0, keepdims=True)
        o = dot(v_ref[rows, :], e.astype(BF16), 1, 0)
        m_ref[rows, :] = (o / total).astype(BF16)
        lse_ref[0, pl.ds(h, 1), :] = top + jnp.log(total)
        return carry
    lax.fori_loop(0, heads, one, 0)

def attn_fwd(xT, gain, cosT, sinT, w):
    width, length = xT.shape
    block = 256
    n = width // block
    col = pl.BlockSpec((block, length), lambda i: (i, 0))
    t = jax.ShapeDtypeStruct((width, length), BF16)
    return pl.pallas_call(
        attn_fwd_kernel, grid=(n,), name="attn_fwd", cost_estimate=cost(34),
        in_specs=[whole((width, length)), whole(gain.shape), whole(cosT.shape), whole(sinT.shape),
                  pl.BlockSpec((3, width, block), lambda i: (0, 0, i))],
        out_specs=[whole((width, length)), col, col, col, col, pl.BlockSpec((1, 8, length), lambda i: (i, 0, 0))],
        out_shape=[t, t, t, t, t, jax.ShapeDtypeStruct((n, 8, length), F32)],
        scratch_shapes=[pltpu.VMEM((block // HEAD, length, HEAD), BF16)],
        compiler_params=params(),
    )(xT, gain, cosT, sinT, w)

def attn_bwd_kernel(x_ref, gain_ref, cos_ref, sin_ref, sg_ref, h_ref, q_ref, k_ref, v_ref, m_ref, lse_ref, w_ref, wo_ref,
                    first_ref, gg_ref, dw_ref, hg_ref, low_ref, do_ref, kn_ref, vn_ref, dk_ref, dv_ref, dq_ref, dwo_ref):
    width, length = x_ref.shape
    block = q_ref.shape[0]
    heads = block // HEAD
    half = HEAD // 2
    step = min(BSTEP, length)
    i = pl.program_id(0)

    @pl.when(i == 0)
    def _():
        low_ref[...] = sg_ref[...].astype(BF16)
        hg_ref[...] = jnp.zeros_like(hg_ref)

    do_ref[...] = dot(wo_ref[0], low_ref[...], 1, 0).astype(BF16)
    fs, _, each, _ = dw_ref.shape
    dwo_ref[pl.ds(pl.multiple_of(i * block, block), block), :] = dot(m_ref[...], low_ref[...], 1, 1).astype(BF16)
    cosine, sine = cos_ref[...], sin_ref[...]
    for h in range(heads):
        rows = slice(h * HEAD, (h + 1) * HEAD)
        kn_ref[h] = k_ref[rows, :].T
        vn_ref[h] = v_ref[rows, :].T
    def one(h, carry):
        rows = pl.ds(pl.multiple_of(h * HEAD, HEAD), HEAD)
        for c in range(length // step):
            at = slice(c * step, (c + 1) * step)
            s = dot(kn_ref[h], q_ref[rows, at], 1, 0)
            p = jnp.exp(s - lse_ref[0, pl.ds(h, 1), at])
            dp = dot(vn_ref[h], do_ref[rows, at], 1, 0)
            centre = jnp.sum(p * dp, axis=0, keepdims=True)
            ds = (p * (dp - centre)).astype(BF16)
            pb = p.astype(BF16)
            dv = dot(do_ref[rows, at], pb, 1, 1)
            dk = dot(q_ref[rows, at], ds, 1, 1)
            if c == 0:
                dv_ref[rows, :] = dv
                dk_ref[rows, :] = dk
            else:
                dv_ref[rows, :] += dv
                dk_ref[rows, :] += dk
            dq_ref[rows, at] = dot(k_ref[rows, :], ds, 1, 0) * 0.125
        return carry
    lax.fori_loop(0, heads, one, 0)
    hidden = h_ref[...]
    for j, ref in ((0, dq_ref), (1, dk_ref), (2, dv_ref)):
        if j == 2:
            g = ref[...].astype(BF16)
        else:
            parts = []
            for h in range(heads):
                a = ref[h * HEAD : h * HEAD + half, :]
                b = ref[h * HEAD + half : (h + 1) * HEAD, :]
                parts += [(a * cosine + b * sine).astype(BF16), (b * cosine - a * sine).astype(BF16)]
            g = jnp.concatenate(parts, axis=0)
        dw_ref[:, j, :, pl.ds(pl.multiple_of(i * block, block), block)] = dot(hidden, g, 1, 1).astype(BF16).reshape(fs, each, block)
        hg_ref[...] += dot(w_ref[j], g, 1, 0)

    @pl.when(i == pl.num_programs(0) - 1)
    def _():
        dw_ref[:, 3] = dwo_ref[...].reshape(fs, each, width)
        def cols(c, acc):
            at = pl.ds(pl.multiple_of(c * 128, 128), 128)
            dx, gg = ln_back(x_ref[:, at].astype(F32), hg_ref[:, at], gain_ref[:, 0:1])
            first_ref[:, at] = (sg_ref[:, at] + dx).astype(BF16)
            return acc + gg
        acc = lax.fori_loop(0, length // 128, cols, jnp.zeros((width, 128), F32))
        gg_ref[...] = jnp.sum(acc, axis=1, keepdims=True)

def ln_back(x, g, gain):
    centred = x - jnp.mean(x, axis=0, keepdims=True)
    spread = jnp.mean(centred * centred, axis=0, keepdims=True)
    rs = lax.rsqrt(spread + EPS)
    xh = centred * rs
    gx = g * gain
    dx = rs * (gx - jnp.mean(gx, axis=0, keepdims=True) - xh * jnp.mean(gx * xh, axis=0, keepdims=True))
    return dx, g * xh

def attn_bwd(xT, gain, cosT, sinT, sg, hT, q, k, v, m, lse, w, fs):
    width, length = xT.shape
    block = 256
    n = width // block
    col = pl.BlockSpec((block, length), lambda i: (i, 0))
    full = whole((width, length))
    return pl.pallas_call(
        attn_bwd_kernel, grid=(n,), name="attn_bwd", cost_estimate=cost(62),
        in_specs=[full, whole(gain.shape), whole(cosT.shape), whole(sinT.shape), full, full, col, col, col, col,
                  pl.BlockSpec((1, 8, length), lambda i: (i, 0, 0)),
                  pl.BlockSpec((3, width, block), lambda i: (0, 0, i)),
                  pl.BlockSpec((1, block, width), lambda i: (3, i, 0))],
        out_specs=[full, whole((width, 1)), whole((fs, 4, width // fs, width))],
        out_shape=[jax.ShapeDtypeStruct((width, length), BF16), jax.ShapeDtypeStruct((width, 1), F32),
                   jax.ShapeDtypeStruct((fs, 4, width // fs, width), BF16)],
        scratch_shapes=[pltpu.VMEM((width, length), F32), pltpu.VMEM((width, length), BF16), pltpu.VMEM((block, length), BF16),
                        pltpu.VMEM((block // HEAD, length, HEAD), BF16), pltpu.VMEM((block // HEAD, length, HEAD), BF16),
                        pltpu.VMEM((block, length), F32), pltpu.VMEM((block, length), F32), pltpu.VMEM((block, length), F32),
                        pltpu.VMEM((width, width), BF16)],
        compiler_params=params(),
    )(xT, gain, cosT, sinT, sg, hT, q, k, v, m, lse, w, w)
def ff_fwd_kernel(x_ref, m_ref, g2_ref, g3_ref, pos_ref, wo_ref, up_ref, down_ref,
                  x2_ref, h2_ref, x3_ref, head_ref, fin_ref):
    width, length = x_ref.shape
    i = pl.program_id(0)

    @pl.when(i == 0)
    def _():
        x2_ref[...] = x_ref[...].astype(F32) + dot(wo_ref[0], m_ref[...], 0, 0)
        x3_ref[...] = x2_ref[...]
        def cols(c, carry):
            at = pl.ds(pl.multiple_of(c * 128, 128), 128)
            h2_ref[:, at] = ln(x2_ref[:, at], g2_ref[:, 1:2]).astype(BF16)
            return carry
        lax.fori_loop(0, length // 128, cols, 0)

    pre = dot(up_ref[0], h2_ref[...], 1, 0)
    act = jax.nn.gelu(pre, approximate=True).astype(BF16)
    x3_ref[...] += dot(down_ref[0], act, 0, 0)

    @pl.when(i == pl.num_programs(0) - 1)
    def _():
        def cols(c, carry):
            at = pl.ds(pl.multiple_of(c * 128, 128), 128)
            fin_ref[:, at] = ln(x3_ref[:, at], g3_ref[:, 2:3]).astype(BF16)
            return carry
        lax.fori_loop(0, length // 128, cols, 0)
        slots = pos_ref.shape[0]
        onehot = (pos_ref[...] == lax.broadcasted_iota(jnp.int32, (slots, length), 1)).astype(BF16)
        head_ref[...] = dot(onehot, fin_ref[...], 1, 1).astype(BF16)

def ln(x, gain):
    centred = x - jnp.mean(x, axis=0, keepdims=True)
    spread = jnp.mean(centred * centred, axis=0, keepdims=True)
    return centred * lax.rsqrt(spread + EPS) * gain

def ff_fwd(xT, m, g2, g3, pos, attn_w, ff_w):
    width, length = xT.shape
    hidden = ff_w.shape[1]
    block = 512
    n = hidden // block
    slots = pos.shape[0]
    full = whole((width, length))
    f = jax.ShapeDtypeStruct((width, length), F32)
    return pl.pallas_call(
        ff_fwd_kernel, grid=(n,), name="ff_fwd", cost_estimate=cost(34),
        in_specs=[full, full, whole(g2.shape), whole(g3.shape), whole((slots, 1)),
                  pl.BlockSpec((1, width, width), lambda i: (3, 0, 0)),
                  pl.BlockSpec((1, block, width), lambda i: (0, i, 0)),
                  pl.BlockSpec((1, block, width), lambda i: (1, i, 0))],
        out_specs=[full, full, full, whole((slots, width))],
        out_shape=[f, jax.ShapeDtypeStruct((width, length), BF16), f, jax.ShapeDtypeStruct((slots, width), BF16)],
        scratch_shapes=[pltpu.VMEM((width, length), BF16)],
        compiler_params=params(),
    )(xT, m, g2, g3, pos, attn_w, ff_w, ff_w)

def ff_bwd_kernel(x3_ref, x2_ref, h2_ref, rg_ref, pos_ref, g2_ref, g3_ref, up_ref, down_ref,
                  sg_ref, gg2_ref, gg3_ref, dw_ref, low_ref, hg_ref):
    width, length = x3_ref.shape
    i = pl.program_id(0)
    slots = pos_ref.shape[0]

    @pl.when(i == 0)
    def _():
        rows = rg_ref[...]
        high = rows.astype(BF16)
        rest = (rows - high.astype(F32)).astype(BF16)
        hg_ref[...] = jnp.zeros_like(hg_ref)
        def cols(c, acc):
            at = pl.ds(pl.multiple_of(c * 128, 128), 128)
            onehot = (pos_ref[...] == c * 128 + lax.broadcasted_iota(jnp.int32, (slots, 128), 1)).astype(BF16)
            fg = dot(high, onehot, 0, 0) + dot(rest, onehot, 0, 0)
            dx, gg = ln_back(x3_ref[:, at], fg, g3_ref[:, 2:3])
            sg_ref[:, at] = dx
            low_ref[:, at] = dx.astype(BF16)
            return acc + gg
        acc = lax.fori_loop(0, length // 128, cols, jnp.zeros((width, 128), F32))
        gg3_ref[...] = jnp.sum(acc, axis=1, keepdims=True)

    ag = dot(down_ref[0], low_ref[...], 1, 0)
    pre = dot(up_ref[0], h2_ref[...], 1, 0)
    c0, c1 = 0.7978845608028654, 0.044715
    t = jnp.tanh(c0 * (pre + c1 * pre * pre * pre))
    half = 0.5 * (1.0 + t)
    act = (pre * half).astype(BF16)
    slope = half + 0.5 * pre * (1.0 - t * t) * (c0 * (1.0 + 3.0 * c1 * pre * pre))
    pg = (slope * ag).astype(BF16)
    shape = (dw_ref.shape[0],) + dw_ref.shape[2:]
    dw_ref[:, 1] = dot(act, low_ref[...], 1, 1).astype(BF16).reshape(shape)
    dw_ref[:, 0] = dot(pg, h2_ref[...], 1, 1).astype(BF16).reshape(shape)
    hg_ref[...] += dot(up_ref[0], pg, 0, 0)

    @pl.when(i == pl.num_programs(0) - 1)
    def _():
        def cols(c, acc):
            at = pl.ds(pl.multiple_of(c * 128, 128), 128)
            dx, gg = ln_back(x2_ref[:, at], hg_ref[:, at], g2_ref[:, 1:2])
            sg_ref[:, at] += dx
            return acc + gg
        acc = lax.fori_loop(0, length // 128, cols, jnp.zeros((width, 128), F32))
        gg2_ref[...] = jnp.sum(acc, axis=1, keepdims=True)

def ff_bwd(x3, x2, h2, rg, pos, g2, g3, ff_w, fs):
    width, length = x3.shape
    hidden = ff_w.shape[1]
    each = hidden // fs
    block = each * max(1, 768 // each)
    n = hidden // block
    slots = pos.shape[0]
    full = whole((width, length))
    wb = pl.BlockSpec((block // each, 2, each, width), lambda i: (i, 0, 0, 0))
    g = jax.ShapeDtypeStruct((width, 1), F32)
    return pl.pallas_call(
        ff_bwd_kernel, grid=(n,), name="ff_bwd", cost_estimate=cost(45),
        in_specs=[full, full, full, whole((slots, width)), whole((slots, 1)), whole(g2.shape), whole(g3.shape),
                  pl.BlockSpec((1, block, width), lambda i: (0, i, 0)),
                  pl.BlockSpec((1, block, width), lambda i: (1, i, 0))],
        out_specs=[full, whole((width, 1)), whole((width, 1)), wb],
        out_shape=[jax.ShapeDtypeStruct((width, length), F32), g, g, jax.ShapeDtypeStruct((fs, 2, each, width), BF16)],
        scratch_shapes=[pltpu.VMEM((width, length), BF16), pltpu.VMEM((width, length), F32)],
        compiler_params=params(),
    )(x3, x2, h2, rg, pos, g2, g3, ff_w, ff_w)
RB = 256
FCH, BCH = 8, 8

def pick(n, top=8):
    return max(k for k in range(1, top + 1) if n % k == 0)

def table_kernel(source_ref, low_ref, turned_ref, *, shard):
    block = source_ref.shape[0]
    ids = pl.program_id(0) * block + lax.broadcasted_iota(jnp.int32, source_ref.shape, 0)
    low = jnp.where(ids < shard, source_ref[...], 0.0).astype(BF16)
    low_ref[...] = low
    turned_ref[...] = low.T

def table_both(table):
    shard, width = table.shape
    vocab = -(-shard // 128) * 128
    block = 640 if vocab % 640 == 0 else 128
    return pl.pallas_call(
        functools.partial(table_kernel, shard=shard), name="table_both", grid=(vocab // block,), cost_estimate=cost(12),
        in_specs=[pl.BlockSpec((block, width), lambda i: (i, 0))],
        out_specs=[pl.BlockSpec((block, width), lambda i: (i, 0)), pl.BlockSpec((width, block), lambda i: (0, i))],
        out_shape=[jax.ShapeDtypeStruct((vocab, width), BF16), jax.ShapeDtypeStruct((width, vocab), BF16)],
        compiler_params=params())(table)

def compact(meta_ref, rows_ref, comp_ref):
    nseq, slots, width = rows_ref.shape
    def clear(b, carry):
        comp_ref[pl.ds(pl.multiple_of(b * RB, RB), RB), :] = jnp.zeros((RB, width), BF16)
        return carry
    lax.fori_loop(0, meta_ref[2, 0], clear, 0)
    def seq(s, carry):
        def part(c, c2):
            comp_ref[pl.ds(pl.multiple_of((meta_ref[1, s] + c) * 16, 16), 16), :] = rows_ref[s, pl.ds(pl.multiple_of(c * 16, 16), 16), :]
            return c2
        lax.fori_loop(0, meta_ref[0, s], part, 0)
        return carry
    lax.fori_loop(0, nseq, seq, 0)

def vocab_fwd_kernel(meta_ref, limit_ref, rows_ref, table_ref, target_ref, lse_ref, chosen_ref, *outs, chunk, least, inside):
    comp_ref = outs[0] if inside else rows_ref
    vocab = table_ref.shape[0]
    if inside:
        nseq, slots, width = rows_ref.shape
        compact(meta_ref, rows_ref, comp_ref)
    lse_ref[...] = jnp.zeros_like(lse_ref)
    chosen_ref[...] = jnp.zeros_like(chosen_ref)
    limit = limit_ref[0]
    def block(b, carry):
        rows = comp_ref[pl.ds(pl.multiple_of(b * RB, RB), RB), :]
        target = target_ref[b]
        top = total = chosen = None
        for v in range(vocab // chunk):
            l = dot(table_ref[v * chunk:(v + 1) * chunk, :], rows, 1, 1)
            ids = v * chunk + lax.broadcasted_iota(jnp.int32, (chunk, RB), 0)
            hit = jnp.sum(jnp.where(ids == target, l, 0.0), axis=0, keepdims=True)
            if (v + 1) * chunk > least:
                l = jnp.where(ids < limit, l, -jnp.inf)
            m = jnp.max(l, axis=0, keepdims=True)
            if v == 0:
                top = m
                total = jnp.sum(jnp.exp(l - top), axis=0, keepdims=True)
                chosen = hit
            else:
                new = jnp.maximum(top, m)
                total = total * jnp.exp(top - new) + jnp.sum(jnp.exp(l - new), axis=0, keepdims=True)
                chosen = chosen + hit
                top = new
        lse_ref[b] = top + jnp.log(total)
        chosen_ref[b] = chosen
        return carry
    lax.fori_loop(0, meta_ref[2, 0], block, 0)

def vocab_fwd(meta, limit, rows, table, target, least):
    inside = rows.ndim == 3
    width = rows.shape[-1]
    nblk = target.shape[0]
    vocab = table.shape[0]
    chunk = 128 * pick(vocab // 128, FCH)
    smem = pl.BlockSpec(memory_space=pltpu.SMEM)
    vm = pl.BlockSpec(memory_space=pltpu.VMEM)
    st = jax.ShapeDtypeStruct((nblk, 1, RB), F32)
    comp = [jax.ShapeDtypeStruct((nblk * RB, width), BF16)] if inside else []
    out = pl.pallas_call(
        functools.partial(vocab_fwd_kernel, chunk=chunk, least=least, inside=inside), name="vocab_fwd", cost_estimate=cost(20),
        in_specs=[smem, smem, vm, vm, vm], out_specs=[vm] * (2 + len(comp)),
        out_shape=[st, st] + comp,
        compiler_params=params())(meta, limit, rows, table, target)
    return out[2] if inside else rows, out[0], out[1]

def vocab_bwd_kernel(meta_ref, limit_ref, comp_ref, table_ref, turned_ref, target_ref, lse_ref, scale_ref,
                     og_ref, og2_ref, rg_ref, acc_ref, rc_ref, low_ref, back_ref, sem, *, chunk, least, inside):
    vocab, width = table_ref.shape
    limit = limit_ref[0]
    nch = vocab // chunk
    def clear(b, carry):
        acc_ref[pl.ds(pl.multiple_of(b * 128, 128), 128), :] = jnp.zeros((128, width), F32)
        return carry
    lax.fori_loop(0, vocab // 128, clear, 0)
    def block(b, carry):
        rows = comp_ref[pl.ds(pl.multiple_of(b * RB, RB), RB), :]
        target, lse, scale = target_ref[b], lse_ref[b], scale_ref[b]
        rg = None
        for v in range(nch):
            l = dot(table_ref[v * chunk:(v + 1) * chunk, :], rows, 1, 1)
            ids = v * chunk + lax.broadcasted_iota(jnp.int32, (chunk, RB), 0)
            p = jnp.exp(l - lse)
            p = jnp.where(ids == target, p - 1.0, p)
            if (v + 1) * chunk > least:
                p = jnp.where(ids < limit, p, 0.0)
            g = (scale * p).astype(BF16)
            acc_ref[v * chunk:(v + 1) * chunk, :] += dot(g, rows, 1, 0)
            part = dot(turned_ref[:, v * chunk:(v + 1) * chunk], g, 1, 0)
            rg = part if rg is None else rg + part
        rc_ref[pl.ds(pl.multiple_of(b * RB, RB), RB), :] = rg.T.astype(BF16)
        return carry
    lax.fori_loop(0, meta_ref[2, 0], block, 0)
    if inside:
        nseq, slots, _ = back_ref.shape
        def seq(s, carry):
            back_ref[s] = jnp.zeros((slots, width), BF16)
            def part(c, c2):
                back_ref[s, pl.ds(pl.multiple_of(c * 16, 16), 16), :] = rc_ref[pl.ds(pl.multiple_of((meta_ref[1, s] + c) * 16, 16), 16), :]
                return c2
            lax.fori_loop(0, meta_ref[0, s], part, 0)
            return carry
        lax.fori_loop(0, nseq, seq, 0)
        out = pltpu.make_async_copy(back_ref, rg_ref, sem.at[0])
    else:
        out = pltpu.make_async_copy(rc_ref, rg_ref, sem.at[0])
    out.start()
    outs = [out]
    part = og_ref.shape[0]
    for v, (ref, start) in enumerate(((og_ref, 0), (og2_ref, part))):
        at = pl.ds(start, ref.shape[0])
        low_ref[at, :] = acc_ref[at, :].astype(BF16)
        outs.append(pltpu.make_async_copy(low_ref.at[at], ref, sem.at[1 + v]))
        outs[-1].start()
    for o in outs:
        o.wait()

def vocab_bwd(meta, limit, comp, table, turned, target, lse, scale, least, nseq, slots, inside):
    rows, width = comp.shape
    vocab = table.shape[0]
    chunk = 128 * pick(vocab // 128, BCH)
    smem = pl.BlockSpec(memory_space=pltpu.SMEM)
    vm = pl.BlockSpec(memory_space=pltpu.VMEM)
    hbm = pl.BlockSpec(memory_space=pl.ANY)
    shape = (nseq, slots, width) if inside else (rows, width)
    part = vocab // 256 * 128
    return pl.pallas_call(
        functools.partial(vocab_bwd_kernel, chunk=chunk, least=least, inside=inside), name="vocab_bwd", cost_estimate=cost(40),
        in_specs=[smem, smem] + [vm] * 6, out_specs=[hbm, hbm, hbm],
        out_shape=[jax.ShapeDtypeStruct((part, width), BF16), jax.ShapeDtypeStruct((vocab - part, width), BF16), jax.ShapeDtypeStruct(shape, BF16)],
        scratch_shapes=[pltpu.VMEM((vocab, width), F32), pltpu.VMEM((rows, width), BF16),
                        pltpu.VMEM((vocab, width), BF16), pltpu.VMEM(shape if inside else (1, 16, width), BF16),
                        pltpu.SemaphoreType.DMA((3,))],
        compiler_params=params())(meta, limit, comp, table, turned, target, lse, scale)

def plan(counts, slots, length):
    nseq = counts.shape[0]
    units = (counts + 15) // 16
    ends = jnp.cumsum(units)
    offs = ends - units
    total = ends[-1] * 16
    nblk = (total + RB - 1) // RB
    cap = (nseq * slots + RB - 1) // RB * RB
    at = jnp.arange(cap, dtype=jnp.int32)
    seq = jnp.minimum(jnp.sum((at[:, None] >= ends[None, :] * 16).astype(jnp.int32), axis=1), nseq - 1)
    mine = (seq[:, None] == jnp.arange(nseq, dtype=jnp.int32)[None, :])
    slot = at - jnp.sum(jnp.where(mine, offs[None, :] * 16, 0), axis=1)
    cnt = jnp.sum(jnp.where(mine, counts[None, :], 0), axis=1)
    live = slot < cnt
    weight = jnp.where(live, length / cnt.astype(F32), 0.0)
    meta = jnp.stack([units, offs, jnp.full((nseq,), nblk)]).astype(jnp.int32)
    return meta, seq, slot, weight

def spread(values, seq, slot):
    nseq, slots = values.shape
    parts = jnp.concatenate([values // 256, values % 256], axis=1).astype(BF16)
    mine = (seq[:, None] == jnp.arange(nseq, dtype=jnp.int32)[None, :]).astype(BF16)
    rows = jnp.dot(mine, parts, preferred_element_type=F32)
    hit = slot[:, None] == jnp.arange(slots, dtype=jnp.int32)[None, :]
    both = rows[:, :slots] * 256.0 + rows[:, slots:]
    return jnp.sum(jnp.where(hit, both, 0.0), axis=1).astype(jnp.int32)

def halves(vocab):
    nb = vocab // 128
    low = (nb + 1) // 2
    return nb, low

def sections(count, size):
    return [(s, min(size, count - s)) for s in range(0, count, size)]

def gather_kernel(ids_ref, flag_ref, emb_ref, out_ref, tab_ref, raw_ref, row_ref, sem):
    feat, vocab = emb_ref.shape
    nseq, _, length = out_ref.shape
    nb, low = halves(vocab)
    size = -(-low // 6)
    secs = sections(low, size)
    def copies(k):
        s, n = secs[k]
        out = [pltpu.make_async_copy(emb_ref.at[:, pl.ds(s * 128, n * 128)], raw_ref.at[:, pl.ds(s * 128, n * 128)], sem.at[2 * k])]
        m = min(n, nb - low - s)
        if m > 0:
            out.append(pltpu.make_async_copy(emb_ref.at[:, pl.ds((low + s) * 128, m * 128)], raw_ref.at[:, pl.ds((low + s) * 128, m * 128)], sem.at[2 * k + 1]))
        return out
    for k in range(len(secs)):
        for c in copies(k):
            c.start()
    pad = jnp.zeros((64 - feat, 128), F32)
    for k in range(len(secs)):
        for c in copies(k):
            c.wait()
        s, n = secs[k]
        m = max(0, min(n, nb - low - s))
        def turn(b, carry):
            a = raw_ref[:, pl.ds(pl.multiple_of(b * 128, 128), 128)]
            h = raw_ref[:, pl.ds(pl.multiple_of((low + b) * 128, 128), 128)]
            tab_ref[pl.ds(pl.multiple_of(b * 128, 128), 128), :] = jnp.concatenate([a, pad, h, pad], axis=0).T
            return carry
        lax.fori_loop(s, s + m, turn, 0, unroll=3)
        for b in range(s + m, s + n):
            a = raw_ref[:, b * 128:(b + 1) * 128]
            tab_ref[b * 128:(b + 1) * 128, :] = jnp.concatenate([a, pad, pad, jnp.zeros((feat, 128), F32)], axis=0).T
    U = 32
    def seq(s, carry):
        def grp(g, c2):
            base = pl.multiple_of(g * U, U)
            for j in range(U):
                i = ids_ref[s * length + base + j]
                row_ref[pl.ds(base + j, 1), :] = tab_ref[pl.ds(i, 1), :]
            return c2
        lax.fori_loop(0, length // U, grp, 0)
        for c in range(length // 128):
            t = row_ref[c * 128:(c + 1) * 128, :].T
            f = flag_ref[s, :, c * 128:(c + 1) * 128] > 0
            out_ref[s, :, c * 128:(c + 1) * 128] = jnp.where(f, t[64:64 + feat], t[:feat]).astype(BF16)
        return carry
    lax.fori_loop(0, nseq, seq, 0)

def split_ids(ids, vocab):
    nb, low = halves(vocab)
    high = ids >= low * 128
    return jnp.where(high, ids - low * 128, ids), high.astype(jnp.int32)

def gather(ids, emb):
    nseq, length = ids.shape
    feat, vocab = emb.shape
    nb, low = halves(vocab)
    rid, flag = split_ids(ids, vocab)
    return pl.pallas_call(gather_kernel, name="emb_gather", cost_estimate=cost(32),
        in_specs=[pl.BlockSpec(memory_space=pltpu.SMEM), pl.BlockSpec(memory_space=pltpu.VMEM), pl.BlockSpec(memory_space=pl.ANY)],
        out_specs=pl.BlockSpec(memory_space=pltpu.VMEM),
        out_shape=jax.ShapeDtypeStruct((nseq, feat, length), BF16),
        scratch_shapes=[pltpu.VMEM((low * 128, 128), F32), pltpu.VMEM((feat, vocab), F32), pltpu.VMEM((length, 128), F32), pltpu.SemaphoreType.DMA((12,))],
        compiler_params=params())(rid.reshape(-1), flag.reshape(nseq, 1, length), emb)

def scatter_kernel(ids_ref, flag_ref, *refs, ng, per):
    g_refs = refs[:ng]
    out_ref, sq_ref, raw_ref, row_ref, sem = refs[ng:ng + 5]
    tabs = refs[ng + 5:]
    feat, vocab = out_ref.shape
    nseq, _, length = g_refs[0].shape
    nb, low = halves(vocab)
    zero128 = jnp.zeros((128, 128), F32)
    def zero(b, carry):
        for t in tabs:
            t[pl.ds(pl.multiple_of(b * 128, 128), 128), :] = zero128
        return carry
    lax.fori_loop(0, low, zero, 0)
    pad = jnp.zeros((64 - feat, 128), F32)
    U = 8
    streams = [(g, p) for g in range(ng) for p in range(per)]
    each = nseq // per
    def seq(s, carry):
        for k, (g, p) in enumerate(streams):
            q = p * each + s
            for c in range(length // 128):
                at = slice(c * 128, (c + 1) * 128)
                v = g_refs[g][q, :, at].astype(F32)
                f = flag_ref[g * nseq + q, :, at] > 0
                row_ref[k, at, :] = jnp.concatenate([jnp.where(f, 0.0, v), pad, jnp.where(f, v, 0.0), pad], axis=0).T
        def grp(n, c2):
            base = pl.multiple_of(n * U, U)
            for j in range(U):
                idx = [ids_ref[(g * nseq + p * each + s) * length + base + j] for g, p in streams]
                old = [tabs[k][pl.ds(idx[k], 1), :] for k in range(len(streams))]
                new = [old[k] + row_ref[k, pl.ds(base + j, 1), :] for k in range(len(streams))]
                for k in range(len(streams)):
                    tabs[k][pl.ds(idx[k], 1), :] = new[k]
            return c2
        lax.fori_loop(0, length // U, grp, 0)
        return carry
    lax.fori_loop(0, each, seq, 0)
    def tile(b):
        at = pl.ds(pl.multiple_of(b * 128, 128), 128)
        parts = [sum((tabs[g * per + p][at, :] for p in range(1, per)), tabs[g * per][at, :]) for g in range(ng)]
        return sum(parts[1:], parts[0]).T
    size = -(-low // 6)
    secs = sections(low, size)
    def copies(k):
        s, n = secs[k]
        out = [pltpu.make_async_copy(raw_ref.at[k % 2, 0, :, pl.ds(0, n * 128)], out_ref.at[:, pl.ds(s * 128, n * 128)], sem.at[2 * k])]
        m = min(n, nb - low - s)
        if m > 0:
            out.append(pltpu.make_async_copy(raw_ref.at[k % 2, 1, :, pl.ds(0, m * 128)], out_ref.at[:, pl.ds((low + s) * 128, m * 128)], sem.at[2 * k + 1]))
        return out
    squares = jnp.zeros((128, 128), F32)
    for k, (s, n) in enumerate(secs):
        if k >= 2:
            for c in copies(k - 2):
                c.wait()
        def turn(b, carry, s=s, k=k):
            t = tile(b)
            at = pl.ds(pl.multiple_of((b - s) * 128, 128), 128)
            raw_ref[k % 2, 0, :, at] = t[:feat]
            raw_ref[k % 2, 1, :, at] = t[64:64 + feat]
            return carry + t * t
        squares = lax.fori_loop(s, s + n, turn, squares, unroll=3)
        for c in copies(k):
            c.start()
    sq_ref[...] = squares
    for k in range(max(0, len(secs) - 2), len(secs)):
        for c in copies(k):
            c.wait()

def scatter(ids, gs, vocab, per):
    nseq, feat, length = gs[0].shape
    nb, low = halves(vocab)
    rid, flag = split_ids(ids, vocab)
    ng = len(gs)
    size = -(-low // 6)
    vm = pl.BlockSpec(memory_space=pltpu.VMEM)
    return pl.pallas_call(functools.partial(scatter_kernel, ng=ng, per=per), name="emb_scatter", cost_estimate=cost(1),
        in_specs=[pl.BlockSpec(memory_space=pltpu.SMEM), vm] + [vm] * ng,
        out_specs=[pl.BlockSpec(memory_space=pl.ANY), vm],
        out_shape=[jax.ShapeDtypeStruct((feat, vocab), F32), jax.ShapeDtypeStruct((128, 128), F32)],
        scratch_shapes=[pltpu.VMEM((2, 2, feat, size * 128), F32), pltpu.VMEM((ng * per, length, 128), F32), pltpu.SemaphoreType.DMA((12,))]
            + [pltpu.VMEM((low * 128, 128), F32)] * (ng * per),
        compiler_params=params(62 * 1024 * 1024))(rid.reshape(-1), flag.reshape(-1, 1, length), *gs)
AHEAD = 2
MESH_ID = pl.DeviceIdType.MESH

def comm_params(ident):
    return pltpu.CompilerParams(collective_id=ident, has_side_effects=True, vmem_limit_bytes=VL)

def meet(peers):
    barrier = pltpu.get_barrier_semaphore()
    for p in peers:
        pl.semaphore_signal(barrier, inc=1, device_id=p, device_id_type=MESH_ID)
    pl.semaphore_wait(barrier, len(peers))

def remote(src, dst, send, recv, peer):
    return pltpu.make_async_remote_copy(src_ref=src, dst_ref=dst, send_sem=send, recv_sem=recv, device_id=peer, device_id_type=MESH_ID)

def small_kernel(x_ref, *refs, fs, dps, wide, finish):
    out_ref = refs[0]
    got_ref = refs[1] if finish else out_ref
    send, recv = refs[-2:]
    d, f = lax.axis_index("dp"), lax.axis_index("fsdp")
    n = fs * dps if wide else fs
    me = d * fs + f if wide else f
    def peer(k):
        j = lax.rem(me + k, n)
        return (lax.div(j, fs), lax.rem(j, fs)) if wide else (d, j)
    barrier = pltpu.get_barrier_semaphore()
    def greet(k, carry):
        pl.semaphore_signal(barrier, inc=1, device_id=peer(k), device_id_type=MESH_ID)
        return carry
    lax.fori_loop(1, n, greet, 0)
    pl.semaphore_wait(barrier, n - 1)
    def copy(k):
        return remote(x_ref, got_ref.at[me], send.at[k], recv.at[k], peer(k))
    def begin(k, carry):
        copy(k).start()
        return carry
    lax.fori_loop(1, n, begin, 0)
    got_ref[me] = x_ref[...]
    def end(k, carry):
        copy(k).wait()
        return carry
    lax.fori_loop(1, n, end, 0)
    if finish:
        finish(got_ref, out_ref, n)

def lse_finish(got_ref, out_ref, n):
    top = got_ref[0]
    for i in range(1, n):
        top = jnp.maximum(top, got_ref[i])
    total = jnp.exp(got_ref[0] - top)
    for i in range(1, n):
        total = total + jnp.exp(got_ref[i] - top)
    out_ref[...] = top + jnp.log(total)

def sum_finish(got_ref, out_ref, n):
    total = got_ref[0]
    for i in range(1, n):
        total = total + got_ref[i]
    out_ref[...] = total

def small_gather(x, ident, wide=False, finish=None, name="small_gather"):
    fs, dps = lax.axis_size("fsdp"), lax.axis_size("dp")
    n = fs * dps if wide else fs
    vm = pl.BlockSpec(memory_space=pltpu.VMEM)
    got = (n,) + x.shape
    return pl.pallas_call(
        functools.partial(small_kernel, fs=fs, dps=dps, wide=wide, finish=finish), name=name,
        in_specs=[vm], out_specs=vm,
        out_shape=jax.ShapeDtypeStruct(x.shape if finish else got, x.dtype),
        scratch_shapes=([pltpu.VMEM(got, x.dtype)] if finish else []) + [pltpu.SemaphoreType.DMA((n,)), pltpu.SemaphoreType.DMA((n,))],
        cost_estimate=cost(12), compiler_params=comm_params(ident))(x)

def exchange_kernel(*refs, fs, both, aux, reduce, pairs):
    refs = list(refs)
    x_ref = refs.pop(0)
    aux_ref = refs.pop(0) if aux else None
    w_ref = refs.pop(0) if reduce else None
    pair_refs = [refs.pop(0) for _ in range(2 * pairs)]
    out_ref = refs.pop(0)
    other_ref = refs.pop(0) if both else None
    sum_ref = refs.pop(0) if aux else None
    red_ref = refs.pop(0) if reduce else None
    if pairs:
        sq_ref = refs.pop(0)
        held = [refs.pop() for _ in range(2 * pairs)]
        held_sem = refs.pop()
    send, recv, send2, recv2, own = refs[:5]
    refs = refs[5:]
    if aux:
        near_ref, over_ref = refs.pop(0), refs.pop(0)
    if reduce:
        _, parts, red_begin, red_middle, red_end = reduce_phases(w_ref, red_ref, *refs, high=fs // 4, both=both)
    d, f = lax.axis_index("dp"), lax.axis_index("fsdp")
    across = (1 - d, f)
    barrier = pltpu.get_barrier_semaphore()
    def greet(k, carry):
        pl.semaphore_signal(barrier, inc=1, device_id=(d, lax.rem(f + k, fs)), device_id_type=MESH_ID)
        return carry
    lax.fori_loop(1, fs, greet, 0)
    if both:
        pl.semaphore_signal(barrier, inc=1, device_id=across, device_id_type=MESH_ID)
    pl.semaphore_wait(barrier, fs if both else fs - 1)
    def copies(k):
        j = lax.rem(f + k, fs)
        out = [remote(x_ref.at[j], out_ref.at[f], send.at[0, k], recv.at[0, k], (d, j))]
        if aux:
            out.append(remote(aux_ref, near_ref.at[f], send.at[1, k], recv.at[1, k], (d, j)))
        return out
    def passed(k):
        s = lax.rem(f + fs - k, fs)
        out = [remote(out_ref.at[s], other_ref.at[s], send2.at[0, k], recv2.at[0, k], across)]
        if aux:
            out.append(remote(near_ref.at[s], over_ref.at[s], send2.at[1, k], recv2.at[1, k], across))
        return out
    def first():
        out = [remote(x_ref.at[f], other_ref.at[f], send2.at[0, 0], recv2.at[0, 0], across)]
        if aux:
            out.append(remote(aux_ref, over_ref.at[f], send2.at[1, 0], recv2.at[1, 0], across))
        return out
    if reduce:
        red_begin()
    if both:
        for c in first():
            c.start()
    def begin(k, carry):
        for c in copies(k):
            c.start()
        return carry
    lax.fori_loop(1, fs, begin, 0)
    mine = pltpu.make_async_copy(x_ref.at[f], out_ref.at[f], own)
    mine.start()
    if aux:
        near_ref[f] = aux_ref[...]
    mine.wait()
    def arrive(k, carry):
        for c in copies(k):
            c.wait_recv()
        if both:
            for c in passed(k):
                c.start()
        return carry
    if pairs:
        loads = [pltpu.make_async_copy(a, b, held_sem.at[i]) for i, (a, b) in enumerate(zip(pair_refs, held))]
        for l in loads:
            l.start()
        for l in loads:
            l.wait()
        total = jnp.zeros((8, held[0].shape[1]), F32)
        for i in range(pairs):
            a_ref, b_ref = held[2 * i], held[2 * i + 1]
            def add(n, t, a_ref=a_ref, b_ref=b_ref):
                at = pl.ds(pl.multiple_of(n * 64, 64), 64)
                s = a_ref[at, :].astype(F32) + b_ref[at, :].astype(F32)
                s = s * s
                for j in range(0, 64, 8):
                    t = t + s[j:j + 8]
                return t
            total = lax.fori_loop(0, a_ref.shape[0] // 64, add, total)
        sq_ref[...] = total
    steps = parts + 1 if reduce else 1
    marks = [1 + (fs - 1) * i // steps for i in range(steps + 1)]
    for i in range(steps):
        if reduce:
            red_middle(i)
        lax.fori_loop(marks[i], marks[i + 1], arrive, 0)
    if reduce:
        red_end()
    def end(k, carry):
        for c in copies(k):
            c.wait_send()
        if both:
            for c in passed(k):
                c.wait()
        return carry
    lax.fori_loop(1, fs, end, 0)
    if both:
        for c in first():
            c.wait()
    if aux:
        total = near_ref[0]
        for i in range(1, fs):
            total = total + near_ref[i]
        if both:
            rest = over_ref[0]
            for i in range(1, fs):
                rest = rest + over_ref[i]
            total = total + rest
        sum_ref[...] = total

def exchange(x, ident, both, name, aux=None, reduce=None, pairs=()):
    fs = lax.axis_size("fsdp")
    vm = pl.BlockSpec(memory_space=pltpu.VMEM)
    shape = jax.ShapeDtypeStruct(x.shape, x.dtype)
    sem = pltpu.SemaphoreType.DMA((2, fs))
    more = [] if aux is None else [pltpu.VMEM((fs,) + aux.shape, F32)] * 2
    outs = [shape] * (2 if both else 1) + ([] if aux is None else [jax.ShapeDtypeStruct(aux.shape, F32)])
    args = [x] + [a for a in (aux, reduce) if a is not None]
    if reduce is not None:
        block = reduce.shape[1:]
        outs.append(jax.ShapeDtypeStruct(block, F32))
        more = more + reduce_scratch(block, reduce.dtype, fs // 4)
    ins = [vm] * len(args) + [pl.BlockSpec(memory_space=pl.ANY)] * len(pairs)
    if pairs:
        outs.append(jax.ShapeDtypeStruct((8, pairs[0].shape[1]), F32))
        more = more + [pltpu.SemaphoreType.DMA((len(pairs),))] + [pltpu.VMEM(p.shape, p.dtype) for p in reversed(pairs)]
    return pl.pallas_call(
        functools.partial(exchange_kernel, fs=fs, both=both, aux=aux is not None, reduce=reduce is not None, pairs=len(pairs) // 2), name=name,
        in_specs=ins, out_specs=[vm] * len(outs), out_shape=outs,
        scratch_shapes=[sem, sem, sem, sem, pltpu.SemaphoreType.DMA] + more,
        cost_estimate=cost(55),
        compiler_params=comm_params(ident))(*args, *pairs)

def cuts(rows):
    n = 4 if rows % 64 == 0 else 1
    return n, rows // n

def rows_gather_kernel(x_ref, out_ref, send, recv, *, high):
    d, f = lax.axis_index("dp"), lax.axis_index("fsdp")
    h, m, c = lax.div(f, 4), lax.rem(lax.div(f, 2), 2), lax.rem(f, 2)
    side, twin = (d, h * 4 + (1 - m) * 2 + c), (d, h * 4 + m * 2 + 1 - c)
    parts, size = cuts(x_ref.shape[0])
    def far(k):
        return (d, lax.rem(h + k, high) * 4 + m * 2 + c)
    meet([far(k) for k in range(1, high)] + [side, twin])
    sent = []
    def go(src, block, p, peer):
        at = pl.ds(p * size, size)
        r = remote(src.at[at], out_ref.at[block, at], send.at[len(sent)], recv.at[block, p], peer)
        r.start()
        sent.append(r)
    def arrived(block, p):
        at = pl.ds(p * size, size)
        remote(x_ref.at[at], out_ref.at[block, at], send.at[0], recv.at[block, p], twin).wait_recv()
    def back(k, row):
        return lax.rem(h + high - k, high) * 4 + row * 2 + c
    def launch(p):
        for k in range(1, high):
            go(x_ref, f, p, far(k))
        go(x_ref, f, p, side)
        go(x_ref, f, p, twin)
    ahead = min(AHEAD, parts)
    for p in range(ahead):
        launch(p)
    out_ref[f] = x_ref[...]
    for p in range(parts + 1):
        if p < parts:
            for k in range(1, high):
                b = back(k, m)
                arrived(b, p)
                go(out_ref.at[b], b, p, side)
                go(out_ref.at[b], b, p, twin)
            if p + ahead < parts:
                launch(p + ahead)
        if p > 0:
            for k in range(high):
                b = back(k, 1 - m)
                arrived(b, p - 1)
                go(out_ref.at[b], b, p - 1, twin)
    for row in range(2):
        for k in range(high):
            for p in range(parts):
                arrived(lax.rem(h + high - k, high) * 4 + lax.rem(m + row, 2) * 2 + 1 - c, p)
    for r in sent:
        r.wait_send()

def rows_gather(x, ident, name="rows_gather"):
    fs = lax.axis_size("fsdp")
    vm = pl.BlockSpec(memory_space=pltpu.VMEM)
    high = fs // 4
    parts = cuts(x.shape[0])[0]
    return pl.pallas_call(
        functools.partial(rows_gather_kernel, high=high), name=name,
        in_specs=[vm], out_specs=vm, out_shape=jax.ShapeDtypeStruct((fs,) + x.shape, x.dtype),
        scratch_shapes=[pltpu.SemaphoreType.DMA((4 * high * parts,)), pltpu.SemaphoreType.DMA((fs, parts))],
        cost_estimate=cost(40), compiler_params=comm_params(ident))(x)

def reduce_phases(x_ref, out_ref, twin_ref, side_ref, far_ref, a_ref, b_ref, s1, r1, s2, r2, s3, r3, *, high, both):
    d, f = lax.axis_index("dp"), lax.axis_index("fsdp")
    h, m, c = lax.div(f, 4), lax.rem(lax.div(f, 2), 2), lax.rem(f, 2)
    side, twin = (d, h * 4 + (1 - m) * 2 + c), (d, h * 4 + m * 2 + 1 - c)
    def far(k):
        return (d, lax.rem(h + k, high) * 4 + m * 2 + c)
    across = (1 - d, f)
    peers = [far(k) for k in range(1, high)] + [side, twin] + ([across] if both else [])
    order = list(range(1, high)) + [0]
    parts, size = cuts(x_ref.shape[1])
    def rows(p):
        return pl.ds(p * size, size)
    def at(k):
        return lax.rem(h + k, high)
    def one(k, row, p):
        slot = at(k) * 2 + row
        return remote(x_ref.at[at(k) * 4 + row * 2 + 1 - c, rows(p)], twin_ref.at[slot, rows(p)], s1.at[slot, p], r1.at[slot, p], twin)
    def two(k, p):
        return remote(a_ref.at[at(k), rows(p)], side_ref.at[at(k), rows(p)], s2.at[at(k), p], r2.at[at(k), p], side)
    def three(k, p):
        return remote(b_ref.at[k, rows(p)], far_ref.at[k, rows(p)], s3.at[k, p], r3.at[k, p], far(k))
    def last(p):
        return remote(b_ref.at[0, rows(p)], far_ref.at[0, rows(p)], s3.at[0, p], r3.at[0, p], across)
    def begin():
        for p in range(parts):
            for k in order:
                one(k, 1 - m, p).start()
            for k in order:
                one(k, m, p).start()
    def middle(p):
        if p < parts:
            if p >= 2:
                for k in order:
                    two(k, p - 2).wait_send()
            for k in order:
                one(k, 1 - m, p).wait_recv()
                a_ref[at(k), rows(p)] = (x_ref[at(k) * 4 + (1 - m) * 2 + c, rows(p)].astype(F32) + twin_ref[at(k) * 2 + 1 - m, rows(p)].astype(F32)).astype(a_ref.dtype)
                two(k, p).start()
        if p > 0:
            q = p - 1
            for k in order:
                one(k, m, q).wait_recv()
                two(k, q).wait_recv()
                total = x_ref[at(k) * 4 + m * 2 + c, rows(q)].astype(F32) + twin_ref[at(k) * 2 + m, rows(q)].astype(F32) + side_ref[at(k), rows(q)].astype(F32)
                if k == 0:
                    out_ref[rows(q)] = total
                else:
                    b_ref[k, rows(q)] = total.astype(b_ref.dtype)
                    three(k, q).start()
    def end():
        for p in range(parts):
            for k in range(1, high):
                three(k, p).wait_recv()
                out_ref[rows(p)] += far_ref[k, rows(p)].astype(F32)
            if both:
                b_ref[0, rows(p)] = out_ref[rows(p)].astype(b_ref.dtype)
                last(p).start()
        for p in range(parts):
            if both:
                last(p).wait()
                out_ref[rows(p)] = b_ref[0, rows(p)].astype(F32) + far_ref[0, rows(p)].astype(F32)
            for k in order:
                one(k, m, p).wait_send()
                one(k, 1 - m, p).wait_send()
                if p + 2 >= parts:
                    two(k, p).wait_send()
                if k:
                    three(k, p).wait_send()
    return peers, parts, begin, middle, end

def rows_reduce_kernel(*refs, high, both):
    peers, parts, begin, middle, end = reduce_phases(*refs, high=high, both=both)
    meet(peers)
    begin()
    for p in range(parts + 1):
        middle(p)
    end()

def reduce_scratch(block, dtype, high):
    parts = cuts(block[0])[0]
    def sem(n):
        return pltpu.SemaphoreType.DMA((n, parts))
    def buf(n):
        return pltpu.VMEM((n,) + block, dtype)
    return [buf(2 * high), buf(high), buf(high), buf(high), buf(high),
            sem(2 * high), sem(2 * high), sem(high), sem(high), sem(high), sem(high)]

def rows_reduce(x, ident, name="rows_reduce", both=False):
    vm = pl.BlockSpec(memory_space=pltpu.VMEM)
    high = lax.axis_size("fsdp") // 4
    block = x.shape[1:]
    return pl.pallas_call(
        functools.partial(rows_reduce_kernel, high=high, both=both), name=name,
        in_specs=[vm], out_specs=vm, out_shape=jax.ShapeDtypeStruct(block, F32),
        scratch_shapes=reduce_scratch(block, x.dtype, high),
        cost_estimate=cost(45), compiler_params=comm_params(ident))(x)
def adam_kernel(factor_ref, w_ref, one_ref, two_ref, avg_ref, *refs, rate, first):
    outs = refs[-4:]
    grads = [r[...].astype(F32) for r in refs[:-4]]
    if first is None:
        g = grads[0]
    else:
        g = jnp.where(pl.program_id(0) < first, grads[0] + grads[1], grads[2] + grads[3])
    new, one, two = adamw(w_ref[...], one_ref[...], two_ref[...], g * factor_ref[0], rate)
    outs[0][...] = new
    outs[1][...] = one
    outs[2][...] = two
    outs[3][...] = ema_decay * avg_ref[...] + (1 - ema_decay) * new

def adam_table(factor, w, one, two, avg, grads, rate, by_rows):
    rows, cols = w.shape
    if by_rows:
        block, first = (768, cols), grads[0].shape[0] // 768
        steps = -(-rows // 768)
        spec = pl.BlockSpec(block, lambda i: (i, 0))
        early = pl.BlockSpec(block, lambda i: (jnp.minimum(i, first - 1), 0))
        late = pl.BlockSpec(block, lambda i: (jnp.maximum(i - first, 0), 0))
        gspecs = [early, early, late, late]
    else:
        block, first = (rows, 12672), None
        steps = -(-cols // 12672)
        spec = pl.BlockSpec(block, lambda i: (0, i))
        gspecs = [spec]
    shape = jax.ShapeDtypeStruct(w.shape, F32)
    return pl.pallas_call(
        functools.partial(adam_kernel, rate=rate, first=first), name="adam_rows" if by_rows else "adam_columns",
        grid=(steps,), cost_estimate=cost(1),
        in_specs=[pl.BlockSpec(memory_space=pltpu.SMEM)] + [spec] * 4 + gspecs, out_specs=[spec] * 4, out_shape=[shape] * 4,
        compiler_params=params())(factor.reshape(1), w, one, two, avg, *grads)
def shampoo_kernel(factor_ref, w_ref, grad_ref, left_ref, right_ref, root_ref, whole_ref, full_ref, avg_ref,
                   new_ref, clip_ref, left_out, right_out, avg_out):
    columns, width = right_ref.shape[1:]
    factor = factor_ref[0]
    mix = (1 - stat_decay) * factor * factor
    full = full_ref[0]
    grad = grad_ref[0]
    at = lax.axis_index("fsdp") * columns + lax.broadcasted_iota(jnp.int32, (columns, width), 0)
    pick = (at == lax.broadcasted_iota(jnp.int32, (columns, width), 1)).astype(BF16)
    turned = dot(pick, full, 1, 1).astype(BF16)
    left_out[0] = stat_decay * left_ref[0] + mix * dot(grad.astype(BF16), full, 1, 1)
    right_out[0] = stat_decay * right_ref[0] + mix * dot(turned, full, 1, 0)
    part = dot(root_ref[0].astype(BF16), full, 1, 0)
    update = dot(part.astype(BF16), whole_ref[0], 1, 0) * factor
    w = w_ref[0]
    new = w - rate_shampoo * (update + shampoo_decay * w)
    new_ref[0] = new
    clip_ref[0] = grad * factor
    avg_out[0] = ema_decay * avg_ref[0] + (1 - ema_decay) * new

def shampoo(factor, w, grad, left, right, root, whole_root, full, avg, name):
    def one(x):
        return pl.BlockSpec((1,) + x.shape[1:], lambda i: (i, 0, 0))
    ins = (w, grad, left, right, root, whole_root, full, avg)
    outs = (w, w, left, right, w)
    return pl.pallas_call(
        shampoo_kernel, grid=(w.shape[0],), name=name, cost_estimate=cost(10),
        in_specs=[pl.BlockSpec(memory_space=pltpu.SMEM)] + [one(x) for x in ins],
        out_specs=[one(x) for x in outs], out_shape=[jax.ShapeDtypeStruct(x.shape, F32) for x in outs],
        compiler_params=params())(factor.reshape(1), *ins)
MASK_ID = 50257
STRATA = 16
STEP = 10

clip_level = 1.0
beta_one = 0.9
beta_two = 0.95
adam_eps = 1e-08
adam_decay = 0.01
rate_embed = 2.0
rate_out = 0.25
rate_gain = 0.5
rate_shampoo = 0.3
shampoo_decay = 0.01
stat_decay = 0.5
ema_decay = 0.7


def rotary_tables(length, half_width):
    inverse = 10000.0 ** (-np.arange(half_width, dtype=np.float64) / half_width)
    angles = inverse[:, None] * np.arange(length, dtype=np.float64)[None, :]
    return (jnp.asarray(np.cos(angles), F32), jnp.asarray(np.sin(angles), F32))


def adamw(weight, moment_one, moment_two, gradient, step_rate):
    one_new = beta_one * moment_one + (1 - beta_one) * gradient
    two_new = beta_two * moment_two + (1 - beta_two) * gradient * gradient
    one_hat = one_new * (1 / (1 - beta_one**STEP))
    two_hat = two_new * (1 / (1 - beta_two**STEP))
    weight_new = weight - step_rate * (
        one_hat / (jnp.sqrt(two_hat) + adam_eps) + adam_decay * weight
    )
    return (weight_new, one_new, two_new)


def dp_other(x):
    return lax.ppermute(x, "dp", [(0, 1), (1, 0)])


def dp_sum(x):
    count = lax.axis_size("dp")
    if count == 1:
        return x.astype(F32)
    if count == 2:
        return x.astype(F32) + dp_other(x).astype(F32)
    return lax.psum(x, "dp").astype(F32)


def spread_out(x):
    return lax.all_gather(x.astype(BF16), "fsdp", axis=1, tiled=True)


def per_device(
    tokens, positions, strata, groups, embedding, out_table, norm_gains, attention, feedforward,
    embed_moment_one, embed_moment_two, out_moment_one, out_moment_two, gain_moment_one, gain_moment_two,
    attention_left, attention_right, attention_left_root, attention_right_root,
    ff_left, ff_right, ff_left_root, ff_right_root,
    ema_embed, ema_out, ema_gains, ema_attention, ema_feedforward,
):
    fs = lax.axis_size("fsdp")
    dps = lax.axis_size("dp")
    me = lax.axis_index("fsdp")
    replica = lax.axis_index("dp")
    seq_count, length = tokens.shape
    slots = positions.shape[1]
    features, vocab = embedding.shape
    width = features * fs
    shard = out_table.shape[0]

    counts = jnp.maximum(1, (strata + 1) * slots * (1 + groups) // (2 * STRATA))
    in_use = jnp.arange(slots, dtype=jnp.int32)[None, :] < counts[:, None]
    places = jnp.arange(length, dtype=jnp.int32)
    same = positions[0][:, None] == places[None, :]
    marked = jnp.any(same & in_use[0][:, None], axis=0)
    ids_in = jnp.where(marked, MASK_ID, tokens[0])
    targets = jnp.sum(jnp.where(same, tokens[0][None, :], 0), axis=1)
    packed = jnp.concatenate([ids_in, targets, counts])
    packed = jnp.pad(packed, (0, -packed.shape[0] % 1024))
    everyone = small_gather(packed.reshape(-1, 128), 1, wide=True, name="ids_gather").reshape(fs * dps, -1)
    group = lax.dynamic_slice_in_dim(everyone, replica * fs, fs, 0)
    all_ids = everyone[:, :length]
    group_ids = group[:, :length]
    group_targets = group[:, length:length + slots]
    group_counts = group[:, length + slots]

    attn_w = spread_out(attention)
    ff_w = spread_out(feedforward)
    attn_root = spread_out(attention_right_root)
    ff_root = spread_out(ff_right_root)

    picked = gather(group_ids, embedding)
    xT = exchange(picked, 2, False, "features")[0].reshape(width, length)

    cosT, sinT = rotary_tables(length, HEAD // 2)
    gain = [norm_gains.T] * 3
    place = positions[0][:, None]
    hT, qT, kT, vT, mixT, lse = attn_fwd(xT, gain[0], cosT, sinT, attn_w)
    hT, source = lax.optimization_barrier((hT, out_table))
    low, turned = table_both(source)
    mixT, low, turned = lax.optimization_barrier((mixT, low, turned))
    x2, h2, x3, head = ff_fwd(xT, mixT, gain[1], gain[2], place, attn_w, ff_w)

    rows = rows_gather(head, 3)
    first_id = me * shard
    limit = jnp.clip(MASK_ID - first_id, 0, shard).reshape(1)
    least = min(shard, MASK_ID - (fs - 1) * shard)
    meta, seq, slot, weight = plan(group_counts, slots, length)
    nblk = seq.shape[0] // RB
    target = (spread(group_targets, seq, slot) - first_id).reshape(nblk, 1, RB)
    inside = fs * slots <= 4096
    if not inside:
        rows = jnp.take(rows.reshape(fs * slots, width), jnp.clip(seq * slots + slot, 0, fs * slots - 1), axis=0)
    comp, lse_own, chosen = vocab_fwd(meta, limit, rows, low, target, least)
    lse_sum = small_gather(lse_own, 4, finish=lse_finish, name="lse_gather")
    own_loss = jnp.sum(weight * (jnp.where(seq == me, lse_sum.reshape(-1), 0.0) - chosen.reshape(-1)))
    scale = weight / (seq_count * fs * dps)
    out_one, out_two, row_grads = vocab_bwd(
        meta, limit, comp, low, turned, target, lse_sum, scale.reshape(nblk, 1, RB),
        least, fs, slots, inside,
    )
    if not inside:
        at = jnp.arange(slots, dtype=jnp.int32)[None, :]
        row_grads = jnp.take(row_grads, jnp.minimum(meta[1][:, None] * 16 + at, seq.shape[0] - 1), axis=0)
        row_grads = jnp.where((at < group_counts[:, None])[:, :, None], row_grads, 0)
    own_rows = rows_reduce(row_grads, 5)
    halves_low = (out_one, out_two)
    if dps == 2:
        others = [dp_other(x) for x in halves_low]

    own_rows, attn_root, ff_root = lax.optimization_barrier((own_rows, attn_root, ff_root))
    second, gg2, gg3, dff = ff_bwd(x3, x2, h2, own_rows, place, gain[1], gain[2], ff_w, fs)
    if dps == 2:
        second, others[0] = lax.optimization_barrier((second, others[0]))
    first, gg1, dattn = attn_bwd(xT, gain[0], cosT, sinT, second, hT, qT, kT, vT, mixT, lse, attn_w, fs)

    ff_part = lax.psum_scatter(dff.reshape(-1, width), "fsdp", scatter_dimension=0, tiled=True)

    aux = jnp.concatenate([jnp.concatenate([gg1, gg2, gg3], axis=1).T.reshape(-1), own_loss[None]])
    aux = jnp.pad(aux, (0, -aux.shape[0] % 1024)).reshape(-1, 128)
    if dps == 2:
        first, others[1] = lax.optimization_barrier((first, others[1]))
        pairs = (halves_low[0], others[0], halves_low[1], others[1])
    else:
        pairs = ()
        out_grad = jnp.concatenate([dp_sum(a) for a in halves_low])[:shard]
        out_sq = jnp.sum(out_grad * out_grad)
    out = list(exchange(first.reshape(fs, features, length), 6, dps == 2, "gradients", aux, dattn.reshape(fs, -1, width), pairs))
    if dps == 2:
        out_sq = jnp.sum(out.pop())
    attn_grad = out[-1].reshape(4, -1, width)
    aux, ff_part = lax.optimization_barrier((out[-2], ff_part))
    ff_grad = dp_sum(ff_part.reshape(2, -1, width))
    if dps != 2:
        attn_grad = dp_sum(attn_grad.astype(BF16))
    if dps == 2:
        parts, other = out[:2]
        other_ids = lax.dynamic_slice_in_dim(everyone, (1 - replica) * fs, fs, 0)[:, :length]
        embed_grad, embed_sq = scatter(jnp.concatenate([group_ids, other_ids]), (parts, other), vocab, 2)
        embed_sq = jnp.sum(embed_sq)
    else:
        parts = out[0]
        embed_grad = dp_sum(scatter(group_ids, (parts,), vocab, 2)[0].astype(BF16))
        embed_sq = jnp.sum(embed_grad * embed_grad)
        if dps > 1:
            aux = lax.psum(aux, "dp")
    aux = aux.reshape(-1)
    gain_grad, loss_sum = aux[: 3 * width].reshape(3, width), aux[3 * width]
    squares = (
        jnp.sum(attn_grad * attn_grad)
        + jnp.sum(ff_grad * ff_grad)
        + embed_sq
        + out_sq
    )
    ff_grad, embed_sq = lax.optimization_barrier((ff_grad, embed_sq))
    attn_full, ff_full = spread_out(attn_grad), spread_out(ff_grad)
    squares, attn_full = lax.optimization_barrier((squares, attn_full))
    squares = small_gather(jnp.full((8, 128), squares), 7, finish=sum_finish, name="squares")[0, 0]
    clip_norm = jnp.sqrt(squares + jnp.sum(gain_grad * gain_grad))
    factor = jnp.minimum(1.0, clip_level / clip_norm)
    embed_new, embed_one_new, embed_two_new, ema_embed_new = adam_table(
        factor, embedding, embed_moment_one, embed_moment_two, ema_embed, [embed_grad], rate_embed, False
    )
    if dps == 2:
        out_new, out_one_new, out_two_new, ema_out_new = adam_table(
            factor, out_table, out_moment_one, out_moment_two, ema_out,
            [halves_low[0], others[0], halves_low[1], others[1]], rate_out, True
        )
    else:
        out_new, out_one_new, out_two_new = adamw(
            out_table, out_moment_one, out_moment_two, out_grad * factor, rate_out
        )
        ema_out_new = ema_decay * ema_out + (1 - ema_decay) * out_new
    gains_new, gains_one_new, gains_two_new = adamw(
        norm_gains, gain_moment_one, gain_moment_two, gain_grad * factor, rate_gain
    )

    attention_new, attn_clip, attention_left_new, attention_right_new, ema_attn_new = shampoo(
        factor, attention, attn_grad, attention_left, attention_right, attention_left_root,
        attn_root, attn_full, ema_attention, "shampoo_attention"
    )
    ff_new, ff_clip, ff_left_new, ff_right_new, ema_ff_new = shampoo(
        factor, feedforward, ff_grad, ff_left, ff_right, ff_left_root,
        ff_root, ff_full, ema_feedforward, "shampoo_ff"
    )

    def averaged(average, new):
        return ema_decay * average + (1 - ema_decay) * new

    return (
        loss_sum, clip_norm, embed_new, embed_one_new, embed_two_new, out_new, out_one_new, out_two_new,
        gains_new, gains_one_new, gains_two_new, attention_new, attn_clip, attention_left_new, attention_right_new,
        ff_new, ff_clip, ff_left_new, ff_right_new,
        ema_embed_new, ema_out_new, averaged(ema_gains, gains_new),
        ema_attn_new, ema_ff_new,
    )


def solution(mesh):
    seqs, rows, stack, none = P(("dp", "fsdp")), P("fsdp", None), P(None, "fsdp", None), P()
    in_specs = (
        seqs, seqs, seqs, seqs, rows, rows, none, stack, stack, rows, rows, rows, rows, none, none,
        stack, stack, stack, stack, stack, stack, stack, stack, rows, rows, none, stack, stack,
    )
    out_specs = (
        none, none, rows, rows, rows, rows, rows, rows, none, none, none, stack, stack, stack, stack,
        stack, stack, stack, stack, rows, rows, none, stack, stack,
    )
    return jax.shard_map(
        per_device, mesh=mesh, in_specs=in_specs, out_specs=out_specs, check_vma=False
    )
```

```python
import functools

import jax
import jax.numpy as jnp
import numpy as np
from jax import lax
from jax.experimental import pallas as pl
from jax.experimental.pallas import tpu as pltpu
from jax.sharding import PartitionSpec as P

F32, BF16 = jnp.float32, jnp.bfloat16
HEAD = 64
EPS = 1e-5
BSTEP = 1024
VL = 60 * 1024 * 1024

def dot(a, b, ca, cb):
    return lax.dot_general(a, b, (((ca,), (cb,)), ((), ())), preferred_element_type=F32)

def params(limit=VL):
    return pltpu.CompilerParams(vmem_limit_bytes=limit)

def cost(us):
    return pl.CostEstimate(flops=int(us * 1.15e9), bytes_accessed=0, transcendentals=0)

def whole(shape):
    return pl.BlockSpec(shape, lambda *a: (0,) * len(shape))

def attn_fwd_kernel(x_ref, gain_ref, cos_ref, sin_ref, w_ref, h_ref, q_ref, k_ref, v_ref, m_ref, lse_ref, kn_ref):
    width, length = x_ref.shape
    block = q_ref.shape[0]
    heads = block // HEAD
    half = HEAD // 2

    @pl.when(pl.program_id(0) == 0)
    def _():
        def cols(c, carry):
            at = pl.ds(pl.multiple_of(c * 128, 128), 128)
            x = x_ref[:, at].astype(F32)
            centred = x - jnp.mean(x, axis=0, keepdims=True)
            spread = jnp.mean(centred * centred, axis=0, keepdims=True)
            h_ref[:, at] = (centred * lax.rsqrt(spread + EPS) * gain_ref[:, 0:1]).astype(BF16)
            return carry
        lax.fori_loop(0, length // 128, cols, 0)

    cosine, sine = cos_ref[...], sin_ref[...]
    hidden = h_ref[...]
    for j, out in ((0, q_ref), (1, k_ref)):
        p = dot(w_ref[:, j].reshape(width, block), hidden, 0, 0)
        for h in range(heads):
            a = p[h * HEAD : h * HEAD + half]
            b = p[h * HEAD + half : (h + 1) * HEAD]
            ra = (a * cosine - b * sine).astype(BF16)
            rb = (b * cosine + a * sine).astype(BF16)
            if j == 0:
                ra, rb = ra * 0.125, rb * 0.125
            out[h * HEAD : h * HEAD + half, :] = ra
            out[h * HEAD + half : (h + 1) * HEAD, :] = rb
    v_ref[...] = dot(w_ref[:, 2].reshape(width, block), hidden, 0, 0).astype(BF16)
    for h in range(heads):
        rows = slice(h * HEAD, (h + 1) * HEAD)
        kn_ref[h] = k_ref[rows, :].T
    def one(h, carry):
        rows = pl.ds(pl.multiple_of(h * HEAD, HEAD), HEAD)
        s = dot(kn_ref[h], q_ref[rows, :], 1, 0)
        top = jnp.max(s, axis=0, keepdims=True)
        e = jnp.exp(s - top)
        total = jnp.sum(e, axis=0, keepdims=True)
        o = dot(v_ref[rows, :], e.astype(BF16), 1, 0)
        m_ref[rows, :] = (o / total).astype(BF16)
        lse_ref[0, pl.ds(h, 1), :] = top + jnp.log(total)
        return carry
    lax.fori_loop(0, heads, one, 0)

def attn_fwd(xT, gain, cosT, sinT, w):
    width, length = xT.shape
    block = 256
    n = width // block
    col = pl.BlockSpec((block, length), lambda i: (i, 0))
    t = jax.ShapeDtypeStruct((width, length), BF16)
    return pl.pallas_call(
        attn_fwd_kernel, grid=(n,), name="attn_fwd", cost_estimate=cost(34),
        in_specs=[whole((width, length)), whole(gain.shape), whole(cosT.shape), whole(sinT.shape),
                  pl.BlockSpec((w.shape[0], 3, w.shape[2], block), lambda i: (0, 0, 0, i))],
        out_specs=[whole((width, length)), col, col, col, col, pl.BlockSpec((1, 8, length), lambda i: (i, 0, 0))],
        out_shape=[t, t, t, t, t, jax.ShapeDtypeStruct((n, 8, length), F32)],
        scratch_shapes=[pltpu.VMEM((block // HEAD, length, HEAD), BF16)],
        compiler_params=params(),
    )(xT, gain, cosT, sinT, w)

def attn_bwd_kernel(x_ref, gain_ref, cos_ref, sin_ref, sg_ref, h_ref, q_ref, k_ref, v_ref, m_ref, lse_ref, w_ref, wo_ref,
                    first_ref, gg_ref, dw_ref, hg_ref, low_ref, do_ref, kn_ref, vn_ref, dk_ref, dv_ref, dq_ref, dwo_ref):
    width, length = x_ref.shape
    block = q_ref.shape[0]
    heads = block // HEAD
    half = HEAD // 2
    step = min(BSTEP, length)
    i = pl.program_id(0)

    @pl.when(i == 0)
    def _():
        low_ref[...] = sg_ref[...].astype(BF16)
        dwo_ref[...] = wo_ref[:, 0].reshape(width, width)
        hg_ref[...] = jnp.zeros_like(hg_ref)

    mine = pl.ds(pl.multiple_of(i * block, block), block)
    do_ref[...] = dot(dwo_ref[mine, :], low_ref[...], 1, 0).astype(BF16)
    fs, _, each, _ = dw_ref.shape
    dwo_ref[mine, :] = dot(m_ref[...], low_ref[...], 1, 1).astype(BF16)
    cosine, sine = cos_ref[...], sin_ref[...]
    for h in range(heads):
        rows = slice(h * HEAD, (h + 1) * HEAD)
        kn_ref[h] = k_ref[rows, :].T
        vn_ref[h] = v_ref[rows, :].T
    def one(h, carry):
        rows = pl.ds(pl.multiple_of(h * HEAD, HEAD), HEAD)
        for c in range(length // step):
            at = slice(c * step, (c + 1) * step)
            s = dot(kn_ref[h], q_ref[rows, at], 1, 0)
            p = jnp.exp(s - lse_ref[0, pl.ds(h, 1), at])
            dp = dot(vn_ref[h], do_ref[rows, at], 1, 0)
            centre = jnp.sum(p * dp, axis=0, keepdims=True)
            ds = (p * (dp - centre)).astype(BF16)
            pb = p.astype(BF16)
            dv = dot(pb, do_ref[rows, at], 1, 1).T
            dk = dot(ds, q_ref[rows, at], 1, 1).T
            if c == 0:
                dv_ref[rows, :] = dv
                dk_ref[rows, :] = dk
            else:
                dv_ref[rows, :] += dv
                dk_ref[rows, :] += dk
            dq_ref[rows, at] = dot(k_ref[rows, :], ds, 1, 0) * 0.125
        return carry
    lax.fori_loop(0, heads, one, 0)
    hidden = h_ref[...]
    for j, ref in ((0, dq_ref), (1, dk_ref), (2, dv_ref)):
        if j == 2:
            g = ref[...].astype(BF16)
        else:
            parts = []
            for h in range(heads):
                a = ref[h * HEAD : h * HEAD + half, :]
                b = ref[h * HEAD + half : (h + 1) * HEAD, :]
                parts += [(a * cosine + b * sine).astype(BF16), (b * cosine - a * sine).astype(BF16)]
            g = jnp.concatenate(parts, axis=0)
        dw_ref[:, j, :, pl.ds(pl.multiple_of(i * block, block), block)] = dot(hidden, g, 1, 1).astype(BF16).reshape(fs, each, block)
        hg_ref[...] += dot(w_ref[:, j].reshape(width, block), g, 1, 0)

    @pl.when(i == pl.num_programs(0) - 1)
    def _():
        dw_ref[:, 3] = dwo_ref[...].reshape(fs, each, width)
        def cols(c, acc):
            at = pl.ds(pl.multiple_of(c * 128, 128), 128)
            dx, gg = ln_back(x_ref[:, at].astype(F32), hg_ref[:, at], gain_ref[:, 0:1])
            first_ref[:, at] = (sg_ref[:, at] + dx).astype(BF16)
            return acc + gg
        acc = lax.fori_loop(0, length // 128, cols, jnp.zeros((width, 128), F32))
        gg_ref[...] = jnp.sum(acc, axis=1, keepdims=True)

def ln_back(x, g, gain):
    centred = x - jnp.mean(x, axis=0, keepdims=True)
    spread = jnp.mean(centred * centred, axis=0, keepdims=True)
    rs = lax.rsqrt(spread + EPS)
    xh = centred * rs
    gx = g * gain
    dx = rs * (gx - jnp.mean(gx, axis=0, keepdims=True) - xh * jnp.mean(gx * xh, axis=0, keepdims=True))
    return dx, g * xh

def attn_bwd(xT, gain, cosT, sinT, sg, hT, q, k, v, m, lse, w, fs):
    width, length = xT.shape
    block = 256
    n = width // block
    col = pl.BlockSpec((block, length), lambda i: (i, 0))
    full = whole((width, length))
    return pl.pallas_call(
        attn_bwd_kernel, grid=(n,), name="attn_bwd", cost_estimate=cost(62),
        in_specs=[full, whole(gain.shape), whole(cosT.shape), whole(sinT.shape), full, full, col, col, col, col,
                  pl.BlockSpec((1, 8, length), lambda i: (i, 0, 0)),
                  pl.BlockSpec((w.shape[0], 3, w.shape[2], block), lambda i: (0, 0, 0, i)),
                  pl.BlockSpec((w.shape[0], 1, w.shape[2], width), lambda i: (0, 3, 0, 0))],
        out_specs=[full, whole((width, 1)), whole((fs, 4, width // fs, width))],
        out_shape=[jax.ShapeDtypeStruct((width, length), BF16), jax.ShapeDtypeStruct((width, 1), F32),
                   jax.ShapeDtypeStruct((fs, 4, width // fs, width), BF16)],
        scratch_shapes=[pltpu.VMEM((width, length), F32), pltpu.VMEM((width, length), BF16), pltpu.VMEM((block, length), BF16),
                        pltpu.VMEM((block // HEAD, length, HEAD), BF16), pltpu.VMEM((block // HEAD, length, HEAD), BF16),
                        pltpu.VMEM((block, length), F32), pltpu.VMEM((block, length), F32), pltpu.VMEM((block, length), F32),
                        pltpu.VMEM((width, width), BF16)],
        compiler_params=params(),
    )(xT, gain, cosT, sinT, sg, hT, q, k, v, m, lse, w, w)
def ff_fwd_kernel(x_ref, m_ref, g2_ref, g3_ref, pos_ref, wo_ref, up_ref, down_ref,
                  x2_ref, h2_ref, x3_ref, head_ref, fin_ref):
    width, length = x_ref.shape
    i = pl.program_id(0)

    @pl.when(i == 0)
    def _():
        x2_ref[...] = x_ref[...].astype(F32) + dot(wo_ref[:, 0].reshape(width, width), m_ref[...], 0, 0)
        x3_ref[...] = x2_ref[...]
        def cols(c, carry):
            at = pl.ds(pl.multiple_of(c * 128, 128), 128)
            h2_ref[:, at] = ln(x2_ref[:, at], g2_ref[:, 1:2]).astype(BF16)
            return carry
        lax.fori_loop(0, length // 128, cols, 0)

    pre = dot(up_ref[0], h2_ref[...], 1, 0)
    act = jax.nn.gelu(pre, approximate=True).astype(BF16)
    x3_ref[...] += dot(down_ref[0], act, 0, 0)

    @pl.when(i == pl.num_programs(0) - 1)
    def _():
        def cols(c, carry):
            at = pl.ds(pl.multiple_of(c * 128, 128), 128)
            fin_ref[:, at] = ln(x3_ref[:, at], g3_ref[:, 2:3]).astype(BF16)
            return carry
        lax.fori_loop(0, length // 128, cols, 0)
        slots = pos_ref.shape[0]
        onehot = (pos_ref[...] == lax.broadcasted_iota(jnp.int32, (slots, length), 1)).astype(BF16)
        head_ref[...] = dot(onehot, fin_ref[...], 1, 1).astype(BF16)

def ln(x, gain):
    centred = x - jnp.mean(x, axis=0, keepdims=True)
    spread = jnp.mean(centred * centred, axis=0, keepdims=True)
    return centred * lax.rsqrt(spread + EPS) * gain

def ff_fwd(xT, m, g2, g3, pos, attn_w, ff_w):
    width, length = xT.shape
    hidden = ff_w.shape[1]
    block = 512
    n = hidden // block
    slots = pos.shape[0]
    full = whole((width, length))
    f = jax.ShapeDtypeStruct((width, length), F32)
    return pl.pallas_call(
        ff_fwd_kernel, grid=(n,), name="ff_fwd", cost_estimate=cost(34),
        in_specs=[full, full, whole(g2.shape), whole(g3.shape), whole((slots, 1)),
                  pl.BlockSpec((attn_w.shape[0], 1, attn_w.shape[2], width), lambda i: (0, 3, 0, 0)),
                  pl.BlockSpec((1, block, width), lambda i: (0, i, 0)),
                  pl.BlockSpec((1, block, width), lambda i: (1, i, 0))],
        out_specs=[full, full, full, whole((slots, width))],
        out_shape=[f, jax.ShapeDtypeStruct((width, length), BF16), f, jax.ShapeDtypeStruct((slots, width), BF16)],
        scratch_shapes=[pltpu.VMEM((width, length), BF16)],
        compiler_params=params(),
    )(xT, m, g2, g3, pos, attn_w, ff_w, ff_w)

def ff_bwd_kernel(x3_ref, x2_ref, h2_ref, rg_ref, pos_ref, g2_ref, g3_ref, up_ref, down_ref,
                  sg_ref, gg2_ref, gg3_ref, dw_ref, low_ref, hg_ref):
    width, length = x3_ref.shape
    i = pl.program_id(0)
    slots = pos_ref.shape[0]

    @pl.when(i == 0)
    def _():
        rows = rg_ref[...]
        high = rows.astype(BF16)
        rest = (rows - high.astype(F32)).astype(BF16)
        hg_ref[...] = jnp.zeros_like(hg_ref)
        def cols(c, acc):
            at = pl.ds(pl.multiple_of(c * 128, 128), 128)
            onehot = (pos_ref[...] == c * 128 + lax.broadcasted_iota(jnp.int32, (slots, 128), 1)).astype(BF16)
            fg = dot(high, onehot, 0, 0) + dot(rest, onehot, 0, 0)
            dx, gg = ln_back(x3_ref[:, at], fg, g3_ref[:, 2:3])
            sg_ref[:, at] = dx
            low_ref[:, at] = dx.astype(BF16)
            return acc + gg
        acc = lax.fori_loop(0, length // 128, cols, jnp.zeros((width, 128), F32))
        gg3_ref[...] = jnp.sum(acc, axis=1, keepdims=True)

    ag = dot(down_ref[0], low_ref[...], 1, 0)
    pre = dot(up_ref[0], h2_ref[...], 1, 0)
    c0, c1 = 0.7978845608028654, 0.044715
    t = jnp.tanh(c0 * (pre + c1 * pre * pre * pre))
    half = 0.5 * (1.0 + t)
    act = (pre * half).astype(BF16)
    slope = half + 0.5 * pre * (1.0 - t * t) * (c0 * (1.0 + 3.0 * c1 * pre * pre))
    pg = (slope * ag).astype(BF16)
    shape = (dw_ref.shape[0],) + dw_ref.shape[2:]
    dw_ref[:, 1] = dot(act, low_ref[...], 1, 1).astype(BF16).reshape(shape)
    dw_ref[:, 0] = dot(pg, h2_ref[...], 1, 1).astype(BF16).reshape(shape)
    hg_ref[...] += dot(up_ref[0], pg, 0, 0)

    @pl.when(i == pl.num_programs(0) - 1)
    def _():
        def cols(c, acc):
            at = pl.ds(pl.multiple_of(c * 128, 128), 128)
            dx, gg = ln_back(x2_ref[:, at], hg_ref[:, at], g2_ref[:, 1:2])
            sg_ref[:, at] += dx
            return acc + gg
        acc = lax.fori_loop(0, length // 128, cols, jnp.zeros((width, 128), F32))
        gg2_ref[...] = jnp.sum(acc, axis=1, keepdims=True)

def ff_bwd(x3, x2, h2, rg, pos, g2, g3, ff_w, fs):
    width, length = x3.shape
    hidden = ff_w.shape[1]
    each = hidden // fs
    block = each * max(1, 768 // each)
    n = hidden // block
    slots = pos.shape[0]
    full = whole((width, length))
    wb = pl.BlockSpec((block // each, 2, each, width), lambda i: (i, 0, 0, 0))
    g = jax.ShapeDtypeStruct((width, 1), F32)
    return pl.pallas_call(
        ff_bwd_kernel, grid=(n,), name="ff_bwd", cost_estimate=cost(45),
        in_specs=[full, full, full, whole((slots, width)), whole((slots, 1)), whole(g2.shape), whole(g3.shape),
                  pl.BlockSpec((1, block, width), lambda i: (0, i, 0)),
                  pl.BlockSpec((1, block, width), lambda i: (1, i, 0))],
        out_specs=[full, whole((width, 1)), whole((width, 1)), wb],
        out_shape=[jax.ShapeDtypeStruct((width, length), F32), g, g, jax.ShapeDtypeStruct((fs, 2, each, width), BF16)],
        scratch_shapes=[pltpu.VMEM((width, length), BF16), pltpu.VMEM((width, length), F32)],
        compiler_params=params(),
    )(x3, x2, h2, rg, pos, g2, g3, ff_w, ff_w)
RB = 256
FCH, BCH = 8, 8

def pick(n, top=8):
    return max(k for k in range(1, top + 1) if n % k == 0)

def table_kernel(source_ref, low_ref, turned_ref, *, shard):
    block = source_ref.shape[0]
    ids = pl.program_id(0) * block + lax.broadcasted_iota(jnp.int32, source_ref.shape, 0)
    low = jnp.where(ids < shard, source_ref[...], 0.0).astype(BF16)
    low_ref[...] = low
    turned_ref[...] = low.T

def table_both(table):
    shard, width = table.shape
    vocab = -(-shard // 128) * 128
    block = 640 if vocab % 640 == 0 else 128
    return pl.pallas_call(
        functools.partial(table_kernel, shard=shard), name="table_both", grid=(vocab // block,), cost_estimate=cost(12),
        in_specs=[pl.BlockSpec((block, width), lambda i: (i, 0))],
        out_specs=[pl.BlockSpec((block, width), lambda i: (i, 0)), pl.BlockSpec((width, block), lambda i: (0, i))],
        out_shape=[jax.ShapeDtypeStruct((vocab, width), BF16), jax.ShapeDtypeStruct((width, vocab), BF16)],
        compiler_params=params())(table)

def compact(meta_ref, rows_ref, comp_ref):
    nseq, slots, width = rows_ref.shape
    def clear(b, carry):
        comp_ref[pl.ds(pl.multiple_of(b * RB, RB), RB), :] = jnp.zeros((RB, width), BF16)
        return carry
    lax.fori_loop(0, meta_ref[2, 0], clear, 0)
    def seq(s, carry):
        def part(c, c2):
            comp_ref[pl.ds(pl.multiple_of((meta_ref[1, s] + c) * 16, 16), 16), :] = rows_ref[s, pl.ds(pl.multiple_of(c * 16, 16), 16), :]
            return c2
        lax.fori_loop(0, meta_ref[0, s], part, 0)
        return carry
    lax.fori_loop(0, nseq, seq, 0)

def vocab_fwd_kernel(meta_ref, limit_ref, rows_ref, table_ref, target_ref, lse_ref, chosen_ref, *outs, chunk, least, inside):
    comp_ref = outs[0] if inside else rows_ref
    vocab = table_ref.shape[0]
    if inside:
        nseq, slots, width = rows_ref.shape
        compact(meta_ref, rows_ref, comp_ref)
    lse_ref[...] = jnp.zeros_like(lse_ref)
    chosen_ref[...] = jnp.zeros_like(chosen_ref)
    limit = limit_ref[0]
    def block(b, carry):
        rows = comp_ref[pl.ds(pl.multiple_of(b * RB, RB), RB), :]
        target = target_ref[b]
        top = total = chosen = None
        for v in range(vocab // chunk):
            l = dot(table_ref[v * chunk:(v + 1) * chunk, :], rows, 1, 1)
            ids = v * chunk + lax.broadcasted_iota(jnp.int32, (chunk, RB), 0)
            hit = jnp.sum(jnp.where(ids == target, l, 0.0), axis=0, keepdims=True)
            if (v + 1) * chunk > least:
                l = jnp.where(ids < limit, l, -jnp.inf)
            m = jnp.max(l, axis=0, keepdims=True)
            if v == 0:
                top = m
                total = jnp.sum(jnp.exp(l - top), axis=0, keepdims=True)
                chosen = hit
            else:
                new = jnp.maximum(top, m)
                total = total * jnp.exp(top - new) + jnp.sum(jnp.exp(l - new), axis=0, keepdims=True)
                chosen = chosen + hit
                top = new
        lse_ref[b] = top + jnp.log(total)
        chosen_ref[b] = chosen
        return carry
    lax.fori_loop(0, meta_ref[2, 0], block, 0)

def vocab_fwd(meta, limit, rows, table, target, least):
    inside = rows.ndim == 3
    width = rows.shape[-1]
    nblk = target.shape[0]
    vocab = table.shape[0]
    chunk = 128 * pick(vocab // 128, FCH)
    smem = pl.BlockSpec(memory_space=pltpu.SMEM)
    vm = pl.BlockSpec(memory_space=pltpu.VMEM)
    st = jax.ShapeDtypeStruct((nblk, 1, RB), F32)
    comp = [jax.ShapeDtypeStruct((nblk * RB, width), BF16)] if inside else []
    out = pl.pallas_call(
        functools.partial(vocab_fwd_kernel, chunk=chunk, least=least, inside=inside), name="vocab_fwd", cost_estimate=cost(20),
        in_specs=[smem, smem, vm, vm, vm], out_specs=[vm] * (2 + len(comp)),
        out_shape=[st, st] + comp,
        compiler_params=params())(meta, limit, rows, table, target)
    return out[2] if inside else rows, out[0], out[1]

def vocab_bwd_kernel(meta_ref, limit_ref, comp_ref, table_ref, turned_ref, target_ref, lse_ref, scale_ref,
                     og_ref, og2_ref, rg_ref, acc_ref, rc_ref, low_ref, back_ref, sem, *, chunk, least, inside):
    vocab, width = table_ref.shape
    limit = limit_ref[0]
    nch = vocab // chunk
    def clear(b, carry):
        acc_ref[pl.ds(pl.multiple_of(b * 128, 128), 128), :] = jnp.zeros((128, width), F32)
        return carry
    lax.fori_loop(0, vocab // 128, clear, 0)
    def block(b, carry):
        rows = comp_ref[pl.ds(pl.multiple_of(b * RB, RB), RB), :]
        target, lse, scale = target_ref[b], lse_ref[b], scale_ref[b]
        rg = None
        for v in range(nch):
            l = dot(table_ref[v * chunk:(v + 1) * chunk, :], rows, 1, 1)
            ids = v * chunk + lax.broadcasted_iota(jnp.int32, (chunk, RB), 0)
            p = jnp.exp(l - lse)
            p = jnp.where(ids == target, p - 1.0, p)
            if (v + 1) * chunk > least:
                p = jnp.where(ids < limit, p, 0.0)
            g = (scale * p).astype(BF16)
            acc_ref[v * chunk:(v + 1) * chunk, :] += dot(g, rows, 1, 0)
            part = dot(turned_ref[:, v * chunk:(v + 1) * chunk], g, 1, 0)
            rg = part if rg is None else rg + part
        rc_ref[pl.ds(pl.multiple_of(b * RB, RB), RB), :] = rg.T.astype(BF16)
        return carry
    lax.fori_loop(0, meta_ref[2, 0], block, 0)
    if inside:
        nseq, slots, _ = back_ref.shape
        def seq(s, carry):
            back_ref[s] = jnp.zeros((slots, width), BF16)
            def part(c, c2):
                back_ref[s, pl.ds(pl.multiple_of(c * 16, 16), 16), :] = rc_ref[pl.ds(pl.multiple_of((meta_ref[1, s] + c) * 16, 16), 16), :]
                return c2
            lax.fori_loop(0, meta_ref[0, s], part, 0)
            return carry
        lax.fori_loop(0, nseq, seq, 0)
        out = pltpu.make_async_copy(back_ref, rg_ref, sem.at[0])
    else:
        out = pltpu.make_async_copy(rc_ref, rg_ref, sem.at[0])
    out.start()
    outs = [out]
    part = og_ref.shape[0]
    for v, (ref, start) in enumerate(((og_ref, 0), (og2_ref, part))):
        at = pl.ds(start, ref.shape[0])
        low_ref[at, :] = acc_ref[at, :].astype(BF16)
        outs.append(pltpu.make_async_copy(low_ref.at[at], ref, sem.at[1 + v]))
        outs[-1].start()
    for o in outs:
        o.wait()

def vocab_bwd(meta, limit, comp, table, turned, target, lse, scale, least, nseq, slots, inside):
    rows, width = comp.shape
    vocab = table.shape[0]
    chunk = 128 * pick(vocab // 128, BCH)
    smem = pl.BlockSpec(memory_space=pltpu.SMEM)
    vm = pl.BlockSpec(memory_space=pltpu.VMEM)
    hbm = pl.BlockSpec(memory_space=pl.ANY)
    shape = (nseq, slots, width) if inside else (rows, width)
    part = vocab // 256 * 128
    return pl.pallas_call(
        functools.partial(vocab_bwd_kernel, chunk=chunk, least=least, inside=inside), name="vocab_bwd", cost_estimate=cost(40),
        in_specs=[smem, smem] + [vm] * 6, out_specs=[hbm, hbm, hbm],
        out_shape=[jax.ShapeDtypeStruct((part, width), BF16), jax.ShapeDtypeStruct((vocab - part, width), BF16), jax.ShapeDtypeStruct(shape, BF16)],
        scratch_shapes=[pltpu.VMEM((vocab, width), F32), pltpu.VMEM((rows, width), BF16),
                        pltpu.VMEM((vocab, width), BF16), pltpu.VMEM(shape if inside else (1, 16, width), BF16),
                        pltpu.SemaphoreType.DMA((3,))],
        compiler_params=params())(meta, limit, comp, table, turned, target, lse, scale)

def plan(counts, slots, length):
    nseq = counts.shape[0]
    units = (counts + 15) // 16
    ends = jnp.cumsum(units)
    offs = ends - units
    total = ends[-1] * 16
    nblk = (total + RB - 1) // RB
    cap = (nseq * slots + RB - 1) // RB * RB
    at = jnp.arange(cap, dtype=jnp.int32)
    seq = jnp.minimum(jnp.sum((at[:, None] >= ends[None, :] * 16).astype(jnp.int32), axis=1), nseq - 1)
    mine = (seq[:, None] == jnp.arange(nseq, dtype=jnp.int32)[None, :])
    slot = at - jnp.sum(jnp.where(mine, offs[None, :] * 16, 0), axis=1)
    cnt = jnp.sum(jnp.where(mine, counts[None, :], 0), axis=1)
    live = slot < cnt
    weight = jnp.where(live, length / cnt.astype(F32), 0.0)
    meta = jnp.stack([units, offs, jnp.full((nseq,), nblk)]).astype(jnp.int32)
    return meta, seq, slot, weight

def spread(values, seq, slot):
    nseq, slots = values.shape
    parts = jnp.concatenate([values // 256, values % 256], axis=1).astype(BF16)
    mine = (seq[:, None] == jnp.arange(nseq, dtype=jnp.int32)[None, :]).astype(BF16)
    rows = jnp.dot(mine, parts, preferred_element_type=F32)
    hit = slot[:, None] == jnp.arange(slots, dtype=jnp.int32)[None, :]
    both = rows[:, :slots] * 256.0 + rows[:, slots:]
    return jnp.sum(jnp.where(hit, both, 0.0), axis=1).astype(jnp.int32)

def halves(vocab):
    nb = vocab // 128
    low = (nb + 1) // 2
    return nb, low

def sections(count, size):
    return [(s, min(size, count - s)) for s in range(0, count, size)]

def gather_kernel(ids_ref, flag_ref, emb_ref, out_ref, tab_ref, raw_ref, row_ref, sem):
    feat, vocab = emb_ref.shape
    nseq, _, length = out_ref.shape
    nb, low = halves(vocab)
    size = -(-low // 6)
    secs = sections(low, size)
    def copies(k):
        s, n = secs[k]
        out = [pltpu.make_async_copy(emb_ref.at[:, pl.ds(s * 128, n * 128)], raw_ref.at[:, pl.ds(s * 128, n * 128)], sem.at[2 * k])]
        m = min(n, nb - low - s)
        if m > 0:
            out.append(pltpu.make_async_copy(emb_ref.at[:, pl.ds((low + s) * 128, m * 128)], raw_ref.at[:, pl.ds((low + s) * 128, m * 128)], sem.at[2 * k + 1]))
        return out
    for k in range(len(secs)):
        for c in copies(k):
            c.start()
    pad = jnp.zeros((64 - feat, 128), F32)
    for k in range(len(secs)):
        for c in copies(k):
            c.wait()
        s, n = secs[k]
        m = max(0, min(n, nb - low - s))
        def turn(b, carry):
            a = raw_ref[:, pl.ds(pl.multiple_of(b * 128, 128), 128)]
            h = raw_ref[:, pl.ds(pl.multiple_of((low + b) * 128, 128), 128)]
            tab_ref[pl.ds(pl.multiple_of(b * 128, 128), 128), :] = jnp.concatenate([a, pad, h, pad], axis=0).T
            return carry
        lax.fori_loop(s, s + m, turn, 0, unroll=3)
        for b in range(s + m, s + n):
            a = raw_ref[:, b * 128:(b + 1) * 128]
            tab_ref[b * 128:(b + 1) * 128, :] = jnp.concatenate([a, pad, pad, jnp.zeros((feat, 128), F32)], axis=0).T
    U = 32
    def seq(s, carry):
        def grp(g, c2):
            base = pl.multiple_of(g * U, U)
            for j in range(U):
                i = ids_ref[s * length + base + j]
                row_ref[pl.ds(base + j, 1), :] = tab_ref[pl.ds(i, 1), :]
            return c2
        lax.fori_loop(0, length // U, grp, 0)
        for c in range(length // 128):
            t = row_ref[c * 128:(c + 1) * 128, :].T
            f = flag_ref[s, :, c * 128:(c + 1) * 128] > 0
            out_ref[s, :, c * 128:(c + 1) * 128] = jnp.where(f, t[64:64 + feat], t[:feat]).astype(BF16)
        return carry
    lax.fori_loop(0, nseq, seq, 0)

def split_ids(ids, vocab):
    nb, low = halves(vocab)
    high = ids >= low * 128
    return jnp.where(high, ids - low * 128, ids), high.astype(jnp.int32)

def gather(ids, emb):
    nseq, length = ids.shape
    feat, vocab = emb.shape
    nb, low = halves(vocab)
    rid, flag = split_ids(ids, vocab)
    return pl.pallas_call(gather_kernel, name="emb_gather", cost_estimate=cost(32),
        in_specs=[pl.BlockSpec(memory_space=pltpu.SMEM), pl.BlockSpec(memory_space=pltpu.VMEM), pl.BlockSpec(memory_space=pl.ANY)],
        out_specs=pl.BlockSpec(memory_space=pltpu.VMEM),
        out_shape=jax.ShapeDtypeStruct((nseq, feat, length), BF16),
        scratch_shapes=[pltpu.VMEM((low * 128, 128), F32), pltpu.VMEM((feat, vocab), F32), pltpu.VMEM((length, 128), F32), pltpu.SemaphoreType.DMA((12,))],
        compiler_params=params())(rid.reshape(-1), flag.reshape(nseq, 1, length), emb)

def scatter_kernel(ids_ref, flag_ref, *refs, ng, per):
    g_refs = refs[:ng]
    out_ref, sq_ref, raw_ref, row_ref, sem = refs[ng:ng + 5]
    tabs = refs[ng + 5:]
    feat, vocab = out_ref.shape
    nseq, _, length = g_refs[0].shape
    nb, low = halves(vocab)
    zero128 = jnp.zeros((128, 128), F32)
    def zero(b, carry):
        for t in tabs:
            t[pl.ds(pl.multiple_of(b * 128, 128), 128), :] = zero128
        return carry
    lax.fori_loop(0, low, zero, 0)
    pad = jnp.zeros((64 - feat, 128), F32)
    U = 8
    streams = [(g, p) for g in range(ng) for p in range(per)]
    each = nseq // per
    def seq(s, carry):
        for k, (g, p) in enumerate(streams):
            q = p * each + s
            for c in range(length // 128):
                at = slice(c * 128, (c + 1) * 128)
                v = g_refs[g][q, :, at].astype(F32)
                f = flag_ref[g * nseq + q, :, at] > 0
                row_ref[k, at, :] = jnp.concatenate([jnp.where(f, 0.0, v), pad, jnp.where(f, v, 0.0), pad], axis=0).T
        def grp(n, c2):
            base = pl.multiple_of(n * U, U)
            for j in range(U):
                idx = [ids_ref[(g * nseq + p * each + s) * length + base + j] for g, p in streams]
                old = [tabs[k][pl.ds(idx[k], 1), :] for k in range(len(streams))]
                new = [old[k] + row_ref[k, pl.ds(base + j, 1), :] for k in range(len(streams))]
                for k in range(len(streams)):
                    tabs[k][pl.ds(idx[k], 1), :] = new[k]
            return c2
        lax.fori_loop(0, length // U, grp, 0)
        return carry
    lax.fori_loop(0, each, seq, 0)
    def tile(b):
        at = pl.ds(pl.multiple_of(b * 128, 128), 128)
        parts = [sum((tabs[g * per + p][at, :] for p in range(1, per)), tabs[g * per][at, :]) for g in range(ng)]
        return sum(parts[1:], parts[0]).T
    size = -(-low // 6)
    secs = sections(low, size)
    def copies(k):
        s, n = secs[k]
        out = [pltpu.make_async_copy(raw_ref.at[k % 2, 0, :, pl.ds(0, n * 128)], out_ref.at[:, pl.ds(s * 128, n * 128)], sem.at[2 * k])]
        m = min(n, nb - low - s)
        if m > 0:
            out.append(pltpu.make_async_copy(raw_ref.at[k % 2, 1, :, pl.ds(0, m * 128)], out_ref.at[:, pl.ds((low + s) * 128, m * 128)], sem.at[2 * k + 1]))
        return out
    squares = jnp.zeros((128, 128), F32)
    for k, (s, n) in enumerate(secs):
        if k >= 2:
            for c in copies(k - 2):
                c.wait()
        def turn(b, carry, s=s, k=k):
            t = tile(b)
            at = pl.ds(pl.multiple_of((b - s) * 128, 128), 128)
            raw_ref[k % 2, 0, :, at] = t[:feat]
            raw_ref[k % 2, 1, :, at] = t[64:64 + feat]
            return carry + t * t
        squares = lax.fori_loop(s, s + n, turn, squares, unroll=3)
        for c in copies(k):
            c.start()
    sq_ref[...] = squares
    for k in range(max(0, len(secs) - 2), len(secs)):
        for c in copies(k):
            c.wait()

def scatter(ids, gs, vocab, per):
    nseq, feat, length = gs[0].shape
    nb, low = halves(vocab)
    rid, flag = split_ids(ids, vocab)
    ng = len(gs)
    size = -(-low // 6)
    vm = pl.BlockSpec(memory_space=pltpu.VMEM)
    return pl.pallas_call(functools.partial(scatter_kernel, ng=ng, per=per), name="emb_scatter", cost_estimate=cost(1),
        in_specs=[pl.BlockSpec(memory_space=pltpu.SMEM), vm] + [vm] * ng,
        out_specs=[pl.BlockSpec(memory_space=pl.ANY), vm],
        out_shape=[jax.ShapeDtypeStruct((feat, vocab), F32), jax.ShapeDtypeStruct((128, 128), F32)],
        scratch_shapes=[pltpu.VMEM((2, 2, feat, size * 128), F32), pltpu.VMEM((ng * per, length, 128), F32), pltpu.SemaphoreType.DMA((12,))]
            + [pltpu.VMEM((low * 128, 128), F32)] * (ng * per),
        compiler_params=params(62 * 1024 * 1024))(rid.reshape(-1), flag.reshape(-1, 1, length), *gs)
AHEAD = 2
MESH_ID = pl.DeviceIdType.MESH

def comm_params(ident):
    return pltpu.CompilerParams(collective_id=ident, has_side_effects=True, vmem_limit_bytes=VL)

def meet(peers):
    barrier = pltpu.get_barrier_semaphore()
    for p in peers:
        pl.semaphore_signal(barrier, inc=1, device_id=p, device_id_type=MESH_ID)
    pl.semaphore_wait(barrier, len(peers))

def remote(src, dst, send, recv, peer):
    return pltpu.make_async_remote_copy(src_ref=src, dst_ref=dst, send_sem=send, recv_sem=recv, device_id=peer, device_id_type=MESH_ID)

def small_kernel(x_ref, *refs, fs, dps, wide, finish):
    out_ref = refs[0]
    got_ref = refs[1] if finish else out_ref
    send, recv = refs[-2:]
    d, f = lax.axis_index("dp"), lax.axis_index("fsdp")
    n = fs * dps if wide else fs
    me = d * fs + f if wide else f
    def peer(k):
        j = lax.rem(me + k, n)
        return (lax.div(j, fs), lax.rem(j, fs)) if wide else (d, j)
    barrier = pltpu.get_barrier_semaphore()
    def greet(k, carry):
        pl.semaphore_signal(barrier, inc=1, device_id=peer(k), device_id_type=MESH_ID)
        return carry
    lax.fori_loop(1, n, greet, 0)
    pl.semaphore_wait(barrier, n - 1)
    def copy(k):
        return remote(x_ref, got_ref.at[me], send.at[k], recv.at[k], peer(k))
    def begin(k, carry):
        copy(k).start()
        return carry
    lax.fori_loop(1, n, begin, 0)
    got_ref[me] = x_ref[...]
    def end(k, carry):
        copy(k).wait()
        return carry
    lax.fori_loop(1, n, end, 0)
    if finish:
        finish(got_ref, out_ref, n)

def lse_finish(got_ref, out_ref, n):
    top = got_ref[0]
    for i in range(1, n):
        top = jnp.maximum(top, got_ref[i])
    total = jnp.exp(got_ref[0] - top)
    for i in range(1, n):
        total = total + jnp.exp(got_ref[i] - top)
    out_ref[...] = top + jnp.log(total)

def sum_finish(got_ref, out_ref, n):
    total = got_ref[0]
    for i in range(1, n):
        total = total + got_ref[i]
    out_ref[...] = total

def small_gather(x, ident, wide=False, finish=None, name="small_gather"):
    fs, dps = lax.axis_size("fsdp"), lax.axis_size("dp")
    n = fs * dps if wide else fs
    vm = pl.BlockSpec(memory_space=pltpu.VMEM)
    got = (n,) + x.shape
    return pl.pallas_call(
        functools.partial(small_kernel, fs=fs, dps=dps, wide=wide, finish=finish), name=name,
        in_specs=[vm], out_specs=vm,
        out_shape=jax.ShapeDtypeStruct(x.shape if finish else got, x.dtype),
        scratch_shapes=([pltpu.VMEM(got, x.dtype)] if finish else []) + [pltpu.SemaphoreType.DMA((n,)), pltpu.SemaphoreType.DMA((n,))],
        cost_estimate=cost(12), compiler_params=comm_params(ident))(x)

def exchange_kernel(*refs, fs, both, aux, reduce, pairs):
    refs = list(refs)
    x_ref = refs.pop(0)
    aux_ref = refs.pop(0) if aux else None
    w_ref = refs.pop(0) if reduce else None
    pair_refs = [refs.pop(0) for _ in range(2 * pairs)]
    out_ref = refs.pop(0)
    other_ref = refs.pop(0) if both else None
    sum_ref = refs.pop(0) if aux else None
    red_ref = refs.pop(0) if reduce else None
    if pairs:
        sq_ref = refs.pop(0)
        held = [refs.pop() for _ in range(2 * pairs)]
        held_sem = refs.pop()
    send, recv, send2, recv2, own = refs[:5]
    refs = refs[5:]
    if aux:
        near_ref, over_ref = refs.pop(0), refs.pop(0)
    if reduce:
        _, parts, red_begin, red_middle, red_end = reduce_phases(w_ref, red_ref, *refs, high=fs // 4, both=both)
    d, f = lax.axis_index("dp"), lax.axis_index("fsdp")
    across = (1 - d, f)
    barrier = pltpu.get_barrier_semaphore()
    def greet(k, carry):
        pl.semaphore_signal(barrier, inc=1, device_id=(d, lax.rem(f + k, fs)), device_id_type=MESH_ID)
        return carry
    lax.fori_loop(1, fs, greet, 0)
    if both:
        pl.semaphore_signal(barrier, inc=1, device_id=across, device_id_type=MESH_ID)
    pl.semaphore_wait(barrier, fs if both else fs - 1)
    def copies(k):
        j = lax.rem(f + k, fs)
        out = [remote(x_ref.at[j], out_ref.at[f], send.at[0, k], recv.at[0, k], (d, j))]
        if aux:
            out.append(remote(aux_ref, near_ref.at[f], send.at[1, k], recv.at[1, k], (d, j)))
        return out
    def passed(k):
        s = lax.rem(f + fs - k, fs)
        out = [remote(out_ref.at[s], other_ref.at[s], send2.at[0, k], recv2.at[0, k], across)]
        if aux:
            out.append(remote(near_ref.at[s], over_ref.at[s], send2.at[1, k], recv2.at[1, k], across))
        return out
    def first():
        out = [remote(x_ref.at[f], other_ref.at[f], send2.at[0, 0], recv2.at[0, 0], across)]
        if aux:
            out.append(remote(aux_ref, over_ref.at[f], send2.at[1, 0], recv2.at[1, 0], across))
        return out
    if reduce:
        red_begin()
    if both:
        for c in first():
            c.start()
    def begin(k, carry):
        for c in copies(k):
            c.start()
        return carry
    lax.fori_loop(1, fs, begin, 0)
    mine = pltpu.make_async_copy(x_ref.at[f], out_ref.at[f], own)
    mine.start()
    if aux:
        near_ref[f] = aux_ref[...]
    mine.wait()
    def arrive(k, carry):
        for c in copies(k):
            c.wait_recv()
        if both:
            for c in passed(k):
                c.start()
        return carry
    if pairs:
        loads = [pltpu.make_async_copy(a, b, held_sem.at[i]) for i, (a, b) in enumerate(zip(pair_refs, held))]
        for l in loads:
            l.start()
        for l in loads:
            l.wait()
        total = jnp.zeros((8, held[0].shape[1]), F32)
        for i in range(pairs):
            a_ref, b_ref = held[2 * i], held[2 * i + 1]
            def add(n, t, a_ref=a_ref, b_ref=b_ref):
                at = pl.ds(pl.multiple_of(n * 64, 64), 64)
                s = a_ref[at, :].astype(F32) + b_ref[at, :].astype(F32)
                s = s * s
                for j in range(0, 64, 8):
                    t = t + s[j:j + 8]
                return t
            total = lax.fori_loop(0, a_ref.shape[0] // 64, add, total)
        sq_ref[...] = total
    steps = parts + 1 if reduce else 1
    marks = [1 + (fs - 1) * i // steps for i in range(steps + 1)]
    for i in range(steps):
        if reduce:
            red_middle(i)
        lax.fori_loop(marks[i], marks[i + 1], arrive, 0)
    if reduce:
        red_end()
    def end(k, carry):
        for c in copies(k):
            c.wait_send()
        if both:
            for c in passed(k):
                c.wait()
        return carry
    lax.fori_loop(1, fs, end, 0)
    if both:
        for c in first():
            c.wait()
    if aux:
        total = near_ref[0]
        for i in range(1, fs):
            total = total + near_ref[i]
        if both:
            rest = over_ref[0]
            for i in range(1, fs):
                rest = rest + over_ref[i]
            total = total + rest
        sum_ref[...] = total

def exchange(x, ident, both, name, aux=None, reduce=None, pairs=()):
    fs = lax.axis_size("fsdp")
    vm = pl.BlockSpec(memory_space=pltpu.VMEM)
    shape = jax.ShapeDtypeStruct(x.shape, x.dtype)
    sem = pltpu.SemaphoreType.DMA((2, fs))
    more = [] if aux is None else [pltpu.VMEM((fs,) + aux.shape, F32)] * 2
    outs = [shape] * (2 if both else 1) + ([] if aux is None else [jax.ShapeDtypeStruct(aux.shape, F32)])
    args = [x] + [a for a in (aux, reduce) if a is not None]
    if reduce is not None:
        block = reduce.shape[1:]
        outs.append(jax.ShapeDtypeStruct(block, F32))
        more = more + reduce_scratch(block, reduce.dtype, fs // 4)
    ins = [vm] * len(args) + [pl.BlockSpec(memory_space=pl.ANY)] * len(pairs)
    if pairs:
        outs.append(jax.ShapeDtypeStruct((8, pairs[0].shape[1]), F32))
        more = more + [pltpu.SemaphoreType.DMA((len(pairs),))] + [pltpu.VMEM(p.shape, p.dtype) for p in reversed(pairs)]
    return pl.pallas_call(
        functools.partial(exchange_kernel, fs=fs, both=both, aux=aux is not None, reduce=reduce is not None, pairs=len(pairs) // 2), name=name,
        in_specs=ins, out_specs=[vm] * len(outs), out_shape=outs,
        scratch_shapes=[sem, sem, sem, sem, pltpu.SemaphoreType.DMA] + more,
        cost_estimate=cost(55),
        compiler_params=comm_params(ident))(*args, *pairs)

def cuts(rows):
    n = 4 if rows % 64 == 0 else 1
    return n, rows // n

def gather_phases(x_ref, out_ref, send, recv, *, high):
    d, f = lax.axis_index("dp"), lax.axis_index("fsdp")
    h, m, c = lax.div(f, 4), lax.rem(lax.div(f, 2), 2), lax.rem(f, 2)
    side, twin = (d, h * 4 + (1 - m) * 2 + c), (d, h * 4 + m * 2 + 1 - c)
    parts, size = cuts(x_ref.shape[0])
    def far(k):
        return (d, lax.rem(h + k, high) * 4 + m * 2 + c)
    peers = [far(k) for k in range(1, high)] + [side, twin]
    sent = []
    def go(src, block, p, peer):
        at = pl.ds(p * size, size)
        r = remote(src.at[at], out_ref.at[block, at], send.at[len(sent)], recv.at[block, p], peer)
        r.start()
        sent.append(r)
    def arrived(block, p):
        at = pl.ds(p * size, size)
        remote(x_ref.at[at], out_ref.at[block, at], send.at[0], recv.at[block, p], twin).wait_recv()
    def back(k, row):
        return lax.rem(h + high - k, high) * 4 + row * 2 + c
    def launch(p):
        for k in range(1, high):
            go(x_ref, f, p, far(k))
        go(x_ref, f, p, side)
        go(x_ref, f, p, twin)
    ahead = min(AHEAD, parts)
    def begin():
        for p in range(ahead):
            launch(p)
        out_ref[f] = x_ref[...]
    def middle(p):
        if p < parts:
            for k in range(1, high):
                b = back(k, m)
                arrived(b, p)
                go(out_ref.at[b], b, p, side)
                go(out_ref.at[b], b, p, twin)
            if p + ahead < parts:
                launch(p + ahead)
        if p > 0:
            for k in range(high):
                b = back(k, 1 - m)
                arrived(b, p - 1)
                go(out_ref.at[b], b, p - 1, twin)
    def end():
        for row in range(2):
            for k in range(high):
                for p in range(parts):
                    arrived(lax.rem(h + high - k, high) * 4 + lax.rem(m + row, 2) * 2 + 1 - c, p)
        for r in sent:
            r.wait_send()
    return peers, parts, begin, middle, end

def rows_gather_kernel(x_ref, out_ref, send, recv, *, high):
    peers, parts, begin, middle, end = gather_phases(x_ref, out_ref, send, recv, high=high)
    meet(peers)
    begin()
    for p in range(parts + 1):
        middle(p)
    end()

def rows_gather(x, ident, name="rows_gather"):
    fs = lax.axis_size("fsdp")
    vm = pl.BlockSpec(memory_space=pltpu.VMEM)
    high = fs // 4
    parts = cuts(x.shape[0])[0]
    return pl.pallas_call(
        functools.partial(rows_gather_kernel, high=high), name=name,
        in_specs=[vm], out_specs=vm, out_shape=jax.ShapeDtypeStruct((fs,) + x.shape, x.dtype),
        scratch_shapes=[pltpu.SemaphoreType.DMA((4 * high * parts,)), pltpu.SemaphoreType.DMA((fs, parts))],
        cost_estimate=cost(40), compiler_params=comm_params(ident))(x)

def reduce_phases(x_ref, out_ref, twin_ref, side_ref, far_ref, a_ref, b_ref, s1, r1, s2, r2, s3, r3, *, high, both):
    d, f = lax.axis_index("dp"), lax.axis_index("fsdp")
    h, m, c = lax.div(f, 4), lax.rem(lax.div(f, 2), 2), lax.rem(f, 2)
    side, twin = (d, h * 4 + (1 - m) * 2 + c), (d, h * 4 + m * 2 + 1 - c)
    def far(k):
        return (d, lax.rem(h + k, high) * 4 + m * 2 + c)
    across = (1 - d, f)
    peers = [far(k) for k in range(1, high)] + [side, twin] + ([across] if both else [])
    order = list(range(1, high)) + [0]
    parts, size = cuts(x_ref.shape[1])
    def rows(p):
        return pl.ds(p * size, size)
    def at(k):
        return lax.rem(h + k, high)
    def one(k, row, p):
        slot = at(k) * 2 + row
        return remote(x_ref.at[at(k) * 4 + row * 2 + 1 - c, rows(p)], twin_ref.at[slot, rows(p)], s1.at[slot, p], r1.at[slot, p], twin)
    def two(k, p):
        return remote(a_ref.at[at(k), rows(p)], side_ref.at[at(k), rows(p)], s2.at[at(k), p], r2.at[at(k), p], side)
    def three(k, p):
        return remote(b_ref.at[k, rows(p)], far_ref.at[k, rows(p)], s3.at[k, p], r3.at[k, p], far(k))
    def last(p):
        return remote(b_ref.at[0, rows(p)], far_ref.at[0, rows(p)], s3.at[0, p], r3.at[0, p], across)
    def begin():
        for p in range(parts):
            for k in order:
                one(k, 1 - m, p).start()
            for k in order:
                one(k, m, p).start()
    def middle(p):
        if p < parts:
            if p >= 2:
                for k in order:
                    two(k, p - 2).wait_send()
            for k in order:
                one(k, 1 - m, p).wait_recv()
                a_ref[at(k), rows(p)] = (x_ref[at(k) * 4 + (1 - m) * 2 + c, rows(p)].astype(F32) + twin_ref[at(k) * 2 + 1 - m, rows(p)].astype(F32)).astype(a_ref.dtype)
                two(k, p).start()
        if p > 0:
            q = p - 1
            for k in order:
                one(k, m, q).wait_recv()
                two(k, q).wait_recv()
                total = x_ref[at(k) * 4 + m * 2 + c, rows(q)].astype(F32) + twin_ref[at(k) * 2 + m, rows(q)].astype(F32) + side_ref[at(k), rows(q)].astype(F32)
                if k == 0:
                    out_ref[rows(q)] = total
                else:
                    b_ref[k, rows(q)] = total.astype(b_ref.dtype)
                    three(k, q).start()
    def end():
        for p in range(parts):
            for k in range(1, high):
                three(k, p).wait_recv()
                out_ref[rows(p)] += far_ref[k, rows(p)].astype(F32)
            if both:
                b_ref[0, rows(p)] = out_ref[rows(p)].astype(b_ref.dtype)
                last(p).start()
        for p in range(parts):
            if both:
                last(p).wait()
                out_ref[rows(p)] = b_ref[0, rows(p)].astype(F32) + far_ref[0, rows(p)].astype(F32)
            for k in order:
                one(k, m, p).wait_send()
                one(k, 1 - m, p).wait_send()
                if p + 2 >= parts:
                    two(k, p).wait_send()
                if k:
                    three(k, p).wait_send()
    return peers, parts, begin, middle, end

def rows_reduce_kernel(*refs, high, both):
    peers, parts, begin, middle, end = reduce_phases(*refs, high=high, both=both)
    meet(peers)
    begin()
    for p in range(parts + 1):
        middle(p)
    end()

def reduce_scratch(block, dtype, high):
    parts = cuts(block[0])[0]
    def sem(n):
        return pltpu.SemaphoreType.DMA((n, parts))
    def buf(n):
        return pltpu.VMEM((n,) + block, dtype)
    return [buf(2 * high), buf(high), buf(high), buf(high), buf(high),
            sem(2 * high), sem(2 * high), sem(high), sem(high), sem(high), sem(high)]

def rows_reduce(x, ident, name="rows_reduce", both=False):
    vm = pl.BlockSpec(memory_space=pltpu.VMEM)
    high = lax.axis_size("fsdp") // 4
    block = x.shape[1:]
    return pl.pallas_call(
        functools.partial(rows_reduce_kernel, high=high, both=both), name=name,
        in_specs=[vm], out_specs=vm, out_shape=jax.ShapeDtypeStruct(block, F32),
        scratch_shapes=reduce_scratch(block, x.dtype, high),
        cost_estimate=cost(45), compiler_params=comm_params(ident))(x)
def front_kernel(ids_ref, w_ref, emb_ref, all_ref, x_ref, full_ref, tab_ref, raw_ref, row_ref, picked_ref, smem_ref,
                 raw_sem, ids_send, ids_recv, x_send, x_recv, smem_sem, w_send, w_recv, *, fs, dps):
    feat, vocab = emb_ref.shape
    length = x_ref.shape[2]
    lines = length // 128
    nb, low = halves(vocab)
    secs = sections(low, -(-low // 6))
    d, f = lax.axis_index("dp"), lax.axis_index("fsdp")
    n, me = fs * dps, d * fs + f
    def load(k):
        s, c = secs[k]
        out = [pltpu.make_async_copy(emb_ref.at[:, pl.ds(s * 128, c * 128)], raw_ref.at[:, pl.ds(s * 128, c * 128)], raw_sem.at[2 * k])]
        m = min(c, nb - low - s)
        if m > 0:
            out.append(pltpu.make_async_copy(emb_ref.at[:, pl.ds((low + s) * 128, m * 128)], raw_ref.at[:, pl.ds((low + s) * 128, m * 128)], raw_sem.at[2 * k + 1]))
        return out
    for k in range(len(secs)):
        for c in load(k):
            c.start()
    _, parts, w_begin, w_middle, w_end = gather_phases(w_ref, full_ref, w_send, w_recv, high=fs // 4)
    def peer(k):
        j = lax.rem(me + k, n)
        return (lax.div(j, fs), lax.rem(j, fs))
    barrier = pltpu.get_barrier_semaphore()
    def greet(k, carry):
        pl.semaphore_signal(barrier, inc=1, device_id=peer(k), device_id_type=MESH_ID)
        return carry
    lax.fori_loop(1, n, greet, 0)
    pl.semaphore_wait(barrier, n - 1)
    def ids_copy(k):
        return remote(ids_ref, all_ref.at[me], ids_send.at[k], ids_recv.at[k], peer(k))
    def ids_begin(k, carry):
        ids_copy(k).start()
        return carry
    lax.fori_loop(1, n, ids_begin, 0)
    all_ref[me] = ids_ref[...]
    w_begin()

    pad = jnp.zeros((64 - feat, 128), F32)
    for k in range(len(secs)):
        for c in load(k):
            c.wait()
        s, c = secs[k]
        m = max(0, min(c, nb - low - s))
        def turn(b, carry):
            a = raw_ref[:, pl.ds(pl.multiple_of(b * 128, 128), 128)]
            h = raw_ref[:, pl.ds(pl.multiple_of((low + b) * 128, 128), 128)]
            tab_ref[pl.ds(pl.multiple_of(b * 128, 128), 128), :] = jnp.concatenate([a, pad, h, pad], axis=0).T
            return carry
        lax.fori_loop(s, s + m, turn, 0, unroll=3)
        for b in range(s + m, s + c):
            a = raw_ref[:, b * 128:(b + 1) * 128]
            tab_ref[b * 128:(b + 1) * 128, :] = jnp.concatenate([a, pad, pad, jnp.zeros((feat, 128), F32)], axis=0).T

    def ids_end(k, carry):
        ids_copy(k).wait()
        return carry
    lax.fori_loop(1, n, ids_end, 0)
    def to_smem(s):
        return pltpu.make_async_copy(all_ref.at[d * fs + s, pl.ds(0, lines)], smem_ref.at[s], smem_sem.at[s])
    def smem_begin(s, carry):
        to_smem(s).start()
        return carry
    def smem_end(s, carry):
        to_smem(s).wait()
        return carry
    lax.fori_loop(0, fs, smem_begin, 0)
    lax.fori_loop(0, fs, smem_end, 0)

    U = 32
    def fetch(s, put):
        def grp(g, carry):
            line, base = lax.div(g, 128 // U), lax.rem(g, 128 // U) * U
            for j in range(U):
                i = smem_ref[s, line, base + j]
                i = jnp.where(i >= low * 128, i - low * 128, i)
                row_ref[pl.ds(pl.multiple_of(g * U, U) + j, 1), :] = tab_ref[pl.ds(i, 1), :]
            return carry
        lax.fori_loop(0, length // U, grp, 0)
        ids = all_ref[d * fs + s]
        for c in range(lines):
            t = row_ref[c * 128:(c + 1) * 128, :].T
            high = ids[c:c + 1] >= low * 128
            put(c, jnp.where(high, t[64:64 + feat], t[:feat]).astype(BF16))
    def x_copy(k):
        s = lax.rem(f + k, fs)
        return remote(picked_ref.at[s], x_ref.at[f], x_send.at[k], x_recv.at[k], (d, s))
    def one(k, carry):
        s = lax.rem(f + k, fs)
        def put(c, v):
            picked_ref[s, :, c * 128:(c + 1) * 128] = v
        fetch(s, put)
        x_copy(k).start()
        return carry
    steps = parts + 1
    marks = [1 + (fs - 1) * i // steps for i in range(steps + 1)]
    for i in range(steps):
        lax.fori_loop(marks[i], marks[i + 1], one, 0)
        w_middle(i)
    def mine(c, v):
        x_ref[f, :, c * 128:(c + 1) * 128] = v
    fetch(f, mine)
    w_end()
    def x_end(k, carry):
        x_copy(k).wait()
        return carry
    lax.fori_loop(1, fs, x_end, 0)

def front(ids, w, emb, length, ident):
    fs, dps = lax.axis_size("fsdp"), lax.axis_size("dp")
    feat, vocab = emb.shape
    low = halves(vocab)[1]
    vm = pl.BlockSpec(memory_space=pltpu.VMEM)
    parts = cuts(w.shape[0])[0]
    def sem(*shape):
        return pltpu.SemaphoreType.DMA(shape)
    return pl.pallas_call(
        functools.partial(front_kernel, fs=fs, dps=dps), name="front",
        in_specs=[vm, vm, pl.BlockSpec(memory_space=pl.ANY)], out_specs=[vm, vm, vm],
        out_shape=[jax.ShapeDtypeStruct((fs * dps,) + ids.shape, ids.dtype), jax.ShapeDtypeStruct((fs, feat, length), BF16),
                   jax.ShapeDtypeStruct((fs,) + w.shape, w.dtype)],
        scratch_shapes=[pltpu.VMEM((low * 128, 128), F32), pltpu.VMEM((feat, vocab), F32), pltpu.VMEM((length, 128), F32),
                        pltpu.VMEM((fs, feat, length), BF16), pltpu.SMEM((fs, length // 128, 128), jnp.int32),
                        sem(12), sem(fs * dps), sem(fs * dps), sem(fs), sem(fs), sem(fs), sem(fs * parts), sem(fs, parts)],
        cost_estimate=cost(85), compiler_params=comm_params(ident))(ids, w, emb)
def adam_kernel(factor_ref, w_ref, one_ref, two_ref, avg_ref, *refs, rate, first):
    outs = refs[-4:]
    grads = [r[...].astype(F32) for r in refs[:-4]]
    if first is None:
        g = grads[0]
    else:
        g = jnp.where(pl.program_id(0) < first, grads[0] + grads[1], grads[2] + grads[3])
    new, one, two = adamw(w_ref[...], one_ref[...], two_ref[...], g * factor_ref[0], rate)
    outs[0][...] = new
    outs[1][...] = one
    outs[2][...] = two
    outs[3][...] = ema_decay * avg_ref[...] + (1 - ema_decay) * new

def adam_table(factor, w, one, two, avg, grads, rate, by_rows):
    rows, cols = w.shape
    if by_rows:
        block, first = (768, cols), grads[0].shape[0] // 768
        steps = -(-rows // 768)
        spec = pl.BlockSpec(block, lambda i: (i, 0))
        early = pl.BlockSpec(block, lambda i: (jnp.minimum(i, first - 1), 0))
        late = pl.BlockSpec(block, lambda i: (jnp.maximum(i - first, 0), 0))
        gspecs = [early, early, late, late]
    else:
        block, first = (rows, 12672), None
        steps = -(-cols // 12672)
        spec = pl.BlockSpec(block, lambda i: (0, i))
        gspecs = [spec]
    shape = jax.ShapeDtypeStruct(w.shape, F32)
    return pl.pallas_call(
        functools.partial(adam_kernel, rate=rate, first=first), name="adam_rows" if by_rows else "adam_columns",
        grid=(steps,), cost_estimate=cost(1),
        in_specs=[pl.BlockSpec(memory_space=pltpu.SMEM)] + [spec] * 4 + gspecs, out_specs=[spec] * 4, out_shape=[shape] * 4,
        compiler_params=params())(factor.reshape(1), w, one, two, avg, *grads)
def shampoo_kernel(factor_ref, w_ref, grad_ref, left_ref, right_ref, root_ref, whole_ref, full_ref, avg_ref,
                   new_ref, clip_ref, left_out, right_out, avg_out):
    columns, width = right_ref.shape[1:]
    factor = factor_ref[0]
    mix = (1 - stat_decay) * factor * factor
    full = full_ref[0]
    grad = grad_ref[0]
    at = lax.axis_index("fsdp") * columns + lax.broadcasted_iota(jnp.int32, (columns, width), 0)
    pick = (at == lax.broadcasted_iota(jnp.int32, (columns, width), 1)).astype(BF16)
    turned = dot(pick, full, 1, 1).astype(BF16)
    left_out[0] = stat_decay * left_ref[0] + mix * dot(grad.astype(BF16), full, 1, 1)
    right_out[0] = stat_decay * right_ref[0] + mix * dot(turned, full, 1, 0)
    part = dot(root_ref[0].astype(BF16), full, 1, 0)
    update = dot(part.astype(BF16), whole_ref[0], 1, 0) * factor
    w = w_ref[0]
    new = w - rate_shampoo * (update + shampoo_decay * w)
    new_ref[0] = new
    clip_ref[0] = grad * factor
    avg_out[0] = ema_decay * avg_ref[0] + (1 - ema_decay) * new

def shampoo(factor, w, grad, left, right, root, whole_root, full, avg, name):
    def one(x):
        return pl.BlockSpec((1,) + x.shape[1:], lambda i: (i, 0, 0))
    ins = (w, grad, left, right, root, whole_root, full, avg)
    outs = (w, w, left, right, w)
    return pl.pallas_call(
        shampoo_kernel, grid=(w.shape[0],), name=name, cost_estimate=cost(10),
        in_specs=[pl.BlockSpec(memory_space=pltpu.SMEM)] + [one(x) for x in ins],
        out_specs=[one(x) for x in outs], out_shape=[jax.ShapeDtypeStruct(x.shape, F32) for x in outs],
        compiler_params=params())(factor.reshape(1), *ins)
MASK_ID = 50257
STRATA = 16
STEP = 10

clip_level = 1.0
beta_one = 0.9
beta_two = 0.95
adam_eps = 1e-08
adam_decay = 0.01
rate_embed = 2.0
rate_out = 0.25
rate_gain = 0.5
rate_shampoo = 0.3
shampoo_decay = 0.01
stat_decay = 0.5
ema_decay = 0.7


def rotary_tables(length, half_width):
    inverse = 10000.0 ** (-np.arange(half_width, dtype=np.float64) / half_width)
    angles = inverse[:, None] * np.arange(length, dtype=np.float64)[None, :]
    return (jnp.asarray(np.cos(angles), F32), jnp.asarray(np.sin(angles), F32))


def adamw(weight, moment_one, moment_two, gradient, step_rate):
    one_new = beta_one * moment_one + (1 - beta_one) * gradient
    two_new = beta_two * moment_two + (1 - beta_two) * gradient * gradient
    one_hat = one_new * (1 / (1 - beta_one**STEP))
    two_hat = two_new * (1 / (1 - beta_two**STEP))
    weight_new = weight - step_rate * (
        one_hat / (jnp.sqrt(two_hat) + adam_eps) + adam_decay * weight
    )
    return (weight_new, one_new, two_new)


def dp_other(x):
    return lax.ppermute(x, "dp", [(0, 1), (1, 0)])


def dp_sum(x):
    count = lax.axis_size("dp")
    if count == 1:
        return x.astype(F32)
    if count == 2:
        return x.astype(F32) + dp_other(x).astype(F32)
    return lax.psum(x, "dp").astype(F32)


def spread_out(x):
    return lax.all_gather(x.astype(BF16), "fsdp", axis=1, tiled=True)


def per_device(
    tokens, positions, strata, groups, embedding, out_table, norm_gains, attention, feedforward,
    embed_moment_one, embed_moment_two, out_moment_one, out_moment_two, gain_moment_one, gain_moment_two,
    attention_left, attention_right, attention_left_root, attention_right_root,
    ff_left, ff_right, ff_left_root, ff_right_root,
    ema_embed, ema_out, ema_gains, ema_attention, ema_feedforward,
):
    fs = lax.axis_size("fsdp")
    dps = lax.axis_size("dp")
    me = lax.axis_index("fsdp")
    replica = lax.axis_index("dp")
    seq_count, length = tokens.shape
    slots = positions.shape[1]
    features, vocab = embedding.shape
    width = features * fs
    shard = out_table.shape[0]

    ff_w = spread_out(feedforward)

    counts = jnp.maximum(1, (strata + 1) * slots * (1 + groups) // (2 * STRATA))
    in_use = jnp.arange(slots, dtype=jnp.int32)[None, :] < counts[:, None]
    places = jnp.arange(length, dtype=jnp.int32)
    same = positions[0][:, None] == places[None, :]
    marked = jnp.any(same & in_use[0][:, None], axis=0)
    ids_in = jnp.where(marked, MASK_ID, tokens[0])
    targets = jnp.sum(jnp.where(same, tokens[0][None, :], 0), axis=1)
    packed = jnp.concatenate([ids_in, targets, counts])
    packed = jnp.pad(packed, (0, -packed.shape[0] % 1024))
    everyone, xT, attn_w = front(packed.reshape(-1, 128), attention.astype(BF16).reshape(-1, width), embedding, length, 1)
    everyone = everyone.reshape(fs * dps, -1)
    xT = xT.reshape(width, length)
    attn_w = attn_w.reshape(fs, 4, -1, width)
    group = lax.dynamic_slice_in_dim(everyone, replica * fs, fs, 0)
    all_ids = everyone[:, :length]
    group_ids = group[:, :length]
    group_targets = group[:, length:length + slots]
    group_counts = group[:, length + slots]

    cosT, sinT = rotary_tables(length, HEAD // 2)
    gain = [norm_gains.T] * 3
    place = positions[0][:, None]
    hT, qT, kT, vT, mixT, lse = attn_fwd(xT, gain[0], cosT, sinT, attn_w)
    hT, source = lax.optimization_barrier((hT, out_table))
    low, turned = table_both(source)
    mixT, low, turned = lax.optimization_barrier((mixT, low, turned))
    x2, h2, x3, head = ff_fwd(xT, mixT, gain[1], gain[2], place, attn_w, ff_w)

    rows = rows_gather(head, 3)
    first_id = me * shard
    limit = jnp.clip(MASK_ID - first_id, 0, shard).reshape(1)
    least = min(shard, MASK_ID - (fs - 1) * shard)
    meta, seq, slot, weight = plan(group_counts, slots, length)
    nblk = seq.shape[0] // RB
    target = (spread(group_targets, seq, slot) - first_id).reshape(nblk, 1, RB)
    inside = fs * slots <= 4096
    if not inside:
        rows = jnp.take(rows.reshape(fs * slots, width), jnp.clip(seq * slots + slot, 0, fs * slots - 1), axis=0)
    comp, lse_own, chosen = vocab_fwd(meta, limit, rows, low, target, least)
    lse_own, root = lax.optimization_barrier((lse_own, attention_right_root))
    attn_root = spread_out(root)
    lse_sum = small_gather(lse_own, 4, finish=lse_finish, name="lse_gather")
    own_loss = jnp.sum(weight * (jnp.where(seq == me, lse_sum.reshape(-1), 0.0) - chosen.reshape(-1)))
    scale = weight / (seq_count * fs * dps)
    out_one, out_two, row_grads = vocab_bwd(
        meta, limit, comp, low, turned, target, lse_sum, scale.reshape(nblk, 1, RB),
        least, fs, slots, inside,
    )
    if not inside:
        at = jnp.arange(slots, dtype=jnp.int32)[None, :]
        row_grads = jnp.take(row_grads, jnp.minimum(meta[1][:, None] * 16 + at, seq.shape[0] - 1), axis=0)
        row_grads = jnp.where((at < group_counts[:, None])[:, :, None], row_grads, 0)
    own_rows = rows_reduce(row_grads, 5)
    halves_low = (out_one, out_two)
    if dps == 2:
        others = [dp_other(x) for x in halves_low]

    own_rows, attn_root, root = lax.optimization_barrier((own_rows, attn_root, ff_right_root))
    ff_root = spread_out(root)
    second, gg2, gg3, dff = ff_bwd(x3, x2, h2, own_rows, place, gain[1], gain[2], ff_w, fs)
    if dps == 2:
        second, others[0], ff_root = lax.optimization_barrier((second, others[0], ff_root))
    first, gg1, dattn = attn_bwd(xT, gain[0], cosT, sinT, second, hT, qT, kT, vT, mixT, lse, attn_w, fs)

    ff_part = lax.psum_scatter(dff.reshape(-1, width), "fsdp", scatter_dimension=0, tiled=True)

    aux = jnp.concatenate([jnp.concatenate([gg1, gg2, gg3], axis=1).T.reshape(-1), own_loss[None]])
    aux = jnp.pad(aux, (0, -aux.shape[0] % 1024)).reshape(-1, 128)
    if dps == 2:
        first, others[1] = lax.optimization_barrier((first, others[1]))
        pairs = (halves_low[0], others[0], halves_low[1], others[1])
    else:
        pairs = ()
        out_grad = jnp.concatenate([dp_sum(a) for a in halves_low])[:shard]
        out_sq = jnp.sum(out_grad * out_grad)
    out = list(exchange(first.reshape(fs, features, length), 6, dps == 2, "gradients", aux, dattn.reshape(fs, -1, width), pairs))
    if dps == 2:
        out_sq = jnp.sum(out.pop())
    attn_grad = out[-1].reshape(4, -1, width)
    aux, ff_part = lax.optimization_barrier((out[-2], ff_part))
    ff_grad = dp_sum(ff_part.reshape(2, -1, width))
    if dps != 2:
        attn_grad = dp_sum(attn_grad.astype(BF16))
    if dps == 2:
        parts, other = out[:2]
        other_ids = lax.dynamic_slice_in_dim(everyone, (1 - replica) * fs, fs, 0)[:, :length]
        embed_grad, embed_sq = scatter(jnp.concatenate([group_ids, other_ids]), (parts, other), vocab, 2)
        embed_sq = jnp.sum(embed_sq)
    else:
        parts = out[0]
        embed_grad = dp_sum(scatter(group_ids, (parts,), vocab, 2)[0].astype(BF16))
        embed_sq = jnp.sum(embed_grad * embed_grad)
        if dps > 1:
            aux = lax.psum(aux, "dp")
    aux = aux.reshape(-1)
    gain_grad, loss_sum = aux[: 3 * width].reshape(3, width), aux[3 * width]
    squares = (
        jnp.sum(attn_grad * attn_grad)
        + jnp.sum(ff_grad * ff_grad)
        + embed_sq
        + out_sq
    )
    ff_grad, embed_sq = lax.optimization_barrier((ff_grad, embed_sq))
    attn_full, ff_full = spread_out(attn_grad), spread_out(ff_grad)
    squares, attn_full = lax.optimization_barrier((squares, attn_full))
    squares = small_gather(jnp.full((8, 128), squares), 7, finish=sum_finish, name="squares")[0, 0]
    clip_norm = jnp.sqrt(squares + jnp.sum(gain_grad * gain_grad))
    factor = jnp.minimum(1.0, clip_level / clip_norm)
    embed_new, embed_one_new, embed_two_new, ema_embed_new = adam_table(
        factor, embedding, embed_moment_one, embed_moment_two, ema_embed, [embed_grad], rate_embed, False
    )
    if dps == 2:
        out_new, out_one_new, out_two_new, ema_out_new = adam_table(
            factor, out_table, out_moment_one, out_moment_two, ema_out,
            [halves_low[0], others[0], halves_low[1], others[1]], rate_out, True
        )
    else:
        out_new, out_one_new, out_two_new = adamw(
            out_table, out_moment_one, out_moment_two, out_grad * factor, rate_out
        )
        ema_out_new = ema_decay * ema_out + (1 - ema_decay) * out_new
    gains_new, gains_one_new, gains_two_new = adamw(
        norm_gains, gain_moment_one, gain_moment_two, gain_grad * factor, rate_gain
    )

    attention_new, attn_clip, attention_left_new, attention_right_new, ema_attn_new = shampoo(
        factor, attention, attn_grad, attention_left, attention_right, attention_left_root,
        attn_root, attn_full, ema_attention, "shampoo_attention"
    )
    ff_new, ff_clip, ff_left_new, ff_right_new, ema_ff_new = shampoo(
        factor, feedforward, ff_grad, ff_left, ff_right, ff_left_root,
        ff_root, ff_full, ema_feedforward, "shampoo_ff"
    )

    def averaged(average, new):
        return ema_decay * average + (1 - ema_decay) * new

    return (
        loss_sum, clip_norm, embed_new, embed_one_new, embed_two_new, out_new, out_one_new, out_two_new,
        gains_new, gains_one_new, gains_two_new, attention_new, attn_clip, attention_left_new, attention_right_new,
        ff_new, ff_clip, ff_left_new, ff_right_new,
        ema_embed_new, ema_out_new, averaged(ema_gains, gains_new),
        ema_attn_new, ema_ff_new,
    )


def solution(mesh):
    seqs, rows, stack, none = P(("dp", "fsdp")), P("fsdp", None), P(None, "fsdp", None), P()
    in_specs = (
        seqs, seqs, seqs, seqs, rows, rows, none, stack, stack, rows, rows, rows, rows, none, none,
        stack, stack, stack, stack, stack, stack, stack, stack, rows, rows, none, stack, stack,
    )
    out_specs = (
        none, none, rows, rows, rows, rows, rows, rows, none, none, none, stack, stack, stack, stack,
        stack, stack, stack, stack, rows, rows, none, stack, stack,
    )
    return jax.shard_map(
        per_device, mesh=mesh, in_specs=in_specs, out_specs=out_specs, check_vma=False
    )
```

```python
import functools

import jax
import jax.numpy as jnp
import numpy as np
from jax import lax
from jax.experimental import pallas as pl
from jax.experimental.pallas import tpu as pltpu
from jax.sharding import PartitionSpec as P

F32, BF16 = jnp.float32, jnp.bfloat16
HEAD = 64
EPS = 1e-5
BSTEP = 1024
VL = 60 * 1024 * 1024

def dot(a, b, ca, cb):
    return lax.dot_general(a, b, (((ca,), (cb,)), ((), ())), preferred_element_type=F32)

def params(limit=VL):
    return pltpu.CompilerParams(vmem_limit_bytes=limit)

def cost(us):
    return pl.CostEstimate(flops=int(us * 1.15e9), bytes_accessed=0, transcendentals=0)

def whole(shape):
    return pl.BlockSpec(shape, lambda *a: (0,) * len(shape))

def attn_fwd_kernel(x_ref, gain_ref, cos_ref, sin_ref, w_ref, h_ref, q_ref, k_ref, v_ref, m_ref, lse_ref, kn_ref):
    width, length = x_ref.shape
    block = q_ref.shape[0]
    heads = block // HEAD
    half = HEAD // 2

    @pl.when(pl.program_id(0) == 0)
    def _():
        def cols(c, carry):
            at = pl.ds(pl.multiple_of(c * 128, 128), 128)
            x = x_ref[:, at].astype(F32)
            centred = x - jnp.mean(x, axis=0, keepdims=True)
            spread = jnp.mean(centred * centred, axis=0, keepdims=True)
            h_ref[:, at] = (centred * lax.rsqrt(spread + EPS) * gain_ref[:, 0:1]).astype(BF16)
            return carry
        lax.fori_loop(0, length // 128, cols, 0)

    cosine, sine = cos_ref[...], sin_ref[...]
    hidden = h_ref[...]
    for j, out in ((0, q_ref), (1, k_ref)):
        p = dot(w_ref[:, j].reshape(width, block), hidden, 0, 0)
        for h in range(heads):
            a = p[h * HEAD : h * HEAD + half]
            b = p[h * HEAD + half : (h + 1) * HEAD]
            ra = (a * cosine - b * sine).astype(BF16)
            rb = (b * cosine + a * sine).astype(BF16)
            if j == 0:
                ra, rb = ra * 0.125, rb * 0.125
            out[h * HEAD : h * HEAD + half, :] = ra
            out[h * HEAD + half : (h + 1) * HEAD, :] = rb
    v_ref[...] = dot(w_ref[:, 2].reshape(width, block), hidden, 0, 0).astype(BF16)
    for h in range(heads):
        rows = slice(h * HEAD, (h + 1) * HEAD)
        kn_ref[h] = k_ref[rows, :].T
    def one(h, carry):
        rows = pl.ds(pl.multiple_of(h * HEAD, HEAD), HEAD)
        s = dot(kn_ref[h], q_ref[rows, :], 1, 0)
        top = jnp.max(s, axis=0, keepdims=True)
        e = jnp.exp(s - top)
        total = jnp.sum(e, axis=0, keepdims=True)
        o = dot(v_ref[rows, :], e.astype(BF16), 1, 0)
        m_ref[rows, :] = (o / total).astype(BF16)
        lse_ref[0, pl.ds(h, 1), :] = top + jnp.log(total)
        return carry
    lax.fori_loop(0, heads, one, 0)

def attn_fwd(xT, gain, cosT, sinT, w):
    width, length = xT.shape
    block = 256
    n = width // block
    col = pl.BlockSpec((block, length), lambda i: (i, 0))
    t = jax.ShapeDtypeStruct((width, length), BF16)
    return pl.pallas_call(
        attn_fwd_kernel, grid=(n,), name="attn_fwd", cost_estimate=cost(34),
        in_specs=[whole((width, length)), whole(gain.shape), whole(cosT.shape), whole(sinT.shape),
                  pl.BlockSpec((w.shape[0], 3, w.shape[2], block), lambda i: (0, 0, 0, i))],
        out_specs=[whole((width, length)), col, col, col, col, pl.BlockSpec((1, 8, length), lambda i: (i, 0, 0))],
        out_shape=[t, t, t, t, t, jax.ShapeDtypeStruct((n, 8, length), F32)],
        scratch_shapes=[pltpu.VMEM((block // HEAD, length, HEAD), BF16)],
        compiler_params=params(),
    )(xT, gain, cosT, sinT, w)

def attn_bwd_kernel(x_ref, gain_ref, cos_ref, sin_ref, sg_ref, h_ref, q_ref, k_ref, v_ref, m_ref, lse_ref, w_ref, wo_ref,
                    first_ref, gg_ref, dw_ref, hg_ref, low_ref, do_ref, kn_ref, vn_ref, dk_ref, dv_ref, dq_ref, dwo_ref):
    width, length = x_ref.shape
    block = q_ref.shape[0]
    heads = block // HEAD
    half = HEAD // 2
    step = min(BSTEP, length)
    i = pl.program_id(0)

    @pl.when(i == 0)
    def _():
        low_ref[...] = sg_ref[...].astype(BF16)
        dwo_ref[...] = wo_ref[:, 0].reshape(width, width)
        hg_ref[...] = jnp.zeros_like(hg_ref)

    mine = pl.ds(pl.multiple_of(i * block, block), block)
    do_ref[...] = dot(dwo_ref[mine, :], low_ref[...], 1, 0).astype(BF16)
    fs, _, each, _ = dw_ref.shape
    dwo_ref[mine, :] = dot(m_ref[...], low_ref[...], 1, 1).astype(BF16)
    cosine, sine = cos_ref[...], sin_ref[...]
    for h in range(heads):
        rows = slice(h * HEAD, (h + 1) * HEAD)
        kn_ref[h] = k_ref[rows, :].T
        vn_ref[h] = v_ref[rows, :].T
    def one(h, carry):
        rows = pl.ds(pl.multiple_of(h * HEAD, HEAD), HEAD)
        for c in range(length // step):
            at = slice(c * step, (c + 1) * step)
            s = dot(kn_ref[h], q_ref[rows, at], 1, 0)
            p = jnp.exp(s - lse_ref[0, pl.ds(h, 1), at])
            dp = dot(vn_ref[h], do_ref[rows, at], 1, 0)
            centre = jnp.sum(p * dp, axis=0, keepdims=True)
            ds = (p * (dp - centre)).astype(BF16)
            pb = p.astype(BF16)
            dv = dot(pb, do_ref[rows, at], 1, 1).T
            dk = dot(ds, q_ref[rows, at], 1, 1).T
            if c == 0:
                dv_ref[rows, :] = dv
                dk_ref[rows, :] = dk
            else:
                dv_ref[rows, :] += dv
                dk_ref[rows, :] += dk
            dq_ref[rows, at] = dot(k_ref[rows, :], ds, 1, 0) * 0.125
        return carry
    lax.fori_loop(0, heads, one, 0)
    hidden = h_ref[...]
    for j, ref in ((0, dq_ref), (1, dk_ref), (2, dv_ref)):
        if j == 2:
            g = ref[...].astype(BF16)
        else:
            parts = []
            for h in range(heads):
                a = ref[h * HEAD : h * HEAD + half, :]
                b = ref[h * HEAD + half : (h + 1) * HEAD, :]
                parts += [(a * cosine + b * sine).astype(BF16), (b * cosine - a * sine).astype(BF16)]
            g = jnp.concatenate(parts, axis=0)
        dw_ref[:, j, :, pl.ds(pl.multiple_of(i * block, block), block)] = dot(hidden, g, 1, 1).astype(BF16).reshape(fs, each, block)
        hg_ref[...] += dot(w_ref[:, j].reshape(width, block), g, 1, 0)

    @pl.when(i == pl.num_programs(0) - 1)
    def _():
        dw_ref[:, 3] = dwo_ref[...].reshape(fs, each, width)
        def cols(c, acc):
            at = pl.ds(pl.multiple_of(c * 128, 128), 128)
            dx, gg = ln_back(x_ref[:, at].astype(F32), hg_ref[:, at], gain_ref[:, 0:1])
            first_ref[:, at] = (sg_ref[:, at] + dx).astype(BF16)
            return acc + gg
        acc = lax.fori_loop(0, length // 128, cols, jnp.zeros((width, 128), F32))
        gg_ref[...] = jnp.sum(acc, axis=1, keepdims=True)

def ln_back(x, g, gain):
    centred = x - jnp.mean(x, axis=0, keepdims=True)
    spread = jnp.mean(centred * centred, axis=0, keepdims=True)
    rs = lax.rsqrt(spread + EPS)
    xh = centred * rs
    gx = g * gain
    dx = rs * (gx - jnp.mean(gx, axis=0, keepdims=True) - xh * jnp.mean(gx * xh, axis=0, keepdims=True))
    return dx, g * xh

def attn_bwd(xT, gain, cosT, sinT, sg, hT, q, k, v, m, lse, w, fs):
    width, length = xT.shape
    block = 256
    n = width // block
    col = pl.BlockSpec((block, length), lambda i: (i, 0))
    full = whole((width, length))
    return pl.pallas_call(
        attn_bwd_kernel, grid=(n,), name="attn_bwd", cost_estimate=cost(62),
        in_specs=[full, whole(gain.shape), whole(cosT.shape), whole(sinT.shape), full, full, col, col, col, col,
                  pl.BlockSpec((1, 8, length), lambda i: (i, 0, 0)),
                  pl.BlockSpec((w.shape[0], 3, w.shape[2], block), lambda i: (0, 0, 0, i)),
                  pl.BlockSpec((w.shape[0], 1, w.shape[2], width), lambda i: (0, 3, 0, 0))],
        out_specs=[full, whole((width, 1)), whole((fs, 4, width // fs, width))],
        out_shape=[jax.ShapeDtypeStruct((width, length), BF16), jax.ShapeDtypeStruct((width, 1), F32),
                   jax.ShapeDtypeStruct((fs, 4, width // fs, width), BF16)],
        scratch_shapes=[pltpu.VMEM((width, length), F32), pltpu.VMEM((width, length), BF16), pltpu.VMEM((block, length), BF16),
                        pltpu.VMEM((block // HEAD, length, HEAD), BF16), pltpu.VMEM((block // HEAD, length, HEAD), BF16),
                        pltpu.VMEM((block, length), F32), pltpu.VMEM((block, length), F32), pltpu.VMEM((block, length), F32),
                        pltpu.VMEM((width, width), BF16)],
        compiler_params=params(),
    )(xT, gain, cosT, sinT, sg, hT, q, k, v, m, lse, w, w)
def ff_fwd_kernel(x_ref, m_ref, g2_ref, g3_ref, pos_ref, wo_ref, up_a, up_b, down_a, down_b,
                  x2_ref, h2_ref, x3_ref, head_ref, fin_ref):
    width, length = x_ref.shape
    i = pl.program_id(0)

    @pl.when(i == 0)
    def _():
        x2_ref[...] = x_ref[...].astype(F32) + dot(wo_ref[:, 0].reshape(width, width), m_ref[...], 0, 0)
        x3_ref[...] = x2_ref[...]
        def cols(c, carry):
            at = pl.ds(pl.multiple_of(c * 128, 128), 128)
            h2_ref[:, at] = ln(x2_ref[:, at], g2_ref[:, 1:2]).astype(BF16)
            return carry
        lax.fori_loop(0, length // 128, cols, 0)

    up = jnp.concatenate([up_a[0], up_b[0]], axis=0)
    down = jnp.concatenate([down_a[0], down_b[0]], axis=0)
    pre = dot(up, h2_ref[...], 1, 0)
    act = jax.nn.gelu(pre, approximate=True).astype(BF16)
    x3_ref[...] += dot(down, act, 0, 0)

    @pl.when(i == pl.num_programs(0) - 1)
    def _():
        def cols(c, carry):
            at = pl.ds(pl.multiple_of(c * 128, 128), 128)
            fin_ref[:, at] = ln(x3_ref[:, at], g3_ref[:, 2:3]).astype(BF16)
            return carry
        lax.fori_loop(0, length // 128, cols, 0)
        slots = pos_ref.shape[0]
        onehot = (pos_ref[...] == lax.broadcasted_iota(jnp.int32, (slots, length), 1)).astype(BF16)
        head_ref[...] = dot(onehot, fin_ref[...], 1, 1).astype(BF16)

def ln(x, gain):
    centred = x - jnp.mean(x, axis=0, keepdims=True)
    spread = jnp.mean(centred * centred, axis=0, keepdims=True)
    return centred * lax.rsqrt(spread + EPS) * gain

def halves_of(half, width):
    up, down = (pl.BlockSpec((1, half, width), lambda i, j=j: (j, i, 0)) for j in range(2))
    return [up, up, down, down]

def ff_fwd(xT, m, g2, g3, pos, attn_w, ff_w, each):
    width, length = xT.shape
    half = each * max(1, 384 // each)
    n = ff_w[0].shape[1] // half
    slots = pos.shape[0]
    full = whole((width, length))
    f = jax.ShapeDtypeStruct((width, length), F32)
    return pl.pallas_call(
        ff_fwd_kernel, grid=(n,), name="ff_fwd", cost_estimate=cost(34),
        in_specs=[full, full, whole(g2.shape), whole(g3.shape), whole((slots, 1)),
                  pl.BlockSpec((attn_w.shape[0], 1, attn_w.shape[2], width), lambda i: (0, 3, 0, 0)),
                  ] + halves_of(half, width),
        out_specs=[full, full, full, whole((slots, width))],
        out_shape=[f, jax.ShapeDtypeStruct((width, length), BF16), f, jax.ShapeDtypeStruct((slots, width), BF16)],
        scratch_shapes=[pltpu.VMEM((width, length), BF16)],
        compiler_params=params(),
    )(xT, m, g2, g3, pos, attn_w, ff_w[0], ff_w[1], ff_w[0], ff_w[1])

def ff_bwd_kernel(x3_ref, x2_ref, h2_ref, rg_ref, pos_ref, g2_ref, g3_ref, up_a, up_b, down_a, down_b,
                  sg_ref, gg2_ref, gg3_ref, dw_ref, low_ref, hg_ref):
    width, length = x3_ref.shape
    i = pl.program_id(0)
    slots = pos_ref.shape[0]

    @pl.when(i == 0)
    def _():
        rows = rg_ref[...]
        high = rows.astype(BF16)
        rest = (rows - high.astype(F32)).astype(BF16)
        hg_ref[...] = jnp.zeros_like(hg_ref)
        def cols(c, acc):
            at = pl.ds(pl.multiple_of(c * 128, 128), 128)
            onehot = (pos_ref[...] == c * 128 + lax.broadcasted_iota(jnp.int32, (slots, 128), 1)).astype(BF16)
            fg = dot(high, onehot, 0, 0) + dot(rest, onehot, 0, 0)
            dx, gg = ln_back(x3_ref[:, at], fg, g3_ref[:, 2:3])
            sg_ref[:, at] = dx
            low_ref[:, at] = dx.astype(BF16)
            return acc + gg
        acc = lax.fori_loop(0, length // 128, cols, jnp.zeros((width, 128), F32))
        gg3_ref[...] = jnp.sum(acc, axis=1, keepdims=True)

    up = jnp.concatenate([up_a[0], up_b[0]], axis=0)
    down = jnp.concatenate([down_a[0], down_b[0]], axis=0)
    ag = dot(down, low_ref[...], 1, 0)
    pre = dot(up, h2_ref[...], 1, 0)
    c0, c1 = 0.7978845608028654, 0.044715
    t = jnp.tanh(c0 * (pre + c1 * pre * pre * pre))
    half = 0.5 * (1.0 + t)
    act = (pre * half).astype(BF16)
    slope = half + 0.5 * pre * (1.0 - t * t) * (c0 * (1.0 + 3.0 * c1 * pre * pre))
    pg = (slope * ag).astype(BF16)
    core = lax.rem(lax.axis_index("fsdp"), 2)
    count, _, each, _ = dw_ref.shape
    for j, grad in ((1, dot(act, low_ref[...], 1, 1)), (0, dot(pg, h2_ref[...], 1, 1))):
        grad = grad.astype(BF16)
        for s in range(count // 2):
            dw_ref[2 * s + core, j] = grad[s * each:(s + 1) * each]
            dw_ref[2 * s + 1 - core, j] = grad[(count // 2 + s) * each:(count // 2 + s + 1) * each]
    hg_ref[...] += dot(up, pg, 0, 0)

    @pl.when(i == pl.num_programs(0) - 1)
    def _():
        def cols(c, acc):
            at = pl.ds(pl.multiple_of(c * 128, 128), 128)
            dx, gg = ln_back(x2_ref[:, at], hg_ref[:, at], g2_ref[:, 1:2])
            sg_ref[:, at] += dx
            return acc + gg
        acc = lax.fori_loop(0, length // 128, cols, jnp.zeros((width, 128), F32))
        gg2_ref[...] = jnp.sum(acc, axis=1, keepdims=True)

def ff_bwd(x3, x2, h2, rg, pos, g2, g3, ff_w, fs):
    width, length = x3.shape
    hidden = 2 * ff_w[0].shape[1]
    each = hidden // fs
    half = each * max(1, 384 // each)
    block = 2 * half
    n = hidden // block
    slots = pos.shape[0]
    full = whole((width, length))
    wb = pl.BlockSpec((block // each, 2, each, width), lambda i: (i, 0, 0, 0))
    g = jax.ShapeDtypeStruct((width, 1), F32)
    return pl.pallas_call(
        ff_bwd_kernel, grid=(n,), name="ff_bwd", cost_estimate=cost(45),
        in_specs=[full, full, full, whole((slots, width)), whole((slots, 1)), whole(g2.shape), whole(g3.shape),
                  ] + halves_of(half, width),
        out_specs=[full, whole((width, 1)), whole((width, 1)), wb],
        out_shape=[jax.ShapeDtypeStruct((width, length), F32), g, g, jax.ShapeDtypeStruct((fs, 2, each, width), BF16)],
        scratch_shapes=[pltpu.VMEM((width, length), BF16), pltpu.VMEM((width, length), F32)],
        compiler_params=params(),
    )(x3, x2, h2, rg, pos, g2, g3, ff_w[0], ff_w[1], ff_w[0], ff_w[1])
RB = 256
FCH, BCH = 8, 8

def pick(n, top=8):
    return max(k for k in range(1, top + 1) if n % k == 0)

def table_kernel(source_ref, low_ref, turned_ref, *, shard):
    block = source_ref.shape[0]
    ids = pl.program_id(0) * block + lax.broadcasted_iota(jnp.int32, source_ref.shape, 0)
    low = jnp.where(ids < shard, source_ref[...], 0.0).astype(BF16)
    low_ref[...] = low
    turned_ref[...] = low.T

def table_both(table):
    shard, width = table.shape
    vocab = -(-shard // 128) * 128
    block = 640 if vocab % 640 == 0 else 128
    return pl.pallas_call(
        functools.partial(table_kernel, shard=shard), name="table_both", grid=(vocab // block,), cost_estimate=cost(12),
        in_specs=[pl.BlockSpec((block, width), lambda i: (i, 0))],
        out_specs=[pl.BlockSpec((block, width), lambda i: (i, 0)), pl.BlockSpec((width, block), lambda i: (0, i))],
        out_shape=[jax.ShapeDtypeStruct((vocab, width), BF16), jax.ShapeDtypeStruct((width, vocab), BF16)],
        compiler_params=params())(table)

def compact(meta_ref, rows_ref, comp_ref):
    nseq, slots, width = rows_ref.shape
    def clear(b, carry):
        comp_ref[pl.ds(pl.multiple_of(b * RB, RB), RB), :] = jnp.zeros((RB, width), BF16)
        return carry
    lax.fori_loop(0, meta_ref[2, 0], clear, 0)
    def seq(s, carry):
        def part(c, c2):
            comp_ref[pl.ds(pl.multiple_of((meta_ref[1, s] + c) * 16, 16), 16), :] = rows_ref[s, pl.ds(pl.multiple_of(c * 16, 16), 16), :]
            return c2
        lax.fori_loop(0, meta_ref[0, s], part, 0)
        return carry
    lax.fori_loop(0, nseq, seq, 0)

def vocab_fwd_kernel(meta_ref, limit_ref, rows_ref, table_ref, target_ref, lse_ref, chosen_ref, *outs, chunk, least, inside):
    comp_ref = outs[0] if inside else rows_ref
    vocab = table_ref.shape[0]
    if inside:
        nseq, slots, width = rows_ref.shape
        compact(meta_ref, rows_ref, comp_ref)
    lse_ref[...] = jnp.zeros_like(lse_ref)
    chosen_ref[...] = jnp.zeros_like(chosen_ref)
    limit = limit_ref[0]
    def block(b, carry):
        rows = comp_ref[pl.ds(pl.multiple_of(b * RB, RB), RB), :]
        target = target_ref[b]
        top = total = chosen = None
        for v in range(vocab // chunk):
            l = dot(table_ref[v * chunk:(v + 1) * chunk, :], rows, 1, 1)
            ids = v * chunk + lax.broadcasted_iota(jnp.int32, (chunk, RB), 0)
            hit = jnp.sum(jnp.where(ids == target, l, 0.0), axis=0, keepdims=True)
            if (v + 1) * chunk > least:
                l = jnp.where(ids < limit, l, -jnp.inf)
            m = jnp.max(l, axis=0, keepdims=True)
            if v == 0:
                top = m
                total = jnp.sum(jnp.exp(l - top), axis=0, keepdims=True)
                chosen = hit
            else:
                new = jnp.maximum(top, m)
                total = total * jnp.exp(top - new) + jnp.sum(jnp.exp(l - new), axis=0, keepdims=True)
                chosen = chosen + hit
                top = new
        lse_ref[b] = top + jnp.log(total)
        chosen_ref[b] = chosen
        return carry
    lax.fori_loop(0, meta_ref[2, 0], block, 0)

def vocab_fwd(meta, limit, rows, table, target, least):
    inside = rows.ndim == 3
    width = rows.shape[-1]
    nblk = target.shape[0]
    vocab = table.shape[0]
    chunk = 128 * pick(vocab // 128, FCH)
    smem = pl.BlockSpec(memory_space=pltpu.SMEM)
    vm = pl.BlockSpec(memory_space=pltpu.VMEM)
    st = jax.ShapeDtypeStruct((nblk, 1, RB), F32)
    comp = [jax.ShapeDtypeStruct((nblk * RB, width), BF16)] if inside else []
    out = pl.pallas_call(
        functools.partial(vocab_fwd_kernel, chunk=chunk, least=least, inside=inside), name="vocab_fwd", cost_estimate=cost(20),
        in_specs=[smem, smem, vm, vm, vm], out_specs=[vm] * (2 + len(comp)),
        out_shape=[st, st] + comp,
        compiler_params=params())(meta, limit, rows, table, target)
    return out[2] if inside else rows, out[0], out[1]

def vocab_bwd_kernel(meta_ref, limit_ref, comp_ref, table_ref, turned_ref, target_ref, lse_ref, scale_ref,
                     og_ref, og2_ref, rg_ref, acc_ref, rc_ref, low_ref, back_ref, sem, *, chunk, least, inside):
    vocab, width = table_ref.shape
    limit = limit_ref[0]
    nch = vocab // chunk
    def clear(b, carry):
        acc_ref[pl.ds(pl.multiple_of(b * 128, 128), 128), :] = jnp.zeros((128, width), F32)
        return carry
    lax.fori_loop(0, vocab // 128, clear, 0)
    def block(b, carry):
        rows = comp_ref[pl.ds(pl.multiple_of(b * RB, RB), RB), :]
        target, lse, scale = target_ref[b], lse_ref[b], scale_ref[b]
        rg = None
        for v in range(nch):
            l = dot(table_ref[v * chunk:(v + 1) * chunk, :], rows, 1, 1)
            ids = v * chunk + lax.broadcasted_iota(jnp.int32, (chunk, RB), 0)
            p = jnp.exp(l - lse)
            p = jnp.where(ids == target, p - 1.0, p)
            if (v + 1) * chunk > least:
                p = jnp.where(ids < limit, p, 0.0)
            g = (scale * p).astype(BF16)
            acc_ref[v * chunk:(v + 1) * chunk, :] += dot(g, rows, 1, 0)
            part = dot(turned_ref[:, v * chunk:(v + 1) * chunk], g, 1, 0)
            rg = part if rg is None else rg + part
        rc_ref[pl.ds(pl.multiple_of(b * RB, RB), RB), :] = rg.T.astype(BF16)
        return carry
    lax.fori_loop(0, meta_ref[2, 0], block, 0)
    if inside:
        nseq, slots, _ = back_ref.shape
        def seq(s, carry):
            back_ref[s] = jnp.zeros((slots, width), BF16)
            def part(c, c2):
                back_ref[s, pl.ds(pl.multiple_of(c * 16, 16), 16), :] = rc_ref[pl.ds(pl.multiple_of((meta_ref[1, s] + c) * 16, 16), 16), :]
                return c2
            lax.fori_loop(0, meta_ref[0, s], part, 0)
            return carry
        lax.fori_loop(0, nseq, seq, 0)
        out = pltpu.make_async_copy(back_ref, rg_ref, sem.at[0])
    else:
        out = pltpu.make_async_copy(rc_ref, rg_ref, sem.at[0])
    out.start()
    outs = [out]
    part = og_ref.shape[0]
    for v, (ref, start) in enumerate(((og_ref, 0), (og2_ref, part))):
        at = pl.ds(start, ref.shape[0])
        low_ref[at, :] = acc_ref[at, :].astype(BF16)
        outs.append(pltpu.make_async_copy(low_ref.at[at], ref, sem.at[1 + v]))
        outs[-1].start()
    for o in outs:
        o.wait()

def vocab_bwd(meta, limit, comp, table, turned, target, lse, scale, least, nseq, slots, inside):
    rows, width = comp.shape
    vocab = table.shape[0]
    chunk = 128 * pick(vocab // 128, BCH)
    smem = pl.BlockSpec(memory_space=pltpu.SMEM)
    vm = pl.BlockSpec(memory_space=pltpu.VMEM)
    hbm = pl.BlockSpec(memory_space=pl.ANY)
    shape = (nseq, slots, width) if inside else (rows, width)
    part = vocab // 256 * 128
    return pl.pallas_call(
        functools.partial(vocab_bwd_kernel, chunk=chunk, least=least, inside=inside), name="vocab_bwd", cost_estimate=cost(40),
        in_specs=[smem, smem] + [vm] * 6, out_specs=[hbm, hbm, hbm],
        out_shape=[jax.ShapeDtypeStruct((part, width), BF16), jax.ShapeDtypeStruct((vocab - part, width), BF16), jax.ShapeDtypeStruct(shape, BF16)],
        scratch_shapes=[pltpu.VMEM((vocab, width), F32), pltpu.VMEM((rows, width), BF16),
                        pltpu.VMEM((vocab, width), BF16), pltpu.VMEM(shape if inside else (1, 16, width), BF16),
                        pltpu.SemaphoreType.DMA((3,))],
        compiler_params=params())(meta, limit, comp, table, turned, target, lse, scale)

def plan(counts, slots, length):
    nseq = counts.shape[0]
    units = (counts + 15) // 16
    ends = jnp.cumsum(units)
    offs = ends - units
    total = ends[-1] * 16
    nblk = (total + RB - 1) // RB
    cap = (nseq * slots + RB - 1) // RB * RB
    at = jnp.arange(cap, dtype=jnp.int32)
    seq = jnp.minimum(jnp.sum((at[:, None] >= ends[None, :] * 16).astype(jnp.int32), axis=1), nseq - 1)
    mine = (seq[:, None] == jnp.arange(nseq, dtype=jnp.int32)[None, :])
    slot = at - jnp.sum(jnp.where(mine, offs[None, :] * 16, 0), axis=1)
    cnt = jnp.sum(jnp.where(mine, counts[None, :], 0), axis=1)
    live = slot < cnt
    weight = jnp.where(live, length / cnt.astype(F32), 0.0)
    meta = jnp.stack([units, offs, jnp.full((nseq,), nblk)]).astype(jnp.int32)
    return meta, seq, slot, weight

def spread(values, seq, slot):
    nseq, slots = values.shape
    parts = jnp.concatenate([values // 256, values % 256], axis=1).astype(BF16)
    mine = (seq[:, None] == jnp.arange(nseq, dtype=jnp.int32)[None, :]).astype(BF16)
    rows = jnp.dot(mine, parts, preferred_element_type=F32)
    hit = slot[:, None] == jnp.arange(slots, dtype=jnp.int32)[None, :]
    both = rows[:, :slots] * 256.0 + rows[:, slots:]
    return jnp.sum(jnp.where(hit, both, 0.0), axis=1).astype(jnp.int32)

def halves(vocab):
    nb = vocab // 128
    low = (nb + 1) // 2
    return nb, low

def sections(count, size):
    return [(s, min(size, count - s)) for s in range(0, count, size)]

def gather_kernel(ids_ref, flag_ref, emb_ref, out_ref, tab_ref, raw_ref, row_ref, sem):
    feat, vocab = emb_ref.shape
    nseq, _, length = out_ref.shape
    nb, low = halves(vocab)
    size = -(-low // 6)
    secs = sections(low, size)
    def copies(k):
        s, n = secs[k]
        out = [pltpu.make_async_copy(emb_ref.at[:, pl.ds(s * 128, n * 128)], raw_ref.at[:, pl.ds(s * 128, n * 128)], sem.at[2 * k])]
        m = min(n, nb - low - s)
        if m > 0:
            out.append(pltpu.make_async_copy(emb_ref.at[:, pl.ds((low + s) * 128, m * 128)], raw_ref.at[:, pl.ds((low + s) * 128, m * 128)], sem.at[2 * k + 1]))
        return out
    for k in range(len(secs)):
        for c in copies(k):
            c.start()
    pad = jnp.zeros((64 - feat, 128), F32)
    for k in range(len(secs)):
        for c in copies(k):
            c.wait()
        s, n = secs[k]
        m = max(0, min(n, nb - low - s))
        def turn(b, carry):
            a = raw_ref[:, pl.ds(pl.multiple_of(b * 128, 128), 128)]
            h = raw_ref[:, pl.ds(pl.multiple_of((low + b) * 128, 128), 128)]
            tab_ref[pl.ds(pl.multiple_of(b * 128, 128), 128), :] = jnp.concatenate([a, pad, h, pad], axis=0).T
            return carry
        lax.fori_loop(s, s + m, turn, 0, unroll=3)
        for b in range(s + m, s + n):
            a = raw_ref[:, b * 128:(b + 1) * 128]
            tab_ref[b * 128:(b + 1) * 128, :] = jnp.concatenate([a, pad, pad, jnp.zeros((feat, 128), F32)], axis=0).T
    U = 32
    def seq(s, carry):
        def grp(g, c2):
            base = pl.multiple_of(g * U, U)
            for j in range(U):
                i = ids_ref[s * length + base + j]
                row_ref[pl.ds(base + j, 1), :] = tab_ref[pl.ds(i, 1), :]
            return c2
        lax.fori_loop(0, length // U, grp, 0)
        for c in range(length // 128):
            t = row_ref[c * 128:(c + 1) * 128, :].T
            f = flag_ref[s, :, c * 128:(c + 1) * 128] > 0
            out_ref[s, :, c * 128:(c + 1) * 128] = jnp.where(f, t[64:64 + feat], t[:feat]).astype(BF16)
        return carry
    lax.fori_loop(0, nseq, seq, 0)

def split_ids(ids, vocab):
    nb, low = halves(vocab)
    high = ids >= low * 128
    return jnp.where(high, ids - low * 128, ids), high.astype(jnp.int32)

def gather(ids, emb):
    nseq, length = ids.shape
    feat, vocab = emb.shape
    nb, low = halves(vocab)
    rid, flag = split_ids(ids, vocab)
    return pl.pallas_call(gather_kernel, name="emb_gather", cost_estimate=cost(32),
        in_specs=[pl.BlockSpec(memory_space=pltpu.SMEM), pl.BlockSpec(memory_space=pltpu.VMEM), pl.BlockSpec(memory_space=pl.ANY)],
        out_specs=pl.BlockSpec(memory_space=pltpu.VMEM),
        out_shape=jax.ShapeDtypeStruct((nseq, feat, length), BF16),
        scratch_shapes=[pltpu.VMEM((low * 128, 128), F32), pltpu.VMEM((feat, vocab), F32), pltpu.VMEM((length, 128), F32), pltpu.SemaphoreType.DMA((12,))],
        compiler_params=params())(rid.reshape(-1), flag.reshape(nseq, 1, length), emb)

def scatter_kernel(ids_ref, flag_ref, *refs, ng, per):
    g_refs = refs[:ng]
    out_ref, sq_ref, raw_ref, row_ref, sem = refs[ng:ng + 5]
    tabs = refs[ng + 5:]
    feat, vocab = out_ref.shape
    nseq, _, length = g_refs[0].shape
    nb, low = halves(vocab)
    zero128 = jnp.zeros((128, 128), F32)
    def zero(b, carry):
        for t in tabs:
            t[pl.ds(pl.multiple_of(b * 128, 128), 128), :] = zero128
        return carry
    lax.fori_loop(0, low, zero, 0)
    pad = jnp.zeros((64 - feat, 128), F32)
    U = 8
    streams = [(g, p) for g in range(ng) for p in range(per)]
    each = nseq // per
    def seq(s, carry):
        for k, (g, p) in enumerate(streams):
            q = p * each + s
            for c in range(length // 128):
                at = slice(c * 128, (c + 1) * 128)
                v = g_refs[g][q, :, at].astype(F32)
                f = flag_ref[g * nseq + q, :, at] > 0
                row_ref[k, at, :] = jnp.concatenate([jnp.where(f, 0.0, v), pad, jnp.where(f, v, 0.0), pad], axis=0).T
        def grp(n, c2):
            base = pl.multiple_of(n * U, U)
            for j in range(U):
                idx = [ids_ref[(g * nseq + p * each + s) * length + base + j] for g, p in streams]
                old = [tabs[k][pl.ds(idx[k], 1), :] for k in range(len(streams))]
                new = [old[k] + row_ref[k, pl.ds(base + j, 1), :] for k in range(len(streams))]
                for k in range(len(streams)):
                    tabs[k][pl.ds(idx[k], 1), :] = new[k]
            return c2
        lax.fori_loop(0, length // U, grp, 0)
        return carry
    lax.fori_loop(0, each, seq, 0)
    def tile(b):
        at = pl.ds(pl.multiple_of(b * 128, 128), 128)
        parts = [sum((tabs[g * per + p][at, :] for p in range(1, per)), tabs[g * per][at, :]) for g in range(ng)]
        return sum(parts[1:], parts[0]).T
    size = -(-low // 6)
    secs = sections(low, size)
    def copies(k):
        s, n = secs[k]
        out = [pltpu.make_async_copy(raw_ref.at[k % 2, 0, :, pl.ds(0, n * 128)], out_ref.at[:, pl.ds(s * 128, n * 128)], sem.at[2 * k])]
        m = min(n, nb - low - s)
        if m > 0:
            out.append(pltpu.make_async_copy(raw_ref.at[k % 2, 1, :, pl.ds(0, m * 128)], out_ref.at[:, pl.ds((low + s) * 128, m * 128)], sem.at[2 * k + 1]))
        return out
    squares = jnp.zeros((128, 128), F32)
    for k, (s, n) in enumerate(secs):
        if k >= 2:
            for c in copies(k - 2):
                c.wait()
        def turn(b, carry, s=s, k=k):
            t = tile(b)
            at = pl.ds(pl.multiple_of((b - s) * 128, 128), 128)
            raw_ref[k % 2, 0, :, at] = t[:feat]
            raw_ref[k % 2, 1, :, at] = t[64:64 + feat]
            return carry + t * t
        squares = lax.fori_loop(s, s + n, turn, squares, unroll=3)
        for c in copies(k):
            c.start()
    sq_ref[...] = squares
    for k in range(max(0, len(secs) - 2), len(secs)):
        for c in copies(k):
            c.wait()

def scatter(ids, gs, vocab, per):
    nseq, feat, length = gs[0].shape
    nb, low = halves(vocab)
    rid, flag = split_ids(ids, vocab)
    ng = len(gs)
    size = -(-low // 6)
    vm = pl.BlockSpec(memory_space=pltpu.VMEM)
    return pl.pallas_call(functools.partial(scatter_kernel, ng=ng, per=per), name="emb_scatter", cost_estimate=cost(1),
        in_specs=[pl.BlockSpec(memory_space=pltpu.SMEM), vm] + [vm] * ng,
        out_specs=[pl.BlockSpec(memory_space=pl.ANY), vm],
        out_shape=[jax.ShapeDtypeStruct((feat, vocab), F32), jax.ShapeDtypeStruct((128, 128), F32)],
        scratch_shapes=[pltpu.VMEM((2, 2, feat, size * 128), F32), pltpu.VMEM((ng * per, length, 128), F32), pltpu.SemaphoreType.DMA((12,))]
            + [pltpu.VMEM((low * 128, 128), F32)] * (ng * per),
        compiler_params=params(62 * 1024 * 1024))(rid.reshape(-1), flag.reshape(-1, 1, length), *gs)
AHEAD = 2
MESH_ID = pl.DeviceIdType.MESH

def comm_params(ident):
    return pltpu.CompilerParams(collective_id=ident, has_side_effects=True, vmem_limit_bytes=VL)

def meet(peers):
    barrier = pltpu.get_barrier_semaphore()
    for p in peers:
        pl.semaphore_signal(barrier, inc=1, device_id=p, device_id_type=MESH_ID)
    pl.semaphore_wait(barrier, len(peers))

def remote(src, dst, send, recv, peer):
    return pltpu.make_async_remote_copy(src_ref=src, dst_ref=dst, send_sem=send, recv_sem=recv, device_id=peer, device_id_type=MESH_ID)

def small_kernel(x_ref, *refs, fs, dps, wide, finish):
    out_ref = refs[0]
    got_ref = refs[1] if finish else out_ref
    send, recv = refs[-2:]
    d, f = lax.axis_index("dp"), lax.axis_index("fsdp")
    n = fs * dps if wide else fs
    me = d * fs + f if wide else f
    def peer(k):
        j = lax.rem(me + k, n)
        return (lax.div(j, fs), lax.rem(j, fs)) if wide else (d, j)
    barrier = pltpu.get_barrier_semaphore()
    def greet(k, carry):
        pl.semaphore_signal(barrier, inc=1, device_id=peer(k), device_id_type=MESH_ID)
        return carry
    lax.fori_loop(1, n, greet, 0)
    pl.semaphore_wait(barrier, n - 1)
    def copy(k):
        return remote(x_ref, got_ref.at[me], send.at[k], recv.at[k], peer(k))
    def begin(k, carry):
        copy(k).start()
        return carry
    lax.fori_loop(1, n, begin, 0)
    got_ref[me] = x_ref[...]
    def end(k, carry):
        copy(k).wait()
        return carry
    lax.fori_loop(1, n, end, 0)
    if finish:
        finish(got_ref, out_ref, n)

def lse_finish(got_ref, out_ref, n):
    top = got_ref[0]
    for i in range(1, n):
        top = jnp.maximum(top, got_ref[i])
    total = jnp.exp(got_ref[0] - top)
    for i in range(1, n):
        total = total + jnp.exp(got_ref[i] - top)
    out_ref[...] = top + jnp.log(total)

def sum_finish(got_ref, out_ref, n):
    total = got_ref[0]
    for i in range(1, n):
        total = total + got_ref[i]
    out_ref[...] = total

def small_gather(x, ident, wide=False, finish=None, name="small_gather"):
    fs, dps = lax.axis_size("fsdp"), lax.axis_size("dp")
    n = fs * dps if wide else fs
    vm = pl.BlockSpec(memory_space=pltpu.VMEM)
    got = (n,) + x.shape
    return pl.pallas_call(
        functools.partial(small_kernel, fs=fs, dps=dps, wide=wide, finish=finish), name=name,
        in_specs=[vm], out_specs=vm,
        out_shape=jax.ShapeDtypeStruct(x.shape if finish else got, x.dtype),
        scratch_shapes=([pltpu.VMEM(got, x.dtype)] if finish else []) + [pltpu.SemaphoreType.DMA((n,)), pltpu.SemaphoreType.DMA((n,))],
        cost_estimate=cost(12), compiler_params=comm_params(ident))(x)

def exchange_kernel(*refs, fs, both, aux, reduce, pairs):
    refs = list(refs)
    x_ref = refs.pop(0)
    aux_ref = refs.pop(0) if aux else None
    w_ref = refs.pop(0) if reduce else None
    pair_refs = [refs.pop(0) for _ in range(2 * pairs)]
    out_ref = refs.pop(0)
    other_ref = refs.pop(0) if both else None
    sum_ref = refs.pop(0) if aux else None
    red_ref = refs.pop(0) if reduce else None
    if pairs:
        sq_ref = refs.pop(0)
        held = [refs.pop() for _ in range(2 * pairs)]
        held_sem = refs.pop()
    send, recv, send2, recv2, own = refs[:5]
    refs = refs[5:]
    if aux:
        near_ref, over_ref = refs.pop(0), refs.pop(0)
    if reduce:
        _, parts, red_begin, red_middle, red_end = reduce_phases(w_ref, red_ref, *refs, high=fs // 4, both=both)
    d, f = lax.axis_index("dp"), lax.axis_index("fsdp")
    across = (1 - d, f)
    barrier = pltpu.get_barrier_semaphore()
    def greet(k, carry):
        pl.semaphore_signal(barrier, inc=1, device_id=(d, lax.rem(f + k, fs)), device_id_type=MESH_ID)
        return carry
    lax.fori_loop(1, fs, greet, 0)
    if both:
        pl.semaphore_signal(barrier, inc=1, device_id=across, device_id_type=MESH_ID)
    pl.semaphore_wait(barrier, fs if both else fs - 1)
    def copies(k):
        j = lax.rem(f + k, fs)
        out = [remote(x_ref.at[j], out_ref.at[f], send.at[0, k], recv.at[0, k], (d, j))]
        if aux:
            out.append(remote(aux_ref, near_ref.at[f], send.at[1, k], recv.at[1, k], (d, j)))
        return out
    def passed(k):
        s = lax.rem(f + fs - k, fs)
        out = [remote(out_ref.at[s], other_ref.at[s], send2.at[0, k], recv2.at[0, k], across)]
        if aux:
            out.append(remote(near_ref.at[s], over_ref.at[s], send2.at[1, k], recv2.at[1, k], across))
        return out
    def first():
        out = [remote(x_ref.at[f], other_ref.at[f], send2.at[0, 0], recv2.at[0, 0], across)]
        if aux:
            out.append(remote(aux_ref, over_ref.at[f], send2.at[1, 0], recv2.at[1, 0], across))
        return out
    if reduce:
        red_begin()
    if both:
        for c in first():
            c.start()
    def begin(k, carry):
        for c in copies(k):
            c.start()
        return carry
    lax.fori_loop(1, fs, begin, 0)
    mine = pltpu.make_async_copy(x_ref.at[f], out_ref.at[f], own)
    mine.start()
    if aux:
        near_ref[f] = aux_ref[...]
    mine.wait()
    def arrive(k, carry):
        for c in copies(k):
            c.wait_recv()
        if both:
            for c in passed(k):
                c.start()
        return carry
    if pairs:
        loads = [pltpu.make_async_copy(a, b, held_sem.at[i]) for i, (a, b) in enumerate(zip(pair_refs, held))]
        for l in loads:
            l.start()
        for l in loads:
            l.wait()
        total = jnp.zeros((8, held[0].shape[1]), F32)
        for i in range(pairs):
            a_ref, b_ref = held[2 * i], held[2 * i + 1]
            def add(n, t, a_ref=a_ref, b_ref=b_ref):
                at = pl.ds(pl.multiple_of(n * 64, 64), 64)
                s = a_ref[at, :].astype(F32) + b_ref[at, :].astype(F32)
                s = s * s
                for j in range(0, 64, 8):
                    t = t + s[j:j + 8]
                return t
            total = lax.fori_loop(0, a_ref.shape[0] // 64, add, total)
        sq_ref[...] = total
    steps = parts + 1 if reduce else 1
    marks = [1 + (fs - 1) * i // steps for i in range(steps + 1)]
    for i in range(steps):
        if reduce:
            red_middle(i)
        lax.fori_loop(marks[i], marks[i + 1], arrive, 0)
    if reduce:
        red_end()
    def end(k, carry):
        for c in copies(k):
            c.wait_send()
        if both:
            for c in passed(k):
                c.wait()
        return carry
    lax.fori_loop(1, fs, end, 0)
    if both:
        for c in first():
            c.wait()
    if aux:
        total = near_ref[0]
        for i in range(1, fs):
            total = total + near_ref[i]
        if both:
            rest = over_ref[0]
            for i in range(1, fs):
                rest = rest + over_ref[i]
            total = total + rest
        sum_ref[...] = total

def exchange(x, ident, both, name, aux=None, reduce=None, pairs=()):
    fs = lax.axis_size("fsdp")
    vm = pl.BlockSpec(memory_space=pltpu.VMEM)
    shape = jax.ShapeDtypeStruct(x.shape, x.dtype)
    sem = pltpu.SemaphoreType.DMA((2, fs))
    more = [] if aux is None else [pltpu.VMEM((fs,) + aux.shape, F32)] * 2
    outs = [shape] * (2 if both else 1) + ([] if aux is None else [jax.ShapeDtypeStruct(aux.shape, F32)])
    args = [x] + [a for a in (aux, reduce) if a is not None]
    if reduce is not None:
        block = reduce.shape[1:]
        outs.append(jax.ShapeDtypeStruct(block, F32))
        more = more + reduce_scratch(block, reduce.dtype, fs // 4)
    ins = [vm] * len(args) + [pl.BlockSpec(memory_space=pl.ANY)] * len(pairs)
    if pairs:
        outs.append(jax.ShapeDtypeStruct((8, pairs[0].shape[1]), F32))
        more = more + [pltpu.SemaphoreType.DMA((len(pairs),))] + [pltpu.VMEM(p.shape, p.dtype) for p in reversed(pairs)]
    return pl.pallas_call(
        functools.partial(exchange_kernel, fs=fs, both=both, aux=aux is not None, reduce=reduce is not None, pairs=len(pairs) // 2), name=name,
        in_specs=ins, out_specs=[vm] * len(outs), out_shape=outs,
        scratch_shapes=[sem, sem, sem, sem, pltpu.SemaphoreType.DMA] + more,
        cost_estimate=cost(55),
        compiler_params=comm_params(ident))(*args, *pairs)

def cuts(rows):
    n = 4 if rows % 64 == 0 else 1
    return n, rows // n

def gather_phases(x_ref, out_ref, send, recv, *, high):
    d, f = lax.axis_index("dp"), lax.axis_index("fsdp")
    h, m, c = lax.div(f, 4), lax.rem(lax.div(f, 2), 2), lax.rem(f, 2)
    side, twin = (d, h * 4 + (1 - m) * 2 + c), (d, h * 4 + m * 2 + 1 - c)
    parts, size = cuts(x_ref.shape[0])
    def far(k):
        return (d, lax.rem(h + k, high) * 4 + m * 2 + c)
    peers = [far(k) for k in range(1, high)] + [side, twin]
    sent = []
    def go(src, block, p, peer):
        at = pl.ds(p * size, size)
        r = remote(src.at[at], out_ref.at[block, at], send.at[len(sent)], recv.at[block, p], peer)
        r.start()
        sent.append(r)
    def arrived(block, p):
        at = pl.ds(p * size, size)
        remote(x_ref.at[at], out_ref.at[block, at], send.at[0], recv.at[block, p], twin).wait_recv()
    def back(k, row):
        return lax.rem(h + high - k, high) * 4 + row * 2 + c
    def launch(p):
        for k in range(1, high):
            go(x_ref, f, p, far(k))
        go(x_ref, f, p, side)
        go(x_ref, f, p, twin)
    ahead = min(AHEAD, parts)
    def begin():
        for p in range(ahead):
            launch(p)
        out_ref[f] = x_ref[...]
    def middle(p):
        if p < parts:
            for k in range(1, high):
                b = back(k, m)
                arrived(b, p)
                go(out_ref.at[b], b, p, side)
                go(out_ref.at[b], b, p, twin)
            if p + ahead < parts:
                launch(p + ahead)
        if p > 0:
            for k in range(high):
                b = back(k, 1 - m)
                arrived(b, p - 1)
                go(out_ref.at[b], b, p - 1, twin)
    def end():
        for row in range(2):
            for k in range(high):
                for p in range(parts):
                    arrived(lax.rem(h + high - k, high) * 4 + lax.rem(m + row, 2) * 2 + 1 - c, p)
        for r in sent:
            r.wait_send()
    return peers, parts, begin, middle, end

def rows_gather_kernel(x_ref, out_ref, send, recv, *, high):
    peers, parts, begin, middle, end = gather_phases(x_ref, out_ref, send, recv, high=high)
    meet(peers)
    begin()
    for p in range(parts + 1):
        middle(p)
    end()

def rows_gather(x, ident, name="rows_gather"):
    fs = lax.axis_size("fsdp")
    vm = pl.BlockSpec(memory_space=pltpu.VMEM)
    high = fs // 4
    parts = cuts(x.shape[0])[0]
    return pl.pallas_call(
        functools.partial(rows_gather_kernel, high=high), name=name,
        in_specs=[vm], out_specs=vm, out_shape=jax.ShapeDtypeStruct((fs,) + x.shape, x.dtype),
        scratch_shapes=[pltpu.SemaphoreType.DMA((4 * high * parts,)), pltpu.SemaphoreType.DMA((fs, parts))],
        cost_estimate=cost(40), compiler_params=comm_params(ident))(x)

def reduce_phases(x_ref, out_ref, twin_ref, side_ref, far_ref, a_ref, b_ref, s1, r1, s2, r2, s3, r3, *, high, both):
    d, f = lax.axis_index("dp"), lax.axis_index("fsdp")
    h, m, c = lax.div(f, 4), lax.rem(lax.div(f, 2), 2), lax.rem(f, 2)
    side, twin = (d, h * 4 + (1 - m) * 2 + c), (d, h * 4 + m * 2 + 1 - c)
    def far(k):
        return (d, lax.rem(h + k, high) * 4 + m * 2 + c)
    across = (1 - d, f)
    peers = [far(k) for k in range(1, high)] + [side, twin] + ([across] if both else [])
    order = list(range(1, high)) + [0]
    parts, size = cuts(x_ref.shape[1])
    def rows(p):
        return pl.ds(p * size, size)
    def at(k):
        return lax.rem(h + k, high)
    def one(k, row, p):
        slot = at(k) * 2 + row
        return remote(x_ref.at[at(k) * 4 + row * 2 + 1 - c, rows(p)], twin_ref.at[slot, rows(p)], s1.at[slot, p], r1.at[slot, p], twin)
    def two(k, p):
        return remote(a_ref.at[at(k), rows(p)], side_ref.at[at(k), rows(p)], s2.at[at(k), p], r2.at[at(k), p], side)
    def three(k, p):
        return remote(b_ref.at[k, rows(p)], far_ref.at[k, rows(p)], s3.at[k, p], r3.at[k, p], far(k))
    def last(p):
        return remote(b_ref.at[0, rows(p)], far_ref.at[0, rows(p)], s3.at[0, p], r3.at[0, p], across)
    def begin():
        for p in range(parts):
            for k in order:
                one(k, 1 - m, p).start()
            for k in order:
                one(k, m, p).start()
    def middle(p):
        if p < parts:
            if p >= 2:
                for k in order:
                    two(k, p - 2).wait_send()
            for k in order:
                one(k, 1 - m, p).wait_recv()
                a_ref[at(k), rows(p)] = (x_ref[at(k) * 4 + (1 - m) * 2 + c, rows(p)].astype(F32) + twin_ref[at(k) * 2 + 1 - m, rows(p)].astype(F32)).astype(a_ref.dtype)
                two(k, p).start()
        if p > 0:
            q = p - 1
            for k in order:
                one(k, m, q).wait_recv()
                two(k, q).wait_recv()
                total = x_ref[at(k) * 4 + m * 2 + c, rows(q)].astype(F32) + twin_ref[at(k) * 2 + m, rows(q)].astype(F32) + side_ref[at(k), rows(q)].astype(F32)
                if k == 0:
                    out_ref[rows(q)] = total
                else:
                    b_ref[k, rows(q)] = total.astype(b_ref.dtype)
                    three(k, q).start()
    def end():
        for p in range(parts):
            for k in range(1, high):
                three(k, p).wait_recv()
                out_ref[rows(p)] += far_ref[k, rows(p)].astype(F32)
            if both:
                b_ref[0, rows(p)] = out_ref[rows(p)].astype(b_ref.dtype)
                last(p).start()
        for p in range(parts):
            if both:
                last(p).wait()
                out_ref[rows(p)] = b_ref[0, rows(p)].astype(F32) + far_ref[0, rows(p)].astype(F32)
            for k in order:
                one(k, m, p).wait_send()
                one(k, 1 - m, p).wait_send()
                if p + 2 >= parts:
                    two(k, p).wait_send()
                if k:
                    three(k, p).wait_send()
    return peers, parts, begin, middle, end

def rows_reduce_kernel(*refs, high, both):
    peers, parts, begin, middle, end = reduce_phases(*refs, high=high, both=both)
    meet(peers)
    begin()
    for p in range(parts + 1):
        middle(p)
    end()

def reduce_scratch(block, dtype, high):
    parts = cuts(block[0])[0]
    def sem(n):
        return pltpu.SemaphoreType.DMA((n, parts))
    def buf(n):
        return pltpu.VMEM((n,) + block, dtype)
    return [buf(2 * high), buf(high), buf(high), buf(high), buf(high),
            sem(2 * high), sem(2 * high), sem(high), sem(high), sem(high), sem(high)]

def rows_reduce(x, ident, name="rows_reduce", both=False):
    vm = pl.BlockSpec(memory_space=pltpu.VMEM)
    high = lax.axis_size("fsdp") // 4
    block = x.shape[1:]
    return pl.pallas_call(
        functools.partial(rows_reduce_kernel, high=high, both=both), name=name,
        in_specs=[vm], out_specs=vm, out_shape=jax.ShapeDtypeStruct(block, F32),
        scratch_shapes=reduce_scratch(block, x.dtype, high),
        cost_estimate=cost(45), compiler_params=comm_params(ident))(x)
def front_kernel(ids_ref, w_ref, emb_ref, all_ref, x_ref, full_ref, tab_ref, raw_ref, row_ref, picked_ref, smem_ref,
                 raw_sem, ids_send, ids_recv, x_send, x_recv, smem_sem, w_send, w_recv, *, fs, dps):
    feat, vocab = emb_ref.shape
    length = x_ref.shape[2]
    lines = length // 128
    nb, low = halves(vocab)
    secs = sections(low, -(-low // 6))
    d, f = lax.axis_index("dp"), lax.axis_index("fsdp")
    n, me = fs * dps, d * fs + f
    def load(k):
        s, c = secs[k]
        out = [pltpu.make_async_copy(emb_ref.at[:, pl.ds(s * 128, c * 128)], raw_ref.at[:, pl.ds(s * 128, c * 128)], raw_sem.at[2 * k])]
        m = min(c, nb - low - s)
        if m > 0:
            out.append(pltpu.make_async_copy(emb_ref.at[:, pl.ds((low + s) * 128, m * 128)], raw_ref.at[:, pl.ds((low + s) * 128, m * 128)], raw_sem.at[2 * k + 1]))
        return out
    for k in range(len(secs)):
        for c in load(k):
            c.start()
    _, parts, w_begin, w_middle, w_end = gather_phases(w_ref, full_ref, w_send, w_recv, high=fs // 4)
    def peer(k):
        j = lax.rem(me + k, n)
        return (lax.div(j, fs), lax.rem(j, fs))
    barrier = pltpu.get_barrier_semaphore()
    def greet(k, carry):
        pl.semaphore_signal(barrier, inc=1, device_id=peer(k), device_id_type=MESH_ID)
        return carry
    lax.fori_loop(1, n, greet, 0)
    pl.semaphore_wait(barrier, n - 1)
    def ids_copy(k):
        return remote(ids_ref, all_ref.at[me], ids_send.at[k], ids_recv.at[k], peer(k))
    def ids_begin(k, carry):
        ids_copy(k).start()
        return carry
    lax.fori_loop(1, n, ids_begin, 0)
    all_ref[me] = ids_ref[...]
    w_begin()

    pad = jnp.zeros((64 - feat, 128), F32)
    for k in range(len(secs)):
        for c in load(k):
            c.wait()
        s, c = secs[k]
        m = max(0, min(c, nb - low - s))
        def turn(b, carry):
            a = raw_ref[:, pl.ds(pl.multiple_of(b * 128, 128), 128)]
            h = raw_ref[:, pl.ds(pl.multiple_of((low + b) * 128, 128), 128)]
            tab_ref[pl.ds(pl.multiple_of(b * 128, 128), 128), :] = jnp.concatenate([a, pad, h, pad], axis=0).T
            return carry
        lax.fori_loop(s, s + m, turn, 0, unroll=3)
        for b in range(s + m, s + c):
            a = raw_ref[:, b * 128:(b + 1) * 128]
            tab_ref[b * 128:(b + 1) * 128, :] = jnp.concatenate([a, pad, pad, jnp.zeros((feat, 128), F32)], axis=0).T

    def ids_end(k, carry):
        ids_copy(k).wait()
        return carry
    lax.fori_loop(1, n, ids_end, 0)
    def to_smem(s):
        return pltpu.make_async_copy(all_ref.at[d * fs + s, pl.ds(0, lines)], smem_ref.at[s], smem_sem.at[s])
    def smem_begin(s, carry):
        to_smem(s).start()
        return carry
    def smem_end(s, carry):
        to_smem(s).wait()
        return carry
    lax.fori_loop(0, fs, smem_begin, 0)
    lax.fori_loop(0, fs, smem_end, 0)

    U = 32
    def fetch(s, put):
        def grp(g, carry):
            line, base = lax.div(g, 128 // U), lax.rem(g, 128 // U) * U
            for j in range(U):
                i = smem_ref[s, line, base + j]
                i = jnp.where(i >= low * 128, i - low * 128, i)
                row_ref[pl.ds(pl.multiple_of(g * U, U) + j, 1), :] = tab_ref[pl.ds(i, 1), :]
            return carry
        lax.fori_loop(0, length // U, grp, 0)
        ids = all_ref[d * fs + s]
        for c in range(lines):
            t = row_ref[c * 128:(c + 1) * 128, :].T
            high = ids[c:c + 1] >= low * 128
            put(c, jnp.where(high, t[64:64 + feat], t[:feat]).astype(BF16))
    def x_copy(k):
        s = lax.rem(f + k, fs)
        return remote(picked_ref.at[s], x_ref.at[f], x_send.at[k], x_recv.at[k], (d, s))
    def one(k, carry):
        s = lax.rem(f + k, fs)
        def put(c, v):
            picked_ref[s, :, c * 128:(c + 1) * 128] = v
        fetch(s, put)
        x_copy(k).start()
        return carry
    steps = parts + 1
    marks = [1 + (fs - 1) * i // steps for i in range(steps + 1)]
    for i in range(steps):
        lax.fori_loop(marks[i], marks[i + 1], one, 0)
        w_middle(i)
    def mine(c, v):
        x_ref[f, :, c * 128:(c + 1) * 128] = v
    fetch(f, mine)
    w_end()
    def x_end(k, carry):
        x_copy(k).wait()
        return carry
    lax.fori_loop(1, fs, x_end, 0)

def front(ids, w, emb, length, ident):
    fs, dps = lax.axis_size("fsdp"), lax.axis_size("dp")
    feat, vocab = emb.shape
    low = halves(vocab)[1]
    vm = pl.BlockSpec(memory_space=pltpu.VMEM)
    parts = cuts(w.shape[0])[0]
    def sem(*shape):
        return pltpu.SemaphoreType.DMA(shape)
    return pl.pallas_call(
        functools.partial(front_kernel, fs=fs, dps=dps), name="front",
        in_specs=[vm, vm, pl.BlockSpec(memory_space=pl.ANY)], out_specs=[vm, vm, vm],
        out_shape=[jax.ShapeDtypeStruct((fs * dps,) + ids.shape, ids.dtype), jax.ShapeDtypeStruct((fs, feat, length), BF16),
                   jax.ShapeDtypeStruct((fs,) + w.shape, w.dtype)],
        scratch_shapes=[pltpu.VMEM((low * 128, 128), F32), pltpu.VMEM((feat, vocab), F32), pltpu.VMEM((length, 128), F32),
                        pltpu.VMEM((fs, feat, length), BF16), pltpu.SMEM((fs, length // 128, 128), jnp.int32),
                        sem(12), sem(fs * dps), sem(fs * dps), sem(fs), sem(fs), sem(fs), sem(fs * parts), sem(fs, parts)],
        cost_estimate=cost(85), compiler_params=comm_params(ident))(ids, w, emb)
def adam_kernel(factor_ref, w_ref, one_ref, two_ref, avg_ref, *refs, rate, first):
    outs = refs[-4:]
    grads = [r[...].astype(F32) for r in refs[:-4]]
    if first is None:
        g = grads[0]
    else:
        g = jnp.where(pl.program_id(0) < first, grads[0] + grads[1], grads[2] + grads[3])
    new, one, two = adamw(w_ref[...], one_ref[...], two_ref[...], g * factor_ref[0], rate)
    outs[0][...] = new
    outs[1][...] = one
    outs[2][...] = two
    outs[3][...] = ema_decay * avg_ref[...] + (1 - ema_decay) * new

def adam_table(factor, w, one, two, avg, grads, rate, by_rows):
    rows, cols = w.shape
    if by_rows:
        block, first = (768, cols), grads[0].shape[0] // 768
        steps = -(-rows // 768)
        spec = pl.BlockSpec(block, lambda i: (i, 0))
        early = pl.BlockSpec(block, lambda i: (jnp.minimum(i, first - 1), 0))
        late = pl.BlockSpec(block, lambda i: (jnp.maximum(i - first, 0), 0))
        gspecs = [early, early, late, late]
    else:
        block, first = (rows, 12672), None
        steps = -(-cols // 12672)
        spec = pl.BlockSpec(block, lambda i: (0, i))
        gspecs = [spec]
    shape = jax.ShapeDtypeStruct(w.shape, F32)
    return pl.pallas_call(
        functools.partial(adam_kernel, rate=rate, first=first), name="adam_rows" if by_rows else "adam_columns",
        grid=(steps,), cost_estimate=cost(1),
        in_specs=[pl.BlockSpec(memory_space=pltpu.SMEM)] + [spec] * 4 + gspecs, out_specs=[spec] * 4, out_shape=[shape] * 4,
        compiler_params=params())(factor.reshape(1), w, one, two, avg, *grads)
def shampoo_kernel(factor_ref, w_ref, grad_ref, left_ref, right_ref, root_ref, whole_ref, full_ref, avg_ref,
                   new_ref, clip_ref, left_out, right_out, avg_out):
    columns, width = right_ref.shape[1:]
    factor = factor_ref[0]
    mix = (1 - stat_decay) * factor * factor
    full = full_ref[0]
    grad = grad_ref[0]
    at = lax.axis_index("fsdp") * columns + lax.broadcasted_iota(jnp.int32, (columns, width), 0)
    pick = (at == lax.broadcasted_iota(jnp.int32, (columns, width), 1)).astype(BF16)
    turned = dot(pick, full, 1, 1).astype(BF16)
    left_out[0] = stat_decay * left_ref[0] + mix * dot(grad.astype(BF16), full, 1, 1)
    right_out[0] = stat_decay * right_ref[0] + mix * dot(turned, full, 1, 0)
    part = dot(root_ref[0].astype(BF16), full, 1, 0)
    update = dot(part.astype(BF16), whole_ref[0], 1, 0) * factor
    w = w_ref[0]
    new = w - rate_shampoo * (update + shampoo_decay * w)
    new_ref[0] = new
    clip_ref[0] = grad * factor
    avg_out[0] = ema_decay * avg_ref[0] + (1 - ema_decay) * new

def shampoo(factor, w, grad, left, right, root, whole_root, full, avg, name):
    def one(x):
        return pl.BlockSpec((1,) + x.shape[1:], lambda i: (i, 0, 0))
    ins = (w, grad, left, right, root, whole_root, full, avg)
    outs = (w, w, left, right, w)
    return pl.pallas_call(
        shampoo_kernel, grid=(w.shape[0],), name=name, cost_estimate=cost(10),
        in_specs=[pl.BlockSpec(memory_space=pltpu.SMEM)] + [one(x) for x in ins],
        out_specs=[one(x) for x in outs], out_shape=[jax.ShapeDtypeStruct(x.shape, F32) for x in outs],
        compiler_params=params())(factor.reshape(1), *ins)
MASK_ID = 50257
STRATA = 16
STEP = 10

clip_level = 1.0
beta_one = 0.9
beta_two = 0.95
adam_eps = 1e-08
adam_decay = 0.01
rate_embed = 2.0
rate_out = 0.25
rate_gain = 0.5
rate_shampoo = 0.3
shampoo_decay = 0.01
stat_decay = 0.5
ema_decay = 0.7


def rotary_tables(length, half_width):
    inverse = 10000.0 ** (-np.arange(half_width, dtype=np.float64) / half_width)
    angles = inverse[:, None] * np.arange(length, dtype=np.float64)[None, :]
    return (jnp.asarray(np.cos(angles), F32), jnp.asarray(np.sin(angles), F32))


def adamw(weight, moment_one, moment_two, gradient, step_rate):
    one_new = beta_one * moment_one + (1 - beta_one) * gradient
    two_new = beta_two * moment_two + (1 - beta_two) * gradient * gradient
    one_hat = one_new * (1 / (1 - beta_one**STEP))
    two_hat = two_new * (1 / (1 - beta_two**STEP))
    weight_new = weight - step_rate * (
        one_hat / (jnp.sqrt(two_hat) + adam_eps) + adam_decay * weight
    )
    return (weight_new, one_new, two_new)


def dp_other(x):
    return lax.ppermute(x, "dp", [(0, 1), (1, 0)])


def dp_sum(x):
    count = lax.axis_size("dp")
    if count == 1:
        return x.astype(F32)
    if count == 2:
        return x.astype(F32) + dp_other(x).astype(F32)
    return lax.psum(x, "dp").astype(F32)


def spread_out(x):
    return lax.all_gather(x.astype(BF16), "fsdp", axis=1, tiled=True)


def per_device(
    tokens, positions, strata, groups, embedding, out_table, norm_gains, attention, feedforward,
    embed_moment_one, embed_moment_two, out_moment_one, out_moment_two, gain_moment_one, gain_moment_two,
    attention_left, attention_right, attention_left_root, attention_right_root,
    ff_left, ff_right, ff_left_root, ff_right_root,
    ema_embed, ema_out, ema_gains, ema_attention, ema_feedforward,
):
    fs = lax.axis_size("fsdp")
    dps = lax.axis_size("dp")
    me = lax.axis_index("fsdp")
    replica = lax.axis_index("dp")
    seq_count, length = tokens.shape
    slots = positions.shape[1]
    features, vocab = embedding.shape
    width = features * fs
    shard = out_table.shape[0]

    near = lax.all_gather(
        feedforward.astype(BF16), "fsdp", axis=1, tiled=True,
        axis_index_groups=[list(range(c, fs, 2)) for c in range(2)],
    )

    counts = jnp.maximum(1, (strata + 1) * slots * (1 + groups) // (2 * STRATA))
    in_use = jnp.arange(slots, dtype=jnp.int32)[None, :] < counts[:, None]
    places = jnp.arange(length, dtype=jnp.int32)
    same = positions[0][:, None] == places[None, :]
    marked = jnp.any(same & in_use[0][:, None], axis=0)
    ids_in = jnp.where(marked, MASK_ID, tokens[0])
    targets = jnp.sum(jnp.where(same, tokens[0][None, :], 0), axis=1)
    packed = jnp.concatenate([ids_in, targets, counts])
    packed = jnp.pad(packed, (0, -packed.shape[0] % 1024))
    everyone, xT, attn_w = front(packed.reshape(-1, 128), attention.astype(BF16).reshape(-1, width), embedding, length, 1)
    everyone = everyone.reshape(fs * dps, -1)
    xT = xT.reshape(width, length)
    attn_w = attn_w.reshape(fs, 4, -1, width)
    group = lax.dynamic_slice_in_dim(everyone, replica * fs, fs, 0)
    all_ids = everyone[:, :length]
    group_ids = group[:, :length]
    group_targets = group[:, length:length + slots]
    group_counts = group[:, length + slots]

    cosT, sinT = rotary_tables(length, HEAD // 2)
    gain = [norm_gains.T] * 3
    place = positions[0][:, None]
    hT, qT, kT, vT, mixT, lse = attn_fwd(xT, gain[0], cosT, sinT, attn_w)
    hT, source, near = lax.optimization_barrier((hT, out_table, near))
    ff_w = (near, lax.ppermute(near, "fsdp", [(i, i ^ 1) for i in range(fs)]))
    low, turned = table_both(source)
    mixT, low, turned = lax.optimization_barrier((mixT, low, turned))
    x2, h2, x3, head = ff_fwd(xT, mixT, gain[1], gain[2], place, attn_w, ff_w, feedforward.shape[1])

    rows = rows_gather(head, 3)
    first_id = me * shard
    limit = jnp.clip(MASK_ID - first_id, 0, shard).reshape(1)
    least = min(shard, MASK_ID - (fs - 1) * shard)
    meta, seq, slot, weight = plan(group_counts, slots, length)
    nblk = seq.shape[0] // RB
    target = (spread(group_targets, seq, slot) - first_id).reshape(nblk, 1, RB)
    inside = fs * slots <= 4096
    if not inside:
        rows = jnp.take(rows.reshape(fs * slots, width), jnp.clip(seq * slots + slot, 0, fs * slots - 1), axis=0)
    comp, lse_own, chosen = vocab_fwd(meta, limit, rows, low, target, least)
    lse_own, root = lax.optimization_barrier((lse_own, attention_right_root))
    attn_root = spread_out(root)
    lse_sum = small_gather(lse_own, 4, finish=lse_finish, name="lse_gather")
    own_loss = jnp.sum(weight * (jnp.where(seq == me, lse_sum.reshape(-1), 0.0) - chosen.reshape(-1)))
    scale = weight / (seq_count * fs * dps)
    out_one, out_two, row_grads = vocab_bwd(
        meta, limit, comp, low, turned, target, lse_sum, scale.reshape(nblk, 1, RB),
        least, fs, slots, inside,
    )
    if not inside:
        at = jnp.arange(slots, dtype=jnp.int32)[None, :]
        row_grads = jnp.take(row_grads, jnp.minimum(meta[1][:, None] * 16 + at, seq.shape[0] - 1), axis=0)
        row_grads = jnp.where((at < group_counts[:, None])[:, :, None], row_grads, 0)
    own_rows = rows_reduce(row_grads, 5)
    halves_low = (out_one, out_two)
    if dps == 2:
        others = [dp_other(x) for x in halves_low]

    own_rows, attn_root, root = lax.optimization_barrier((own_rows, attn_root, ff_right_root))
    ff_root = spread_out(root)
    second, gg2, gg3, dff = ff_bwd(x3, x2, h2, own_rows, place, gain[1], gain[2], ff_w, fs)
    if dps == 2:
        second, others[0], ff_root = lax.optimization_barrier((second, others[0], ff_root))
    first, gg1, dattn = attn_bwd(xT, gain[0], cosT, sinT, second, hT, qT, kT, vT, mixT, lse, attn_w, fs)

    ff_part = lax.psum_scatter(dff.reshape(-1, width), "fsdp", scatter_dimension=0, tiled=True)

    aux = jnp.concatenate([jnp.concatenate([gg1, gg2, gg3], axis=1).T.reshape(-1), own_loss[None]])
    aux = jnp.pad(aux, (0, -aux.shape[0] % 1024)).reshape(-1, 128)
    if dps == 2:
        first, others[1] = lax.optimization_barrier((first, others[1]))
        pairs = (halves_low[0], others[0], halves_low[1], others[1])
    else:
        pairs = ()
        out_grad = jnp.concatenate([dp_sum(a) for a in halves_low])[:shard]
        out_sq = jnp.sum(out_grad * out_grad)
    out = list(exchange(first.reshape(fs, features, length), 6, dps == 2, "gradients", aux, dattn.reshape(fs, -1, width), pairs))
    if dps == 2:
        out_sq = jnp.sum(out.pop())
    attn_grad = out[-1].reshape(4, -1, width)
    aux, ff_part = lax.optimization_barrier((out[-2], ff_part))
    ff_grad = dp_sum(ff_part.reshape(2, -1, width))
    if dps != 2:
        attn_grad = dp_sum(attn_grad.astype(BF16))
    if dps == 2:
        parts, other = out[:2]
        other_ids = lax.dynamic_slice_in_dim(everyone, (1 - replica) * fs, fs, 0)[:, :length]
        embed_grad, embed_sq = scatter(jnp.concatenate([group_ids, other_ids]), (parts, other), vocab, 2)
        embed_sq = jnp.sum(embed_sq)
    else:
        parts = out[0]
        embed_grad = dp_sum(scatter(group_ids, (parts,), vocab, 2)[0].astype(BF16))
        embed_sq = jnp.sum(embed_grad * embed_grad)
        if dps > 1:
            aux = lax.psum(aux, "dp")
    aux = aux.reshape(-1)
    gain_grad, loss_sum = aux[: 3 * width].reshape(3, width), aux[3 * width]
    squares = (
        jnp.sum(attn_grad * attn_grad)
        + jnp.sum(ff_grad * ff_grad)
        + embed_sq
        + out_sq
    )
    ff_grad, embed_sq = lax.optimization_barrier((ff_grad, embed_sq))
    attn_full, ff_full = spread_out(attn_grad), spread_out(ff_grad)
    squares, attn_full = lax.optimization_barrier((squares, attn_full))
    squares = small_gather(jnp.full((8, 128), squares), 7, finish=sum_finish, name="squares")[0, 0]
    clip_norm = jnp.sqrt(squares + jnp.sum(gain_grad * gain_grad))
    factor = jnp.minimum(1.0, clip_level / clip_norm)
    embed_new, embed_one_new, embed_two_new, ema_embed_new = adam_table(
        factor, embedding, embed_moment_one, embed_moment_two, ema_embed, [embed_grad], rate_embed, False
    )
    if dps == 2:
        out_new, out_one_new, out_two_new, ema_out_new = adam_table(
            factor, out_table, out_moment_one, out_moment_two, ema_out,
            [halves_low[0], others[0], halves_low[1], others[1]], rate_out, True
        )
    else:
        out_new, out_one_new, out_two_new = adamw(
            out_table, out_moment_one, out_moment_two, out_grad * factor, rate_out
        )
        ema_out_new = ema_decay * ema_out + (1 - ema_decay) * out_new
    gains_new, gains_one_new, gains_two_new = adamw(
        norm_gains, gain_moment_one, gain_moment_two, gain_grad * factor, rate_gain
    )

    attention_new, attn_clip, attention_left_new, attention_right_new, ema_attn_new = shampoo(
        factor, attention, attn_grad, attention_left, attention_right, attention_left_root,
        attn_root, attn_full, ema_attention, "shampoo_attention"
    )
    ff_new, ff_clip, ff_left_new, ff_right_new, ema_ff_new = shampoo(
        factor, feedforward, ff_grad, ff_left, ff_right, ff_left_root,
        ff_root, ff_full, ema_feedforward, "shampoo_ff"
    )

    def averaged(average, new):
        return ema_decay * average + (1 - ema_decay) * new

    return (
        loss_sum, clip_norm, embed_new, embed_one_new, embed_two_new, out_new, out_one_new, out_two_new,
        gains_new, gains_one_new, gains_two_new, attention_new, attn_clip, attention_left_new, attention_right_new,
        ff_new, ff_clip, ff_left_new, ff_right_new,
        ema_embed_new, ema_out_new, averaged(ema_gains, gains_new),
        ema_attn_new, ema_ff_new,
    )


def solution(mesh):
    seqs, rows, stack, none = P(("dp", "fsdp")), P("fsdp", None), P(None, "fsdp", None), P()
    in_specs = (
        seqs, seqs, seqs, seqs, rows, rows, none, stack, stack, rows, rows, rows, rows, none, none,
        stack, stack, stack, stack, stack, stack, stack, stack, rows, rows, none, stack, stack,
    )
    out_specs = (
        none, none, rows, rows, rows, rows, rows, rows, none, none, none, stack, stack, stack, stack,
        stack, stack, stack, stack, rows, rows, none, stack, stack,
    )
    return jax.shard_map(
        per_device, mesh=mesh, in_specs=in_specs, out_specs=out_specs, check_vma=False
    )
```

```python
import functools

import jax
import jax.numpy as jnp
import numpy as np
from jax import lax
from jax.experimental import pallas as pl
from jax.experimental.pallas import tpu as pltpu
from jax.sharding import PartitionSpec as P

F32, BF16 = jnp.float32, jnp.bfloat16
HEAD = 64
EPS = 1e-5
BSTEP = 1024
VL = 60 * 1024 * 1024

def dot(a, b, ca, cb):
    return lax.dot_general(a, b, (((ca,), (cb,)), ((), ())), preferred_element_type=F32)

def params(limit=VL):
    return pltpu.CompilerParams(vmem_limit_bytes=limit)

def cost(us):
    return pl.CostEstimate(flops=int(us * 1.15e9), bytes_accessed=0, transcendentals=0)

def whole(shape):
    return pl.BlockSpec(shape, lambda *a: (0,) * len(shape))

def attn_fwd_kernel(x_ref, gain_ref, cos_ref, sin_ref, w_ref, h_ref, q_ref, k_ref, v_ref, m_ref, lse_ref, kn_ref):
    width, length = x_ref.shape
    block = q_ref.shape[0]
    heads = block // HEAD
    half = HEAD // 2

    @pl.when(pl.program_id(0) == 0)
    def _():
        def cols(c, carry):
            at = pl.ds(pl.multiple_of(c * 128, 128), 128)
            x = x_ref[:, at].astype(F32)
            centred = x - jnp.mean(x, axis=0, keepdims=True)
            spread = jnp.mean(centred * centred, axis=0, keepdims=True)
            h_ref[:, at] = (centred * lax.rsqrt(spread + EPS) * gain_ref[:, 0:1]).astype(BF16)
            return carry
        lax.fori_loop(0, length // 128, cols, 0)

    cosine, sine = cos_ref[...], sin_ref[...]
    hidden = h_ref[...]
    for j, out in ((0, q_ref), (1, k_ref)):
        p = dot(w_ref[:, j].reshape(width, block), hidden, 0, 0)
        for h in range(heads):
            a = p[h * HEAD : h * HEAD + half]
            b = p[h * HEAD + half : (h + 1) * HEAD]
            ra = (a * cosine - b * sine).astype(BF16)
            rb = (b * cosine + a * sine).astype(BF16)
            if j == 0:
                ra, rb = ra * 0.125, rb * 0.125
            out[h * HEAD : h * HEAD + half, :] = ra
            out[h * HEAD + half : (h + 1) * HEAD, :] = rb
    v_ref[...] = dot(w_ref[:, 2].reshape(width, block), hidden, 0, 0).astype(BF16)
    for h in range(heads):
        rows = slice(h * HEAD, (h + 1) * HEAD)
        kn_ref[h] = k_ref[rows, :].T
    def one(h, carry):
        rows = pl.ds(pl.multiple_of(h * HEAD, HEAD), HEAD)
        s = dot(kn_ref[h], q_ref[rows, :], 1, 0)
        top = jnp.max(s, axis=0, keepdims=True)
        e = jnp.exp(s - top)
        total = jnp.sum(e, axis=0, keepdims=True)
        o = dot(v_ref[rows, :], e.astype(BF16), 1, 0)
        m_ref[rows, :] = (o / total).astype(BF16)
        lse_ref[0, pl.ds(h, 1), :] = top + jnp.log(total)
        return carry
    lax.fori_loop(0, heads, one, 0)

def attn_fwd(xT, gain, cosT, sinT, w):
    width, length = xT.shape
    block = 256
    n = width // block
    col = pl.BlockSpec((block, length), lambda i: (i, 0))
    t = jax.ShapeDtypeStruct((width, length), BF16)
    return pl.pallas_call(
        attn_fwd_kernel, grid=(n,), name="attn_fwd", cost_estimate=cost(34),
        in_specs=[whole((width, length)), whole(gain.shape), whole(cosT.shape), whole(sinT.shape),
                  pl.BlockSpec((w.shape[0], 3, w.shape[2], block), lambda i: (0, 0, 0, i))],
        out_specs=[whole((width, length)), col, col, col, col, pl.BlockSpec((1, 8, length), lambda i: (i, 0, 0))],
        out_shape=[t, t, t, t, t, jax.ShapeDtypeStruct((n, 8, length), F32)],
        scratch_shapes=[pltpu.VMEM((block // HEAD, length, HEAD), BF16)],
        compiler_params=params(),
    )(xT, gain, cosT, sinT, w)

def attn_bwd_kernel(x_ref, gain_ref, cos_ref, sin_ref, sg_ref, h_ref, q_ref, k_ref, v_ref, m_ref, lse_ref, w_ref, wo_ref,
                    first_ref, gg_ref, dw_ref, hg_ref, low_ref, do_ref, kn_ref, vn_ref, dk_ref, dv_ref, dq_ref, dwo_ref):
    width, length = x_ref.shape
    block = q_ref.shape[0]
    heads = block // HEAD
    half = HEAD // 2
    step = min(BSTEP, length)
    i = pl.program_id(0)

    @pl.when(i == 0)
    def _():
        low_ref[...] = sg_ref[...].astype(BF16)
        dwo_ref[...] = wo_ref[:, 0].reshape(width, width)
        hg_ref[...] = jnp.zeros_like(hg_ref)

    mine = pl.ds(pl.multiple_of(i * block, block), block)
    do_ref[...] = dot(dwo_ref[mine, :], low_ref[...], 1, 0).astype(BF16)
    fs, _, each, _ = dw_ref.shape
    dwo_ref[mine, :] = dot(m_ref[...], low_ref[...], 1, 1).astype(BF16)
    cosine, sine = cos_ref[...], sin_ref[...]
    for h in range(heads):
        rows = slice(h * HEAD, (h + 1) * HEAD)
        kn_ref[h] = k_ref[rows, :].T
        vn_ref[h] = v_ref[rows, :].T
    def one(h, carry):
        rows = pl.ds(pl.multiple_of(h * HEAD, HEAD), HEAD)
        for c in range(length // step):
            at = slice(c * step, (c + 1) * step)
            s = dot(kn_ref[h], q_ref[rows, at], 1, 0)
            p = jnp.exp(s - lse_ref[0, pl.ds(h, 1), at])
            dp = dot(vn_ref[h], do_ref[rows, at], 1, 0)
            centre = jnp.sum(p * dp, axis=0, keepdims=True)
            ds = (p * (dp - centre)).astype(BF16)
            pb = p.astype(BF16)
            dv = dot(pb, do_ref[rows, at], 1, 1).T
            dk = dot(ds, q_ref[rows, at], 1, 1).T
            if c == 0:
                dv_ref[rows, :] = dv
                dk_ref[rows, :] = dk
            else:
                dv_ref[rows, :] += dv
                dk_ref[rows, :] += dk
            dq_ref[rows, at] = dot(k_ref[rows, :], ds, 1, 0) * 0.125
        return carry
    lax.fori_loop(0, heads, one, 0)
    hidden = h_ref[...]
    for j, ref in ((0, dq_ref), (1, dk_ref), (2, dv_ref)):
        if j == 2:
            g = ref[...].astype(BF16)
        else:
            parts = []
            for h in range(heads):
                a = ref[h * HEAD : h * HEAD + half, :]
                b = ref[h * HEAD + half : (h + 1) * HEAD, :]
                parts += [(a * cosine + b * sine).astype(BF16), (b * cosine - a * sine).astype(BF16)]
            g = jnp.concatenate(parts, axis=0)
        dw_ref[:, j, :, pl.ds(pl.multiple_of(i * block, block), block)] = dot(hidden, g, 1, 1).astype(BF16).reshape(fs, each, block)
        hg_ref[...] += dot(w_ref[:, j].reshape(width, block), g, 1, 0)

    @pl.when(i == pl.num_programs(0) - 1)
    def _():
        dw_ref[:, 3] = dwo_ref[...].reshape(fs, each, width)
        def cols(c, acc):
            at = pl.ds(pl.multiple_of(c * 128, 128), 128)
            dx, gg = ln_back(x_ref[:, at].astype(F32), hg_ref[:, at], gain_ref[:, 0:1])
            first_ref[:, at] = (sg_ref[:, at] + dx).astype(BF16)
            return acc + gg
        acc = lax.fori_loop(0, length // 128, cols, jnp.zeros((width, 128), F32))
        gg_ref[...] = jnp.sum(acc, axis=1, keepdims=True)

def ln_back(x, g, gain):
    centred = x - jnp.mean(x, axis=0, keepdims=True)
    spread = jnp.mean(centred * centred, axis=0, keepdims=True)
    rs = lax.rsqrt(spread + EPS)
    xh = centred * rs
    gx = g * gain
    dx = rs * (gx - jnp.mean(gx, axis=0, keepdims=True) - xh * jnp.mean(gx * xh, axis=0, keepdims=True))
    return dx, g * xh

def attn_bwd(xT, gain, cosT, sinT, sg, hT, q, k, v, m, lse, w, fs):
    width, length = xT.shape
    block = 256
    n = width // block
    col = pl.BlockSpec((block, length), lambda i: (i, 0))
    full = whole((width, length))
    return pl.pallas_call(
        attn_bwd_kernel, grid=(n,), name="attn_bwd", cost_estimate=cost(62),
        in_specs=[full, whole(gain.shape), whole(cosT.shape), whole(sinT.shape), full, full, col, col, col, col,
                  pl.BlockSpec((1, 8, length), lambda i: (i, 0, 0)),
                  pl.BlockSpec((w.shape[0], 3, w.shape[2], block), lambda i: (0, 0, 0, i)),
                  pl.BlockSpec((w.shape[0], 1, w.shape[2], width), lambda i: (0, 3, 0, 0))],
        out_specs=[full, whole((width, 1)), whole((fs, 4, width // fs, width))],
        out_shape=[jax.ShapeDtypeStruct((width, length), BF16), jax.ShapeDtypeStruct((width, 1), F32),
                   jax.ShapeDtypeStruct((fs, 4, width // fs, width), BF16)],
        scratch_shapes=[pltpu.VMEM((width, length), F32), pltpu.VMEM((width, length), BF16), pltpu.VMEM((block, length), BF16),
                        pltpu.VMEM((block // HEAD, length, HEAD), BF16), pltpu.VMEM((block // HEAD, length, HEAD), BF16),
                        pltpu.VMEM((block, length), F32), pltpu.VMEM((block, length), F32), pltpu.VMEM((block, length), F32),
                        pltpu.VMEM((width, width), BF16)],
        compiler_params=params(),
    )(xT, gain, cosT, sinT, sg, hT, q, k, v, m, lse, w, w)
def ff_fwd_kernel(x_ref, m_ref, g2_ref, g3_ref, pos_ref, wo_ref, up_ref, down_ref,
                  x2_ref, h2_ref, x3_ref, head_ref, fin_ref):
    width, length = x_ref.shape
    i = pl.program_id(0)

    @pl.when(i == 0)
    def _():
        x2_ref[...] = x_ref[...].astype(F32) + dot(wo_ref[:, 0].reshape(width, width), m_ref[...], 0, 0)
        x3_ref[...] = x2_ref[...]
        def cols(c, carry):
            at = pl.ds(pl.multiple_of(c * 128, 128), 128)
            h2_ref[:, at] = ln(x2_ref[:, at], g2_ref[:, 1:2]).astype(BF16)
            return carry
        lax.fori_loop(0, length // 128, cols, 0)

    pre = dot(up_ref[0], h2_ref[...], 1, 0)
    act = jax.nn.gelu(pre, approximate=True).astype(BF16)
    x3_ref[...] += dot(down_ref[0], act, 0, 0)

    @pl.when(i == pl.num_programs(0) - 1)
    def _():
        def cols(c, carry):
            at = pl.ds(pl.multiple_of(c * 128, 128), 128)
            fin_ref[:, at] = ln(x3_ref[:, at], g3_ref[:, 2:3]).astype(BF16)
            return carry
        lax.fori_loop(0, length // 128, cols, 0)
        slots = pos_ref.shape[0]
        onehot = (pos_ref[...] == lax.broadcasted_iota(jnp.int32, (slots, length), 1)).astype(BF16)
        head_ref[...] = dot(onehot, fin_ref[...], 1, 1).astype(BF16)

def ln(x, gain):
    centred = x - jnp.mean(x, axis=0, keepdims=True)
    spread = jnp.mean(centred * centred, axis=0, keepdims=True)
    return centred * lax.rsqrt(spread + EPS) * gain

def ff_fwd(xT, m, g2, g3, pos, attn_w, ff_w):
    width, length = xT.shape
    hidden = ff_w.shape[1]
    block = 512
    n = hidden // block
    slots = pos.shape[0]
    full = whole((width, length))
    f = jax.ShapeDtypeStruct((width, length), F32)
    return pl.pallas_call(
        ff_fwd_kernel, grid=(n,), name="ff_fwd", cost_estimate=cost(34),
        in_specs=[full, full, whole(g2.shape), whole(g3.shape), whole((slots, 1)),
                  pl.BlockSpec((attn_w.shape[0], 1, attn_w.shape[2], width), lambda i: (0, 3, 0, 0)),
                  pl.BlockSpec((1, block, width), lambda i: (0, i, 0)),
                  pl.BlockSpec((1, block, width), lambda i: (1, i, 0))],
        out_specs=[full, full, full, whole((slots, width))],
        out_shape=[f, jax.ShapeDtypeStruct((width, length), BF16), f, jax.ShapeDtypeStruct((slots, width), BF16)],
        scratch_shapes=[pltpu.VMEM((width, length), BF16)],
        compiler_params=params(),
    )(xT, m, g2, g3, pos, attn_w, ff_w, ff_w)

def ff_bwd_kernel(x3_ref, x2_ref, h2_ref, rg_ref, pos_ref, g2_ref, g3_ref, up_ref, down_ref,
                  sg_ref, gg2_ref, gg3_ref, dw_ref, low_ref, hg_ref):
    width, length = x3_ref.shape
    i = pl.program_id(0)
    slots = pos_ref.shape[0]

    @pl.when(i == 0)
    def _():
        rows = rg_ref[...]
        high = rows.astype(BF16)
        rest = (rows - high.astype(F32)).astype(BF16)
        hg_ref[...] = jnp.zeros_like(hg_ref)
        def cols(c, acc):
            at = pl.ds(pl.multiple_of(c * 128, 128), 128)
            onehot = (pos_ref[...] == c * 128 + lax.broadcasted_iota(jnp.int32, (slots, 128), 1)).astype(BF16)
            fg = dot(high, onehot, 0, 0) + dot(rest, onehot, 0, 0)
            dx, gg = ln_back(x3_ref[:, at], fg, g3_ref[:, 2:3])
            sg_ref[:, at] = dx
            low_ref[:, at] = dx.astype(BF16)
            return acc + gg
        acc = lax.fori_loop(0, length // 128, cols, jnp.zeros((width, 128), F32))
        gg3_ref[...] = jnp.sum(acc, axis=1, keepdims=True)

    ag = dot(down_ref[0], low_ref[...], 1, 0)
    pre = dot(up_ref[0], h2_ref[...], 1, 0)
    c0, c1 = 0.7978845608028654, 0.044715
    t = jnp.tanh(c0 * (pre + c1 * pre * pre * pre))
    half = 0.5 * (1.0 + t)
    act = (pre * half).astype(BF16)
    slope = half + 0.5 * pre * (1.0 - t * t) * (c0 * (1.0 + 3.0 * c1 * pre * pre))
    pg = (slope * ag).astype(BF16)
    shape = (dw_ref.shape[0],) + dw_ref.shape[2:]
    dw_ref[:, 1] = dot(act, low_ref[...], 1, 1).astype(BF16).reshape(shape)
    dw_ref[:, 0] = dot(pg, h2_ref[...], 1, 1).astype(BF16).reshape(shape)
    hg_ref[...] += dot(up_ref[0], pg, 0, 0)

    @pl.when(i == pl.num_programs(0) - 1)
    def _():
        def cols(c, acc):
            at = pl.ds(pl.multiple_of(c * 128, 128), 128)
            dx, gg = ln_back(x2_ref[:, at], hg_ref[:, at], g2_ref[:, 1:2])
            sg_ref[:, at] += dx
            return acc + gg
        acc = lax.fori_loop(0, length // 128, cols, jnp.zeros((width, 128), F32))
        gg2_ref[...] = jnp.sum(acc, axis=1, keepdims=True)

def ff_bwd(x3, x2, h2, rg, pos, g2, g3, ff_w, fs):
    width, length = x3.shape
    hidden = ff_w.shape[1]
    each = hidden // fs
    block = each * max(1, 768 // each)
    n = hidden // block
    slots = pos.shape[0]
    full = whole((width, length))
    wb = pl.BlockSpec((block // each, 2, each, width), lambda i: (i, 0, 0, 0))
    g = jax.ShapeDtypeStruct((width, 1), F32)
    return pl.pallas_call(
        ff_bwd_kernel, grid=(n,), name="ff_bwd", cost_estimate=cost(45),
        in_specs=[full, full, full, whole((slots, width)), whole((slots, 1)), whole(g2.shape), whole(g3.shape),
                  pl.BlockSpec((1, block, width), lambda i: (0, i, 0)),
                  pl.BlockSpec((1, block, width), lambda i: (1, i, 0))],
        out_specs=[full, whole((width, 1)), whole((width, 1)), wb],
        out_shape=[jax.ShapeDtypeStruct((width, length), F32), g, g, jax.ShapeDtypeStruct((fs, 2, each, width), BF16)],
        scratch_shapes=[pltpu.VMEM((width, length), BF16), pltpu.VMEM((width, length), F32)],
        compiler_params=params(),
    )(x3, x2, h2, rg, pos, g2, g3, ff_w, ff_w)
RB = 256
FCH, BCH = 8, 8

def pick(n, top=8):
    return max(k for k in range(1, top + 1) if n % k == 0)

def table_kernel(source_ref, low_ref, turned_ref, *, shard):
    block = source_ref.shape[0]
    ids = pl.program_id(0) * block + lax.broadcasted_iota(jnp.int32, source_ref.shape, 0)
    low = jnp.where(ids < shard, source_ref[...], 0.0).astype(BF16)
    low_ref[...] = low
    turned_ref[...] = low.T

def table_both(table):
    shard, width = table.shape
    vocab = -(-shard // 128) * 128
    block = 640 if vocab % 640 == 0 else 128
    return pl.pallas_call(
        functools.partial(table_kernel, shard=shard), name="table_both", grid=(vocab // block,), cost_estimate=cost(12),
        in_specs=[pl.BlockSpec((block, width), lambda i: (i, 0))],
        out_specs=[pl.BlockSpec((block, width), lambda i: (i, 0)), pl.BlockSpec((width, block), lambda i: (0, i))],
        out_shape=[jax.ShapeDtypeStruct((vocab, width), BF16), jax.ShapeDtypeStruct((width, vocab), BF16)],
        compiler_params=params())(table)

def compact(meta_ref, rows_ref, comp_ref):
    nseq, slots, width = rows_ref.shape
    def clear(b, carry):
        comp_ref[pl.ds(pl.multiple_of(b * RB, RB), RB), :] = jnp.zeros((RB, width), BF16)
        return carry
    lax.fori_loop(0, meta_ref[2, 0], clear, 0)
    def seq(s, carry):
        def part(c, c2):
            comp_ref[pl.ds(pl.multiple_of((meta_ref[1, s] + c) * 16, 16), 16), :] = rows_ref[s, pl.ds(pl.multiple_of(c * 16, 16), 16), :]
            return c2
        lax.fori_loop(0, meta_ref[0, s], part, 0)
        return carry
    lax.fori_loop(0, nseq, seq, 0)

def vocab_fwd_kernel(meta_ref, limit_ref, rows_ref, table_ref, target_ref, lse_ref, chosen_ref, *outs, chunk, least, inside):
    comp_ref = outs[0] if inside else rows_ref
    vocab = table_ref.shape[0]
    if inside:
        nseq, slots, width = rows_ref.shape
        compact(meta_ref, rows_ref, comp_ref)
    lse_ref[...] = jnp.zeros_like(lse_ref)
    chosen_ref[...] = jnp.zeros_like(chosen_ref)
    limit = limit_ref[0]
    def block(b, carry):
        rows = comp_ref[pl.ds(pl.multiple_of(b * RB, RB), RB), :]
        target = target_ref[b]
        top = total = chosen = None
        for v in range(vocab // chunk):
            l = dot(table_ref[v * chunk:(v + 1) * chunk, :], rows, 1, 1)
            ids = v * chunk + lax.broadcasted_iota(jnp.int32, (chunk, RB), 0)
            hit = jnp.sum(jnp.where(ids == target, l, 0.0), axis=0, keepdims=True)
            if (v + 1) * chunk > least:
                l = jnp.where(ids < limit, l, -jnp.inf)
            m = jnp.max(l, axis=0, keepdims=True)
            if v == 0:
                top = m
                total = jnp.sum(jnp.exp(l - top), axis=0, keepdims=True)
                chosen = hit
            else:
                new = jnp.maximum(top, m)
                total = total * jnp.exp(top - new) + jnp.sum(jnp.exp(l - new), axis=0, keepdims=True)
                chosen = chosen + hit
                top = new
        lse_ref[b] = top + jnp.log(total)
        chosen_ref[b] = chosen
        return carry
    lax.fori_loop(0, meta_ref[2, 0], block, 0)

def vocab_fwd(meta, limit, rows, table, target, least):
    inside = rows.ndim == 3
    width = rows.shape[-1]
    nblk = target.shape[0]
    vocab = table.shape[0]
    chunk = 128 * pick(vocab // 128, FCH)
    smem = pl.BlockSpec(memory_space=pltpu.SMEM)
    vm = pl.BlockSpec(memory_space=pltpu.VMEM)
    st = jax.ShapeDtypeStruct((nblk, 1, RB), F32)
    comp = [jax.ShapeDtypeStruct((nblk * RB, width), BF16)] if inside else []
    out = pl.pallas_call(
        functools.partial(vocab_fwd_kernel, chunk=chunk, least=least, inside=inside), name="vocab_fwd", cost_estimate=cost(20),
        in_specs=[smem, smem, vm, vm, vm], out_specs=[vm] * (2 + len(comp)),
        out_shape=[st, st] + comp,
        compiler_params=params())(meta, limit, rows, table, target)
    return out[2] if inside else rows, out[0], out[1]

def vocab_bwd_kernel(meta_ref, limit_ref, comp_ref, table_ref, turned_ref, target_ref, lse_ref, scale_ref,
                     og_ref, og2_ref, rg_ref, acc_ref, rc_ref, low_ref, back_ref, sem, *, chunk, least, inside):
    vocab, width = table_ref.shape
    limit = limit_ref[0]
    nch = vocab // chunk
    def clear(b, carry):
        acc_ref[pl.ds(pl.multiple_of(b * 128, 128), 128), :] = jnp.zeros((128, width), F32)
        return carry
    lax.fori_loop(0, vocab // 128, clear, 0)
    def block(b, carry):
        rows = comp_ref[pl.ds(pl.multiple_of(b * RB, RB), RB), :]
        target, lse, scale = target_ref[b], lse_ref[b], scale_ref[b]
        rg = None
        for v in range(nch):
            l = dot(table_ref[v * chunk:(v + 1) * chunk, :], rows, 1, 1)
            ids = v * chunk + lax.broadcasted_iota(jnp.int32, (chunk, RB), 0)
            p = jnp.exp(l - lse)
            p = jnp.where(ids == target, p - 1.0, p)
            if (v + 1) * chunk > least:
                p = jnp.where(ids < limit, p, 0.0)
            g = (scale * p).astype(BF16)
            acc_ref[v * chunk:(v + 1) * chunk, :] += dot(g, rows, 1, 0)
            part = dot(turned_ref[:, v * chunk:(v + 1) * chunk], g, 1, 0)
            rg = part if rg is None else rg + part
        rc_ref[pl.ds(pl.multiple_of(b * RB, RB), RB), :] = rg.T.astype(BF16)
        return carry
    lax.fori_loop(0, meta_ref[2, 0], block, 0)
    if inside:
        nseq, slots, _ = back_ref.shape
        def seq(s, carry):
            back_ref[s] = jnp.zeros((slots, width), BF16)
            def part(c, c2):
                back_ref[s, pl.ds(pl.multiple_of(c * 16, 16), 16), :] = rc_ref[pl.ds(pl.multiple_of((meta_ref[1, s] + c) * 16, 16), 16), :]
                return c2
            lax.fori_loop(0, meta_ref[0, s], part, 0)
            return carry
        lax.fori_loop(0, nseq, seq, 0)
        out = pltpu.make_async_copy(back_ref, rg_ref, sem.at[0])
    else:
        out = pltpu.make_async_copy(rc_ref, rg_ref, sem.at[0])
    out.start()
    outs = [out]
    part = og_ref.shape[0]
    for v, (ref, start) in enumerate(((og_ref, 0), (og2_ref, part))):
        at = pl.ds(start, ref.shape[0])
        low_ref[at, :] = acc_ref[at, :].astype(BF16)
        outs.append(pltpu.make_async_copy(low_ref.at[at], ref, sem.at[1 + v]))
        outs[-1].start()
    for o in outs:
        o.wait()

def vocab_bwd(meta, limit, comp, table, turned, target, lse, scale, least, nseq, slots, inside):
    rows, width = comp.shape
    vocab = table.shape[0]
    chunk = 128 * pick(vocab // 128, BCH)
    smem = pl.BlockSpec(memory_space=pltpu.SMEM)
    vm = pl.BlockSpec(memory_space=pltpu.VMEM)
    hbm = pl.BlockSpec(memory_space=pl.ANY)
    shape = (nseq, slots, width) if inside else (rows, width)
    part = vocab // 256 * 128
    return pl.pallas_call(
        functools.partial(vocab_bwd_kernel, chunk=chunk, least=least, inside=inside), name="vocab_bwd", cost_estimate=cost(40),
        in_specs=[smem, smem] + [vm] * 6, out_specs=[hbm, hbm, hbm],
        out_shape=[jax.ShapeDtypeStruct((part, width), BF16), jax.ShapeDtypeStruct((vocab - part, width), BF16), jax.ShapeDtypeStruct(shape, BF16)],
        scratch_shapes=[pltpu.VMEM((vocab, width), F32), pltpu.VMEM((rows, width), BF16),
                        pltpu.VMEM((vocab, width), BF16), pltpu.VMEM(shape if inside else (1, 16, width), BF16),
                        pltpu.SemaphoreType.DMA((3,))],
        compiler_params=params())(meta, limit, comp, table, turned, target, lse, scale)

def plan(counts, slots, length):
    nseq = counts.shape[0]
    units = (counts + 15) // 16
    ends = jnp.cumsum(units)
    offs = ends - units
    total = ends[-1] * 16
    nblk = (total + RB - 1) // RB
    cap = (nseq * slots + RB - 1) // RB * RB
    at = jnp.arange(cap, dtype=jnp.int32)
    seq = jnp.minimum(jnp.sum((at[:, None] >= ends[None, :] * 16).astype(jnp.int32), axis=1), nseq - 1)
    mine = (seq[:, None] == jnp.arange(nseq, dtype=jnp.int32)[None, :])
    slot = at - jnp.sum(jnp.where(mine, offs[None, :] * 16, 0), axis=1)
    cnt = jnp.sum(jnp.where(mine, counts[None, :], 0), axis=1)
    live = slot < cnt
    weight = jnp.where(live, length / cnt.astype(F32), 0.0)
    meta = jnp.stack([units, offs, jnp.full((nseq,), nblk)]).astype(jnp.int32)
    return meta, seq, slot, weight

def spread(values, seq, slot):
    nseq, slots = values.shape
    parts = jnp.concatenate([values // 256, values % 256], axis=1).astype(BF16)
    mine = (seq[:, None] == jnp.arange(nseq, dtype=jnp.int32)[None, :]).astype(BF16)
    rows = jnp.dot(mine, parts, preferred_element_type=F32)
    hit = slot[:, None] == jnp.arange(slots, dtype=jnp.int32)[None, :]
    both = rows[:, :slots] * 256.0 + rows[:, slots:]
    return jnp.sum(jnp.where(hit, both, 0.0), axis=1).astype(jnp.int32)

def halves(vocab):
    nb = vocab // 128
    low = (nb + 1) // 2
    return nb, low

def sections(count, size):
    return [(s, min(size, count - s)) for s in range(0, count, size)]

def gather_kernel(ids_ref, flag_ref, emb_ref, out_ref, tab_ref, raw_ref, row_ref, sem):
    feat, vocab = emb_ref.shape
    nseq, _, length = out_ref.shape
    nb, low = halves(vocab)
    size = -(-low // 6)
    secs = sections(low, size)
    def copies(k):
        s, n = secs[k]
        out = [pltpu.make_async_copy(emb_ref.at[:, pl.ds(s * 128, n * 128)], raw_ref.at[:, pl.ds(s * 128, n * 128)], sem.at[2 * k])]
        m = min(n, nb - low - s)
        if m > 0:
            out.append(pltpu.make_async_copy(emb_ref.at[:, pl.ds((low + s) * 128, m * 128)], raw_ref.at[:, pl.ds((low + s) * 128, m * 128)], sem.at[2 * k + 1]))
        return out
    for k in range(len(secs)):
        for c in copies(k):
            c.start()
    pad = jnp.zeros((64 - feat, 128), F32)
    for k in range(len(secs)):
        for c in copies(k):
            c.wait()
        s, n = secs[k]
        m = max(0, min(n, nb - low - s))
        def turn(b, carry):
            a = raw_ref[:, pl.ds(pl.multiple_of(b * 128, 128), 128)]
            h = raw_ref[:, pl.ds(pl.multiple_of((low + b) * 128, 128), 128)]
            tab_ref[pl.ds(pl.multiple_of(b * 128, 128), 128), :] = jnp.concatenate([a, pad, h, pad], axis=0).T
            return carry
        lax.fori_loop(s, s + m, turn, 0, unroll=3)
        for b in range(s + m, s + n):
            a = raw_ref[:, b * 128:(b + 1) * 128]
            tab_ref[b * 128:(b + 1) * 128, :] = jnp.concatenate([a, pad, pad, jnp.zeros((feat, 128), F32)], axis=0).T
    U = 32
    def seq(s, carry):
        def grp(g, c2):
            base = pl.multiple_of(g * U, U)
            for j in range(U):
                i = ids_ref[s * length + base + j]
                row_ref[pl.ds(base + j, 1), :] = tab_ref[pl.ds(i, 1), :]
            return c2
        lax.fori_loop(0, length // U, grp, 0)
        for c in range(length // 128):
            t = row_ref[c * 128:(c + 1) * 128, :].T
            f = flag_ref[s, :, c * 128:(c + 1) * 128] > 0
            out_ref[s, :, c * 128:(c + 1) * 128] = jnp.where(f, t[64:64 + feat], t[:feat]).astype(BF16)
        return carry
    lax.fori_loop(0, nseq, seq, 0)

def split_ids(ids, vocab):
    nb, low = halves(vocab)
    high = ids >= low * 128
    return jnp.where(high, ids - low * 128, ids), high.astype(jnp.int32)

def gather(ids, emb):
    nseq, length = ids.shape
    feat, vocab = emb.shape
    nb, low = halves(vocab)
    rid, flag = split_ids(ids, vocab)
    return pl.pallas_call(gather_kernel, name="emb_gather", cost_estimate=cost(32),
        in_specs=[pl.BlockSpec(memory_space=pltpu.SMEM), pl.BlockSpec(memory_space=pltpu.VMEM), pl.BlockSpec(memory_space=pl.ANY)],
        out_specs=pl.BlockSpec(memory_space=pltpu.VMEM),
        out_shape=jax.ShapeDtypeStruct((nseq, feat, length), BF16),
        scratch_shapes=[pltpu.VMEM((low * 128, 128), F32), pltpu.VMEM((feat, vocab), F32), pltpu.VMEM((length, 128), F32), pltpu.SemaphoreType.DMA((12,))],
        compiler_params=params())(rid.reshape(-1), flag.reshape(nseq, 1, length), emb)

def scatter_kernel(ids_ref, flag_ref, *refs, ng, per):
    g_refs = refs[:ng]
    out_ref, sq_ref, raw_ref, row_ref, sem = refs[ng:ng + 5]
    tabs = refs[ng + 5:]
    feat, vocab = out_ref.shape
    nseq, _, length = g_refs[0].shape
    nb, low = halves(vocab)
    zero128 = jnp.zeros((128, 128), F32)
    def zero(b, carry):
        for t in tabs:
            t[pl.ds(pl.multiple_of(b * 128, 128), 128), :] = zero128
        return carry
    lax.fori_loop(0, low, zero, 0)
    pad = jnp.zeros((64 - feat, 128), F32)
    U = 16
    streams = [(g, p) for g in range(ng) for p in range(per)]
    each = nseq // per
    def seq(s, carry):
        for k, (g, p) in enumerate(streams):
            q = p * each + s
            for c in range(length // 128):
                at = slice(c * 128, (c + 1) * 128)
                v = g_refs[g][q, :, at].astype(F32)
                f = flag_ref[g * nseq + q, :, at] > 0
                row_ref[k, at, :] = jnp.concatenate([jnp.where(f, 0.0, v), pad, jnp.where(f, v, 0.0), pad], axis=0).T
        def grp(n, c2):
            base = pl.multiple_of(n * U, U)
            for j in range(U):
                idx = [ids_ref[(g * nseq + p * each + s) * length + base + j] for g, p in streams]
                old = [tabs[k][pl.ds(idx[k], 1), :] for k in range(len(streams))]
                new = [old[k] + row_ref[k, pl.ds(base + j, 1), :] for k in range(len(streams))]
                for k in range(len(streams)):
                    tabs[k][pl.ds(idx[k], 1), :] = new[k]
            return c2
        lax.fori_loop(0, length // U, grp, 0)
        return carry
    lax.fori_loop(0, each, seq, 0)
    def tile(b):
        at = pl.ds(pl.multiple_of(b * 128, 128), 128)
        parts = [sum((tabs[g * per + p][at, :] for p in range(1, per)), tabs[g * per][at, :]) for g in range(ng)]
        return sum(parts[1:], parts[0]).T
    size = -(-low // 6)
    secs = sections(low, size)
    def copies(k):
        s, n = secs[k]
        out = [pltpu.make_async_copy(raw_ref.at[k % 2, 0, :, pl.ds(0, n * 128)], out_ref.at[:, pl.ds(s * 128, n * 128)], sem.at[2 * k])]
        m = min(n, nb - low - s)
        if m > 0:
            out.append(pltpu.make_async_copy(raw_ref.at[k % 2, 1, :, pl.ds(0, m * 128)], out_ref.at[:, pl.ds((low + s) * 128, m * 128)], sem.at[2 * k + 1]))
        return out
    squares = jnp.zeros((128, 128), F32)
    for k, (s, n) in enumerate(secs):
        if k >= 2:
            for c in copies(k - 2):
                c.wait()
        def turn(b, carry, s=s, k=k):
            t = tile(b)
            at = pl.ds(pl.multiple_of((b - s) * 128, 128), 128)
            raw_ref[k % 2, 0, :, at] = t[:feat].astype(BF16)
            raw_ref[k % 2, 1, :, at] = t[64:64 + feat].astype(BF16)
            return carry + t * t
        squares = lax.fori_loop(s, s + n, turn, squares, unroll=3)
        for c in copies(k):
            c.start()
    sq_ref[...] = squares
    for k in range(max(0, len(secs) - 2), len(secs)):
        for c in copies(k):
            c.wait()

def scatter(ids, gs, vocab, per):
    nseq, feat, length = gs[0].shape
    nb, low = halves(vocab)
    rid, flag = split_ids(ids, vocab)
    ng = len(gs)
    size = -(-low // 6)
    vm = pl.BlockSpec(memory_space=pltpu.VMEM)
    return pl.pallas_call(functools.partial(scatter_kernel, ng=ng, per=per), name="emb_scatter", cost_estimate=cost(1),
        in_specs=[pl.BlockSpec(memory_space=pltpu.SMEM), vm] + [vm] * ng,
        out_specs=[pl.BlockSpec(memory_space=pl.ANY), vm],
        out_shape=[jax.ShapeDtypeStruct((feat, vocab), BF16), jax.ShapeDtypeStruct((128, 128), F32)],
        scratch_shapes=[pltpu.VMEM((2, 2, feat, size * 128), BF16), pltpu.VMEM((ng * per, length, 128), F32), pltpu.SemaphoreType.DMA((12,))]
            + [pltpu.VMEM((low * 128, 128), F32)] * (ng * per),
        compiler_params=params(62 * 1024 * 1024))(rid.reshape(-1), flag.reshape(-1, 1, length), *gs)
AHEAD = 2
MESH_ID = pl.DeviceIdType.MESH

def comm_params(ident):
    return pltpu.CompilerParams(collective_id=ident, has_side_effects=True, vmem_limit_bytes=VL)

def meet(peers):
    barrier = pltpu.get_barrier_semaphore()
    for p in peers:
        pl.semaphore_signal(barrier, inc=1, device_id=p, device_id_type=MESH_ID)
    pl.semaphore_wait(barrier, len(peers))

def remote(src, dst, send, recv, peer):
    return pltpu.make_async_remote_copy(src_ref=src, dst_ref=dst, send_sem=send, recv_sem=recv, device_id=peer, device_id_type=MESH_ID)

def small_kernel(x_ref, *refs, fs, dps, wide, finish):
    out_ref = refs[0]
    got_ref = refs[1] if finish else out_ref
    send, recv = refs[-2:]
    d, f = lax.axis_index("dp"), lax.axis_index("fsdp")
    n = fs * dps if wide else fs
    me = d * fs + f if wide else f
    def peer(k):
        j = lax.rem(me + k, n)
        return (lax.div(j, fs), lax.rem(j, fs)) if wide else (d, j)
    barrier = pltpu.get_barrier_semaphore()
    def greet(k, carry):
        pl.semaphore_signal(barrier, inc=1, device_id=peer(k), device_id_type=MESH_ID)
        return carry
    lax.fori_loop(1, n, greet, 0)
    pl.semaphore_wait(barrier, n - 1)
    def copy(k):
        return remote(x_ref, got_ref.at[me], send.at[k], recv.at[k], peer(k))
    def begin(k, carry):
        copy(k).start()
        return carry
    lax.fori_loop(1, n, begin, 0)
    got_ref[me] = x_ref[...]
    def end(k, carry):
        copy(k).wait()
        return carry
    lax.fori_loop(1, n, end, 0)
    if finish:
        finish(got_ref, out_ref, n)

def lse_finish(got_ref, out_ref, n):
    top = got_ref[0]
    for i in range(1, n):
        top = jnp.maximum(top, got_ref[i])
    total = jnp.exp(got_ref[0] - top)
    for i in range(1, n):
        total = total + jnp.exp(got_ref[i] - top)
    out_ref[...] = top + jnp.log(total)

def sum_finish(got_ref, out_ref, n):
    total = got_ref[0]
    for i in range(1, n):
        total = total + got_ref[i]
    out_ref[...] = total

def small_gather(x, ident, wide=False, finish=None, name="small_gather"):
    fs, dps = lax.axis_size("fsdp"), lax.axis_size("dp")
    n = fs * dps if wide else fs
    vm = pl.BlockSpec(memory_space=pltpu.VMEM)
    got = (n,) + x.shape
    return pl.pallas_call(
        functools.partial(small_kernel, fs=fs, dps=dps, wide=wide, finish=finish), name=name,
        in_specs=[vm], out_specs=vm,
        out_shape=jax.ShapeDtypeStruct(x.shape if finish else got, x.dtype),
        scratch_shapes=([pltpu.VMEM(got, x.dtype)] if finish else []) + [pltpu.SemaphoreType.DMA((n,)), pltpu.SemaphoreType.DMA((n,))],
        cost_estimate=cost(12), compiler_params=comm_params(ident))(x)

def exchange_kernel(*refs, fs, both, aux, reduce, pairs):
    refs = list(refs)
    x_ref = refs.pop(0)
    aux_ref = refs.pop(0) if aux else None
    w_ref = refs.pop(0) if reduce else None
    pair_refs = [refs.pop(0) for _ in range(2 * pairs)]
    out_ref = refs.pop(0)
    other_ref = refs.pop(0) if both else None
    sum_ref = refs.pop(0) if aux else None
    red_ref = refs.pop(0) if reduce else None
    if pairs:
        sq_ref = refs.pop(0)
        held = [refs.pop() for _ in range(2 * pairs)]
        held_sem = refs.pop()
    send, recv, send2, recv2, own = refs[:5]
    refs = refs[5:]
    if aux:
        near_ref, over_ref = refs.pop(0), refs.pop(0)
    if reduce:
        _, parts, red_begin, red_middle, red_end = reduce_phases(w_ref, red_ref, *refs, high=fs // 4, both=both)
    d, f = lax.axis_index("dp"), lax.axis_index("fsdp")
    across = (1 - d, f)
    barrier = pltpu.get_barrier_semaphore()
    def greet(k, carry):
        pl.semaphore_signal(barrier, inc=1, device_id=(d, lax.rem(f + k, fs)), device_id_type=MESH_ID)
        return carry
    lax.fori_loop(1, fs, greet, 0)
    if both:
        pl.semaphore_signal(barrier, inc=1, device_id=across, device_id_type=MESH_ID)
    pl.semaphore_wait(barrier, fs if both else fs - 1)
    def copies(k):
        j = lax.rem(f + k, fs)
        out = [remote(x_ref.at[j], out_ref.at[f], send.at[0, k], recv.at[0, k], (d, j))]
        if aux:
            out.append(remote(aux_ref, near_ref.at[f], send.at[1, k], recv.at[1, k], (d, j)))
        return out
    def passed(k):
        s = lax.rem(f + fs - k, fs)
        out = [remote(out_ref.at[s], other_ref.at[s], send2.at[0, k], recv2.at[0, k], across)]
        if aux:
            out.append(remote(near_ref.at[s], over_ref.at[s], send2.at[1, k], recv2.at[1, k], across))
        return out
    def first():
        out = [remote(x_ref.at[f], other_ref.at[f], send2.at[0, 0], recv2.at[0, 0], across)]
        if aux:
            out.append(remote(aux_ref, over_ref.at[f], send2.at[1, 0], recv2.at[1, 0], across))
        return out
    if reduce:
        red_begin()
    if both:
        for c in first():
            c.start()
    def begin(k, carry):
        for c in copies(k):
            c.start()
        return carry
    lax.fori_loop(1, fs, begin, 0)
    mine = pltpu.make_async_copy(x_ref.at[f], out_ref.at[f], own)
    mine.start()
    if aux:
        near_ref[f] = aux_ref[...]
    mine.wait()
    def arrive(k, carry):
        for c in copies(k):
            c.wait_recv()
        if both:
            for c in passed(k):
                c.start()
        return carry
    if pairs:
        loads = [pltpu.make_async_copy(a, b, held_sem.at[i]) for i, (a, b) in enumerate(zip(pair_refs, held))]
        for l in loads:
            l.start()
        for l in loads:
            l.wait()
        total = jnp.zeros((8, held[0].shape[1]), F32)
        for i in range(pairs):
            a_ref, b_ref = held[2 * i], held[2 * i + 1]
            def add(n, t, a_ref=a_ref, b_ref=b_ref):
                at = pl.ds(pl.multiple_of(n * 64, 64), 64)
                s = a_ref[at, :].astype(F32) + b_ref[at, :].astype(F32)
                s = s * s
                for j in range(0, 64, 8):
                    t = t + s[j:j + 8]
                return t
            total = lax.fori_loop(0, a_ref.shape[0] // 64, add, total)
        sq_ref[...] = total
    steps = parts + 1 if reduce else 1
    marks = [1 + (fs - 1) * i // steps for i in range(steps + 1)]
    for i in range(steps):
        if reduce:
            red_middle(i)
        lax.fori_loop(marks[i], marks[i + 1], arrive, 0)
    if reduce:
        red_end()
    def end(k, carry):
        for c in copies(k):
            c.wait_send()
        if both:
            for c in passed(k):
                c.wait()
        return carry
    lax.fori_loop(1, fs, end, 0)
    if both:
        for c in first():
            c.wait()
    if aux:
        total = near_ref[0]
        for i in range(1, fs):
            total = total + near_ref[i]
        if both:
            rest = over_ref[0]
            for i in range(1, fs):
                rest = rest + over_ref[i]
            total = total + rest
        sum_ref[...] = total

def exchange(x, ident, both, name, aux=None, reduce=None, pairs=()):
    fs = lax.axis_size("fsdp")
    vm = pl.BlockSpec(memory_space=pltpu.VMEM)
    shape = jax.ShapeDtypeStruct(x.shape, x.dtype)
    sem = pltpu.SemaphoreType.DMA((2, fs))
    more = [] if aux is None else [pltpu.VMEM((fs,) + aux.shape, F32)] * 2
    outs = [shape] * (2 if both else 1) + ([] if aux is None else [jax.ShapeDtypeStruct(aux.shape, F32)])
    args = [x] + [a for a in (aux, reduce) if a is not None]
    if reduce is not None:
        block = reduce.shape[1:]
        outs.append(jax.ShapeDtypeStruct(block, F32))
        more = more + reduce_scratch(block, reduce.dtype, fs // 4)
    ins = [vm] * len(args) + [pl.BlockSpec(memory_space=pl.ANY)] * len(pairs)
    if pairs:
        outs.append(jax.ShapeDtypeStruct((8, pairs[0].shape[1]), F32))
        more = more + [pltpu.SemaphoreType.DMA((len(pairs),))] + [pltpu.VMEM(p.shape, p.dtype) for p in reversed(pairs)]
    return pl.pallas_call(
        functools.partial(exchange_kernel, fs=fs, both=both, aux=aux is not None, reduce=reduce is not None, pairs=len(pairs) // 2), name=name,
        in_specs=ins, out_specs=[vm] * len(outs), out_shape=outs,
        scratch_shapes=[sem, sem, sem, sem, pltpu.SemaphoreType.DMA] + more,
        cost_estimate=cost(55),
        compiler_params=comm_params(ident))(*args, *pairs)

def cuts(rows):
    n = 4 if rows % 64 == 0 else 1
    return n, rows // n

def gather_phases(x_ref, out_ref, send, recv, *, high):
    d, f = lax.axis_index("dp"), lax.axis_index("fsdp")
    h, m, c = lax.div(f, 4), lax.rem(lax.div(f, 2), 2), lax.rem(f, 2)
    side, twin = (d, h * 4 + (1 - m) * 2 + c), (d, h * 4 + m * 2 + 1 - c)
    parts, size = cuts(x_ref.shape[0])
    def far(k):
        return (d, lax.rem(h + k, high) * 4 + m * 2 + c)
    peers = [far(k) for k in range(1, high)] + [side, twin]
    sent = []
    def go(src, block, p, peer):
        at = pl.ds(p * size, size)
        r = remote(src.at[at], out_ref.at[block, at], send.at[len(sent)], recv.at[block, p], peer)
        r.start()
        sent.append(r)
    def arrived(block, p):
        at = pl.ds(p * size, size)
        remote(x_ref.at[at], out_ref.at[block, at], send.at[0], recv.at[block, p], twin).wait_recv()
    def back(k, row):
        return lax.rem(h + high - k, high) * 4 + row * 2 + c
    def launch(p):
        for k in range(1, high):
            go(x_ref, f, p, far(k))
        go(x_ref, f, p, side)
        go(x_ref, f, p, twin)
    ahead = min(AHEAD, parts)
    def begin():
        for p in range(ahead):
            launch(p)
        out_ref[f] = x_ref[...]
    def middle(p):
        if p < parts:
            for k in range(1, high):
                b = back(k, m)
                arrived(b, p)
                go(out_ref.at[b], b, p, side)
                go(out_ref.at[b], b, p, twin)
            if p + ahead < parts:
                launch(p + ahead)
        if p > 0:
            for k in range(high):
                b = back(k, 1 - m)
                arrived(b, p - 1)
                go(out_ref.at[b], b, p - 1, twin)
    def end():
        for row in range(2):
            for k in range(high):
                for p in range(parts):
                    arrived(lax.rem(h + high - k, high) * 4 + lax.rem(m + row, 2) * 2 + 1 - c, p)
        for r in sent:
            r.wait_send()
    return peers, parts, begin, middle, end

def rows_gather_kernel(x_ref, out_ref, send, recv, *, high):
    peers, parts, begin, middle, end = gather_phases(x_ref, out_ref, send, recv, high=high)
    meet(peers)
    begin()
    for p in range(parts + 1):
        middle(p)
    end()

def rows_gather(x, ident, name="rows_gather"):
    fs = lax.axis_size("fsdp")
    vm = pl.BlockSpec(memory_space=pltpu.VMEM)
    high = fs // 4
    parts = cuts(x.shape[0])[0]
    return pl.pallas_call(
        functools.partial(rows_gather_kernel, high=high), name=name,
        in_specs=[vm], out_specs=vm, out_shape=jax.ShapeDtypeStruct((fs,) + x.shape, x.dtype),
        scratch_shapes=[pltpu.SemaphoreType.DMA((4 * high * parts,)), pltpu.SemaphoreType.DMA((fs, parts))],
        cost_estimate=cost(40), compiler_params=comm_params(ident))(x)

def reduce_phases(x_ref, out_ref, twin_ref, side_ref, far_ref, a_ref, b_ref, s1, r1, s2, r2, s3, r3, *, high, both):
    d, f = lax.axis_index("dp"), lax.axis_index("fsdp")
    h, m, c = lax.div(f, 4), lax.rem(lax.div(f, 2), 2), lax.rem(f, 2)
    side, twin = (d, h * 4 + (1 - m) * 2 + c), (d, h * 4 + m * 2 + 1 - c)
    def far(k):
        return (d, lax.rem(h + k, high) * 4 + m * 2 + c)
    across = (1 - d, f)
    peers = [far(k) for k in range(1, high)] + [side, twin] + ([across] if both else [])
    order = list(range(1, high)) + [0]
    parts, size = cuts(x_ref.shape[1])
    def rows(p):
        return pl.ds(p * size, size)
    def at(k):
        return lax.rem(h + k, high)
    def one(k, row, p):
        slot = at(k) * 2 + row
        return remote(x_ref.at[at(k) * 4 + row * 2 + 1 - c, rows(p)], twin_ref.at[slot, rows(p)], s1.at[slot, p], r1.at[slot, p], twin)
    def two(k, p):
        return remote(a_ref.at[at(k), rows(p)], side_ref.at[at(k), rows(p)], s2.at[at(k), p], r2.at[at(k), p], side)
    def three(k, p):
        return remote(b_ref.at[k, rows(p)], far_ref.at[k, rows(p)], s3.at[k, p], r3.at[k, p], far(k))
    def last(p):
        return remote(b_ref.at[0, rows(p)], far_ref.at[0, rows(p)], s3.at[0, p], r3.at[0, p], across)
    def begin():
        for p in range(parts):
            for k in order:
                one(k, 1 - m, p).start()
            for k in order:
                one(k, m, p).start()
    def middle(p):
        if p < parts:
            if p >= 2:
                for k in order:
                    two(k, p - 2).wait_send()
            for k in order:
                one(k, 1 - m, p).wait_recv()
                a_ref[at(k), rows(p)] = (x_ref[at(k) * 4 + (1 - m) * 2 + c, rows(p)].astype(F32) + twin_ref[at(k) * 2 + 1 - m, rows(p)].astype(F32)).astype(a_ref.dtype)
                two(k, p).start()
        if p > 0:
            q = p - 1
            for k in order:
                one(k, m, q).wait_recv()
                two(k, q).wait_recv()
                total = x_ref[at(k) * 4 + m * 2 + c, rows(q)].astype(F32) + twin_ref[at(k) * 2 + m, rows(q)].astype(F32) + side_ref[at(k), rows(q)].astype(F32)
                if k == 0:
                    out_ref[rows(q)] = total
                else:
                    b_ref[k, rows(q)] = total.astype(b_ref.dtype)
                    three(k, q).start()
    def end():
        for p in range(parts):
            for k in range(1, high):
                three(k, p).wait_recv()
                out_ref[rows(p)] += far_ref[k, rows(p)].astype(F32)
            if both:
                b_ref[0, rows(p)] = out_ref[rows(p)].astype(b_ref.dtype)
                last(p).start()
        for p in range(parts):
            if both:
                last(p).wait()
                out_ref[rows(p)] = b_ref[0, rows(p)].astype(F32) + far_ref[0, rows(p)].astype(F32)
            for k in order:
                one(k, m, p).wait_send()
                one(k, 1 - m, p).wait_send()
                if p + 2 >= parts:
                    two(k, p).wait_send()
                if k:
                    three(k, p).wait_send()
    return peers, parts, begin, middle, end

def rows_reduce_kernel(*refs, high, both):
    peers, parts, begin, middle, end = reduce_phases(*refs, high=high, both=both)
    meet(peers)
    begin()
    for p in range(parts + 1):
        middle(p)
    end()

def reduce_scratch(block, dtype, high):
    parts = cuts(block[0])[0]
    def sem(n):
        return pltpu.SemaphoreType.DMA((n, parts))
    def buf(n):
        return pltpu.VMEM((n,) + block, dtype)
    return [buf(2 * high), buf(high), buf(high), buf(high), buf(high),
            sem(2 * high), sem(2 * high), sem(high), sem(high), sem(high), sem(high)]

def rows_reduce(x, ident, name="rows_reduce", both=False):
    vm = pl.BlockSpec(memory_space=pltpu.VMEM)
    high = lax.axis_size("fsdp") // 4
    block = x.shape[1:]
    return pl.pallas_call(
        functools.partial(rows_reduce_kernel, high=high, both=both), name=name,
        in_specs=[vm], out_specs=vm, out_shape=jax.ShapeDtypeStruct(block, F32),
        scratch_shapes=reduce_scratch(block, x.dtype, high),
        cost_estimate=cost(45), compiler_params=comm_params(ident))(x)
def front_kernel(ids_ref, w_ref, emb_ref, all_ref, x_ref, full_ref, low_ref, tab_ref, raw_ref, row_ref, picked_ref, smem_ref,
                 raw_sem, ids_send, ids_recv, x_send, x_recv, smem_sem, w_send, w_recv, *, fs, dps):
    feat, vocab = emb_ref.shape
    length = x_ref.shape[2]
    lines = length // 128
    nb, low = halves(vocab)
    secs = sections(low, -(-low // 6))
    d, f = lax.axis_index("dp"), lax.axis_index("fsdp")
    n, me = fs * dps, d * fs + f
    def load(k):
        s, c = secs[k]
        out = [pltpu.make_async_copy(emb_ref.at[:, pl.ds(s * 128, c * 128)], raw_ref.at[:, pl.ds(s * 128, c * 128)], raw_sem.at[2 * k])]
        m = min(c, nb - low - s)
        if m > 0:
            out.append(pltpu.make_async_copy(emb_ref.at[:, pl.ds((low + s) * 128, m * 128)], raw_ref.at[:, pl.ds((low + s) * 128, m * 128)], raw_sem.at[2 * k + 1]))
        return out
    for k in range(len(secs)):
        for c in load(k):
            c.start()
    low_ref[...] = w_ref[...].astype(BF16)
    _, parts, w_begin, w_middle, w_end = gather_phases(low_ref, full_ref, w_send, w_recv, high=fs // 4)
    def peer(k):
        j = lax.rem(me + k, n)
        return (lax.div(j, fs), lax.rem(j, fs))
    barrier = pltpu.get_barrier_semaphore()
    def greet(k, carry):
        pl.semaphore_signal(barrier, inc=1, device_id=peer(k), device_id_type=MESH_ID)
        return carry
    lax.fori_loop(1, n, greet, 0)
    pl.semaphore_wait(barrier, n - 1)
    def ids_copy(k):
        return remote(ids_ref, all_ref.at[me], ids_send.at[k], ids_recv.at[k], peer(k))
    def ids_begin(k, carry):
        ids_copy(k).start()
        return carry
    lax.fori_loop(1, n, ids_begin, 0)
    all_ref[me] = ids_ref[...]
    w_begin()

    pad = jnp.zeros((64 - feat, 128), F32)
    for k in range(len(secs)):
        for c in load(k):
            c.wait()
        s, c = secs[k]
        m = max(0, min(c, nb - low - s))
        def turn(b, carry):
            a = raw_ref[:, pl.ds(pl.multiple_of(b * 128, 128), 128)]
            h = raw_ref[:, pl.ds(pl.multiple_of((low + b) * 128, 128), 128)]
            tab_ref[pl.ds(pl.multiple_of(b * 128, 128), 128), :] = jnp.concatenate([a, pad, h, pad], axis=0).T
            return carry
        lax.fori_loop(s, s + m, turn, 0, unroll=3)
        for b in range(s + m, s + c):
            a = raw_ref[:, b * 128:(b + 1) * 128]
            tab_ref[b * 128:(b + 1) * 128, :] = jnp.concatenate([a, pad, pad, jnp.zeros((feat, 128), F32)], axis=0).T

    def ids_end(k, carry):
        ids_copy(k).wait()
        return carry
    lax.fori_loop(1, n, ids_end, 0)
    def to_smem(s):
        return pltpu.make_async_copy(all_ref.at[d * fs + s, pl.ds(0, lines)], smem_ref.at[s], smem_sem.at[s])
    def smem_begin(s, carry):
        to_smem(s).start()
        return carry
    def smem_end(s, carry):
        to_smem(s).wait()
        return carry
    lax.fori_loop(0, fs, smem_begin, 0)
    lax.fori_loop(0, fs, smem_end, 0)

    U = 32
    def fetch(s, put):
        def grp(g, carry):
            line, base = lax.div(g, 128 // U), lax.rem(g, 128 // U) * U
            for j in range(U):
                i = smem_ref[s, line, base + j]
                i = jnp.where(i >= low * 128, i - low * 128, i)
                row_ref[pl.ds(pl.multiple_of(g * U, U) + j, 1), :] = tab_ref[pl.ds(i, 1), :]
            return carry
        lax.fori_loop(0, length // U, grp, 0)
        ids = all_ref[d * fs + s]
        for c in range(lines):
            t = row_ref[c * 128:(c + 1) * 128, :].T
            high = ids[c:c + 1] >= low * 128
            put(c, jnp.where(high, t[64:64 + feat], t[:feat]).astype(BF16))
    def x_copy(k):
        s = lax.rem(f + k, fs)
        return remote(picked_ref.at[s], x_ref.at[f], x_send.at[k], x_recv.at[k], (d, s))
    def one(k, carry):
        s = lax.rem(f + k, fs)
        def put(c, v):
            picked_ref[s, :, c * 128:(c + 1) * 128] = v
        fetch(s, put)
        x_copy(k).start()
        return carry
    steps = parts + 1
    marks = [1 + (fs - 1) * i // steps for i in range(steps + 1)]
    for i in range(steps):
        lax.fori_loop(marks[i], marks[i + 1], one, 0)
        w_middle(i)
    def mine(c, v):
        x_ref[f, :, c * 128:(c + 1) * 128] = v
    fetch(f, mine)
    w_end()
    def x_end(k, carry):
        x_copy(k).wait()
        return carry
    lax.fori_loop(1, fs, x_end, 0)

def front(ids, w, emb, length, ident):
    fs, dps = lax.axis_size("fsdp"), lax.axis_size("dp")
    feat, vocab = emb.shape
    low = halves(vocab)[1]
    vm = pl.BlockSpec(memory_space=pltpu.VMEM)
    parts = cuts(w.shape[0])[0]
    def sem(*shape):
        return pltpu.SemaphoreType.DMA(shape)
    return pl.pallas_call(
        functools.partial(front_kernel, fs=fs, dps=dps), name="front",
        in_specs=[vm, vm, pl.BlockSpec(memory_space=pl.ANY)], out_specs=[vm, vm, vm],
        out_shape=[jax.ShapeDtypeStruct((fs * dps,) + ids.shape, ids.dtype), jax.ShapeDtypeStruct((fs, feat, length), BF16),
                   jax.ShapeDtypeStruct((fs,) + w.shape, BF16)],
        scratch_shapes=[pltpu.VMEM(w.shape, BF16), pltpu.VMEM((low * 128, 128), F32), pltpu.VMEM((feat, vocab), F32), pltpu.VMEM((length, 128), F32),
                        pltpu.VMEM((fs, feat, length), BF16), pltpu.SMEM((fs, length // 128, 128), jnp.int32),
                        sem(12), sem(fs * dps), sem(fs * dps), sem(fs), sem(fs), sem(fs), sem(fs * parts), sem(fs, parts)],
        cost_estimate=cost(85), compiler_params=comm_params(ident))(ids, w, emb)
def adam_kernel(factor_ref, w_ref, one_ref, two_ref, avg_ref, *refs, rate, first):
    outs = refs[-4:]
    grads = [r[...].astype(F32) for r in refs[:-4]]
    if first is None:
        g = grads[0]
    else:
        g = jnp.where(pl.program_id(0) < first, grads[0] + grads[1], grads[2] + grads[3])
    new, one, two = adamw(w_ref[...], one_ref[...], two_ref[...], g * factor_ref[0], rate)
    outs[0][...] = new
    outs[1][...] = one
    outs[2][...] = two
    outs[3][...] = ema_decay * avg_ref[...] + (1 - ema_decay) * new

def adam_table(factor, w, one, two, avg, grads, rate, by_rows):
    rows, cols = w.shape
    if by_rows:
        block, first = (768, cols), grads[0].shape[0] // 768
        steps = -(-rows // 768)
        spec = pl.BlockSpec(block, lambda i: (i, 0))
        early = pl.BlockSpec(block, lambda i: (jnp.minimum(i, first - 1), 0))
        late = pl.BlockSpec(block, lambda i: (jnp.maximum(i - first, 0), 0))
        gspecs = [early, early, late, late]
    else:
        block, first = (rows, 12672), None
        steps = -(-cols // 12672)
        spec = pl.BlockSpec(block, lambda i: (0, i))
        gspecs = [spec]
    shape = jax.ShapeDtypeStruct(w.shape, F32)
    return pl.pallas_call(
        functools.partial(adam_kernel, rate=rate, first=first), name="adam_rows" if by_rows else "adam_columns",
        grid=(steps,), cost_estimate=cost(1),
        in_specs=[pl.BlockSpec(memory_space=pltpu.SMEM)] + [spec] * 4 + gspecs, out_specs=[spec] * 4, out_shape=[shape] * 4,
        compiler_params=params())(factor.reshape(1), w, one, two, avg, *grads)
def shampoo_kernel(factor_ref, w_ref, grad_ref, left_ref, right_ref, root_ref, whole_ref, full_ref, avg_ref,
                   new_ref, clip_ref, left_out, right_out, avg_out):
    columns, width = right_ref.shape[1:]
    factor = factor_ref[0]
    mix = (1 - stat_decay) * factor * factor
    full = full_ref[0]
    grad = grad_ref[0]
    at = lax.axis_index("fsdp") * columns + lax.broadcasted_iota(jnp.int32, (columns, width), 0)
    pick = (at == lax.broadcasted_iota(jnp.int32, (columns, width), 1)).astype(BF16)
    turned = dot(pick, full, 1, 1).astype(BF16)
    left_out[0] = stat_decay * left_ref[0] + mix * dot(grad.astype(BF16), full, 1, 1)
    right_out[0] = stat_decay * right_ref[0] + mix * dot(turned, full, 1, 0)
    part = dot(root_ref[0].astype(BF16), full, 1, 0)
    update = dot(part.astype(BF16), whole_ref[0], 1, 0) * factor
    w = w_ref[0]
    new = w - rate_shampoo * (update + shampoo_decay * w)
    new_ref[0] = new
    clip_ref[0] = grad * factor
    avg_out[0] = ema_decay * avg_ref[0] + (1 - ema_decay) * new

def shampoo(factor, w, grad, left, right, root, whole_root, full, avg, name):
    def one(x):
        return pl.BlockSpec((1,) + x.shape[1:], lambda i: (i, 0, 0))
    ins = (w, grad, left, right, root, whole_root, full, avg)
    outs = (w, w, left, right, w)
    return pl.pallas_call(
        shampoo_kernel, grid=(w.shape[0],), name=name, cost_estimate=cost(10),
        in_specs=[pl.BlockSpec(memory_space=pltpu.SMEM)] + [one(x) for x in ins],
        out_specs=[one(x) for x in outs], out_shape=[jax.ShapeDtypeStruct(x.shape, F32) for x in outs],
        compiler_params=params())(factor.reshape(1), *ins)
MASK_ID = 50257
STRATA = 16
STEP = 10

clip_level = 1.0
beta_one = 0.9
beta_two = 0.95
adam_eps = 1e-08
adam_decay = 0.01
rate_embed = 2.0
rate_out = 0.25
rate_gain = 0.5
rate_shampoo = 0.3
shampoo_decay = 0.01
stat_decay = 0.5
ema_decay = 0.7


def rotary_tables(length, half_width):
    inverse = 10000.0 ** (-np.arange(half_width, dtype=np.float64) / half_width)
    angles = inverse[:, None] * np.arange(length, dtype=np.float64)[None, :]
    return (jnp.asarray(np.cos(angles), F32), jnp.asarray(np.sin(angles), F32))


def adamw(weight, moment_one, moment_two, gradient, step_rate):
    one_new = beta_one * moment_one + (1 - beta_one) * gradient
    two_new = beta_two * moment_two + (1 - beta_two) * gradient * gradient
    one_hat = one_new * (1 / (1 - beta_one**STEP))
    two_hat = two_new * (1 / (1 - beta_two**STEP))
    weight_new = weight - step_rate * (
        one_hat / (jnp.sqrt(two_hat) + adam_eps) + adam_decay * weight
    )
    return (weight_new, one_new, two_new)


def dp_other(x):
    return lax.ppermute(x, "dp", [(0, 1), (1, 0)])


def dp_sum(x):
    count = lax.axis_size("dp")
    if count == 1:
        return x.astype(F32)
    if count == 2:
        return x.astype(F32) + dp_other(x).astype(F32)
    return lax.psum(x, "dp").astype(F32)


def spread_out(x):
    return lax.all_gather(x.astype(BF16), "fsdp", axis=1, tiled=True)


def per_device(
    tokens, positions, strata, groups, embedding, out_table, norm_gains, attention, feedforward,
    embed_moment_one, embed_moment_two, out_moment_one, out_moment_two, gain_moment_one, gain_moment_two,
    attention_left, attention_right, attention_left_root, attention_right_root,
    ff_left, ff_right, ff_left_root, ff_right_root,
    ema_embed, ema_out, ema_gains, ema_attention, ema_feedforward,
):
    fs = lax.axis_size("fsdp")
    dps = lax.axis_size("dp")
    me = lax.axis_index("fsdp")
    replica = lax.axis_index("dp")
    seq_count, length = tokens.shape
    slots = positions.shape[1]
    features, vocab = embedding.shape
    width = features * fs
    shard = out_table.shape[0]

    ff_w = spread_out(feedforward)

    counts = jnp.maximum(1, (strata + 1) * slots * (1 + groups) // (2 * STRATA))
    in_use = jnp.arange(slots, dtype=jnp.int32)[None, :] < counts[:, None]
    places = jnp.arange(length, dtype=jnp.int32)
    same = positions[0][:, None] == places[None, :]
    marked = jnp.any(same & in_use[0][:, None], axis=0)
    ids_in = jnp.where(marked, MASK_ID, tokens[0])
    targets = jnp.sum(jnp.where(same, tokens[0][None, :], 0), axis=1)
    packed = jnp.concatenate([ids_in, targets, counts])
    packed = jnp.pad(packed, (0, -packed.shape[0] % 1024))
    low, turned = table_both(out_table)
    packed, low, turned = lax.optimization_barrier((packed, low, turned))
    everyone, xT, attn_w = front(packed.reshape(-1, 128), attention.reshape(-1, width), embedding, length, 1)
    everyone = everyone.reshape(fs * dps, -1)
    xT = xT.reshape(width, length)
    attn_w = attn_w.reshape(fs, 4, -1, width)
    group = lax.dynamic_slice_in_dim(everyone, replica * fs, fs, 0)
    all_ids = everyone[:, :length]
    group_ids = group[:, :length]
    group_targets = group[:, length:length + slots]
    group_counts = group[:, length + slots]

    cosT, sinT = rotary_tables(length, HEAD // 2)
    gain = [norm_gains.T] * 3
    place = positions[0][:, None]
    hT, qT, kT, vT, mixT, lse = attn_fwd(xT, gain[0], cosT, sinT, attn_w)
    x2, h2, x3, head = ff_fwd(xT, mixT, gain[1], gain[2], place, attn_w, ff_w)

    rows = rows_gather(head, 3)
    first_id = me * shard
    limit = jnp.clip(MASK_ID - first_id, 0, shard).reshape(1)
    least = min(shard, MASK_ID - (fs - 1) * shard)
    meta, seq, slot, weight = plan(group_counts, slots, length)
    nblk = seq.shape[0] // RB
    target = (spread(group_targets, seq, slot) - first_id).reshape(nblk, 1, RB)
    inside = fs * slots <= 4096
    if not inside:
        rows = jnp.take(rows.reshape(fs * slots, width), jnp.clip(seq * slots + slot, 0, fs * slots - 1), axis=0)
    comp, lse_own, chosen = vocab_fwd(meta, limit, rows, low, target, least)
    lse_own, root = lax.optimization_barrier((lse_own, attention_right_root))
    attn_root = spread_out(root)
    lse_sum = small_gather(lse_own, 4, finish=lse_finish, name="lse_gather")
    own_loss = jnp.sum(weight * (jnp.where(seq == me, lse_sum.reshape(-1), 0.0) - chosen.reshape(-1)))
    scale = weight / (seq_count * fs * dps)
    out_one, out_two, row_grads = vocab_bwd(
        meta, limit, comp, low, turned, target, lse_sum, scale.reshape(nblk, 1, RB),
        least, fs, slots, inside,
    )
    if not inside:
        at = jnp.arange(slots, dtype=jnp.int32)[None, :]
        row_grads = jnp.take(row_grads, jnp.minimum(meta[1][:, None] * 16 + at, seq.shape[0] - 1), axis=0)
        row_grads = jnp.where((at < group_counts[:, None])[:, :, None], row_grads, 0)
    own_rows = rows_reduce(row_grads, 5)
    halves_low = (out_one, out_two)
    if dps == 2:
        others = [dp_other(x) for x in halves_low]

    own_rows, attn_root, root = lax.optimization_barrier((own_rows, attn_root, ff_right_root))
    ff_root = spread_out(root)
    second, gg2, gg3, dff = ff_bwd(x3, x2, h2, own_rows, place, gain[1], gain[2], ff_w, fs)
    if dps == 2:
        second, others[0], ff_root = lax.optimization_barrier((second, others[0], ff_root))
    first, gg1, dattn = attn_bwd(xT, gain[0], cosT, sinT, second, hT, qT, kT, vT, mixT, lse, attn_w, fs)

    ff_part = lax.psum_scatter(dff.reshape(-1, width), "fsdp", scatter_dimension=0, tiled=True)

    aux = jnp.concatenate([jnp.concatenate([gg1, gg2, gg3], axis=1).T.reshape(-1), own_loss[None]])
    aux = jnp.pad(aux, (0, -aux.shape[0] % 1024)).reshape(-1, 128)
    if dps == 2:
        first, others[1] = lax.optimization_barrier((first, others[1]))
        pairs = (halves_low[0], others[0], halves_low[1], others[1])
    else:
        pairs = ()
        out_grad = jnp.concatenate([dp_sum(a) for a in halves_low])[:shard]
        out_sq = jnp.sum(out_grad * out_grad)
    out = list(exchange(first.reshape(fs, features, length), 6, dps == 2, "gradients", aux, dattn.reshape(fs, -1, width), pairs))
    if dps == 2:
        out_sq = jnp.sum(out.pop())
    attn_grad = out[-1].reshape(4, -1, width)
    aux, ff_part = lax.optimization_barrier((out[-2], ff_part))
    ff_grad = dp_sum(ff_part.reshape(2, -1, width))
    if dps != 2:
        attn_grad = dp_sum(attn_grad.astype(BF16))
    if dps == 2:
        parts, other = out[:2]
        other_ids = lax.dynamic_slice_in_dim(everyone, (1 - replica) * fs, fs, 0)[:, :length]
        embed_grad, embed_sq = scatter(jnp.concatenate([group_ids, other_ids]), (parts, other), vocab, 2)
        embed_sq = jnp.sum(embed_sq)
    else:
        parts = out[0]
        embed_grad = dp_sum(scatter(group_ids, (parts,), vocab, 2)[0])
        embed_sq = jnp.sum(embed_grad * embed_grad)
        if dps > 1:
            aux = lax.psum(aux, "dp")
    aux = aux.reshape(-1)
    gain_grad, loss_sum = aux[: 3 * width].reshape(3, width), aux[3 * width]
    squares = (
        jnp.sum(attn_grad * attn_grad)
        + jnp.sum(ff_grad * ff_grad)
        + embed_sq
        + out_sq
    )
    ff_grad, embed_sq = lax.optimization_barrier((ff_grad, embed_sq))
    attn_full, ff_full = spread_out(attn_grad), spread_out(ff_grad)
    squares, attn_full = lax.optimization_barrier((squares, attn_full))
    squares = small_gather(jnp.full((8, 128), squares), 7, finish=sum_finish, name="squares")[0, 0]
    clip_norm = jnp.sqrt(squares + jnp.sum(gain_grad * gain_grad))
    factor = jnp.minimum(1.0, clip_level / clip_norm)
    embed_new, embed_one_new, embed_two_new, ema_embed_new = adam_table(
        factor, embedding, embed_moment_one, embed_moment_two, ema_embed, [embed_grad], rate_embed, False
    )
    if dps == 2:
        out_new, out_one_new, out_two_new, ema_out_new = adam_table(
            factor, out_table, out_moment_one, out_moment_two, ema_out,
            [halves_low[0], others[0], halves_low[1], others[1]], rate_out, True
        )
    else:
        out_new, out_one_new, out_two_new = adamw(
            out_table, out_moment_one, out_moment_two, out_grad * factor, rate_out
        )
        ema_out_new = ema_decay * ema_out + (1 - ema_decay) * out_new
    gains_new, gains_one_new, gains_two_new = adamw(
        norm_gains, gain_moment_one, gain_moment_two, gain_grad * factor, rate_gain
    )

    attention_new, attn_clip, attention_left_new, attention_right_new, ema_attn_new = shampoo(
        factor, attention, attn_grad, attention_left, attention_right, attention_left_root,
        attn_root, attn_full, ema_attention, "shampoo_attention"
    )
    ff_new, ff_clip, ff_left_new, ff_right_new, ema_ff_new = shampoo(
        factor, feedforward, ff_grad, ff_left, ff_right, ff_left_root,
        ff_root, ff_full, ema_feedforward, "shampoo_ff"
    )

    def averaged(average, new):
        return ema_decay * average + (1 - ema_decay) * new

    return (
        loss_sum, clip_norm, embed_new, embed_one_new, embed_two_new, out_new, out_one_new, out_two_new,
        gains_new, gains_one_new, gains_two_new, attention_new, attn_clip, attention_left_new, attention_right_new,
        ff_new, ff_clip, ff_left_new, ff_right_new,
        ema_embed_new, ema_out_new, averaged(ema_gains, gains_new),
        ema_attn_new, ema_ff_new,
    )


def solution(mesh):
    seqs, rows, stack, none = P(("dp", "fsdp")), P("fsdp", None), P(None, "fsdp", None), P()
    in_specs = (
        seqs, seqs, seqs, seqs, rows, rows, none, stack, stack, rows, rows, rows, rows, none, none,
        stack, stack, stack, stack, stack, stack, stack, stack, rows, rows, none, stack, stack,
    )
    out_specs = (
        none, none, rows, rows, rows, rows, rows, rows, none, none, none, stack, stack, stack, stack,
        stack, stack, stack, stack, rows, rows, none, stack, stack,
    )
    return jax.shard_map(
        per_device, mesh=mesh, in_specs=in_specs, out_specs=out_specs, check_vma=False
    )
```
